32 devices in a mesh: shard: 8 (over y, x, core), rep: 4 (over z).
Axes of the slice: x: 2, y: 2, z: 4, core: 2. Of those that a mesh axis runs over, the one named last changes fastest.
Arguments:
- source: bfloat16 [32, 384, 512], P(('shard', 'rep')), may hold values from -6 to 6
- target: bfloat16 [32, 384, 512], P(('shard', 'rep')), may hold values from -6 to 6
- source_seg: int32 [32, 384], P(('shard', 'rep')), may hold values from 0 to 32, as said below
- target_seg: int32 [32, 384], P(('shard', 'rep')), may hold values from 0 to 32, as said below
- attn_in: bfloat16 [3, 512, 1536], P(None, 'shard'), may hold values from -0.25 to 0.25
- attn_out: bfloat16 [3, 512, 512], P(None, 'shard'), may hold values from -0.75 to 0.75
- ffn_up: bfloat16 [2, 512, 2048], P(None, 'shard'), may hold values from -0.25 to 0.25
- ffn_down: bfloat16 [2, 2048, 512], P(None, 'shard'), may hold values from -0.125 to 0.125
- norm_gain: bfloat16 [5, 512], P(None, 'shard'), may hold values from 0.5 to 1.5
- norm_bias: bfloat16 [5, 512], P(None, 'shard'), may hold values from -3 to 3
- cotangent: bfloat16 [32, 384, 512], P(('shard', 'rep')), may hold values from -6 to 6
Outputs:
- decoded: bfloat16 [32, 384, 512], P(('shard', 'rep'))
- source_grad: float32 [32, 384, 512], P(('shard', 'rep'))
- target_grad: float32 [32, 384, 512], P(('shard', 'rep'))
- attn_in_grad: float32 [3, 512, 1536], P(None, 'shard')
- attn_out_grad: float32 [3, 512, 512], P(None, 'shard')
- ffn_up_grad: float32 [2, 512, 2048], P(None, 'shard')
- ffn_down_grad: float32 [2, 2048, 512], P(None, 'shard')
- gain_grad: float32 [5, 512], P(None, 'shard')
- bias_grad: float32 [5, 512], P(None, 'shard')
The draws below stay inside these ranges and needn't reach their ends.
Inputs may be any that keep to these rules, and one draw needn't show every extreme that they name: `source_seg`: per sequence the ids are 1, 2, ... in order along the tokens (each a document of consecutive tokens, the first token in document 1), followed by 1 to 96 padding tokens with id 0 at the end; a sequence holds at most min(32, 96) documents, and some sequence holds that many in every draw; a source sequence and its target sequence hold the same number of documents. `target_seg`: as for source_seg, with the same number of documents as the source sequence of the same index.
All inputs are finite; a program needn't handle non-finite values.
Results may differ from the reference program's by a relative error of at most 0.023.
Values may be sent and summed in bfloat16 or wider, within the bound.
No kernel may reach another device: no remote copies, remote signals or barrier semaphores. Data moves between devices by JAX's collectives and lax.ppermute only.
A program may use at most 192 MiB of HBM per device.

```python
import jax
import jax.numpy as jnp
from jax import lax

D = 512
HEADS = 8
HEAD = 64
FF = 2048
LEN = 384
SEQS = 32


def doc_counts(key):
    power = jax.random.randint(jax.random.fold_in(key, 7), (SEQS,), 0, 6)
    power = jnp.where(jnp.arange(SEQS) == 0, 5, power)
    counts = jnp.left_shift(jnp.ones_like(power), power)
    return jnp.minimum(counts, LEN // 4).astype(jnp.int32)


def segment_ids(key, salt):
    counts = doc_counts(key)
    inner = jax.random.fold_in(key, salt)
    padding = jax.random.randint(jax.random.fold_in(inner, 1), (SEQS, 1), 1, LEN // 4 + 1)
    used = LEN - padding
    place = jnp.arange(LEN, dtype=jnp.int32)[None, :]
    noise = jax.random.randint(jax.random.fold_in(inner, 2), (SEQS, LEN), 0, LEN)
    score = noise * (2 * LEN) + place
    score = jnp.where((place >= 1) & (place < used), score, score + 4 * LEN * LEN)
    order = jnp.argsort(score, axis=1, stable=True)
    ranks = jnp.argsort(order, axis=1, stable=True)
    starts = ((ranks < counts[:, None] - 1) | (place == 0)).astype(jnp.int32)
    ident = jnp.cumsum(starts, axis=1)
    return jnp.where(place < used, ident, 0).astype(jnp.int32)


def draw_source_seg(key, part):
    return segment_ids(key, 11)


def draw_target_seg(key, part):
    return segment_ids(key, 13)


def block_levels(key, dims, cuts, smallest, largest):
    factor_of = 1.0
    for position, shards_of in cuts:
        steps = jax.random.uniform(jax.random.fold_in(jax.random.fold_in(key, 6), position), (shards_of,), jnp.float32, smallest / len(cuts), largest / len(cuts))
        factor_of = factor_of * jnp.repeat(jnp.exp(steps), dims[position] // shards_of).reshape((-1,) + (1,) * (len(dims) - 1 - position))
    return factor_of


def normal_values(key, extent, width, most, split=(), kind=jnp.bfloat16):
    entries = jax.random.normal(key, extent, jnp.float32) * width
    if len(split) > 0:
        entries = block_levels(key, extent, split, -0.22, 0.18) * entries
    return jnp.clip(entries, min=-most, max=most).astype(kind)


def setup_inputs(seed: int = 0) -> dict:
    key_list = jax.random.split(jax.random.key(seed), 12)
    source = normal_values(key_list[0], (SEQS, LEN, D), 1.0, 6.0, ((0, 32),))
    target = normal_values(key_list[1], (SEQS, LEN, D), 1.0, 6.0, ((0, 32),))
    source_seg = draw_source_seg(jax.random.fold_in(key_list[11], 71), 0)
    target_seg = draw_target_seg(jax.random.fold_in(key_list[11], 71), 0)
    attn_in = normal_values(key_list[4], (3, D, 3 * D), D ** -0.5, 0.25, ((1, 8),))
    attn_out = normal_values(key_list[5], (3, D, D), (D // 8) ** -0.5, 0.75, ((1, 8),))
    ffn_up = normal_values(key_list[6], (2, D, FF), D ** -0.5, 0.25, ((1, 8),))
    ffn_down = normal_values(key_list[7], (2, FF, D), FF ** -0.5, 0.125, ((1, 8),))
    norm_gain = jnp.clip(1.0 + 0.1 * jax.random.normal(key_list[8], (5, D), jnp.float32), 0.5, 1.5).astype(jnp.bfloat16)
    norm_bias = normal_values(key_list[9], (5, D), 0.5, 3.0, ((1, 8),))
    cotangent = normal_values(key_list[10], (SEQS, LEN, D), 1.0, 6.0, ((0, 32),))
    return dict(source=source, target=target, source_seg=source_seg, target_seg=target_seg, attn_in=attn_in, attn_out=attn_out, ffn_up=ffn_up, ffn_down=ffn_down, norm_gain=norm_gain, norm_bias=norm_bias, cotangent=cotangent)


@jax.custom_vjp
def low(v):
    return lax.optimization_barrier(v.astype(jnp.bfloat16)).astype(jnp.float32)

@jax.custom_vjp
def low_back(v):
    return v

def low_keep(v):
    return (low(v), None)

def low_pass(kept, grad):
    return (grad,)

def back_keep(v):
    return (v, None)

def back_low(kept, grad):
    return (low(grad),)
low.defvjp(low_keep, low_pass)
low_back.defvjp(back_keep, back_low)

def both_ways(value):
    return low(low_back(value))

def matmul(left, right):
    return jnp.dot(left, right, precision=lax.Precision.HIGHEST, preferred_element_type=jnp.float32)

def layer_norm(value, gain, shift):
    mean = lax.optimization_barrier(jnp.mean(value, axis=-1, keepdims=True))
    centred = value - mean
    variance = lax.optimization_barrier(jnp.mean(centred * centred, axis=-1, keepdims=True))
    return centred * lax.rsqrt(variance + 1e-05) * gain + shift

def attend(query_in, memory_in, w_in, w_out, allowed):
    rows = query_in.shape[0]
    cols = memory_in.shape[0]
    query = both_ways(matmul(low(query_in), w_in[:, :D]))
    pairs = matmul(low(memory_in), w_in[:, D:])
    keys = both_ways(pairs[:, :D])
    values = both_ways(pairs[:, D:])
    scores = jnp.einsum('qhd,khd->hqk', query.reshape(rows, HEADS, HEAD), keys.reshape(cols, HEADS, HEAD), precision=lax.Precision.HIGHEST) * HEAD ** (-0.5)
    scores = low_back(scores)
    scores = jnp.where(allowed[None], scores, -1e+30)
    top = lax.optimization_barrier(jnp.max(scores, axis=-1, keepdims=True))
    weights = jnp.exp(scores - top)
    probs = weights / lax.optimization_barrier(jnp.sum(weights, axis=-1, keepdims=True))
    mixed = jnp.einsum('hqk,khd->qhd', low(probs), values.reshape(cols, HEADS, HEAD), precision=lax.Precision.HIGHEST)
    mixed = both_ways(mixed.reshape(rows, D))
    return low_back(matmul(mixed, w_out))

def feed_forward(hidden, w_up, w_down):
    pre = low_back(matmul(low(hidden), w_up))
    return low_back(matmul(low(jax.nn.gelu(pre, approximate=True)), w_down))

def layers(src, tgt, attn_in, attn_out, ffn_up, ffn_down, gain, shift, src_seg, tgt_seg):
    length = tgt.shape[0]
    place = jnp.arange(length)
    self_mask = src_seg[:, None] == src_seg[None, :]
    causal = (tgt_seg[:, None] == tgt_seg[None, :]) & (place[:, None] >= place[None, :])
    cross = tgt_seg[:, None] == src_seg[None, :]
    first = layer_norm(src + attend(src, src, attn_in[0], attn_out[0], self_mask), gain[0], shift[0])
    encoded = layer_norm(first + feed_forward(first, ffn_up[0], ffn_down[0]) + src, gain[1], shift[1])
    dec_one = layer_norm(tgt + attend(tgt, tgt, attn_in[1], attn_out[1], causal), gain[2], shift[2])
    dec_two = layer_norm(dec_one + attend(dec_one, encoded, attn_in[2], attn_out[2], cross), gain[3], shift[3])
    return layer_norm(dec_two + feed_forward(dec_two, ffn_up[1], ffn_down[1]) + tgt, gain[4], shift[4])

def reference(source, target, source_seg, target_seg, attn_in, attn_out, ffn_up, ffn_down, norm_gain, norm_bias, cotangent):
    weights = tuple((w.astype(jnp.float32) for w in (attn_in, attn_out, ffn_up, ffn_down, norm_gain, norm_bias)))

    def one(carry, item):
        src, tgt, src_seg, tgt_seg, cot = item

        def run(src_f, tgt_f, w_in, w_out, w_up, w_down, gain, shift):
            return layers(src_f, tgt_f, w_in, w_out, w_up, w_down, gain, shift, src_seg, tgt_seg)
        out, pull = jax.vjp(run, src.astype(jnp.float32), tgt.astype(jnp.float32), *weights)
        grads = pull(cot.astype(jnp.float32))
        carry = tuple((c + g for c, g in zip(carry, grads[2:])))
        return (carry, (out.astype(jnp.bfloat16), grads[0], grads[1]))
    init = tuple((jnp.zeros(w.shape, jnp.float32) for w in weights))
    sums, outs = lax.scan(one, init, (source, target, source_seg, target_seg, cotangent))
    return (outs[0], outs[1], outs[2], sums[0], sums[1], sums[2], sums[3], sums[4], sums[5])
```

```python
import functools

import jax
import jax.numpy as jnp
from jax import lax
from jax.sharding import PartitionSpec as P

HEAD = 64


EPS = 1e-05
NEG = -1e30


def as_sent(value):
    return jax.tree.map(lambda a: a.astype(jnp.bfloat16) if a.dtype == jnp.float32 else a, value)


def matmul(left, right):
    return jnp.dot(left, right, preferred_element_type=jnp.float32)


def matmul_right_t(left, right):
    return lax.dot_general(
        left, right, (((1,), (1,)), ((), ())), preferred_element_type=jnp.float32
    )


def outer_sum(left, right):
    return jnp.einsum("ti,tj->ij", left, right, preferred_element_type=jnp.float32)


def split_heads(value):
    return value.reshape(value.shape[0], value.shape[1] // HEAD, HEAD)


def smooth_gate(value):
    return jax.nn.gelu(value, approximate=True)


def scores_of(query, keys, allowed):
    scores = jnp.einsum(
        "qhd,khd->hqk", split_heads(query), split_heads(keys), preferred_element_type=jnp.float32
    ) * HEAD ** (-0.5)
    return jnp.where(allowed[None], scores, NEG)


def attend_forward(query_in, memory_in, w_in, w_out, allowed):
    width = w_in.shape[0]
    query = matmul(query_in, w_in[:, :width]).astype(jnp.bfloat16)
    pairs = matmul(memory_in, w_in[:, width:]).astype(jnp.bfloat16)
    keys = pairs[:, :width]
    values = pairs[:, width:]
    scores = scores_of(query, keys, allowed)
    top = jnp.max(scores, axis=-1, keepdims=True)
    weights = jnp.exp(scores - top)
    total = jnp.sum(weights, axis=-1, keepdims=True)
    probs = (weights / total).astype(jnp.bfloat16)
    mixed = jnp.einsum(
        "hqk,khd->qhd", probs, split_heads(values), preferred_element_type=jnp.float32
    )
    mixed = mixed.reshape(query.shape[0], width).astype(jnp.bfloat16)
    return (matmul(mixed, w_out), (query, keys, values, top + jnp.log(total), mixed))


def attend_backward(grad, query_in, memory_in, w_in, w_out, allowed, kept):
    query, keys, values, lse, mixed = kept
    width = w_in.shape[0]
    rows = query.shape[0]
    cols = keys.shape[0]
    scale = HEAD ** (-0.5)
    grad_low = grad.astype(jnp.bfloat16)
    out_weight_grad = outer_sum(mixed, grad_low)
    mixed_grad = matmul_right_t(grad_low, w_out).astype(jnp.bfloat16)
    probs = jnp.exp(scores_of(query, keys, allowed) - lse)
    prob_grad = jnp.einsum(
        "qhd,khd->hqk",
        split_heads(mixed_grad),
        split_heads(values),
        preferred_element_type=jnp.float32,
    )
    delta = jnp.sum(probs * prob_grad, axis=-1, keepdims=True)
    score_grad = (probs * (prob_grad - delta)).astype(jnp.bfloat16)
    query_grad = (
        jnp.einsum(
            "hqk,khd->qhd", score_grad, split_heads(keys), preferred_element_type=jnp.float32
        )
        * scale
    )
    query_grad = query_grad.reshape(rows, width).astype(jnp.bfloat16)
    key_grad = (
        jnp.einsum(
            "hqk,qhd->khd", score_grad, split_heads(query), preferred_element_type=jnp.float32
        )
        * scale
    )
    key_grad = key_grad.reshape(cols, width).astype(jnp.bfloat16)
    value_grad = jnp.einsum(
        "hqk,qhd->khd",
        probs.astype(jnp.bfloat16),
        split_heads(mixed_grad),
        preferred_element_type=jnp.float32,
    )
    value_grad = value_grad.reshape(cols, width).astype(jnp.bfloat16)
    pair_grad = jnp.concatenate([key_grad, value_grad], axis=1)
    in_weight_grad = jnp.concatenate(
        [outer_sum(query_in, query_grad), outer_sum(memory_in, pair_grad)], axis=1
    )
    back_query = matmul_right_t(query_grad, w_in[:, :width])
    back_memory = matmul_right_t(pair_grad, w_in[:, width:])
    return (back_query, back_memory, in_weight_grad, out_weight_grad)


def feed_forward(hidden_low, w_up, w_down):
    pre = matmul(hidden_low, w_up)
    active = smooth_gate(pre).astype(jnp.bfloat16)
    return (matmul(active, w_down), (pre, active))


def feed_backward(grad, hidden_low, w_up, w_down, kept):
    pre, active = kept
    grad_low = grad.astype(jnp.bfloat16)
    down_grad = outer_sum(active, grad_low)
    upstream = matmul_right_t(grad_low, w_down)
    gate_value, gate_pull = jax.vjp(smooth_gate, pre)
    pre_grad = gate_pull(upstream)[0].astype(jnp.bfloat16)
    up_grad = outer_sum(hidden_low, pre_grad)
    return (matmul_right_t(pre_grad, w_up), up_grad, down_grad)


def norm_forward(value, gain, shift):
    mean = jnp.mean(value, axis=-1, keepdims=True)
    centred = value - mean
    scale = lax.rsqrt(jnp.mean(centred * centred, axis=-1, keepdims=True) + EPS)
    normal = centred * scale
    return (normal * gain + shift, (normal, scale))


def norm_backward(grad, kept, gain):
    normal, scale = kept
    gain_grad = jnp.sum(grad * normal, axis=0)
    shift_grad = jnp.sum(grad, axis=0)
    inner = grad * gain
    value_grad = scale * (
        inner
        - jnp.mean(inner, axis=-1, keepdims=True)
        - normal * jnp.mean(inner * normal, axis=-1, keepdims=True)
    )
    return (value_grad, gain_grad, shift_grad)


def swap(value, axis, size, bit):
    return lax.ppermute(value, axis, [(i, i ^ bit) for i in range(size)])


CORE, X, Y = 1, 2, 4
Z1, Z2 = 1, 2


def on_chip_order(parts, me):
    for bit in (CORE, X, Y):
        flipped = jnp.stack([parts[k ^ bit] for k in range(8)])
        parts = jnp.where((me & bit) != 0, flipped, parts)
    return parts


def gather_two(first, second, me):
    sw = lambda v, bit: swap(v, "shard", 8, bit)
    first_x, second_y = sw(first, X), sw(second, Y)
    first_y, second_x = sw(first, Y), sw(second, X)
    first_xy, second_xy = sw(first_x, Y), sw(second_y, X)
    out = []
    for own, by_x, by_y, by_xy in (
        (first, first_x, first_y, first_xy),
        (second, second_x, second_y, second_xy),
    ):
        mine = jnp.stack([own, by_x, by_y, by_xy])
        other = sw(mine, CORE)
        parts = jnp.stack([mine[0], other[0], mine[1], other[1], mine[2], other[2], mine[3], other[3]])
        whole = on_chip_order(parts, me)
        out.append(whole.reshape((8 * own.shape[0],) + own.shape[1:]))
    return out


def add_low(left, right):
    return (left.astype(jnp.float32) + right.astype(jnp.float32)).astype(jnp.bfloat16)


def scatter_sum(whole, me, order):
    sw = lambda v, bit: swap(v, "shard", 8, bit)
    parts = whole.reshape((8, whole.shape[0] // 8) + whole.shape[1:])
    parts = on_chip_order(parts, me)
    a, b = order
    keep_core = [parts[0], parts[b], parts[a], parts[a | b]]
    send_core = [parts[1], parts[b | 1], parts[a | 1], parts[a | b | 1]]
    got = sw(jnp.stack(send_core), CORE)
    keep = add_low(jnp.stack(keep_core[:2]), got[:2])
    send = add_low(jnp.stack(keep_core[2:]), got[2:])
    got = sw(send, a)
    keep, send = add_low(keep[0], got[0]), add_low(keep[1], got[1])
    return add_low(keep, sw(send, b))


def sum_replicas(own, z):
    sw = lambda v, bit: swap(v, "rep", 4, bit)
    half = own.shape[0] // 2
    odd = (z & 1) != 0
    low, high = own[:half], own[half:]
    got = sw(jnp.where(odd, low, high), Z1)
    part = lax.optimization_barrier(add_low(jnp.where(odd, high, low), got))
    part = lax.optimization_barrier(add_low(part, sw(part, Z2)))
    other = sw(part, Z1)
    return jnp.where(odd, jnp.concatenate([other, part]), jnp.concatenate([part, other])).astype(jnp.float32)


def gather_weights(attn_in, attn_out, ffn_up, ffn_down, gain, shift, me, size):
    att = [jnp.concatenate([attn_in[k], attn_out[k]], axis=1) for k in range(3)]
    small = jnp.concatenate([gain, shift], axis=0)
    if size != 8:
        whole = lambda v: lax.all_gather(v, "shard", axis=0, tiled=True)
        norm = lax.all_gather(small, "shard", axis=1, tiled=True).astype(jnp.float32)
        return [whole(v) for v in att], [whole(ffn_up[k]) for k in range(2)], [whole(ffn_down[k]) for k in range(2)], norm
    parts = small[None]
    for bit in (CORE, X, Y):
        parts = jnp.concatenate([parts, swap(parts, "shard", 8, bit)])
    norm = on_chip_order(parts, me)
    norm = jnp.moveaxis(norm, 0, 1).reshape(small.shape[0], -1).astype(jnp.float32)
    w0, w1 = gather_two(att[0], att[1], me)
    u0, d0 = gather_two(ffn_up[0], ffn_down[0].reshape(ffn_up[0].shape[0], -1), me)
    left, right = gather_two(att[2][:, :1024], att[2][:, 1024:], me)
    w2 = jnp.concatenate([left, right], axis=1)
    u1, d1 = gather_two(ffn_up[1], ffn_down[1].reshape(ffn_up[1].shape[0], -1), me)
    down = lambda d, like: d.reshape(8 * like.shape[0], like.shape[1])
    return [w0, w1, w2], [u0, u1], [down(d0, ffn_down[0]), down(d1, ffn_down[1])], norm


def owned_sum(whole, me, z, order, sizes):
    if sizes == (8, 4):
        return sum_replicas(scatter_sum(whole, me, order), z)
    own = lax.psum_scatter(whole, "shard", scatter_dimension=0, tiled=True)
    return lax.psum(own, "rep").astype(jnp.float32)


def owned_norm(whole, me, sizes):
    if sizes == (8, 4):
        for bit in (CORE, X, Y):
            whole = whole + swap(whole, "shard", 8, bit)
        for bit in (Z1, Z2):
            whole = whole + swap(whole, "rep", 4, bit)
    else:
        whole = lax.psum(whole, ("shard", "rep"))
    wide = whole.shape[1] // sizes[0]
    return lax.dynamic_slice_in_dim(whole, me * wide, wide, axis=1)


def shards(sizes, source, target, source_seg, target_seg, attn_in, attn_out, ffn_up, ffn_down, norm_gain, norm_bias, cotangent):
    me = lax.axis_index("shard")
    z = lax.axis_index("rep")
    wide = attn_out.shape[2]
    att, ups, downs, norm = gather_weights(attn_in, attn_out, ffn_up, ffn_down, norm_gain, norm_bias, me, sizes[0])
    w_in = [w[:, : 3 * wide] for w in att]
    w_out = [w[:, 3 * wide :] for w in att]
    gain, shift = norm[:5], norm[5:]
    src_low, tgt_low = source[0], target[0]
    src, tgt = src_low.astype(jnp.float32), tgt_low.astype(jnp.float32)
    src_ids, tgt_ids = source_seg[0], target_seg[0]
    place = jnp.arange(tgt_ids.shape[0])
    self_mask = src_ids[:, None] == src_ids[None, :]
    causal = (tgt_ids[:, None] == tgt_ids[None, :]) & (place[:, None] >= place[None, :])
    cross = tgt_ids[:, None] == src_ids[None, :]
    branch, kept_enc_att = attend_forward(src_low, src_low, w_in[0], w_out[0], self_mask)
    first, kept_n0 = norm_forward(src + branch, gain[0], shift[0])
    first_low = first.astype(jnp.bfloat16)
    branch, kept_enc_ffn = feed_forward(first_low, ups[0], downs[0])
    encoded, kept_n1 = norm_forward(first + branch + src, gain[1], shift[1])
    encoded_low = encoded.astype(jnp.bfloat16)
    branch, kept_self = attend_forward(tgt_low, tgt_low, w_in[1], w_out[1], causal)
    dec_one, kept_n2 = norm_forward(tgt + branch, gain[2], shift[2])
    dec_one_low = dec_one.astype(jnp.bfloat16)
    branch, kept_cross = attend_forward(dec_one_low, encoded_low, w_in[2], w_out[2], cross)
    dec_two, kept_n3 = norm_forward(dec_one + branch, gain[3], shift[3])
    dec_two_low = dec_two.astype(jnp.bfloat16)
    branch, kept_dec_ffn = feed_forward(dec_two_low, ups[1], downs[1])
    output, kept_n4 = norm_forward(dec_two + branch + tgt, gain[4], shift[4])
    decoded = output.astype(jnp.bfloat16)[None]
    grad = cotangent[0].astype(jnp.float32)
    low = lambda v: v.astype(jnp.bfloat16)
    last_grad, gain_four, shift_four = norm_backward(grad, kept_n4, gain[4])
    hidden_grad, up_one, down_one = feed_backward(last_grad, dec_two_low, ups[1], downs[1], kept_dec_ffn)
    up_one = owned_sum(low(up_one), me, z, (X, Y), sizes)
    down_one = owned_sum(low(down_one), me, z, (Y, X), sizes)
    two_grad, gain_three, shift_three = norm_backward(last_grad + hidden_grad, kept_n3, gain[3])
    query_back, encoded_grad, in_two, out_two = attend_backward(
        two_grad, dec_one_low, encoded_low, w_in[2], w_out[2], cross, kept_cross
    )
    att_two = owned_sum(jnp.concatenate([low(in_two), low(out_two)], axis=1), me, z, (X, Y), sizes)
    one_grad, gain_two, shift_two = norm_backward(two_grad + query_back, kept_n2, gain[2])
    enc_out_grad, gain_one, shift_one = norm_backward(encoded_grad, kept_n1, gain[1])
    hidden_grad, up_zero, down_zero = feed_backward(enc_out_grad, first_low, ups[0], downs[0], kept_enc_ffn)
    up_zero = owned_sum(low(up_zero), me, z, (X, Y), sizes)
    down_zero = owned_sum(low(down_zero), me, z, (Y, X), sizes)
    query_back, memory_back, in_one, out_one = attend_backward(
        one_grad, tgt_low, tgt_low, w_in[1], w_out[1], causal, kept_self
    )
    att_one = owned_sum(jnp.concatenate([low(in_one), low(out_one)], axis=1), me, z, (Y, X), sizes)
    tgt_grad = last_grad + one_grad + query_back + memory_back
    zero_grad, gain_zero, shift_zero = norm_backward(enc_out_grad + hidden_grad, kept_n0, gain[0])
    query_back, memory_back, in_zero, out_zero = attend_backward(
        zero_grad, src_low, src_low, w_in[0], w_out[0], self_mask, kept_enc_att
    )
    att_zero = owned_sum(jnp.concatenate([low(in_zero), low(out_zero)], axis=1), me, z, (X, Y), sizes)
    src_grad = enc_out_grad + zero_grad + query_back + memory_back
    norms = jnp.stack([gain_zero, gain_one, gain_two, gain_three, gain_four, shift_zero, shift_one, shift_two, shift_three, shift_four])
    norms = owned_norm(norms, me, sizes)
    atts = jnp.stack([att_zero, att_one, att_two])
    return (
        decoded,
        src_grad[None],
        tgt_grad[None],
        atts[:, :, : 3 * wide],
        atts[:, :, 3 * wide :],
        jnp.stack([up_zero, up_one]),
        jnp.stack([down_zero, down_one]),
        norms[:5],
        norms[5:],
    )


def solution(mesh):
    sizes = (mesh.shape["shard"], mesh.shape["rep"])
    tokens = P(("shard", "rep"), None, None)
    ids = P(("shard", "rep"), None)
    weight = P(None, "shard", None)
    norm = P(None, "shard")
    return jax.shard_map(
        functools.partial(shards, sizes),
        mesh=mesh,
        in_specs=(tokens, tokens, ids, ids, weight, weight, weight, weight, norm, norm, tokens),
        out_specs=(tokens, tokens, tokens, weight, weight, weight, weight, norm, norm),
        check_vma=False,
    )
```

```python
import functools

import jax
import jax.numpy as jnp
from jax import lax
from jax.experimental import pallas as pl
from jax.experimental.pallas import tpu as pltpu
from jax.sharding import PartitionSpec as P

HEAD = 64
PAIR = 2 * HEAD
EPS = 1e-05
NEG = -1e30
LOW = jnp.bfloat16
WIDE = jnp.float32
CORE, X, Y = 1, 2, 4
Z1, Z2 = 1, 2
VMEM = pl.BlockSpec(memory_space=pltpu.VMEM)
SMEM = pl.BlockSpec(memory_space=pltpu.SMEM)
ANY = pl.BlockSpec(memory_space=pl.ANY)


def dot(left, right):
    return lax.dot_general(left, right, (((1,), (0,)), ((), ())), preferred_element_type=WIDE)


def dot_nt(left, right):
    return lax.dot_general(left, right, (((1,), (1,)), ((), ())), preferred_element_type=WIDE)


def dot_tn(left, right):
    return lax.dot_general(left, right, (((0,), (0,)), ((), ())), preferred_element_type=WIDE)


def weight_copies(me, stacks, orders, whole, sems, columns=None):
    copies = []
    count = sum(len(order) for order in orders)
    rows = whole.shape[0] // count
    for stack, order in zip(stacks, orders):
        for place, k in enumerate(order):
            at = pl.ds(pl.multiple_of((me ^ k) * rows, rows), rows)
            dst = whole.at[at] if columns is None else whole.at[at, columns]
            copies.append(pltpu.make_async_copy(stack.at[place], dst, sems.at[len(copies)]))
    return copies


def grad_copies(me, whole, stacks, orders, sems):
    copies = []
    count = sum(len(order) for order in orders)
    rows = whole.shape[0] // count
    for stack, order in zip(stacks, orders):
        for place, k in enumerate(order):
            at = pl.ds(pl.multiple_of((me ^ k) * rows, rows), rows)
            copies.append(pltpu.make_async_copy(whole.at[at], stack.at[place], sems.at[len(copies)]))
    return copies


def start(copies):
    for copy in copies:
        copy.start()


def wait(copies):
    for copy in copies:
        copy.wait()


def norm(value, gain, shift):
    mean = jnp.mean(value, axis=-1, keepdims=True)
    centred = value - mean
    scale = lax.rsqrt(jnp.mean(centred * centred, axis=-1, keepdims=True) + EPS)
    normal = centred * scale
    return normal * gain + shift, normal, scale


def norm_back(grad, normal, scale, gain):
    gain_grad = jnp.sum(grad * normal, axis=0, keepdims=True)
    shift_grad = jnp.sum(grad, axis=0, keepdims=True)
    inner = grad * gain
    inner_mean = jnp.mean(inner, axis=-1, keepdims=True)
    cross_mean = jnp.mean(inner * normal, axis=-1, keepdims=True)
    return scale * (inner - inner_mean - normal * cross_mean), gain_grad, shift_grad


def lanes_of(head, value):
    lane = lax.broadcasted_iota(jnp.int32, value.shape, 1)
    return jnp.where((lane < HEAD) if head == 0 else (lane >= HEAD), value, jnp.zeros_like(value))


def pick(first, second):
    lane = lax.broadcasted_iota(jnp.int32, first.shape, 1)
    return jnp.where(lane < HEAD, first, second)


def allowed_bias(memory_ids, query_ids, causal):
    allowed = memory_ids == query_ids
    if causal:
        shape = (memory_ids.shape[0], query_ids.shape[1])
        allowed = allowed & (lax.broadcasted_iota(jnp.int32, shape, 1) >= lax.broadcasted_iota(jnp.int32, shape, 0))
    return jnp.where(allowed, 0.0, NEG)


def attend_forward(qkv, probs, mixed, bias):
    width = mixed.shape[1]
    for pair in range(width // PAIR):
        at = pl.ds(pair * PAIR, PAIR)
        query = qkv[:, pl.ds(pair * PAIR, PAIR)] * LOW(HEAD ** -0.5)
        keys = qkv[:, pl.ds(width + pair * PAIR, PAIR)]
        values = qkv[:, pl.ds(2 * width + pair * PAIR, PAIR)]
        out = []
        for head in range(2):
            scores = dot_nt(keys, lanes_of(head, query)) + bias[...]
            top = jnp.max(scores, axis=0, keepdims=True)
            weights = jnp.exp(scores - top)
            total = jnp.sum(weights, axis=0, keepdims=True)
            low = (weights * (1.0 / total)).astype(LOW)
            probs[2 * pair + head] = low
            out.append(dot_tn(low, values))
        mixed[:, at] = pick(*out).astype(LOW)


def attend_backward(qkv, probs, mixed_grad, qkv_grad):
    width = mixed_grad.shape[1]
    for pair in range(width // PAIR):
        query = qkv[:, pl.ds(pair * PAIR, PAIR)]
        keys = qkv[:, pl.ds(width + pair * PAIR, PAIR)]
        values = qkv[:, pl.ds(2 * width + pair * PAIR, PAIR)]
        grad = mixed_grad[:, pl.ds(pair * PAIR, PAIR)]
        dq, dk, dv = [], [], []
        for head in range(2):
            low = probs[2 * pair + head]
            prob = low.astype(WIDE)
            prob_grad = dot_nt(values, lanes_of(head, grad))
            delta = jnp.sum(prob * prob_grad, axis=0, keepdims=True)
            score_grad = (prob * (prob_grad - delta)).astype(LOW)
            dv.append(dot(low, grad))
            dk.append(dot(score_grad, query))
            dq.append(dot_tn(score_grad, keys))
        scale = HEAD ** -0.5
        qkv_grad[:, pl.ds(pair * PAIR, PAIR)] = (pick(*dq) * scale).astype(LOW)
        qkv_grad[:, pl.ds(width + pair * PAIR, PAIR)] = (pick(*dk) * scale).astype(LOW)
        qkv_grad[:, pl.ds(2 * width + pair * PAIR, PAIR)] = pick(*dv).astype(LOW)


GELU = 0.7978845608028654


def gelu_and_slope(value):
    square = value * value
    inner = GELU * value * (1.0 + 0.044715 * square)
    t = jnp.tanh(inner)
    half = 0.5 + 0.5 * t
    slope = half + 0.5 * value * (1.0 - t * t) * (GELU * (1.0 + 3 * 0.044715 * square))
    return value * half, slope


STEP = 512


def ffn_forward(hidden, up, down, active, slope):
    total = None
    for c in range(up.shape[1] // STEP):
        at = pl.ds(c * STEP, STEP)
        act, sl = gelu_and_slope(dot(hidden, up[:, at]))
        act = act.astype(LOW)
        active[:, at] = act
        slope[:, at] = sl.astype(LOW)
        part = dot(act, down[at, :])
        total = part if total is None else total + part
    return total


def ffn_backward_down(grad, active, down_grad):
    for c in range(active.shape[1] // STEP):
        at = pl.ds(c * STEP, STEP)
        down_grad[at, :] = dot_tn(active[:, at], grad).astype(LOW)


def ffn_backward_up(grad, hidden, up, down, slope, up_grad):
    total = None
    for c in range(up.shape[1] // STEP):
        at = pl.ds(c * STEP, STEP)
        z = (dot_nt(grad, down[at, :]) * slope[:, at].astype(WIDE)).astype(LOW)
        up_grad[:, at] = dot_tn(hidden, z).astype(LOW)
        part = dot_nt(z, up[:, at])
        total = part if total is None else total + part
    return total


class Plan:
    def __init__(self, sizes, dims):
        self.split = sizes == (8, 4)
        self.sizes = sizes
        self.length, self.width, self.hidden = dims
        self.heads = self.width // HEAD
        self.orders = [[0, 2, 4, 6], [1, 3, 5, 7]] if self.split else [[0]]
        self.n = len(self.orders)
        self.shards = 8 if self.split else 1

    def grad_orders(self, order):
        if not self.split:
            return [[0]]
        a, b = order
        return [[0, b], [a, a | b], [1, b | 1, a | 1, a | b | 1]]

    def grad_shapes(self, rows, cols, order):
        rows //= self.shards
        return [jax.ShapeDtypeStruct((len(o), rows, cols), LOW) for o in self.grad_orders(order)]

    def call(self, body, ins, outs, scratch, flops):
        return pl.pallas_call(
            body,
            in_specs=[spec for _, spec in ins],
            out_shape=[jax.ShapeDtypeStruct(shape, dtype) for shape, dtype, _ in outs],
            out_specs=[spec for _, _, spec in outs],
            scratch_shapes=scratch,
            compiler_params=pltpu.CompilerParams(vmem_limit_bytes=56 * 1024 * 1024),
            cost_estimate=pl.CostEstimate(flops=flops, bytes_accessed=8 << 20, transcendentals=0),
        )(*[value for value, _ in ins])


def self_attention(plan, place, tokens, id_row, id_col, stacks, norms, row, causal):
    L, W, H = plan.length, plan.width, plan.heads

    def body(place, tokens, id_row, id_col, norms, *rest):
        stacks, rest = rest[: plan.n], rest[plan.n :]
        out, out_low, normal, scale, qkv, mixed, probs, weight, bias, sems = rest
        copies = weight_copies(place[0], stacks, plan.orders, weight, sems)
        start(copies)
        bias[...] = allowed_bias(id_col[...], id_row[...], causal)
        wait(copies)
        x = tokens[...]
        qkv[...] = dot(x, weight[:, : 3 * W]).astype(LOW)
        attend_forward(qkv, probs, mixed, bias)
        value = x.astype(WIDE) + dot(mixed[...], weight[:, 3 * W :])
        y, n, r = norm(value, norms[row : row + 1, :], norms[5 + row : 6 + row, :])
        out[...] = y
        out_low[...] = y.astype(LOW)
        normal[...] = n
        scale[...] = r

    ins = [(place, SMEM), (tokens, VMEM), (id_row, VMEM), (id_col, VMEM), (norms, VMEM)] + [(s, ANY) for s in stacks]
    outs = [((L, W), WIDE, VMEM), ((L, W), LOW, VMEM), ((L, W), WIDE, VMEM), ((L, 1), WIDE, VMEM)]
    outs += [((L, 3 * W), LOW, VMEM), ((L, W), LOW, VMEM), ((H, L, L), LOW, VMEM)]
    scratch = [pltpu.VMEM((W, 4 * W), LOW), pltpu.VMEM((L, L), WIDE), pltpu.SemaphoreType.DMA((8,))]
    return plan.call(body, ins, outs, scratch, 2 * L * W * 4 * W)


def cross_attention(plan, place, query_in, query_low, memory_low, query_ids, memory_ids, left, right, norms, row):
    L, W, H = plan.length, plan.width, plan.heads

    def body(place, query_in, query_low, memory_low, query_ids, memory_ids, norms, *rest):
        left, right, rest = rest[: plan.n], rest[plan.n : 2 * plan.n], rest[2 * plan.n :]
        out, out_low, normal, scale, qkv, mixed, probs, weight, bias, sems = rest
        copies = weight_copies(place[0], left, plan.orders, weight, sems.at[0], pl.ds(0, 2 * W))
        copies += weight_copies(place[0], right, plan.orders, weight, sems.at[1], pl.ds(2 * W, 2 * W))
        start(copies)
        bias[...] = allowed_bias(memory_ids[...], query_ids[...], False)
        wait(copies)
        qkv[:, :W] = dot(query_low[...], weight[:, :W]).astype(LOW)
        qkv[:, W:] = dot(memory_low[...], weight[:, W : 3 * W]).astype(LOW)
        attend_forward(qkv, probs, mixed, bias)
        value = query_in[...] + dot(mixed[...], weight[:, 3 * W :])
        y, n, r = norm(value, norms[row : row + 1, :], norms[5 + row : 6 + row, :])
        out[...] = y
        out_low[...] = y.astype(LOW)
        normal[...] = n
        scale[...] = r

    ins = [(place, SMEM), (query_in, VMEM), (query_low, VMEM), (memory_low, VMEM), (query_ids, VMEM), (memory_ids, VMEM)]
    ins += [(norms, VMEM)] + [(s, ANY) for s in (*left, *right)]
    outs = [((L, W), WIDE, VMEM), ((L, W), LOW, VMEM), ((L, W), WIDE, VMEM), ((L, 1), WIDE, VMEM)]
    outs += [((L, 3 * W), LOW, VMEM), ((L, W), LOW, VMEM), ((H, L, L), LOW, VMEM)]
    scratch = [pltpu.VMEM((W, 4 * W), LOW), pltpu.VMEM((L, L), WIDE), pltpu.SemaphoreType.DMA((2, 8))]
    return plan.call(body, ins, outs, scratch, 2 * L * W * 4 * W)


def encoder_ffn(plan, place, hidden, hidden_low, tokens, ups, downs, norms, row):
    L, W, F = plan.length, plan.width, plan.hidden

    def body(place, hidden, hidden_low, tokens, norms, *rest):
        ups, downs, rest = rest[: plan.n], rest[plan.n : 2 * plan.n], rest[2 * plan.n :]
        out_low, normal, scale, active, slope, up, down, sems = rest
        up_copies = weight_copies(place[0], ups, plan.orders, up, sems.at[0])
        down_copies = weight_copies(place[0], downs, plan.orders, down, sems.at[1])
        start(up_copies + down_copies)
        wait(up_copies + down_copies)
        branch = ffn_forward(hidden_low[...], up, down, active, slope)
        value = hidden[...] + branch + tokens[...].astype(WIDE)
        y, n, r = norm(value, norms[row : row + 1, :], norms[5 + row : 6 + row, :])
        out_low[...] = y.astype(LOW)
        normal[...] = n
        scale[...] = r

    ins = [(place, SMEM), (hidden, VMEM), (hidden_low, VMEM), (tokens, VMEM), (norms, VMEM)] + [(s, ANY) for s in (*ups, *downs)]
    outs = [((L, W), LOW, VMEM), ((L, W), WIDE, VMEM), ((L, 1), WIDE, VMEM), ((L, F), LOW, VMEM), ((L, F), LOW, VMEM)]
    scratch = [pltpu.VMEM((W, F), LOW), pltpu.VMEM((F, W), LOW), pltpu.SemaphoreType.DMA((2, 8))]
    return plan.call(body, ins, outs, scratch, 4 * L * W * F)


def decoder_ffn(plan, place, hidden, hidden_low, tokens, cotangent, hidden_normal, hidden_scale, ups, downs, norms, row, orders):
    L, W, F = plan.length, plan.width, plan.hidden
    up_orders, down_orders = plan.grad_orders(orders[0]), plan.grad_orders(orders[1])

    def body(place, hidden, hidden_low, tokens, cotangent, hidden_normal, hidden_scale, norms, *rest):
        ups, downs, rest = rest[: plan.n], rest[plan.n : 2 * plan.n], rest[2 * plan.n :]
        decoded, last_grad, two_grad, norm_grads, rest = *rest[:4], rest[4:]
        up_out, down_out, rest = rest[: len(up_orders)], rest[len(up_orders) : 2 * len(up_orders)], rest[2 * len(up_orders) :]
        up, down, active, slope, up_grad, down_grad, sems = rest
        up_copies = weight_copies(place[0], ups, plan.orders, up, sems.at[0])
        down_copies = weight_copies(place[0], downs, plan.orders, down, sems.at[1])
        start(up_copies + down_copies)
        wait(up_copies + down_copies)
        low = hidden_low[...]
        branch = ffn_forward(low, up, down, active, slope)
        value = hidden[...] + branch + tokens[...].astype(WIDE)
        gain = norms[row : row + 1, :]
        y, n, r = norm(value, gain, norms[5 + row : 6 + row, :])
        decoded[...] = y.astype(LOW)
        grad, gain_grad, shift_grad = norm_back(cotangent[...].astype(WIDE), n, r, gain)
        last_grad[...] = grad
        norm_grads[0:1, :] = gain_grad
        norm_grads[1:2, :] = shift_grad
        grad_low = grad.astype(LOW)
        ffn_backward_down(grad_low, active, down_grad)
        down_back = grad_copies(place[0], down_grad, down_out, down_orders, sems.at[1])
        start(down_back)
        back = ffn_backward_up(grad_low, low, up, down, slope, up_grad)
        up_back = grad_copies(place[0], up_grad, up_out, up_orders, sems.at[0])
        start(up_back)
        grad, gain_grad, shift_grad = norm_back(last_grad[...] + back, hidden_normal[...], hidden_scale[...], norms[row - 1 : row, :])
        two_grad[...] = grad
        norm_grads[2:3, :] = gain_grad
        norm_grads[3:4, :] = shift_grad
        wait(down_back + up_back)

    ins = [(place, SMEM), (hidden, VMEM), (hidden_low, VMEM), (tokens, VMEM), (cotangent, VMEM), (hidden_normal, VMEM)]
    ins += [(hidden_scale, VMEM), (norms, VMEM)] + [(s, ANY) for s in (*ups, *downs)]
    outs = [((L, W), LOW, VMEM), ((L, W), WIDE, VMEM), ((L, W), WIDE, VMEM), ((4, W), WIDE, VMEM)]
    outs += [(s.shape, LOW, ANY) for s in (*plan.grad_shapes(W, F, orders[0]), *plan.grad_shapes(F, W, orders[1]))]
    scratch = [pltpu.VMEM((W, F), LOW), pltpu.VMEM((F, W), LOW), pltpu.VMEM((L, F), LOW), pltpu.VMEM((L, F), LOW)]
    scratch += [pltpu.VMEM((W, F), LOW), pltpu.VMEM((F, W), LOW), pltpu.SemaphoreType.DMA((2, 8))]
    got = plan.call(body, ins, outs, scratch, 12 * L * W * F)
    k = len(up_orders)
    return got[:4], got[4 : 4 + k], got[4 + k :]


def encoder_ffn_back(plan, place, grad, hidden_low, active, slope, hidden_normal, hidden_scale, ups, downs, norms, row, orders):
    L, W, F = plan.length, plan.width, plan.hidden
    up_orders, down_orders = plan.grad_orders(orders[0]), plan.grad_orders(orders[1])

    def body(place, grad, hidden_low, active, slope, hidden_normal, hidden_scale, norms, *rest):
        ups, downs, rest = rest[: plan.n], rest[plan.n : 2 * plan.n], rest[2 * plan.n :]
        zero_grad, norm_grads, rest = *rest[:2], rest[2:]
        up_out, down_out, rest = rest[: len(up_orders)], rest[len(up_orders) : 2 * len(up_orders)], rest[2 * len(up_orders) :]
        up, down, up_grad, down_grad, sems = rest
        up_copies = weight_copies(place[0], ups, plan.orders, up, sems.at[0])
        down_copies = weight_copies(place[0], downs, plan.orders, down, sems.at[1])
        start(down_copies + up_copies)
        grad_low = grad[...].astype(LOW)
        ffn_backward_down(grad_low, active, down_grad)
        wait(down_copies + up_copies)
        down_back = grad_copies(place[0], down_grad, down_out, down_orders, sems.at[1])
        start(down_back)
        back = ffn_backward_up(grad_low, hidden_low[...], up, down, slope, up_grad)
        up_back = grad_copies(place[0], up_grad, up_out, up_orders, sems.at[0])
        start(up_back)
        out, gain_grad, shift_grad = norm_back(grad[...] + back, hidden_normal[...], hidden_scale[...], norms[row : row + 1, :])
        zero_grad[...] = out
        norm_grads[0:1, :] = gain_grad
        norm_grads[1:2, :] = shift_grad
        wait(down_back + up_back)

    ins = [(place, SMEM), (grad, VMEM), (hidden_low, VMEM), (active, VMEM), (slope, VMEM), (hidden_normal, VMEM)]
    ins += [(hidden_scale, VMEM), (norms, VMEM)] + [(s, ANY) for s in (*ups, *downs)]
    outs = [((L, W), WIDE, VMEM), ((2, W), WIDE, VMEM)]
    outs += [(s.shape, LOW, ANY) for s in (*plan.grad_shapes(W, F, orders[0]), *plan.grad_shapes(F, W, orders[1]))]
    scratch = [pltpu.VMEM((W, F), LOW), pltpu.VMEM((F, W), LOW), pltpu.VMEM((W, F), LOW), pltpu.VMEM((F, W), LOW)]
    scratch += [pltpu.SemaphoreType.DMA((2, 8))]
    got = plan.call(body, ins, outs, scratch, 8 * L * W * F)
    k = len(up_orders)
    return got[:2], got[2 : 2 + k], got[2 + k :]


def self_attention_back(plan, place, grad, tokens, kept, stacks, extra, order):
    L, W, H = plan.length, plan.width, plan.heads
    qkv, mixed, probs = kept
    orders = plan.grad_orders(order)

    def body(place, grad, extra, tokens, qkv, mixed, probs, *rest):
        stacks, rest = rest[: plan.n], rest[plan.n :]
        total, grads, rest = rest[0], rest[1 : 1 + len(orders)], rest[1 + len(orders) :]
        weight, weight_grad, mixed_grad, qkv_grad, sems = rest
        copies = weight_copies(place[0], stacks, plan.orders, weight, sems)
        start(copies)
        grad_low = grad[...].astype(LOW)
        weight_grad[:, 3 * W :] = dot_tn(mixed[...], grad_low).astype(LOW)
        wait(copies)
        mixed_grad[...] = dot_nt(grad_low, weight[:, 3 * W :]).astype(LOW)
        attend_backward(qkv, probs, mixed_grad, qkv_grad)
        back = qkv_grad[...]
        weight_grad[:, : 3 * W] = dot_tn(tokens[...], back).astype(LOW)
        copies = grad_copies(place[0], weight_grad, grads, orders, sems)
        start(copies)
        total[...] = grad[...] + extra[...] + dot_nt(back, weight[:, : 3 * W])
        wait(copies)

    ins = [(place, SMEM), (grad, VMEM), (extra, VMEM), (tokens, VMEM), (qkv, VMEM), (mixed, VMEM), (probs, VMEM)]
    ins += [(s, ANY) for s in stacks]
    outs = [((L, W), WIDE, VMEM)] + [(s.shape, LOW, ANY) for s in plan.grad_shapes(W, 4 * W, order)]
    scratch = [pltpu.VMEM((W, 4 * W), LOW), pltpu.VMEM((W, 4 * W), LOW), pltpu.VMEM((L, W), LOW), pltpu.VMEM((L, 3 * W), LOW)]
    scratch += [pltpu.SemaphoreType.DMA((8,))]
    got = plan.call(body, ins, outs, scratch, 4 * L * W * 4 * W)
    return got[0], got[1:]


def cross_attention_back(plan, place, grad, query_low, memory_low, kept, left, right, query_norm, memory_norm, norms, rows, order):
    L, W, H = plan.length, plan.width, plan.heads
    qkv, mixed, probs = kept
    orders = plan.grad_orders(order)

    def body(place, grad, query_low, memory_low, qkv, mixed, probs, query_n, query_r, memory_n, memory_r, norms, *rest):
        left, right, rest = rest[: plan.n], rest[plan.n : 2 * plan.n], rest[2 * plan.n :]
        one_grad, enc_grad, norm_grads, grads, rest = *rest[:3], rest[3 : 3 + len(orders)], rest[3 + len(orders) :]
        weight, weight_grad, mixed_grad, qkv_grad, sems = rest
        copies = weight_copies(place[0], left, plan.orders, weight, sems.at[0], pl.ds(0, 2 * W))
        copies += weight_copies(place[0], right, plan.orders, weight, sems.at[1], pl.ds(2 * W, 2 * W))
        start(copies)
        grad_low = grad[...].astype(LOW)
        weight_grad[:, 3 * W :] = dot_tn(mixed[...], grad_low).astype(LOW)
        wait(copies)
        mixed_grad[...] = dot_nt(grad_low, weight[:, 3 * W :]).astype(LOW)
        attend_backward(qkv, probs, mixed_grad, qkv_grad)
        weight_grad[:, :W] = dot_tn(query_low[...], qkv_grad[:, :W]).astype(LOW)
        weight_grad[:, W : 3 * W] = dot_tn(memory_low[...], qkv_grad[:, W:]).astype(LOW)
        copies = grad_copies(place[0], weight_grad, grads, orders, sems.at[0])
        start(copies)
        back = grad[...] + dot_nt(qkv_grad[:, :W], weight[:, :W])
        out, gain_grad, shift_grad = norm_back(back, query_n[...], query_r[...], norms[rows[0] : rows[0] + 1, :])
        one_grad[...] = out
        norm_grads[0:1, :] = gain_grad
        norm_grads[1:2, :] = shift_grad
        back = dot_nt(qkv_grad[:, W:], weight[:, W : 3 * W])
        out, gain_grad, shift_grad = norm_back(back, memory_n[...], memory_r[...], norms[rows[1] : rows[1] + 1, :])
        enc_grad[...] = out
        norm_grads[2:3, :] = gain_grad
        norm_grads[3:4, :] = shift_grad
        wait(copies)

    ins = [(place, SMEM), (grad, VMEM), (query_low, VMEM), (memory_low, VMEM), (qkv, VMEM), (mixed, VMEM), (probs, VMEM)]
    ins += [(v, VMEM) for v in (*query_norm, *memory_norm, norms)] + [(s, ANY) for s in (*left, *right)]
    outs = [((L, W), WIDE, VMEM), ((L, W), WIDE, VMEM), ((4, W), WIDE, VMEM)]
    outs += [(s.shape, LOW, ANY) for s in plan.grad_shapes(W, 4 * W, order)]
    scratch = [pltpu.VMEM((W, 4 * W), LOW), pltpu.VMEM((W, 4 * W), LOW), pltpu.VMEM((L, W), LOW), pltpu.VMEM((L, 3 * W), LOW)]
    scratch += [pltpu.SemaphoreType.DMA((2, 8))]
    got = plan.call(body, ins, outs, scratch, 4 * L * W * 4 * W)
    return got[:3], got[3:]


def swap(value, axis, size, bit):
    return lax.ppermute(value, axis, [(i, i ^ bit) for i in range(size)])


def on_chip_order(parts, me):
    for bit in (CORE, X, Y):
        flipped = jnp.stack([parts[k ^ bit] for k in range(8)])
        parts = jnp.where((me & bit) != 0, flipped, parts)
    return parts


def gather_two(plan, first, second):
    if not plan.split:
        return [[lax.all_gather(v, "shard", axis=0, tiled=True)[None]] for v in (first, second)]
    sw = lambda v, bit: swap(v, "shard", 8, bit)
    first_x, second_y = sw(first, X), sw(second, Y)
    first_y, second_x = sw(first, Y), sw(second, X)
    first_xy, second_xy = sw(first_x, Y), sw(second_y, X)
    out = []
    for stack in ((first, first_x, first_y, first_xy), (second, second_x, second_y, second_xy)):
        mine = jnp.stack(stack)
        out.append([mine, sw(mine, CORE)])
    return out


def add_low(left, right):
    return (left.astype(WIDE) + right.astype(WIDE)).astype(LOW)


def owned_sum(plan, stacks, z, order):
    if not plan.split:
        own = lax.psum_scatter(stacks[0][0], "shard", scatter_dimension=0, tiled=True)
        return lax.psum(own, "rep").astype(WIDE)
    sw = lambda v, bit: swap(v, "shard", 8, bit)
    keep, send, other = stacks
    got = sw(other, CORE)
    keep, send = add_low(keep, got[:2]), add_low(send, got[2:])
    got = sw(send, order[0])
    keep, send = add_low(keep[0], got[0]), add_low(keep[1], got[1])
    own = add_low(keep, sw(send, order[1]))
    sz = lambda v, bit: swap(v, "rep", 4, bit)
    half = own.shape[0] // 2
    odd = (z & 1) != 0
    low, high = own[:half], own[half:]
    got = sz(jnp.where(odd, low, high), Z1)
    part = lax.optimization_barrier(add_low(jnp.where(odd, high, low), got))
    part = lax.optimization_barrier(add_low(part, sz(part, Z2)))
    other = sz(part, Z1)
    return jnp.where(odd, jnp.concatenate([other, part]), jnp.concatenate([part, other])).astype(WIDE)


def gather_norms(plan, small, me):
    if not plan.split:
        return lax.all_gather(small, "shard", axis=1, tiled=True).astype(WIDE)
    parts = small[None]
    for bit in (CORE, X, Y):
        parts = jnp.concatenate([parts, swap(parts, "shard", 8, bit)])
    parts = on_chip_order(parts, me)
    return jnp.moveaxis(parts, 0, 1).reshape(small.shape[0], -1).astype(WIDE)


def owned_norms(plan, whole, me):
    if plan.split:
        for bit in (CORE, X, Y):
            whole = whole + swap(whole, "shard", 8, bit)
        for bit in (Z1, Z2):
            whole = whole + swap(whole, "rep", 4, bit)
    else:
        whole = lax.psum(whole, ("shard", "rep"))
    wide = whole.shape[1] // plan.sizes[0]
    return lax.dynamic_slice_in_dim(whole, me * wide, wide, axis=1)


def shards(sizes, source, target, source_seg, target_seg, attn_in, attn_out, ffn_up, ffn_down, norm_gain, norm_bias, cotangent):
    plan = Plan(sizes, (source.shape[1], source.shape[2], ffn_up.shape[2]))
    W = plan.width
    me = lax.axis_index("shard")
    z = lax.axis_index("rep")
    place = (me if plan.split else jnp.zeros_like(me))[None]
    src, tgt = source[0], target[0]
    src_row, src_col = source_seg, source_seg.reshape(-1, 1)
    tgt_row, tgt_col = target_seg, target_seg.reshape(-1, 1)
    att = [jnp.concatenate([attn_in[k], attn_out[k]], axis=1) for k in range(2)]
    norms = gather_norms(plan, jnp.concatenate([norm_gain, norm_bias]), me)
    w0, w1 = gather_two(plan, att[0], att[1])
    u0, d0 = gather_two(plan, ffn_up[0], ffn_down[0])
    left, right = gather_two(plan, attn_in[2][:, : 2 * W], jnp.concatenate([attn_in[2][:, 2 * W :], attn_out[2]], axis=1))
    u1, d1 = gather_two(plan, ffn_up[1], ffn_down[1])

    first, first_low, n0, r0, *kept_enc = self_attention(plan, place, src, src_row, src_col, w0, norms, 0, False)
    one, one_low, n2, r2, *kept_self = self_attention(plan, place, tgt, tgt_row, tgt_col, w1, norms, 2, True)
    enc_low, n1, r1, active, slope = encoder_ffn(plan, place, first, first_low, src, u0, d0, norms, 1)
    two, two_low, n3, r3, *kept_cross = cross_attention(
        plan, place, one, one_low, enc_low, tgt_row, src_col, left, right, norms, 3
    )
    (decoded, last_grad, two_grad, norm_a), up_one, down_one = decoder_ffn(
        plan, place, two, two_low, tgt, cotangent[0], n3, r3, u1, d1, norms, 4, ((X, Y), (Y, X))
    )
    up_one = owned_sum(plan, up_one, z, (X, Y))
    down_one = owned_sum(plan, down_one, z, (Y, X))
    (one_grad, enc_grad, norm_b), att_two = cross_attention_back(
        plan, place, two_grad, one_low, enc_low, kept_cross, left, right, (n2, r2), (n1, r1), norms, (2, 1), (X, Y)
    )
    att_two = owned_sum(plan, att_two, z, (X, Y))
    (zero_grad, norm_c), up_zero, down_zero = encoder_ffn_back(
        plan, place, enc_grad, first_low, active, slope, n0, r0, u0, d0, norms, 0, ((X, Y), (Y, X))
    )
    up_zero = owned_sum(plan, up_zero, z, (X, Y))
    down_zero = owned_sum(plan, down_zero, z, (Y, X))
    tgt_grad, att_one = self_attention_back(plan, place, one_grad, tgt, kept_self, w1, last_grad, (Y, X))
    att_one = owned_sum(plan, att_one, z, (Y, X))
    src_grad, att_zero = self_attention_back(plan, place, zero_grad, src, kept_enc, w0, enc_grad, (X, Y))
    att_zero = owned_sum(plan, att_zero, z, (X, Y))
    gains = [norm_c[0], norm_b[2], norm_b[0], norm_a[2], norm_a[0]]
    shifts = [norm_c[1], norm_b[3], norm_b[1], norm_a[3], norm_a[1]]
    small = owned_norms(plan, jnp.stack(gains + shifts), me)
    atts = jnp.stack([att_zero, att_one, att_two])
    return (
        decoded[None],
        src_grad[None],
        tgt_grad[None],
        atts[:, :, : 3 * W],
        atts[:, :, 3 * W :],
        jnp.stack([up_zero, up_one]),
        jnp.stack([down_zero, down_one]),
        small[:5],
        small[5:],
    )


def solution(mesh):
    sizes = (mesh.shape["shard"], mesh.shape["rep"])
    tokens = P(("shard", "rep"), None, None)
    ids = P(("shard", "rep"), None)
    weight = P(None, "shard", None)
    norm = P(None, "shard")
    return jax.shard_map(
        functools.partial(shards, sizes),
        mesh=mesh,
        in_specs=(tokens, tokens, ids, ids, weight, weight, weight, weight, norm, norm, tokens),
        out_specs=(tokens, tokens, tokens, weight, weight, weight, weight, norm, norm),
        check_vma=False,
    )
```

```python
import functools

import jax
import jax.numpy as jnp
from jax import lax
from jax.experimental import pallas as pl
from jax.experimental.pallas import tpu as pltpu
from jax.sharding import PartitionSpec as P

HEAD = 64
PAIR = 2 * HEAD
EPS = 1e-05
NEG = -1e30
LOW = jnp.bfloat16
WIDE = jnp.float32
CORE, X, Y = 1, 2, 4
Z1, Z2 = 1, 2
SMALL = 16
NORMS = 5
VMEM = pl.BlockSpec(memory_space=pltpu.VMEM)
SMEM = pl.BlockSpec(memory_space=pltpu.SMEM)
ANY = pl.BlockSpec(memory_space=pl.ANY)


def dot(left, right):
    return lax.dot_general(left, right, (((1,), (0,)), ((), ())), preferred_element_type=WIDE)


def dot_nt(left, right):
    return lax.dot_general(left, right, (((1,), (1,)), ((), ())), preferred_element_type=WIDE)


def dot_tn(left, right):
    return lax.dot_general(left, right, (((0,), (0,)), ((), ())), preferred_element_type=WIDE)


def block(unit, i, r):
    part = unit[:, i * r : (i + 1) * r, :]
    return part.reshape(part.shape[0] * r, part.shape[2])


def set_block(unit, i, r, value, offset=0):
    unit[:, offset + i * r : offset + (i + 1) * r, :] = value.reshape(unit.shape[0], r, unit.shape[2])


def rows_block(unit, i):
    n = unit.shape[0] // 4
    part = unit[i * n : (i + 1) * n, :, :]
    return part.reshape(n * part.shape[1], part.shape[2])


def set_rows_block(unit, i, value):
    n = unit.shape[0] // 4
    unit[i * n : (i + 1) * n, :, :] = value.reshape(n, unit.shape[1], unit.shape[2])


def start(copies):
    for copy in copies:
        copy.start()


def wait(copies):
    for copy in copies:
        copy.wait()


def norm(value, gain, shift):
    mean = jnp.mean(value, axis=-1, keepdims=True)
    centred = value - mean
    scale = lax.rsqrt(jnp.mean(centred * centred, axis=-1, keepdims=True) + EPS)
    normal = centred * scale
    return normal * gain + shift, normal, scale


def norm_back(grad, normal, scale, gain):
    gain_grad = jnp.sum(grad * normal, axis=0, keepdims=True)
    shift_grad = jnp.sum(grad, axis=0, keepdims=True)
    inner = grad * gain
    inner_mean = jnp.mean(inner, axis=-1, keepdims=True)
    cross_mean = jnp.mean(inner * normal, axis=-1, keepdims=True)
    return scale * (inner - inner_mean - normal * cross_mean), gain_grad, shift_grad


def lanes_of(head, value):
    lane = lax.broadcasted_iota(jnp.int32, value.shape, 1)
    return jnp.where((lane < HEAD) if head == 0 else (lane >= HEAD), value, jnp.zeros_like(value))


def pick(first, second):
    lane = lax.broadcasted_iota(jnp.int32, first.shape, 1)
    return jnp.where(lane < HEAD, first, second)


def allowed_bias(memory_ids, query_ids, causal):
    allowed = memory_ids == query_ids
    if causal:
        shape = (memory_ids.shape[0], query_ids.shape[1])
        allowed = allowed & (lax.broadcasted_iota(jnp.int32, shape, 1) >= lax.broadcasted_iota(jnp.int32, shape, 0))
    return jnp.where(allowed, 0.0, NEG)


def attend_forward(qkv, probs, mixed, bias):
    width = mixed.shape[1]
    for pair in range(width // PAIR):
        at = pl.ds(pair * PAIR, PAIR)
        query = qkv[:, pl.ds(pair * PAIR, PAIR)] * LOW(HEAD ** -0.5)
        keys = qkv[:, pl.ds(width + pair * PAIR, PAIR)]
        values = qkv[:, pl.ds(2 * width + pair * PAIR, PAIR)]
        out = []
        for head in range(2):
            scores = dot_nt(keys, lanes_of(head, query)) + bias[...]
            top = jnp.max(scores, axis=0, keepdims=True)
            weights = jnp.exp(scores - top)
            total = jnp.sum(weights, axis=0, keepdims=True)
            low = (weights * (1.0 / total)).astype(LOW)
            probs[2 * pair + head] = low
            out.append(dot_tn(low, values))
        mixed[:, at] = pick(*out).astype(LOW)


def attend_backward(qkv, probs, mixed_grad, qkv_grad):
    width = mixed_grad.shape[1]
    for pair in range(width // PAIR):
        query = qkv[:, pl.ds(pair * PAIR, PAIR)]
        keys = qkv[:, pl.ds(width + pair * PAIR, PAIR)]
        values = qkv[:, pl.ds(2 * width + pair * PAIR, PAIR)]
        grad = mixed_grad[:, pl.ds(pair * PAIR, PAIR)]
        dq, dk, dv = [], [], []
        for head in range(2):
            low = probs[2 * pair + head]
            prob = low.astype(WIDE)
            prob_grad = dot_nt(values, lanes_of(head, grad))
            delta = jnp.sum(prob * prob_grad, axis=0, keepdims=True)
            score_grad = (prob * (prob_grad - delta)).astype(LOW)
            dv.append(dot(low, grad))
            dk.append(dot(score_grad, query))
            dq.append(dot_tn(score_grad, keys))
        scale = HEAD ** -0.5
        qkv_grad[:, pl.ds(pair * PAIR, PAIR)] = (pick(*dq) * scale).astype(LOW)
        qkv_grad[:, pl.ds(width + pair * PAIR, PAIR)] = (pick(*dk) * scale).astype(LOW)
        qkv_grad[:, pl.ds(2 * width + pair * PAIR, PAIR)] = pick(*dv).astype(LOW)


GELU = 0.7978845608028654


def gelu_and_slope(value):
    square = value * value
    inner = GELU * value * (1.0 + 0.044715 * square)
    t = jnp.tanh(inner)
    half = 0.5 + 0.5 * t
    slope = half + 0.5 * value * (1.0 - t * t) * (GELU * (1.0 + 3 * 0.044715 * square))
    return value * half, slope


def ffn_forward(hidden, up, down, active, slope, r):
    W = hidden.shape[1]
    total = None
    for c in range(4):
        at = pl.ds(c * W, W)
        act, sl = gelu_and_slope(dot(hidden, block(up, c, r)))
        act = act.astype(LOW)
        active[:, at] = act
        slope[:, at] = sl.astype(LOW)
        part = dot(act, rows_block(down, c))
        total = part if total is None else total + part
    return total


def ffn_backward_down(grad, active, down_grad):
    W = grad.shape[1]
    for c in range(4):
        set_rows_block(down_grad, c, dot_tn(active[:, pl.ds(c * W, W)], grad).astype(LOW))


def ffn_backward_up(grad, hidden, up, down, slope, up_grad, r):
    W = grad.shape[1]
    total = None
    for c in range(4):
        z = (dot_nt(grad, rows_block(down, c)) * slope[:, pl.ds(c * W, W)].astype(WIDE)).astype(LOW)
        set_block(up_grad, c, r, dot_tn(hidden, z).astype(LOW))
        part = dot_nt(z, block(up, c, r))
        total = part if total is None else total + part
    return total


class Plan:
    def __init__(self, sizes, length, width):
        self.split = sizes == (8, 4)
        self.sizes = sizes
        self.length, self.width = length, width
        self.heads = width // HEAD
        self.shards = sizes[0]
        self.r = width // self.shards
        self.unit = (self.shards, 4 * self.r, width)


    def weight_copies(self, place, stacks, member, unit, sems, rows=None):
        copies = []
        at = () if rows is None else (rows,)
        if self.split:
            for core, stack in enumerate(stacks):
                for j, k in enumerate((0, X, Y, X | Y)):
                    dst = unit.at[(place ^ (k | core), *at)]
                    copies.append(pltpu.make_async_copy(stack.at[2 * j + member], dst, sems.at[len(copies)]))
        elif rows is None:
            copies.append(pltpu.make_async_copy(stacks[0].at[:, member], unit, sems.at[0]))
        else:
            copies.append(pltpu.make_async_copy(stacks[0].at[:, member], unit.at[:, rows], sems.at[0]))
        return copies


    def grad_shapes(self, rows):
        if not self.split:
            return [(self.shards, 2, rows, self.width)]
        return [(8, rows, self.width)] * 2

    def grad_copies(self, place, members, outs, sems):
        if not self.split:
            return [pltpu.make_async_copy(member, outs[0].at[:, m], sems.at[m, 0]) for m, member in enumerate(members)]
        copies = []
        for m, (member, (a, b)) in enumerate(zip(members, ((X, Y), (Y, X)))):
            for core, out in enumerate(outs):
                for j, k in enumerate((0, b, a, a | b)):
                    copies.append(pltpu.make_async_copy(member.at[place ^ (k | core)], out.at[4 * m + j], sems.at[m, 4 * core + j]))
        return copies

    def call(self, body, ins, outs, scratch, us, deps, room):
        def run(*refs):
            body(*refs[len(deps) :])

        return pl.pallas_call(
            run,
            in_specs=[ANY] * len(deps) + [spec for _, spec in ins],
            out_shape=[jax.ShapeDtypeStruct(shape, dtype) for shape, dtype, _ in outs],
            out_specs=[spec for _, _, spec in outs],
            scratch_shapes=scratch,
            compiler_params=pltpu.CompilerParams(vmem_limit_bytes=room << 20),
            cost_estimate=pl.CostEstimate(flops=int(us * 5e9), bytes_accessed=1 << 20, transcendentals=0),
        )(*deps, *[value for value, _ in ins])

    @property
    def n(self):
        return 2 if self.split else 1

    @property
    def g(self):
        return 2 if self.split else 1


def sems(*shape):
    return pltpu.SemaphoreType.DMA(shape)


def self_attention(plan, place, tokens, id_row, id_col, stacks, member, row, causal, deps=()):
    L, W, H, r = plan.length, plan.width, plan.heads, plan.r

    def body(place, tokens, id_row, id_col, *rest):
        stacks, rest = rest[: plan.n], rest[plan.n :]
        out, out_low, normal, scale, qkv, mixed, probs, norms, weight, bias, sem = rest
        copies = plan.weight_copies(place[0], stacks, member, weight, sem)
        start(copies)
        bias[...] = allowed_bias(id_col[...], id_row[...], causal)
        wait(copies)
        norms[...] = jnp.sum(weight[:, 4 * r :, :].astype(WIDE), axis=0)
        x = tokens[...]
        for i in range(3):
            qkv[:, i * W : (i + 1) * W] = dot(x, block(weight, i, r)).astype(LOW)
        attend_forward(qkv, probs, mixed, bias)
        value = x.astype(WIDE) + dot(mixed[...], block(weight, 3, r))
        y, n, s = norm(value, norms[row : row + 1, :], norms[NORMS + row : NORMS + row + 1, :])
        out[...] = y
        out_low[...] = y.astype(LOW)
        normal[...] = n
        scale[...] = s

    ins = [(place, SMEM), (tokens, VMEM), (id_row, VMEM), (id_col, VMEM)] + [(s, ANY) for s in stacks]
    outs = [((L, W), WIDE, VMEM), ((L, W), LOW, VMEM), ((L, W), WIDE, VMEM), ((L, 1), WIDE, VMEM)]
    outs += [((L, 3 * W), LOW, VMEM), ((L, W), LOW, VMEM), ((H, L, L), LOW, VMEM), ((SMALL, W), WIDE, VMEM)]
    unit = (plan.shards, 4 * r + SMALL, W)
    scratch = [pltpu.VMEM(unit, LOW), pltpu.VMEM((L, L), WIDE), sems(8)]
    return plan.call(body, ins, outs, scratch, 10, deps, 14)


def cross_attention(plan, place, query_in, query_low, memory_low, query_ids, memory_ids, stacks, norms, row, deps=()):
    L, W, H, r = plan.length, plan.width, plan.heads, plan.r

    def body(place, query_in, query_low, memory_low, query_ids, memory_ids, norms, *rest):
        stacks, rest = rest[: plan.n], rest[plan.n :]
        out, out_low, normal, scale, qkv, mixed, probs, weight, bias, sem = rest
        copies = plan.weight_copies(place[0], stacks, 0, weight, sem.at[0], pl.ds(0, 2 * r))
        copies += plan.weight_copies(place[0], stacks, 1, weight, sem.at[1], pl.ds(2 * r, 2 * r))
        start(copies)
        bias[...] = allowed_bias(memory_ids[...], query_ids[...], False)
        wait(copies)
        qkv[:, :W] = dot(query_low[...], block(weight, 0, r)).astype(LOW)
        memory = memory_low[...]
        for i in (1, 2):
            qkv[:, i * W : (i + 1) * W] = dot(memory, block(weight, i, r)).astype(LOW)
        attend_forward(qkv, probs, mixed, bias)
        value = query_in[...] + dot(mixed[...], block(weight, 3, r))
        y, n, s = norm(value, norms[row : row + 1, :], norms[NORMS + row : NORMS + row + 1, :])
        out[...] = y
        out_low[...] = y.astype(LOW)
        normal[...] = n
        scale[...] = s

    ins = [(place, SMEM), (query_in, VMEM), (query_low, VMEM), (memory_low, VMEM), (query_ids, VMEM), (memory_ids, VMEM)]
    ins += [(norms, VMEM)] + [(s, ANY) for s in stacks]
    outs = [((L, W), WIDE, VMEM), ((L, W), LOW, VMEM), ((L, W), WIDE, VMEM), ((L, 1), WIDE, VMEM)]
    outs += [((L, 3 * W), LOW, VMEM), ((L, W), LOW, VMEM), ((H, L, L), LOW, VMEM)]
    scratch = [pltpu.VMEM(plan.unit, LOW), pltpu.VMEM((L, L), WIDE), sems(2, 8)]
    return plan.call(body, ins, outs, scratch, 10, deps, 14)


def encoder_ffn(plan, place, hidden, hidden_low, tokens, stacks, norms, row, deps=()):
    L, W, F, r = plan.length, plan.width, 4 * plan.width, plan.r

    def body(place, hidden, hidden_low, tokens, norms, *rest):
        stacks, rest = rest[: plan.n], rest[plan.n :]
        out_low, normal, scale, active, slope, up, down, sem = rest
        copies = plan.weight_copies(place[0], stacks, 0, up, sem.at[0])
        copies += plan.weight_copies(place[0], stacks, 1, down, sem.at[1])
        start(copies)
        wait(copies)
        branch = ffn_forward(hidden_low[...], up, down, active, slope, r)
        value = hidden[...] + branch + tokens[...].astype(WIDE)
        y, n, s = norm(value, norms[row : row + 1, :], norms[NORMS + row : NORMS + row + 1, :])
        out_low[...] = y.astype(LOW)
        normal[...] = n
        scale[...] = s

    ins = [(place, SMEM), (hidden, VMEM), (hidden_low, VMEM), (tokens, VMEM), (norms, VMEM)] + [(s, ANY) for s in stacks]
    outs = [((L, W), LOW, VMEM), ((L, W), WIDE, VMEM), ((L, 1), WIDE, VMEM), ((L, F), LOW, VMEM), ((L, F), LOW, VMEM)]
    scratch = [pltpu.VMEM(plan.unit, LOW), pltpu.VMEM(plan.unit, LOW), sems(2, 8)]
    return plan.call(body, ins, outs, scratch, 9, deps, 14)


def decoder_ffn(plan, place, hidden, hidden_low, tokens, cotangent, hidden_normal, hidden_scale, stacks, norms, row, deps=()):
    L, W, F, r = plan.length, plan.width, 4 * plan.width, plan.r

    def body(place, hidden, hidden_low, tokens, cotangent, hidden_normal, hidden_scale, norms, *rest):
        stacks, rest = rest[: plan.n], rest[plan.n :]
        decoded, last_grad, two_grad, norm_grads, rest = *rest[:4], rest[4:]
        grads, rest = rest[: plan.g], rest[plan.g :]
        up, down, active, slope, up_grad, down_grad, sem, out_sem = rest
        copies = plan.weight_copies(place[0], stacks, 0, up, sem.at[0])
        copies += plan.weight_copies(place[0], stacks, 1, down, sem.at[1])
        start(copies)
        wait(copies)
        low = hidden_low[...]
        branch = ffn_forward(low, up, down, active, slope, r)
        value = hidden[...] + branch + tokens[...].astype(WIDE)
        gain = norms[row : row + 1, :]
        y, n, s = norm(value, gain, norms[NORMS + row : NORMS + row + 1, :])
        decoded[...] = y.astype(LOW)
        grad, gain_grad, shift_grad = norm_back(cotangent[...].astype(WIDE), n, s, gain)
        last_grad[...] = grad
        norm_grads[0:1, :] = gain_grad
        norm_grads[1:2, :] = shift_grad
        grad_low = grad.astype(LOW)
        ffn_backward_down(grad_low, active, down_grad)
        back = ffn_backward_up(grad_low, low, up, down, slope, up_grad, r)
        copies = plan.grad_copies(place[0], (up_grad, down_grad), grads, out_sem)
        start(copies)
        grad, gain_grad, shift_grad = norm_back(last_grad[...] + back, hidden_normal[...], hidden_scale[...], norms[row - 1 : row, :])
        two_grad[...] = grad
        norm_grads[2:3, :] = gain_grad
        norm_grads[3:4, :] = shift_grad
        wait(copies)

    ins = [(place, SMEM), (hidden, VMEM), (hidden_low, VMEM), (tokens, VMEM), (cotangent, VMEM), (hidden_normal, VMEM)]
    ins += [(hidden_scale, VMEM), (norms, VMEM)] + [(s, ANY) for s in stacks]
    outs = [((L, W), LOW, VMEM), ((L, W), WIDE, VMEM), ((L, W), WIDE, VMEM), ((4, W), WIDE, VMEM)]
    outs += [(s, LOW, ANY) for s in plan.grad_shapes(4 * r)]
    scratch = [pltpu.VMEM(plan.unit, LOW), pltpu.VMEM(plan.unit, LOW), pltpu.VMEM((L, F), LOW), pltpu.VMEM((L, F), LOW)]
    scratch += [pltpu.VMEM(plan.unit, LOW), pltpu.VMEM(plan.unit, LOW), sems(2, 8), sems(2, 8)]
    got = plan.call(body, ins, outs, scratch, 15, deps, 24)
    return got[:4], got[4:]


def encoder_ffn_back(plan, place, grad, hidden_low, active, slope, hidden_normal, hidden_scale, stacks, norms, row, deps=()):
    L, W, F, r = plan.length, plan.width, 4 * plan.width, plan.r

    def body(place, grad, hidden_low, active, slope, hidden_normal, hidden_scale, norms, *rest):
        stacks, rest = rest[: plan.n], rest[plan.n :]
        zero_grad, norm_grads, rest = *rest[:2], rest[2:]
        grads, rest = rest[: plan.g], rest[plan.g :]
        up, down, up_grad, down_grad, sem, out_sem = rest
        copies = plan.weight_copies(place[0], stacks, 0, up, sem.at[0])
        copies += plan.weight_copies(place[0], stacks, 1, down, sem.at[1])
        start(copies)
        grad_low = grad[...].astype(LOW)
        ffn_backward_down(grad_low, active, down_grad)
        wait(copies)
        back = ffn_backward_up(grad_low, hidden_low[...], up, down, slope, up_grad, r)
        copies = plan.grad_copies(place[0], (up_grad, down_grad), grads, out_sem)
        start(copies)
        out, gain_grad, shift_grad = norm_back(grad[...] + back, hidden_normal[...], hidden_scale[...], norms[row : row + 1, :])
        zero_grad[...] = out
        norm_grads[0:1, :] = gain_grad
        norm_grads[1:2, :] = shift_grad
        wait(copies)

    ins = [(place, SMEM), (grad, VMEM), (hidden_low, VMEM), (active, VMEM), (slope, VMEM), (hidden_normal, VMEM)]
    ins += [(hidden_scale, VMEM), (norms, VMEM)] + [(s, ANY) for s in stacks]
    outs = [((L, W), WIDE, VMEM), ((2, W), WIDE, VMEM)]
    outs += [(s, LOW, ANY) for s in plan.grad_shapes(4 * r)]
    scratch = [pltpu.VMEM(plan.unit, LOW)] * 4 + [sems(2, 8), sems(2, 8)]
    got = plan.call(body, ins, outs, scratch, 11, deps, 20)
    return got[:2], got[2:]


def halves(unit_grad, r, extra):
    rows = 2 * r + extra
    return unit_grad.at[:, pl.ds(0, rows)], unit_grad.at[:, pl.ds(rows, rows)]


def self_attention_back(plan, place, grad, tokens, kept, stacks, member, extra, small=None, deps=()):
    L, W, H, r = plan.length, plan.width, plan.heads, plan.r
    qkv, mixed, probs = kept
    more = 0 if small is None else SMALL

    def body(place, grad, extra, tokens, qkv, mixed, probs, *rest):
        stacks, rest = rest[: plan.n], rest[plan.n :]
        if more:
            parts, rest = rest[:3], rest[3:]
        total, grads, rest = rest[0], rest[1 : 1 + plan.g], rest[1 + plan.g :]
        weight, weight_grad, mixed_grad, qkv_grad, sem, out_sem = rest
        copies = plan.weight_copies(place[0], stacks, member, weight, sem)
        start(copies)
        grad_low = grad[...].astype(LOW)
        set_block(weight_grad, 3, r, dot_tn(mixed[...], grad_low).astype(LOW), more)
        if more:
            for m in range(2):
                at = (m + 1) * 2 * r + m * SMALL
                rows = [parts[j][i + m : i + m + 1, :] for j, i in ((2, 0), (1, 2), (1, 0), (0, 2), (0, 0))]
                rows = jnp.concatenate(rows + [jnp.zeros((SMALL - NORMS, W), WIDE)]).astype(LOW)[None]
                weight_grad[:, at : at + SMALL, :] = jnp.broadcast_to(rows, (plan.shards, SMALL, W))
        wait(copies)
        mixed_grad[...] = dot_nt(grad_low, block(weight, 3, r)).astype(LOW)
        attend_backward(qkv, probs, mixed_grad, qkv_grad)
        x = tokens[...]
        for i in range(3):
            set_block(weight_grad, i, r, dot_tn(x, qkv_grad[:, i * W : (i + 1) * W]).astype(LOW), more if i == 2 else 0)
        copies = plan.grad_copies(place[0], halves(weight_grad, r, more), grads, out_sem)
        start(copies)
        back = grad[...] + extra[...]
        for i in range(3):
            back += dot_nt(qkv_grad[:, i * W : (i + 1) * W], block(weight, i, r))
        total[...] = back
        wait(copies)

    ins = [(place, SMEM), (grad, VMEM), (extra, VMEM), (tokens, VMEM), (qkv, VMEM), (mixed, VMEM), (probs, VMEM)]
    ins += [(s, ANY) for s in stacks] + [(v, VMEM) for v in small or ()]
    outs = [((L, W), WIDE, VMEM)] + [(s, LOW, ANY) for s in plan.grad_shapes(2 * r + more)]
    unit = (plan.shards, 4 * r + SMALL, W)
    scratch = [pltpu.VMEM(unit, LOW), pltpu.VMEM((plan.shards, 4 * r + 2 * more, W), LOW), pltpu.VMEM((L, W), LOW)]
    scratch += [pltpu.VMEM((L, 3 * W), LOW), sems(8), sems(2, 8)]
    got = plan.call(body, ins, outs, scratch, 12, deps, 18)
    return got[0], got[1:]


def cross_attention_back(plan, place, grad, query_low, memory_low, kept, stacks, query_norm, memory_norm, norms, rows, deps=()):
    L, W, H, r = plan.length, plan.width, plan.heads, plan.r
    qkv, mixed, probs = kept

    def body(place, grad, query_low, memory_low, qkv, mixed, probs, query_n, query_r, memory_n, memory_r, norms, *rest):
        stacks, rest = rest[: plan.n], rest[plan.n :]
        one_grad, enc_grad, norm_grads, grads, rest = *rest[:3], rest[3 : 3 + plan.g], rest[3 + plan.g :]
        weight, weight_grad, mixed_grad, qkv_grad, sem, out_sem = rest
        copies = plan.weight_copies(place[0], stacks, 0, weight, sem.at[0], pl.ds(0, 2 * r))
        copies += plan.weight_copies(place[0], stacks, 1, weight, sem.at[1], pl.ds(2 * r, 2 * r))
        start(copies)
        grad_low = grad[...].astype(LOW)
        set_block(weight_grad, 3, r, dot_tn(mixed[...], grad_low).astype(LOW))
        wait(copies)
        mixed_grad[...] = dot_nt(grad_low, block(weight, 3, r)).astype(LOW)
        attend_backward(qkv, probs, mixed_grad, qkv_grad)
        set_block(weight_grad, 0, r, dot_tn(query_low[...], qkv_grad[:, :W]).astype(LOW))
        memory = memory_low[...]
        for i in (1, 2):
            set_block(weight_grad, i, r, dot_tn(memory, qkv_grad[:, i * W : (i + 1) * W]).astype(LOW))
        copies = plan.grad_copies(place[0], halves(weight_grad, r, 0), grads, out_sem)
        start(copies)
        back = grad[...] + dot_nt(qkv_grad[:, :W], block(weight, 0, r))
        out, gain_grad, shift_grad = norm_back(back, query_n[...], query_r[...], norms[rows[0] : rows[0] + 1, :])
        one_grad[...] = out
        norm_grads[0:1, :] = gain_grad
        norm_grads[1:2, :] = shift_grad
        back = dot_nt(qkv_grad[:, W : 2 * W], block(weight, 1, r)) + dot_nt(qkv_grad[:, 2 * W :], block(weight, 2, r))
        out, gain_grad, shift_grad = norm_back(back, memory_n[...], memory_r[...], norms[rows[1] : rows[1] + 1, :])
        enc_grad[...] = out
        norm_grads[2:3, :] = gain_grad
        norm_grads[3:4, :] = shift_grad
        wait(copies)

    ins = [(place, SMEM), (grad, VMEM), (query_low, VMEM), (memory_low, VMEM), (qkv, VMEM), (mixed, VMEM), (probs, VMEM)]
    ins += [(v, VMEM) for v in (*query_norm, *memory_norm, norms)] + [(s, ANY) for s in stacks]
    outs = [((L, W), WIDE, VMEM), ((L, W), WIDE, VMEM), ((4, W), WIDE, VMEM)]
    outs += [(s, LOW, ANY) for s in plan.grad_shapes(2 * r)]
    scratch = [pltpu.VMEM(plan.unit, LOW), pltpu.VMEM(plan.unit, LOW), pltpu.VMEM((L, W), LOW), pltpu.VMEM((L, 3 * W), LOW)]
    scratch += [sems(2, 8), sems(2, 8)]
    got = plan.call(body, ins, outs, scratch, 13, deps, 20)
    return got[:3], got[3:]


def swap(value, bit):
    return lax.ppermute(value, "shard", [(i, i ^ bit) for i in range(8)])


def swap_rep(value, bit):
    return lax.ppermute(value, "rep", [(i, i ^ bit) for i in range(4)])


def local(body, ins, outs, deps=(), room=12, us=0):
    ins = [v if isinstance(v, tuple) else (v, VMEM) for v in ins]

    def run(*refs):
        body(*refs[len(deps) :])

    return pl.pallas_call(
        run,
        in_specs=[ANY] * len(deps) + [spec for _, spec in ins],
        out_shape=[jax.ShapeDtypeStruct(shape, dtype) for shape, dtype in outs],
        out_specs=[VMEM] * len(outs),
        compiler_params=pltpu.CompilerParams(vmem_limit_bytes=room << 20),
        cost_estimate=pl.CostEstimate(flops=int(us * 5e9), bytes_accessed=1 << 20, transcendentals=0),
    )(*deps, *[v for v, _ in ins])


def mark(out):
    out[...] = jnp.zeros_like(out)


def pack_self(plan, attn_in, attn_out, small):
    W, r = plan.width, plan.r

    def body(attn_in, attn_out, small, out):
        for k in range(2):
            for i in range(3):
                out[k, i * r : (i + 1) * r, :] = attn_in[k, :, i * W : (i + 1) * W]
            out[k, 3 * r : 4 * r, :] = attn_out[k]
            out[k, 4 * r :, :] = small[...]

    return local(body, [attn_in, attn_out, small], [((2, 4 * r + SMALL, W), LOW)])[0]


def pack_rest(plan, attn_in, attn_out, ffn_up, ffn_down, deps):
    W, r = plan.width, plan.r

    def body(attn_in, attn_out, ffn_up, ffn_down, first, cross, second):
        for k, out in enumerate((first, second)):
            for i in range(4):
                out[0, i * r : (i + 1) * r, :] = ffn_up[k, :, i * W : (i + 1) * W]
            out[1] = ffn_down[k]
        for i in range(3):
            cross[i // 2, (i % 2) * r : (i % 2 + 1) * r, :] = attn_in[2, :, i * W : (i + 1) * W]
        cross[1, r:, :] = attn_out[2]

    outs = [((2, 4 * r, W), LOW), ((2, 2 * r, W), LOW), ((2, 4 * r, W), LOW)]
    return local(body, [attn_in, attn_out, ffn_up, ffn_down], outs, deps)


class Gather:
    def __init__(self, plan, pair):
        self.plan, self.pair = plan, pair
        self.near, self.far = [], []
        if plan.split:
            self.near = [swap(pair, X), swap(pair, Y)]

    def onward(self, deps=()):
        if not self.plan.split:
            return []

        def body(by_x, by_y, first, second):
            first[...] = by_x[0]
            second[...] = by_y[1]

        first, second = local(body, self.near, [(self.pair.shape[1:], LOW)] * 2, deps)
        self.far = [swap(first, Y), swap(second, X)]
        return [first]

    def stack(self, deps=()):
        if not self.plan.split:
            self.stacks = [lax.all_gather(self.pair, "shard", axis=0)]
            return []

        def body(pair, by_x, by_y, first, second, out):
            for j, v in enumerate((pair, by_x, by_y)):
                out[2 * j : 2 * j + 2] = v[...]
            out[6] = first[...]
            out[7] = second[...]

        mine = local(body, [self.pair, *self.near, *self.far], [((8, *self.pair.shape[1:]), LOW)], deps)[0]
        self.stacks = [mine, swap(mine, CORE)]
        return [mine]


class Reduction:
    def __init__(self, plan, z):
        self.plan = plan
        self.odd = (z & 1).astype(jnp.int32)[None]
        self.pairs, self.results, self.moving = [], {}, {}

    def add(self, name, outs):
        if not self.plan.split:
            whole = outs[0]
            flat = whole.reshape((-1,) + whole.shape[2:])
            own = lax.psum_scatter(flat, "shard", scatter_dimension=0, tiled=True)
            self.results[name] = lax.psum(own, "rep").astype(WIDE).reshape(whole.shape[1:])
            return
        mine, other = outs
        self.pairs.append(dict(name=name, rows=mine.shape[1], step=0, keep=mine, slot={}, got=swap(other, CORE)))

    def advance(self, deps=()):
        if not self.pairs:
            return []
        W = self.plan.width
        sizes = {"x": 0, "y": 0, "n": 0, "f": 0}

        def place(way, count):
            at = sizes[way]
            sizes[way] += count
            return at

        work = []
        for p in self.pairs:
            R, step = p["rows"], p["step"]
            ways = ({"x": 2 * R, "y": 2 * R}, {"x": R, "y": R}, {"n": R}, {"f": R}, {"n": R})[step]
            work.append(dict(p, out={way: place(way, count) for way, count in ways.items()}, kept=((4, 2, 1, 1, 1)[step] * R, W)))
        ways = [w for w in "xynf" if sizes[w]]
        came = [w for w in "xynf" if w in self.moving]
        cores = [t for t in work if t["step"] == 0]

        def body(odd, *refs):
            keep_in, refs = refs[: len(work)], refs[len(work) :]
            core_in, refs = refs[: len(cores)], refs[len(cores) :]
            got, refs = dict(zip(came, refs[: len(came)])), refs[len(came) :]
            keep_out, refs = refs[: len(work)], refs[len(work) :]
            leave = dict(zip(ways, refs))
            odds = odd[0] != 0

            def total(left, right):
                return (left.astype(WIDE) + right.astype(WIDE)).astype(LOW)

            core = iter(core_in)
            for t, keep, out in zip(work, keep_in, keep_out):
                R, step, slot, to = t["rows"], t["step"], t["slot"], t["out"]
                if step == 0:
                    other = next(core)
                    for m, way in enumerate("xy"):
                        at = 4 * m * R
                        out[2 * m * R : 2 * (m + 1) * R, :] = total(keep[at : at + 2 * R, :], other[at : at + 2 * R, :])
                        at += 2 * R
                        leave[way][to[way] : to[way] + 2 * R, :] = total(keep[at : at + 2 * R, :], other[at : at + 2 * R, :])
                elif step == 1:
                    for m, (way, onward) in enumerate(("xy", "yx")):
                        other, at, kept = got[way], slot[way], 2 * m * R
                        out[m * R : (m + 1) * R, :] = total(keep[kept : kept + R, :], other[at : at + R, :])
                        kept, at = kept + R, at + R
                        leave[onward][to[onward] : to[onward] + R, :] = total(keep[kept : kept + R, :], other[at : at + R, :])
                elif step == 2:
                    first = total(keep[:R, :], got["y"][slot["y"] : slot["y"] + R, :])
                    second = total(keep[R:, :], got["x"][slot["x"] : slot["x"] + R, :])
                    out[...] = jnp.where(odds, second, first)
                    leave["n"][to["n"] : to["n"] + R, :] = jnp.where(odds, first, second)
                else:
                    way, onward = ("n", "f") if step == 3 else ("f", "n")
                    value = total(keep[...], got[way][slot[way] : slot[way] + R, :])
                    out[...] = value
                    leave[onward][to[onward] : to[onward] + R, :] = value

        if cores and came:
            deps = local(mark, [], [((8, 128), WIDE)], [*deps, *self.moving.values()], 2, 20)
        keeps = [t["keep"].reshape(-1, W) for t in work]
        gots = [t["got"].reshape(-1, W) for t in cores]
        outs = [(t["kept"], LOW) for t in work] + [((sizes[w], W), LOW) for w in ways]
        done = local(body, [(self.odd, SMEM), *keeps, *gots, *[self.moving[w] for w in came]], outs, deps)
        self.moving = {}
        for way, value in zip(ways, done[len(work) :]):
            self.moving[way] = swap_rep(value, Z1 if way == "n" else Z2) if way in "nf" else swap(value, X if way == "x" else Y)
        self.pairs = []
        for t, kept in zip(work, done):
            if t["step"] == 4:
                self.results[t["name"]] = (kept, self.moving["n"], t["out"]["n"])
            else:
                self.pairs.append(dict(name=t["name"], rows=t["rows"], step=t["step"] + 1, keep=kept, slot=t["out"]))
        return [done[0]]


ATT, FFN = ("a0", "a1", "a2"), ("f0", "f1")


def outputs(plan, sums, place):
    W, r = plan.width, plan.r
    wide = W // plan.shards
    results = sums.results
    if not plan.split:
        me = lax.axis_index("shard")
        att = [results[k] for k in ATT]
        small = lax.dynamic_slice(att[0], (0, 2 * r, me * wide), (2, NORMS, wide))
        att = jnp.stack([v[:, : 2 * r].reshape(4, r, W) for v in att])
        ffn = jnp.stack([results[k] for k in FFN])

        def unblocks(v):
            return jnp.moveaxis(v, 1, 2).reshape(v.shape[0], r, -1)

        return unblocks(att[:, :3]), att[:, 3], unblocks(ffn[:, 0].reshape(2, 4, r, W)), ffn[:, 1], small[0], small[1]
    names = ATT + FFN
    keeps = [results[k][0] for k in names]
    gots = []
    for k in names:
        if not any(results[k][1] is v for v in gots):
            gots.append(results[k][1])

    def body(odd, place, *refs):
        keep, refs = refs[: len(names)], refs[len(names) :]
        got, refs = refs[: len(gots)], refs[len(gots) :]
        attn_in, attn_out, ffn_up, ffn_down, gain, shift = refs
        odds = odd[0] != 0

        def member(i, m, at, rows):
            _, array, offset = results[names[i]]
            j = [v is array for v in gots].index(True)
            kept, other = keep[i][at : at + rows, :], got[j][offset + at : offset + at + rows, :]
            return (jnp.where(odds, other, kept) if m == 0 else jnp.where(odds, kept, other)).astype(WIDE)

        for a in range(len(ATT)):
            for i in range(3):
                attn_in[a, :, i * W : (i + 1) * W] = member(a, i // 2, (i % 2) * r, r)
            attn_out[a] = member(a, 1, r, r)
        for f in range(len(FFN)):
            for i in range(4):
                ffn_up[f, :, i * W : (i + 1) * W] = member(3 + f, 0, i * r, r)
            ffn_down[f] = member(3 + f, 1, 0, 4 * r)
        turn = lax.rem(W - place[0] * wide, W)
        for m, out in enumerate((gain, shift)):
            out[...] = pltpu.roll(member(0, m, 2 * r, SMALL), turn, axis=1)[:NORMS, :wide]

    outs = [((3, r, 3 * W), WIDE), ((3, r, W), WIDE), ((2, r, 4 * W), WIDE), ((2, 4 * r, W), WIDE)] + [((NORMS, wide), WIDE)] * 2
    return local(body, [(sums.odd, SMEM), (place, SMEM), *keeps, *gots], outs, room=16)


def shards(sizes, source, target, source_seg, target_seg, attn_in, attn_out, ffn_up, ffn_down, norm_gain, norm_bias, cotangent):
    plan = Plan(sizes, source.shape[1], source.shape[2])
    W, r = plan.width, plan.r
    me = lax.axis_index("shard")
    place = (me if plan.split else jnp.zeros_like(me))[None]
    src, tgt = source[0], target[0]
    src_row, src_col = source_seg, source_seg.reshape(-1, 1)
    tgt_row, tgt_col = target_seg, target_seg.reshape(-1, 1)

    small = jnp.concatenate([norm_gain, norm_bias])
    small = lax.dynamic_update_slice(jnp.zeros((SMALL, W), LOW), small, (0, me * small.shape[1]))
    pair = pack_self(plan, attn_in, attn_out, small)
    w01 = Gather(plan, pair)
    pair_f0, pair_2, pair_f1 = pack_rest(plan, attn_in, attn_out, ffn_up, ffn_down, [pair])
    f0 = Gather(plan, pair_f0)
    went = w01.onward()
    w2 = Gather(plan, after(pair_2, went))
    stacked = w01.stack()
    went = f0.onward(stacked)
    f1 = Gather(plan, after(pair_f1, stacked))

    first, first_low, n0, r0, *kept_enc, norms = self_attention(
        plan, place, src, src_row, src_col, w01.stacks, 0, 0, False, went
    )
    went = w2.onward([r0])
    stacked = f0.stack([r0])
    one, one_low, n2, r2, *kept_self, _ = self_attention(
        plan, place, tgt, tgt_row, tgt_col, w01.stacks, 1, 2, True, [r0] + went + stacked
    )
    went = f1.onward([r2])
    stacked = w2.stack([r2])
    enc_low, n1, r1, active, slope = encoder_ffn(
        plan, place, first, first_low, src, f0.stacks, norms, 1, [r2] + went + stacked
    )
    stacked = f1.stack([r1])
    two, two_low, n3, r3, *kept_cross = cross_attention(
        plan, place, one, one_low, enc_low, tgt_row, src_col, w2.stacks, norms, 3, stacked
    )
    (decoded, last_grad, two_grad, norm_a), grads = decoder_ffn(
        plan, place, two, two_low, tgt, cotangent[0], n3, r3, f1.stacks, norms, 4
    )
    sums = Reduction(plan, lax.axis_index("rep"))
    sums.add("f1", grads)
    deps = sums.advance()
    (one_grad, enc_grad, norm_b), grads = cross_attention_back(
        plan, place, two_grad, one_low, enc_low, kept_cross, w2.stacks, (n2, r2), (n1, r1), norms, (2, 1), deps
    )
    sums.add("a2", grads)
    deps = sums.advance([norm_b])
    (zero_grad, norm_c), grads = encoder_ffn_back(
        plan, place, enc_grad, first_low, active, slope, n0, r0, f0.stacks, norms, 0, deps
    )
    sums.add("f0", grads)
    deps = sums.advance([norm_c])
    tgt_grad, grads = self_attention_back(plan, place, one_grad, tgt, kept_self, w01.stacks, 1, last_grad, None, deps)
    sums.add("a1", grads)
    deps = sums.advance([tgt_grad])
    src_grad, grads = self_attention_back(
        plan, place, zero_grad, src, kept_enc, w01.stacks, 0, enc_grad, (norm_a, norm_b, norm_c), deps
    )
    sums.add("a0", grads)
    sums.advance([src_grad])
    while sums.pairs:
        sums.advance()
    return decoded[None], src_grad[None], tgt_grad[None], *outputs(plan, sums, place)


def after(value, deps):
    if not deps:
        return value

    def body(*refs):
        pass

    return pl.pallas_call(
        body,
        in_specs=[ANY] * (1 + len(deps)),
        out_shape=jax.ShapeDtypeStruct(value.shape, value.dtype),
        out_specs=ANY,
        input_output_aliases={0: 0},
        cost_estimate=pl.CostEstimate(flops=0, bytes_accessed=0, transcendentals=0),
    )(value, *deps)


def solution(mesh):
    sizes = (mesh.shape["shard"], mesh.shape["rep"])
    tokens = P(("shard", "rep"), None, None)
    ids = P(("shard", "rep"), None)
    weight = P(None, "shard", None)
    norm = P(None, "shard")
    return jax.shard_map(
        functools.partial(shards, sizes),
        mesh=mesh,
        in_specs=(tokens, tokens, ids, ids, weight, weight, weight, weight, norm, norm, tokens),
        out_specs=(tokens, tokens, tokens, weight, weight, weight, weight, norm, norm),
        check_vma=False,
    )
```

```python
import functools

import jax
import jax.numpy as jnp
from jax import lax
from jax.experimental import pallas as pl
from jax.experimental.pallas import tpu as pltpu
from jax.sharding import PartitionSpec as P

HEAD = 64
PAIR = 2 * HEAD
EPS = 1e-05
NEG = -1e30
LOW = jnp.bfloat16
WIDE = jnp.float32
CORE, X, Y = 1, 2, 4
Z1, Z2 = 1, 2
SMALL = 16
NORMS = 5
VMEM = pl.BlockSpec(memory_space=pltpu.VMEM)
SMEM = pl.BlockSpec(memory_space=pltpu.SMEM)
ANY = pl.BlockSpec(memory_space=pl.ANY)


def dot(left, right):
    return lax.dot_general(left, right, (((1,), (0,)), ((), ())), preferred_element_type=WIDE)


def dot_nt(left, right):
    return lax.dot_general(left, right, (((1,), (1,)), ((), ())), preferred_element_type=WIDE)


def dot_tn(left, right):
    return lax.dot_general(left, right, (((0,), (0,)), ((), ())), preferred_element_type=WIDE)


def block(unit, i, r):
    part = unit[:, i * r : (i + 1) * r, :]
    return part.reshape(part.shape[0] * r, part.shape[2])


def rows_block(unit, i, r):
    n = unit.shape[0] // 4
    part = unit[i * n : (i + 1) * n, 4 * r :, :]
    return part.reshape(n * part.shape[1], part.shape[2])


def norm(value, gain, shift):
    mean = jnp.mean(value, axis=-1, keepdims=True)
    centred = value - mean
    scale = lax.rsqrt(jnp.mean(centred * centred, axis=-1, keepdims=True) + EPS)
    normal = centred * scale
    return normal * gain + shift, normal, scale


def norm_back(grad, normal, scale, gain):
    gain_grad = jnp.sum(grad * normal, axis=0, keepdims=True)
    shift_grad = jnp.sum(grad, axis=0, keepdims=True)
    inner = grad * gain
    inner_mean = jnp.mean(inner, axis=-1, keepdims=True)
    cross_mean = jnp.mean(inner * normal, axis=-1, keepdims=True)
    return scale * (inner - inner_mean - normal * cross_mean), gain_grad, shift_grad


def lanes_of(head, value):
    lane = lax.broadcasted_iota(jnp.int32, value.shape, 1)
    return jnp.where((lane < HEAD) if head == 0 else (lane >= HEAD), value, jnp.zeros_like(value))


def pick(first, second):
    lane = lax.broadcasted_iota(jnp.int32, first.shape, 1)
    return jnp.where(lane < HEAD, first, second)


def allowed_bias(memory_ids, query_ids, causal):
    allowed = memory_ids == query_ids
    if causal:
        shape = (memory_ids.shape[0], query_ids.shape[1])
        allowed = allowed & (lax.broadcasted_iota(jnp.int32, shape, 1) >= lax.broadcasted_iota(jnp.int32, shape, 0))
    return jnp.where(allowed, 0.0, NEG)


def attend_forward(qkv, probs, mixed, bias):
    width = mixed.shape[1]
    for pair in range(width // PAIR):
        at = pl.ds(pair * PAIR, PAIR)
        query = qkv[:, pl.ds(pair * PAIR, PAIR)] * LOW(HEAD ** -0.5)
        keys = qkv[:, pl.ds(width + pair * PAIR, PAIR)]
        values = qkv[:, pl.ds(2 * width + pair * PAIR, PAIR)]
        out = []
        for head in range(2):
            scores = dot_nt(keys, lanes_of(head, query)) + bias[...]
            top = jnp.max(scores, axis=0, keepdims=True)
            weights = jnp.exp(scores - top)
            total = jnp.sum(weights, axis=0, keepdims=True)
            low = (weights * (1.0 / total)).astype(LOW)
            probs[2 * pair + head] = low
            out.append(dot_tn(low, values))
        mixed[:, at] = pick(*out).astype(LOW)


def attend_backward(qkv, probs, mixed_grad, qkv_grad):
    width = mixed_grad.shape[1]
    for pair in range(width // PAIR):
        query = qkv[:, pl.ds(pair * PAIR, PAIR)]
        keys = qkv[:, pl.ds(width + pair * PAIR, PAIR)]
        values = qkv[:, pl.ds(2 * width + pair * PAIR, PAIR)]
        grad = mixed_grad[:, pl.ds(pair * PAIR, PAIR)]
        dq, dk, dv = [], [], []
        for head in range(2):
            low = probs[2 * pair + head]
            prob = low.astype(WIDE)
            prob_grad = dot_nt(values, lanes_of(head, grad))
            delta = jnp.sum(prob * prob_grad, axis=0, keepdims=True)
            score_grad = (prob * (prob_grad - delta)).astype(LOW)
            dv.append(dot(low, grad))
            dk.append(dot(score_grad, query))
            dq.append(dot_tn(score_grad, keys))
        scale = HEAD ** -0.5
        qkv_grad[:, pl.ds(pair * PAIR, PAIR)] = (pick(*dq) * scale).astype(LOW)
        qkv_grad[:, pl.ds(width + pair * PAIR, PAIR)] = (pick(*dk) * scale).astype(LOW)
        qkv_grad[:, pl.ds(2 * width + pair * PAIR, PAIR)] = pick(*dv).astype(LOW)


GELU = 0.7978845608028654


def gelu_and_slope(value):
    square = value * value
    inner = GELU * value * (1.0 + 0.044715 * square)
    t = jnp.tanh(inner)
    half = 0.5 + 0.5 * t
    slope = half + 0.5 * value * (1.0 - t * t) * (GELU * (1.0 + 3 * 0.044715 * square))
    return value * half, slope


def ffn_forward(hidden, weight, active, slope, r):
    W = hidden.shape[1]
    total = None
    for c in range(4):
        at = pl.ds(c * W, W)
        act, sl = gelu_and_slope(dot(hidden, block(weight, c, r)))
        act = act.astype(LOW)
        active[:, at] = act
        slope[:, at] = sl.astype(LOW)
        part = dot(act, rows_block(weight, c, r))
        total = part if total is None else total + part
    return total


def ffn_backward_down(grad, active, put):
    W = grad.shape[1]
    for c in range(4):
        put(c, dot_tn(active[:, pl.ds(c * W, W)], grad).astype(LOW))


def ffn_backward_up(grad, hidden, weight, slope, r, put):
    W = grad.shape[1]
    total = None
    for c in range(4):
        z = (dot_nt(grad, rows_block(weight, c, r)) * slope[:, pl.ds(c * W, W)].astype(WIDE)).astype(LOW)
        put(c, dot_tn(hidden, z).astype(LOW))
        part = dot_nt(z, block(weight, c, r))
        total = part if total is None else total + part
    return total


class Plan:
    def __init__(self, sizes, length, width):
        self.split = sizes == (8, 4)
        self.sizes = sizes
        self.length, self.width = length, width
        self.heads = width // HEAD
        self.shards = sizes[0]
        self.r = width // self.shards
        self.n = self.g = 2 if self.split else 1


    def lay(self, place, stacks, member, rows, unit, at):
        count = rows.stop - rows.start
        if not self.split:
            unit[:, at : at + count, :] = stacks[0][:, member, rows]
            return
        odd, chip = (place & 1) != 0, place >> 1
        for j in range(4):
            k = 2 * (j ^ chip) + member
            mine, other = stacks[0][k, rows, :], stacks[1][k, rows, :]
            unit[2 * j, at : at + count, :] = jnp.where(odd, other, mine)
            unit[2 * j + 1, at : at + count, :] = jnp.where(odd, mine, other)


    def grad_shapes(self, rows):
        if not self.split:
            return [(self.shards, 2, rows, self.width)]
        return [(8, rows, self.width)] * 2

    def leave(self, place, outs, member, at, value, first=0):
        count = value.shape[1]
        if not self.split:
            outs[0][first : first + value.shape[0], member, at : at + count, :] = value
            return
        odd, chip = (place & 1) != 0, place >> 1
        for j in range(value.shape[0] // 2):
            k = (first // 2 + j) ^ chip
            if member == 0:
                k = ((k & 1) << 1) | (k >> 1)
            one, two = value[2 * j], value[2 * j + 1]
            outs[0][4 * member + k, at : at + count, :] = jnp.where(odd, two, one)
            outs[1][4 * member + k, at : at + count, :] = jnp.where(odd, one, two)

    def leave_block(self, place, outs, member, i, value):
        self.leave(place, outs, member, i * self.r, value.reshape(self.shards, self.r, self.width))

    def leave_rows(self, place, outs, member, i, value):
        n = self.shards // 4
        self.leave(place, outs, member, 0, value.reshape(n, 4 * self.r, self.width), i * n)

    def call(self, body, ins, outs, scratch, us, deps, room):
        def run(*refs):
            body(*refs[len(deps) :])

        return pl.pallas_call(
            run,
            in_specs=[ANY] * len(deps) + [spec for _, spec in ins],
            out_shape=[jax.ShapeDtypeStruct(shape, dtype) for shape, dtype in outs],
            out_specs=[VMEM] * len(outs),
            scratch_shapes=scratch,
            compiler_params=pltpu.CompilerParams(vmem_limit_bytes=room << 20),
            cost_estimate=pl.CostEstimate(flops=int(us * 5e9), bytes_accessed=1 << 20, transcendentals=0),
        )(*deps, *[value for value, _ in ins])


def vmem(*arrays):
    return [(v, VMEM) for v in arrays]


def self_attention(plan, place, tokens, id_row, id_col, stacks, member, row, causal, deps=(), us=10):
    L, W, H, r = plan.length, plan.width, plan.heads, plan.r

    def body(place, tokens, id_row, id_col, *rest):
        stacks, rest = rest[: plan.n], rest[plan.n :]
        out, out_low, normal, scale, qkv, mixed, probs, weight, norms, bias = rest
        plan.lay(place[0], stacks, member, slice(0, 4 * r), weight, 0)
        bias[...] = allowed_bias(id_col[...], id_row[...], causal)
        if plan.split:
            norms[...] = sum(jnp.sum(s[...].astype(WIDE), axis=0) for s in (v.at[:, 4 * r : 4 * r + SMALL, :] for v in stacks)) * 0.5
        else:
            norms[...] = jnp.sum(stacks[0][:, member, 4 * r : 4 * r + SMALL].astype(WIDE), axis=0)
        x = tokens[...]
        for i in range(3):
            qkv[:, i * W : (i + 1) * W] = dot(x, block(weight, i, r)).astype(LOW)
        attend_forward(qkv, probs, mixed, bias)
        value = x.astype(WIDE) + dot(mixed[...], block(weight, 3, r))
        y, n, s = norm(value, norms[row : row + 1, :], norms[NORMS + row : NORMS + row + 1, :])
        out[...] = y
        out_low[...] = y.astype(LOW)
        normal[...] = n.astype(LOW)
        scale[...] = s

    ins = [(place, SMEM)] + vmem(tokens, id_row, id_col, *stacks)
    outs = [((L, W), WIDE), ((L, W), LOW), ((L, W), LOW), ((L, 1), WIDE)]
    outs += [((L, 3 * W), LOW), ((L, W), LOW), ((H, L, L), LOW), ((plan.shards, 4 * r, W), LOW), ((SMALL, W), WIDE)]
    return plan.call(body, ins, outs, [pltpu.VMEM((L, L), WIDE)], us, deps, 11)


def cross_attention(plan, place, query_in, query_low, memory_low, query_ids, memory_ids, stacks, norms, row, deps=()):
    L, W, H, r = plan.length, plan.width, plan.heads, plan.r

    def body(place, query_in, query_low, memory_low, query_ids, memory_ids, norms, *rest):
        stacks, rest = rest[: plan.n], rest[plan.n :]
        out, out_low, normal, scale, qkv, mixed, probs, weight, bias = rest
        at = 4 * r
        for m in range(2):
            plan.lay(place[0], stacks, m, slice(at, at + 2 * r), weight, 2 * m * r)
        bias[...] = allowed_bias(memory_ids[...], query_ids[...], False)
        qkv[:, :W] = dot(query_low[...], block(weight, 0, r)).astype(LOW)
        memory = memory_low[...]
        for i in (1, 2):
            qkv[:, i * W : (i + 1) * W] = dot(memory, block(weight, i, r)).astype(LOW)
        attend_forward(qkv, probs, mixed, bias)
        value = query_in[...] + dot(mixed[...], block(weight, 3, r))
        y, n, s = norm(value, norms[row : row + 1, :], norms[NORMS + row : NORMS + row + 1, :])
        out[...] = y
        out_low[...] = y.astype(LOW)
        normal[...] = n.astype(LOW)
        scale[...] = s

    ins = [(place, SMEM)] + vmem(query_in, query_low, memory_low, query_ids, memory_ids, norms, *stacks)
    outs = [((L, W), WIDE), ((L, W), LOW), ((L, W), LOW), ((L, 1), WIDE)]
    outs += [((L, 3 * W), LOW), ((L, W), LOW), ((H, L, L), LOW), ((plan.shards, 4 * r, W), LOW)]
    return plan.call(body, ins, outs, [pltpu.VMEM((L, L), WIDE)], 10, deps, 11)


def encoder_ffn(plan, place, hidden, hidden_low, tokens, stacks, norms, row, deps=()):
    L, W, F, r = plan.length, plan.width, 4 * plan.width, plan.r

    def body(place, hidden, hidden_low, tokens, norms, *rest):
        stacks, rest = rest[: plan.n], rest[plan.n :]
        out_low, normal, scale, active, slope, weight = rest
        for m in range(2):
            plan.lay(place[0], stacks, m, slice(0, 4 * r), weight, 4 * m * r)
        branch = ffn_forward(hidden_low[...], weight, active, slope, r)
        value = hidden[...] + branch + tokens[...].astype(WIDE)
        y, n, s = norm(value, norms[row : row + 1, :], norms[NORMS + row : NORMS + row + 1, :])
        out_low[...] = y.astype(LOW)
        normal[...] = n.astype(LOW)
        scale[...] = s

    ins = [(place, SMEM)] + vmem(hidden, hidden_low, tokens, norms, *stacks)
    outs = [((L, W), LOW), ((L, W), LOW), ((L, 1), WIDE), ((L, F), LOW), ((L, F), LOW), ((plan.shards, 8 * r, W), LOW)]
    return plan.call(body, ins, outs, [], 9, deps, 11)


def decoder_ffn(plan, place, hidden, hidden_low, tokens, cotangent, hidden_normal, hidden_scale, stacks, norms, row, deps=()):
    L, W, F, r, S = plan.length, plan.width, 4 * plan.width, plan.r, plan.shards

    def body(place, hidden, hidden_low, tokens, cotangent, hidden_normal, hidden_scale, norms, *rest):
        stacks, rest = rest[: plan.n], rest[plan.n :]
        decoded, last_grad, two_grad, norm_grads, *grads, weight, active, slope = rest
        for m in range(2):
            plan.lay(place[0], stacks, m, slice(0, 4 * r), weight, 4 * m * r)
        low = hidden_low[...]
        branch = ffn_forward(low, weight, active, slope, r)
        value = hidden[...] + branch + tokens[...].astype(WIDE)
        gain = norms[row : row + 1, :]
        y, n, s = norm(value, gain, norms[NORMS + row : NORMS + row + 1, :])
        decoded[...] = y.astype(LOW)
        grad, gain_grad, shift_grad = norm_back(cotangent[...].astype(WIDE), n, s, gain)
        last_grad[...] = grad
        norm_grads[0:1, :] = gain_grad
        norm_grads[1:2, :] = shift_grad
        grad_low = grad.astype(LOW)
        ffn_backward_down(grad_low, active, lambda i, v: plan.leave_rows(place[0], grads, 1, i, v))
        back = ffn_backward_up(
            grad_low, low, weight, slope, r, lambda i, v: plan.leave_block(place[0], grads, 0, i, v)
        )
        normal = hidden_normal[...].astype(WIDE)
        grad, gain_grad, shift_grad = norm_back(last_grad[...] + back, normal, hidden_scale[...], norms[row - 1 : row, :])
        two_grad[...] = grad
        norm_grads[2:3, :] = gain_grad
        norm_grads[3:4, :] = shift_grad

    ins = [(place, SMEM)] + vmem(hidden, hidden_low, tokens, cotangent, hidden_normal, hidden_scale, norms, *stacks)
    outs = [((L, W), LOW), ((L, W), WIDE), ((L, W), WIDE), ((4, W), WIDE)] + [(s, LOW) for s in plan.grad_shapes(4 * r)]
    scratch = [pltpu.VMEM((S, 8 * r, W), LOW), pltpu.VMEM((L, F), LOW), pltpu.VMEM((L, F), LOW)]
    got = plan.call(body, ins, outs, scratch, 15, deps, 18)
    return got[:4], got[4:]


def encoder_ffn_back(plan, place, grad, hidden_low, active, slope, hidden_normal, hidden_scale, weight, norms, row, deps=()):
    L, W, r = plan.length, plan.width, plan.r

    def body(place, grad, hidden_low, active, slope, hidden_normal, hidden_scale, weight, norms, *rest):
        zero_grad, norm_grads, *grads = rest
        grad_low = grad[...].astype(LOW)
        ffn_backward_down(grad_low, active, lambda i, v: plan.leave_rows(place[0], grads, 1, i, v))
        back = ffn_backward_up(
            grad_low, hidden_low[...], weight, slope, r, lambda i, v: plan.leave_block(place[0], grads, 0, i, v)
        )
        normal = hidden_normal[...].astype(WIDE)
        out, gain_grad, shift_grad = norm_back(grad[...] + back, normal, hidden_scale[...], norms[row : row + 1, :])
        zero_grad[...] = out
        norm_grads[0:1, :] = gain_grad
        norm_grads[1:2, :] = shift_grad

    ins = [(place, SMEM)] + vmem(grad, hidden_low, active, slope, hidden_normal, hidden_scale, weight, norms)
    outs = [((L, W), WIDE), ((2, W), WIDE)] + [(s, LOW) for s in plan.grad_shapes(4 * r)]
    got = plan.call(body, ins, outs, [], 11, deps, 14)
    return got[:2], got[2:]


def self_attention_back(plan, place, grad, tokens, kept, extra, small=None, deps=()):
    L, W, r = plan.length, plan.width, plan.r
    more = 0 if small is None else SMALL

    def body(place, grad, extra, tokens, qkv, mixed, probs, weight, *rest):
        parts, rest = rest[: 3 if more else 0], rest[3 if more else 0 :]
        total, *grads, mixed_grad, qkv_grad = rest
        grad_low = grad[...].astype(LOW)
        plan.leave_block(place[0], grads, 1, 1, dot_tn(mixed[...], grad_low).astype(LOW))
        for m in range(2 if more else 0):
            rows = [parts[j][i + m : i + m + 1, :] for j, i in ((2, 0), (1, 2), (1, 0), (0, 2), (0, 0))]
            rows = jnp.concatenate(rows + [jnp.zeros((SMALL - NORMS, W), WIDE)]).astype(LOW)[None]
            plan.leave(place[0], grads, m, 2 * r, jnp.broadcast_to(rows, (plan.shards, SMALL, W)))
        mixed_grad[...] = dot_nt(grad_low, block(weight, 3, r)).astype(LOW)
        attend_backward(qkv, probs, mixed_grad, qkv_grad)
        x = tokens[...]
        for i in range(3):
            plan.leave_block(place[0], grads, i // 2, i % 2, dot_tn(x, qkv_grad[:, i * W : (i + 1) * W]).astype(LOW))
        back = grad[...] + extra[...]
        for i in range(3):
            back += dot_nt(qkv_grad[:, i * W : (i + 1) * W], block(weight, i, r))
        total[...] = back

    ins = [(place, SMEM)] + vmem(grad, extra, tokens, *kept, *(small or ()))
    outs = [((L, W), WIDE)] + [(s, LOW) for s in plan.grad_shapes(2 * r + more)]
    scratch = [pltpu.VMEM((L, W), LOW), pltpu.VMEM((L, 3 * W), LOW)]
    got = plan.call(body, ins, outs, scratch, 12, deps, 12)
    return got[0], got[1:]


def cross_attention_back(plan, place, grad, query_low, memory_low, kept, query_norm, memory_norm, norms, rows, deps=()):
    L, W, r = plan.length, plan.width, plan.r

    def body(place, grad, query_low, memory_low, qkv, mixed, probs, weight, query_n, query_r, memory_n, memory_r, norms, *rest):
        one_grad, enc_grad, norm_grads, *grads, mixed_grad, qkv_grad = rest
        grad_low = grad[...].astype(LOW)
        plan.leave_block(place[0], grads, 1, 1, dot_tn(mixed[...], grad_low).astype(LOW))
        mixed_grad[...] = dot_nt(grad_low, block(weight, 3, r)).astype(LOW)
        attend_backward(qkv, probs, mixed_grad, qkv_grad)
        plan.leave_block(place[0], grads, 0, 0, dot_tn(query_low[...], qkv_grad[:, :W]).astype(LOW))
        memory = memory_low[...]
        for i in (1, 2):
            value = dot_tn(memory, qkv_grad[:, i * W : (i + 1) * W]).astype(LOW)
            plan.leave_block(place[0], grads, i // 2, i % 2, value)
        back = grad[...] + dot_nt(qkv_grad[:, :W], block(weight, 0, r))
        normal = query_n[...].astype(WIDE)
        out, gain_grad, shift_grad = norm_back(back, normal, query_r[...], norms[rows[0] : rows[0] + 1, :])
        one_grad[...] = out
        norm_grads[0:1, :] = gain_grad
        norm_grads[1:2, :] = shift_grad
        back = dot_nt(qkv_grad[:, W : 2 * W], block(weight, 1, r)) + dot_nt(qkv_grad[:, 2 * W :], block(weight, 2, r))
        normal = memory_n[...].astype(WIDE)
        out, gain_grad, shift_grad = norm_back(back, normal, memory_r[...], norms[rows[1] : rows[1] + 1, :])
        enc_grad[...] = out
        norm_grads[2:3, :] = gain_grad
        norm_grads[3:4, :] = shift_grad

    ins = [(place, SMEM)] + vmem(grad, query_low, memory_low, *kept, *query_norm, *memory_norm, norms)
    outs = [((L, W), WIDE), ((L, W), WIDE), ((4, W), WIDE)] + [(s, LOW) for s in plan.grad_shapes(2 * r)]
    scratch = [pltpu.VMEM((L, W), LOW), pltpu.VMEM((L, 3 * W), LOW)]
    got = plan.call(body, ins, outs, scratch, 13, deps, 13)
    return got[:3], got[3:]


def swap(value, bit):
    return lax.ppermute(value, "shard", [(i, i ^ bit) for i in range(8)])


def swap_rep(value, bit):
    return lax.ppermute(value, "rep", [(i, i ^ bit) for i in range(4)])


def local(body, ins, outs, deps=(), room=6, us=0):
    ins = [v if isinstance(v, tuple) else (v, VMEM) for v in ins]

    def run(*refs):
        body(*refs[len(deps) :])

    return pl.pallas_call(
        run,
        in_specs=[ANY] * len(deps) + [spec for _, spec in ins],
        out_shape=[jax.ShapeDtypeStruct(shape, dtype) for shape, dtype in outs],
        out_specs=[VMEM] * len(outs),
        compiler_params=pltpu.CompilerParams(vmem_limit_bytes=room << 20),
        cost_estimate=pl.CostEstimate(flops=int(us * 5e9), bytes_accessed=1 << 20, transcendentals=0),
    )(*deps, *[v for v, _ in ins])


def mark(out):
    out[...] = jnp.zeros_like(out)


def wait_for(plan, deps, us):
    return local(mark, [], [((8, 128), WIDE)], deps, 2, us) if plan.split else []


def pack(plan, attn_in, attn_out, ffn_up, ffn_down, small, odd):
    W, r = plan.width, plan.r

    def body(attn_in, attn_out, ffn_up, ffn_down, small, odd, most, last):
        for k in range(2):
            for i in range(3):
                most[k, i * r : (i + 1) * r, :] = attn_in[k, :, i * W : (i + 1) * W]
            most[k, 3 * r : 4 * r, :] = attn_out[k]
            most[k, 4 * r : 4 * r + SMALL, :] = small[...]
        for k, (out, at) in enumerate(((most, 4 * r + SMALL), (last, 0))):
            for i in range(4):
                out[0, at + i * r : at + (i + 1) * r, :] = ffn_up[k, :, i * W : (i + 1) * W]
            out[1, at : at + 4 * r] = ffn_down[k]
        for i in range(3):
            at = (8 + i % 2) * r + SMALL
            most[i // 2, at : at + r, :] = attn_in[2, :, i * W : (i + 1) * W]
        most[1, 9 * r + SMALL :, :] = attn_out[2]

    outs = [((2, 10 * r + SMALL, W), LOW), ((2, 4 * r, W), LOW)]
    return local(body, [attn_in, attn_out, ffn_up, ffn_down, small, (odd, SMEM)], outs)


class Gather:
    def __init__(self, plan, pair, parts):
        self.plan, self.pair, self.parts = plan, pair, parts
        self.ends = [sum(parts[: i + 1]) for i in range(len(parts))]
        if plan.split:
            self.near = [swap(pair, X), swap(pair, Y)]

    def onward(self, deps=()):
        if not self.plan.split:
            return []
        parts, ends = self.parts, self.ends

        def body(by_x, by_y, *outs):
            for i, (rows, end) in enumerate(zip(parts, ends)):
                outs[2 * i][...] = by_x[0, end - rows : end, :]
                outs[2 * i + 1][...] = by_y[1, end - rows : end, :]

        outs = local(body, self.near, [((rows, self.plan.width), LOW) for rows in parts for _ in range(2)], deps)
        self.far = [(swap(outs[2 * i], Y), swap(outs[2 * i + 1], X)) for i in range(len(parts))]
        return [outs[0]]

    def stack(self, part, deps=()):
        rows, end = self.parts[part], self.ends[part]
        at = slice(end - rows, end)
        if not self.plan.split:
            return [lax.all_gather(self.pair[:, at], "shard", axis=0)], []

        def body(pair, by_x, by_y, first, second, out):
            for j, v in enumerate((pair, by_x, by_y)):
                out[2 * j : 2 * j + 2] = v[:, at, :]
            out[6] = first[...]
            out[7] = second[...]

        ins = [self.pair, *self.near, *self.far[part]]
        mine = local(body, ins, [((8, rows, self.plan.width), LOW)], deps)[0]
        return [mine, swap(mine, CORE)], [mine]


class Reduction:
    def __init__(self, plan, odd):
        self.plan, self.odd = plan, odd
        self.pairs, self.results, self.moving = [], {}, {}

    def add(self, name, outs):
        if not self.plan.split:
            whole = outs[0]
            flat = whole.reshape((-1,) + whole.shape[2:])
            own = lax.psum_scatter(flat, "shard", scatter_dimension=0, tiled=True)
            self.results[name] = lax.psum(own, "rep").astype(WIDE).reshape(whole.shape[1:])
            return
        mine, other = outs
        self.pairs.append(dict(name=name, rows=mine.shape[1], step=0, keep=mine, slot={}, got=swap(other, CORE)))

    def advance(self, deps=()):
        if not self.pairs:
            return []
        W = self.plan.width
        sizes = {"x": 0, "y": 0, "n": 0, "f": 0}

        def place(way, count):
            at = sizes[way]
            sizes[way] += count
            return at

        work = []
        for p in self.pairs:
            R, step = p["rows"], p["step"]
            ways = ({"x": 2 * R, "y": 2 * R}, {"x": R, "y": R}, {"n": R}, {"f": R}, {"n": R})[step]
            work.append(dict(p, out={way: place(way, count) for way, count in ways.items()}, kept=((4, 2, 1, 1, 1)[step] * R, W)))
        ways = [w for w in "xynf" if sizes[w]]
        came = [w for w in "xynf" if w in self.moving]
        cores = [t for t in work if t["step"] == 0]

        def body(odd, *refs):
            keep_in, refs = refs[: len(work)], refs[len(work) :]
            core_in, refs = refs[: len(cores)], refs[len(cores) :]
            got, refs = dict(zip(came, refs[: len(came)])), refs[len(came) :]
            keep_out, refs = refs[: len(work)], refs[len(work) :]
            leave = dict(zip(ways, refs))
            odds = odd[0] != 0

            def total(left, right):
                return (left.astype(WIDE) + right.astype(WIDE)).astype(LOW)

            core = iter(core_in)
            for t, keep, out in zip(work, keep_in, keep_out):
                R, step, slot, to = t["rows"], t["step"], t["slot"], t["out"]
                if step == 0:
                    other = next(core)
                    for m, way in enumerate("xy"):
                        at = 4 * m * R
                        out[2 * m * R : 2 * (m + 1) * R, :] = total(keep[at : at + 2 * R, :], other[at : at + 2 * R, :])
                        at += 2 * R
                        leave[way][to[way] : to[way] + 2 * R, :] = total(keep[at : at + 2 * R, :], other[at : at + 2 * R, :])
                elif step == 1:
                    for m, (way, onward) in enumerate(("xy", "yx")):
                        other, at, kept = got[way], slot[way], 2 * m * R
                        out[m * R : (m + 1) * R, :] = total(keep[kept : kept + R, :], other[at : at + R, :])
                        kept, at = kept + R, at + R
                        leave[onward][to[onward] : to[onward] + R, :] = total(keep[kept : kept + R, :], other[at : at + R, :])
                elif step == 2:
                    first = total(keep[:R, :], got["y"][slot["y"] : slot["y"] + R, :])
                    second = total(keep[R:, :], got["x"][slot["x"] : slot["x"] + R, :])
                    out[...] = jnp.where(odds, second, first)
                    leave["n"][to["n"] : to["n"] + R, :] = jnp.where(odds, first, second)
                else:
                    way, onward = ("n", "f") if step == 3 else ("f", "n")
                    value = total(keep[...], got[way][slot[way] : slot[way] + R, :])
                    out[...] = value
                    leave[onward][to[onward] : to[onward] + R, :] = value

        if cores and came:
            deps = local(mark, [], [((8, 128), WIDE)], [*deps, *self.moving.values()], 2, 20)
        keeps = [t["keep"].reshape(-1, W) for t in work]
        gots = [t["got"].reshape(-1, W) for t in cores]
        outs = [(t["kept"], LOW) for t in work] + [((sizes[w], W), LOW) for w in ways]
        done = local(body, [(self.odd, SMEM), *keeps, *gots, *[self.moving[w] for w in came]], outs, deps)
        self.moving = {}
        for way, value in zip(ways, done[len(work) :]):
            self.moving[way] = swap_rep(value, Z1 if way == "n" else Z2) if way in "nf" else swap(value, X if way == "x" else Y)
        self.pairs = []
        for t, kept in zip(work, done):
            if t["step"] == 4:
                self.results[t["name"]] = (kept, self.moving["n"], t["out"]["n"])
            else:
                self.pairs.append(dict(name=t["name"], rows=t["rows"], step=t["step"] + 1, keep=kept, slot=t["out"]))
        return [done[0]]


ATT, FFN = ("a0", "a1", "a2"), ("f0", "f1")


def outputs(plan, sums, place):
    W, r = plan.width, plan.r
    wide = W // plan.shards
    results = sums.results
    if not plan.split:
        me = lax.axis_index("shard")
        att = [results[k] for k in ATT]
        small = lax.dynamic_slice(att[0], (0, 2 * r, me * wide), (2, NORMS, wide))
        att = jnp.stack([v[:, : 2 * r].reshape(4, r, W) for v in att])
        ffn = jnp.stack([results[k] for k in FFN])

        def unblocks(v):
            return jnp.moveaxis(v, 1, 2).reshape(v.shape[0], r, -1)

        return unblocks(att[:, :3]), att[:, 3], unblocks(ffn[:, 0].reshape(2, 4, r, W)), ffn[:, 1], small[0], small[1]
    names = ATT + FFN
    keeps = [results[k][0] for k in names]
    gots = []
    for k in names:
        if not any(results[k][1] is v for v in gots):
            gots.append(results[k][1])

    def body(odd, place, *refs):
        keep, refs = refs[: len(names)], refs[len(names) :]
        got, refs = refs[: len(gots)], refs[len(gots) :]
        attn_in, attn_out, ffn_up, ffn_down, gain, shift = refs
        odds = odd[0] != 0

        def member(i, m, at, rows):
            _, array, offset = results[names[i]]
            j = [v is array for v in gots].index(True)
            kept, other = keep[i][at : at + rows, :], got[j][offset + at : offset + at + rows, :]
            return (jnp.where(odds, other, kept) if m == 0 else jnp.where(odds, kept, other)).astype(WIDE)

        for a in range(len(ATT)):
            for i in range(3):
                attn_in[a, :, i * W : (i + 1) * W] = member(a, i // 2, (i % 2) * r, r)
            attn_out[a] = member(a, 1, r, r)
        for f in range(len(FFN)):
            for i in range(4):
                ffn_up[f, :, i * W : (i + 1) * W] = member(3 + f, 0, i * r, r)
            ffn_down[f] = member(3 + f, 1, 0, 4 * r)
        turn = lax.rem(W - place[0] * wide, W)
        for m, out in enumerate((gain, shift)):
            out[...] = pltpu.roll(member(0, m, 2 * r, SMALL), turn, axis=1)[:NORMS, :wide]

    outs = [((3, r, 3 * W), WIDE), ((3, r, W), WIDE), ((2, r, 4 * W), WIDE), ((2, 4 * r, W), WIDE)] + [((NORMS, wide), WIDE)] * 2
    return local(body, [(sums.odd, SMEM), (place, SMEM), *keeps, *gots], outs, room=16)


def shards(sizes, source, target, source_seg, target_seg, attn_in, attn_out, ffn_up, ffn_down, norm_gain, norm_bias, cotangent):
    plan = Plan(sizes, source.shape[1], source.shape[2])
    W, r = plan.width, plan.r
    me = lax.axis_index("shard")
    place = (me if plan.split else jnp.zeros_like(me))[None]
    src, tgt = source[0], target[0]
    src_row, src_col = source_seg, source_seg.reshape(-1, 1)
    tgt_row, tgt_col = target_seg, target_seg.reshape(-1, 1)

    small = jnp.concatenate([norm_gain, norm_bias])
    small = lax.dynamic_update_slice(jnp.zeros((SMALL, W), LOW), small, (0, me * small.shape[1]))
    odd = (lax.axis_index("rep") & 1).astype(jnp.int32)[None]
    most, last = pack(plan, attn_in, attn_out, ffn_up, ffn_down, small, odd)
    most = Gather(plan, most, (4 * r + SMALL, 6 * r))
    went = most.onward()
    last = Gather(plan, after(last, went), (4 * r,))
    self_w, stacked = most.stack(0)
    rest_w, stacked = most.stack(1, stacked)
    first, first_low, n0, r0, *kept_enc, norms = self_attention(
        plan, place, src, src_row, src_col, self_w, 0, 0, False, stacked
    )
    went = last.onward([r0])
    one, one_low, n2, r2, *kept_self, _ = self_attention(
        plan, place, tgt, tgt_row, tgt_col, self_w, 1, 2, True, [r0] + went
    )
    last_w, stacked = last.stack(0, [r2])
    enc_low, n1, r1, active, slope, w_f0 = encoder_ffn(
        plan, place, first, first_low, src, rest_w, norms, 1, [r2] + stacked
    )
    two, two_low, n3, r3, *kept_cross = cross_attention(
        plan, place, one, one_low, enc_low, tgt_row, src_col, rest_w, norms, 3
    )
    (decoded, last_grad, two_grad, norm_a), grads = decoder_ffn(
        plan, place, two, two_low, tgt, cotangent[0], n3, r3, last_w, norms, 4
    )
    sums = Reduction(plan, odd)
    sums.add("f1", grads)
    deps = sums.advance()
    (one_grad, enc_grad, norm_b), grads = cross_attention_back(
        plan, place, two_grad, one_low, enc_low, kept_cross, (n2, r2), (n1, r1), norms, (2, 1), deps
    )
    sums.add("a2", grads)
    deps = sums.advance([norm_b])
    (zero_grad, norm_c), grads = encoder_ffn_back(
        plan, place, enc_grad, first_low, active, slope, n0, r0, w_f0, norms, 0, deps
    )
    sums.add("f0", grads)
    deps = sums.advance([norm_c])
    tgt_grad, grads = self_attention_back(plan, place, one_grad, tgt, kept_self, last_grad, None, deps)
    sums.add("a1", grads)
    deps = sums.advance([tgt_grad])
    src_grad, grads = self_attention_back(
        plan, place, zero_grad, src, kept_enc, enc_grad, (norm_a, norm_b, norm_c), deps
    )
    sums.add("a0", grads)
    sums.advance([src_grad])
    while sums.pairs:
        sums.advance()
    return decoded[None], src_grad[None], tgt_grad[None], *outputs(plan, sums, place)


def after(value, deps):
    if not deps:
        return value

    def body(*refs):
        pass

    return pl.pallas_call(
        body,
        in_specs=[ANY] * (1 + len(deps)),
        out_shape=jax.ShapeDtypeStruct(value.shape, value.dtype),
        out_specs=ANY,
        input_output_aliases={0: 0},
        compiler_params=pltpu.CompilerParams(vmem_limit_bytes=1 << 20),
        cost_estimate=pl.CostEstimate(flops=0, bytes_accessed=0, transcendentals=0),
    )(value, *deps)


def solution(mesh):
    sizes = (mesh.shape["shard"], mesh.shape["rep"])
    tokens = P(("shard", "rep"), None, None)
    ids = P(("shard", "rep"), None)
    weight = P(None, "shard", None)
    norm = P(None, "shard")
    return jax.shard_map(
        functools.partial(shards, sizes),
        mesh=mesh,
        in_specs=(tokens, tokens, ids, ids, weight, weight, weight, weight, norm, norm, tokens),
        out_specs=(tokens, tokens, tokens, weight, weight, weight, weight, norm, norm),
        check_vma=False,
    )
```

```python
import functools

import jax
import jax.numpy as jnp
from jax import lax
from jax.experimental import pallas as pl
from jax.experimental.pallas import tpu as pltpu
from jax.sharding import PartitionSpec as P

HEAD = 64
PAIR = 2 * HEAD
EPS = 1e-05
NEG = -1e30
LOW = jnp.bfloat16
WIDE = jnp.float32
CORE, X, Y = 1, 2, 4
Z1, Z2 = 1, 2
SMALL = 16
NORMS = 5
VMEM = pl.BlockSpec(memory_space=pltpu.VMEM)
SMEM = pl.BlockSpec(memory_space=pltpu.SMEM)
ANY = pl.BlockSpec(memory_space=pl.ANY)


def dot(left, right):
    return lax.dot_general(left, right, (((1,), (0,)), ((), ())), preferred_element_type=WIDE)


def dot_nt(left, right):
    return lax.dot_general(left, right, (((1,), (1,)), ((), ())), preferred_element_type=WIDE)


def dot_tn(left, right):
    return lax.dot_general(left, right, (((0,), (0,)), ((), ())), preferred_element_type=WIDE)


def block(unit, i, r):
    part = unit[:, i * r : (i + 1) * r, :]
    return part.reshape(part.shape[0] * r, part.shape[2])


def rows_block(unit, i, r):
    n = unit.shape[0] // 4
    part = unit[i * n : (i + 1) * n, 4 * r :, :]
    return part.reshape(n * part.shape[1], part.shape[2])


def norm(value, gain, shift):
    mean = jnp.mean(value, axis=-1, keepdims=True)
    centred = value - mean
    scale = lax.rsqrt(jnp.mean(centred * centred, axis=-1, keepdims=True) + EPS)
    normal = centred * scale
    return normal * gain + shift, normal, scale


def norm_back(grad, normal, scale, gain):
    gain_grad = jnp.sum(grad * normal, axis=0, keepdims=True)
    shift_grad = jnp.sum(grad, axis=0, keepdims=True)
    inner = grad * gain
    inner_mean = jnp.mean(inner, axis=-1, keepdims=True)
    cross_mean = jnp.mean(inner * normal, axis=-1, keepdims=True)
    return scale * (inner - inner_mean - normal * cross_mean), gain_grad, shift_grad


def lanes_of(head, value):
    lane = lax.broadcasted_iota(jnp.int32, value.shape, 1)
    return jnp.where((lane < HEAD) if head == 0 else (lane >= HEAD), value, jnp.zeros_like(value))


def pick(first, second):
    lane = lax.broadcasted_iota(jnp.int32, first.shape, 1)
    return jnp.where(lane < HEAD, first, second)


def allowed_bias(memory_ids, query_ids, causal):
    tokens = memory_ids.shape[1]
    turned = jnp.transpose(jnp.broadcast_to(memory_ids.astype(WIDE), (PAIR, tokens)))[:, :1]
    allowed = turned == query_ids.astype(WIDE)
    if causal:
        shape = (tokens, query_ids.shape[1])
        allowed = allowed & (lax.broadcasted_iota(jnp.int32, shape, 1) >= lax.broadcasted_iota(jnp.int32, shape, 0))
    return jnp.where(allowed, 0.0, NEG)


def attend_forward(qkv, probs, mixed, bias):
    width = mixed.shape[1]
    for pair in range(width // PAIR):
        at = pl.ds(pair * PAIR, PAIR)
        query = qkv[:, pl.ds(pair * PAIR, PAIR)] * LOW(HEAD ** -0.5)
        keys = qkv[:, pl.ds(width + pair * PAIR, PAIR)]
        values = qkv[:, pl.ds(2 * width + pair * PAIR, PAIR)]
        out = []
        for head in range(2):
            scores = dot_nt(keys, lanes_of(head, query)) + bias[...]
            top = jnp.max(scores, axis=0, keepdims=True)
            weights = jnp.exp(scores - top)
            total = jnp.sum(weights, axis=0, keepdims=True)
            low = (weights * (1.0 / total)).astype(LOW)
            probs[2 * pair + head] = low
            out.append(dot_tn(low, values))
        mixed[:, at] = pick(*out).astype(LOW)


def attend_backward(qkv, probs, mixed_grad, qkv_grad):
    width = mixed_grad.shape[1]
    for pair in range(width // PAIR):
        query = qkv[:, pl.ds(pair * PAIR, PAIR)]
        keys = qkv[:, pl.ds(width + pair * PAIR, PAIR)]
        values = qkv[:, pl.ds(2 * width + pair * PAIR, PAIR)]
        grad = mixed_grad[:, pl.ds(pair * PAIR, PAIR)]
        dq, dk, dv = [], [], []
        for head in range(2):
            low = probs[2 * pair + head]
            prob = low.astype(WIDE)
            prob_grad = dot_nt(values, lanes_of(head, grad))
            delta = jnp.sum(prob * prob_grad, axis=0, keepdims=True)
            score_grad = (prob * (prob_grad - delta)).astype(LOW)
            dv.append(dot(low, grad))
            dk.append(dot(score_grad, query))
            dq.append(dot_tn(score_grad, keys))
        scale = HEAD ** -0.5
        qkv_grad[:, pl.ds(pair * PAIR, PAIR)] = (pick(*dq) * scale).astype(LOW)
        qkv_grad[:, pl.ds(width + pair * PAIR, PAIR)] = (pick(*dk) * scale).astype(LOW)
        qkv_grad[:, pl.ds(2 * width + pair * PAIR, PAIR)] = pick(*dv).astype(LOW)


GELU = 0.7978845608028654


def gelu_and_slope(value):
    square = value * value
    inner = GELU * value * (1.0 + 0.044715 * square)
    t = jnp.tanh(inner)
    half = 0.5 + 0.5 * t
    slope = half + 0.5 * value * (1.0 - t * t) * (GELU * (1.0 + 3 * 0.044715 * square))
    return value * half, slope


def ffn_forward(hidden, weight, active, slope, r):
    W = hidden.shape[1]
    total = None
    for c in range(4):
        at = pl.ds(c * W, W)
        act, sl = gelu_and_slope(dot(hidden, block(weight, c, r)))
        act = act.astype(LOW)
        active[:, at] = act
        slope[:, at] = sl.astype(LOW)
        part = dot(act, rows_block(weight, c, r))
        total = part if total is None else total + part
    return total


def ffn_backward_down(grad, active, put):
    W = grad.shape[1]
    for c in range(4):
        put(c, dot_tn(active[:, pl.ds(c * W, W)], grad).astype(LOW))


def ffn_backward_up(grad, hidden, weight, slope, r, put):
    W = grad.shape[1]
    total = None
    for c in range(4):
        z = (dot_nt(grad, rows_block(weight, c, r)) * slope[:, pl.ds(c * W, W)].astype(WIDE)).astype(LOW)
        put(c, dot_tn(hidden, z).astype(LOW))
        part = dot_nt(z, block(weight, c, r))
        total = part if total is None else total + part
    return total


class Plan:
    def __init__(self, sizes, length, width):
        self.split = sizes == (8, 4)
        self.sizes = sizes
        self.length, self.width = length, width
        self.heads = width // HEAD
        self.shards = sizes[0]
        self.r = width // self.shards
        self.n = self.g = 2 if self.split else 1


    def lay(self, place, stacks, member, rows, unit, at):
        count = rows.stop - rows.start
        if not self.split:
            unit[:, at : at + count, :] = stacks[0][:, member, rows]
            return
        odd, chip = (place & 1) != 0, place >> 1
        for j in range(4):
            k = 2 * (j ^ chip) + member
            mine, other = stacks[0][k, rows, :], stacks[1][k, rows, :]
            unit[2 * j, at : at + count, :] = jnp.where(odd, other, mine)
            unit[2 * j + 1, at : at + count, :] = jnp.where(odd, mine, other)


    def grad_shapes(self, rows):
        if not self.split:
            return [(self.shards, 2, rows, self.width)]
        return [(8, rows, self.width)] * 2

    def leave(self, place, outs, member, at, value, first=0):
        count = value.shape[1]
        if not self.split:
            outs[0][first : first + value.shape[0], member, at : at + count, :] = value
            return
        odd, chip = (place & 1) != 0, place >> 1
        for j in range(value.shape[0] // 2):
            k = (first // 2 + j) ^ chip
            if member == 0:
                k = ((k & 1) << 1) | (k >> 1)
            one, two = value[2 * j], value[2 * j + 1]
            outs[0][4 * member + k, at : at + count, :] = jnp.where(odd, two, one)
            outs[1][4 * member + k, at : at + count, :] = jnp.where(odd, one, two)

    def leave_block(self, place, outs, member, i, value):
        self.leave(place, outs, member, i * self.r, value.reshape(self.shards, self.r, self.width))

    def leave_rows(self, place, outs, member, i, value):
        n = self.shards // 4
        self.leave(place, outs, member, 0, value.reshape(n, 4 * self.r, self.width), i * n)

    def leave_rows_halved(self, place, outs, i, value):
        n, half = self.shards // 4, 2 * self.r
        value = value.reshape(n, 4 * self.r, self.width)
        for m in range(2):
            self.leave(place, outs, m, 0, value[:, m * half : (m + 1) * half, :], i * n)

    def call(self, body, ins, outs, scratch, us, deps, room):
        def run(*refs):
            body(*refs[len(deps) :])

        return pl.pallas_call(
            run,
            in_specs=[ANY] * len(deps) + [spec for _, spec in ins],
            out_shape=[jax.ShapeDtypeStruct(shape, dtype) for shape, dtype in outs],
            out_specs=[VMEM] * len(outs),
            scratch_shapes=scratch,
            compiler_params=pltpu.CompilerParams(vmem_limit_bytes=room << 20),
            cost_estimate=pl.CostEstimate(flops=int(us * 5e9), bytes_accessed=1 << 20, transcendentals=0),
        )(*deps, *[value for value, _ in ins])


def vmem(*arrays):
    return [(v, VMEM) for v in arrays]


def self_attention(plan, place, tokens, ids, stacks, member, row, causal, deps=(), us=10):
    L, W, H, r = plan.length, plan.width, plan.heads, plan.r

    def body(place, tokens, ids, *rest):
        stacks, rest = rest[: plan.n], rest[plan.n :]
        out, out_low, normal, scale, qkv, mixed, probs, weight, norms, bias = rest
        plan.lay(place[0], stacks, member, slice(0, 4 * r), weight, 0)
        bias[...] = allowed_bias(ids[...], ids[...], causal)
        if plan.split:
            norms[...] = sum(jnp.sum(s[...].astype(WIDE), axis=0) for s in (v.at[:, 4 * r : 4 * r + SMALL, :] for v in stacks)) * 0.5
        else:
            norms[...] = jnp.sum(stacks[0][:, member, 4 * r : 4 * r + SMALL].astype(WIDE), axis=0)
        x = tokens[...]
        for i in range(3):
            qkv[:, i * W : (i + 1) * W] = dot(x, block(weight, i, r)).astype(LOW)
        attend_forward(qkv, probs, mixed, bias)
        value = x.astype(WIDE) + dot(mixed[...], block(weight, 3, r))
        y, n, s = norm(value, norms[row : row + 1, :], norms[NORMS + row : NORMS + row + 1, :])
        out[...] = y
        out_low[...] = y.astype(LOW)
        normal[...] = n.astype(LOW)
        scale[...] = s

    ins = [(place, SMEM)] + vmem(tokens, ids, *stacks)
    outs = [((L, W), WIDE), ((L, W), LOW), ((L, W), LOW), ((L, 1), WIDE)]
    outs += [((L, 3 * W), LOW), ((L, W), LOW), ((H, L, L), LOW), ((plan.shards, 4 * r, W), LOW), ((SMALL, W), WIDE)]
    return plan.call(body, ins, outs, [pltpu.VMEM((L, L), WIDE)], us, deps, 11)


def cross_attention(plan, place, query_in, query_low, memory_low, query_ids, memory_ids, stacks, norms, row, deps=()):
    L, W, H, r = plan.length, plan.width, plan.heads, plan.r

    def body(place, query_in, query_low, memory_low, query_ids, memory_ids, norms, *rest):
        stacks, rest = rest[: plan.n], rest[plan.n :]
        out, out_low, normal, scale, qkv, mixed, probs, weight, bias = rest
        at = 4 * r
        for m in range(2):
            plan.lay(place[0], stacks, m, slice(at, at + 2 * r), weight, 2 * m * r)
        bias[...] = allowed_bias(memory_ids[...], query_ids[...], False)
        qkv[:, :W] = dot(query_low[...], block(weight, 0, r)).astype(LOW)
        memory = memory_low[...]
        for i in (1, 2):
            qkv[:, i * W : (i + 1) * W] = dot(memory, block(weight, i, r)).astype(LOW)
        attend_forward(qkv, probs, mixed, bias)
        value = query_in[...] + dot(mixed[...], block(weight, 3, r))
        y, n, s = norm(value, norms[row : row + 1, :], norms[NORMS + row : NORMS + row + 1, :])
        out[...] = y
        out_low[...] = y.astype(LOW)
        normal[...] = n.astype(LOW)
        scale[...] = s

    ins = [(place, SMEM)] + vmem(query_in, query_low, memory_low, query_ids, memory_ids, norms, *stacks)
    outs = [((L, W), WIDE), ((L, W), LOW), ((L, W), LOW), ((L, 1), WIDE)]
    outs += [((L, 3 * W), LOW), ((L, W), LOW), ((H, L, L), LOW), ((plan.shards, 4 * r, W), LOW)]
    return plan.call(body, ins, outs, [pltpu.VMEM((L, L), WIDE)], 10, deps, 11)


def encoder_ffn(plan, place, hidden, hidden_low, tokens, stacks, norms, row, deps=()):
    L, W, F, r = plan.length, plan.width, 4 * plan.width, plan.r

    def body(place, hidden, hidden_low, tokens, norms, *rest):
        stacks, rest = rest[: plan.n], rest[plan.n :]
        out_low, normal, scale, active, slope, weight = rest
        for m in range(2):
            plan.lay(place[0], stacks, m, slice(0, 4 * r), weight, 4 * m * r)
        branch = ffn_forward(hidden_low[...], weight, active, slope, r)
        value = hidden[...] + branch + tokens[...].astype(WIDE)
        y, n, s = norm(value, norms[row : row + 1, :], norms[NORMS + row : NORMS + row + 1, :])
        out_low[...] = y.astype(LOW)
        normal[...] = n.astype(LOW)
        scale[...] = s

    ins = [(place, SMEM)] + vmem(hidden, hidden_low, tokens, norms, *stacks)
    outs = [((L, W), LOW), ((L, W), LOW), ((L, 1), WIDE), ((L, F), LOW), ((L, F), LOW), ((plan.shards, 8 * r, W), LOW)]
    return plan.call(body, ins, outs, [], 9, deps, 11)


def decoder_ffn(plan, place, hidden, hidden_low, tokens, cotangent, stacks, norms, row, deps=()):
    L, W, F, r = plan.length, plan.width, 4 * plan.width, plan.r

    def body(place, hidden, hidden_low, tokens, cotangent, norms, *rest):
        stacks, rest = rest[: plan.n], rest[plan.n :]
        decoded, last_grad, norm_grads, slope, weight, *grads, active = rest
        for m in range(2):
            plan.lay(place[0], stacks, m, slice(0, 4 * r), weight, 4 * m * r)
        branch = ffn_forward(hidden_low[...], weight, active, slope, r)
        value = hidden[...] + branch + tokens[...].astype(WIDE)
        gain = norms[row : row + 1, :]
        y, n, s = norm(value, gain, norms[NORMS + row : NORMS + row + 1, :])
        decoded[...] = y.astype(LOW)
        grad, gain_grad, shift_grad = norm_back(cotangent[...].astype(WIDE), n, s, gain)
        last_grad[...] = grad
        norm_grads[0:1, :] = gain_grad
        norm_grads[1:2, :] = shift_grad
        ffn_backward_down(grad.astype(LOW), active, lambda i, v: plan.leave_rows_halved(place[0], grads, i, v))

    ins = [(place, SMEM)] + vmem(hidden, hidden_low, tokens, cotangent, norms, *stacks)
    outs = [((L, W), LOW), ((L, W), WIDE), ((2, W), WIDE), ((L, F), LOW), ((plan.shards, 8 * r, W), LOW)]
    outs += [(s, LOW) for s in plan.grad_shapes(2 * r)]
    got = plan.call(body, ins, outs, [pltpu.VMEM((L, F), LOW)], 12, deps, 16)
    return got[:5], got[5:]


def decoder_ffn_back(plan, place, grad, hidden_low, slope, hidden_normal, hidden_scale, weight, norms, row, deps=()):
    L, W, r = plan.length, plan.width, plan.r

    def body(place, grad, hidden_low, slope, hidden_normal, hidden_scale, weight, norms, out, norm_grads, *grads):
        def put(i, value):
            plan.leave(place[0], grads, i // 2, (i % 2) * r, value.reshape(plan.shards, r, W))

        back = ffn_backward_up(grad[...].astype(LOW), hidden_low[...], weight, slope, r, put)
        normal = hidden_normal[...].astype(WIDE)
        total, gain_grad, shift_grad = norm_back(grad[...] + back, normal, hidden_scale[...], norms[row : row + 1, :])
        out[...] = total
        norm_grads[0:1, :] = gain_grad
        norm_grads[1:2, :] = shift_grad

    ins = [(place, SMEM)] + vmem(grad, hidden_low, slope, hidden_normal, hidden_scale, weight, norms)
    outs = [((L, W), WIDE), ((2, W), WIDE)] + [(s, LOW) for s in plan.grad_shapes(2 * r)]
    got = plan.call(body, ins, outs, [], 8, deps, 12)
    return got[:2], got[2:]


def encoder_ffn_back(plan, place, grad, hidden_low, active, slope, hidden_normal, hidden_scale, weight, norms, row, deps=()):
    L, W, r = plan.length, plan.width, plan.r

    def body(place, grad, hidden_low, active, slope, hidden_normal, hidden_scale, weight, norms, *rest):
        zero_grad, norm_grads, *grads = rest
        grad_low = grad[...].astype(LOW)
        ffn_backward_down(grad_low, active, lambda i, v: plan.leave_rows(place[0], grads, 1, i, v))
        back = ffn_backward_up(
            grad_low, hidden_low[...], weight, slope, r, lambda i, v: plan.leave_block(place[0], grads, 0, i, v)
        )
        normal = hidden_normal[...].astype(WIDE)
        out, gain_grad, shift_grad = norm_back(grad[...] + back, normal, hidden_scale[...], norms[row : row + 1, :])
        zero_grad[...] = out
        norm_grads[0:1, :] = gain_grad
        norm_grads[1:2, :] = shift_grad

    ins = [(place, SMEM)] + vmem(grad, hidden_low, active, slope, hidden_normal, hidden_scale, weight, norms)
    outs = [((L, W), WIDE), ((2, W), WIDE)] + [(s, LOW) for s in plan.grad_shapes(4 * r)]
    got = plan.call(body, ins, outs, [], 11, deps, 14)
    return got[:2], got[2:]


def self_attention_back(plan, place, grad, tokens, kept, extra, deps=()):
    L, W, r = plan.length, plan.width, plan.r

    def body(place, grad, extra, tokens, qkv, mixed, probs, weight, *rest):
        total, *grads, mixed_grad, qkv_grad = rest
        grad_low = grad[...].astype(LOW)
        plan.leave_block(place[0], grads, 1, 1, dot_tn(mixed[...], grad_low).astype(LOW))
        mixed_grad[...] = dot_nt(grad_low, block(weight, 3, r)).astype(LOW)
        attend_backward(qkv, probs, mixed_grad, qkv_grad)
        x = tokens[...]
        for i in range(3):
            plan.leave_block(place[0], grads, i // 2, i % 2, dot_tn(x, qkv_grad[:, i * W : (i + 1) * W]).astype(LOW))
        back = grad[...] + extra[...]
        for i in range(3):
            back += dot_nt(qkv_grad[:, i * W : (i + 1) * W], block(weight, i, r))
        total[...] = back

    ins = [(place, SMEM)] + vmem(grad, extra, tokens, *kept)
    outs = [((L, W), WIDE)] + [(s, LOW) for s in plan.grad_shapes(2 * r)]
    scratch = [pltpu.VMEM((L, W), LOW), pltpu.VMEM((L, 3 * W), LOW)]
    got = plan.call(body, ins, outs, scratch, 12, deps, 12)
    return got[0], got[1:]


def attend_backward_values(probs, mixed_grad, value_grad):
    for pair in range(mixed_grad.shape[1] // PAIR):
        at = pl.ds(pair * PAIR, PAIR)
        grad = mixed_grad[:, at]
        value_grad[:, at] = pick(*[dot(probs[2 * pair + head], grad) for head in range(2)]).astype(LOW)


def self_attention_back_values(plan, place, grad, tokens, kept, deps=()):
    L, W, r = plan.length, plan.width, plan.r
    _, mixed, probs, weight = kept

    def body(place, grad, tokens, mixed, probs, weight, mixed_grad, value_grad, *grads):
        grad_low = grad[...].astype(LOW)
        plan.leave_block(place[0], grads, 1, 0, dot_tn(mixed[...], grad_low).astype(LOW))
        mixed_grad[...] = dot_nt(grad_low, block(weight, 3, r)).astype(LOW)
        attend_backward_values(probs, mixed_grad, value_grad)
        plan.leave_block(place[0], grads, 0, 0, dot_tn(tokens[...], value_grad[...]).astype(LOW))

    ins = [(place, SMEM)] + vmem(grad, tokens, mixed, probs, weight)
    outs = [((L, W), LOW), ((L, W), LOW)] + [(s, LOW) for s in plan.grad_shapes(r)]
    got = plan.call(body, ins, outs, [], 6, deps, 12)
    return got[:2], got[2:]


def self_attention_back_scores(plan, place, grad, tokens, kept, mixed_grad, value_grad, extra, small, deps=()):
    L, W, r = plan.length, plan.width, plan.r
    qkv, _, probs, weight = kept

    def body(place, grad, extra, tokens, qkv, probs, weight, mixed_grad, value_grad, *rest):
        parts, (total, *grads, score_grads) = rest[:4], rest[4:]
        for m in range(2):
            rows = [parts[j][i + m : i + m + 1, :] for j, i in ((3, 0), (2, 2), (2, 0), (1, 0), (0, 0))]
            rows = jnp.concatenate(rows + [jnp.zeros((SMALL - NORMS, W), WIDE)]).astype(LOW)[None]
            plan.leave(place[0], grads, m, r, jnp.broadcast_to(rows, (plan.shards, SMALL, W)))
        scale = HEAD ** -0.5
        for pair in range(W // PAIR):
            at = pl.ds(pair * PAIR, PAIR)
            query, keys = qkv[:, at], qkv[:, pl.ds(W + pair * PAIR, PAIR)]
            values, out_grad = qkv[:, pl.ds(2 * W + pair * PAIR, PAIR)], mixed_grad[:, at]
            dq, dk = [], []
            for head in range(2):
                prob = probs[2 * pair + head].astype(WIDE)
                prob_grad = dot_nt(values, lanes_of(head, out_grad))
                delta = jnp.sum(prob * prob_grad, axis=0, keepdims=True)
                score_grad = (prob * (prob_grad - delta)).astype(LOW)
                dk.append(dot(score_grad, query))
                dq.append(dot_tn(score_grad, keys))
            score_grads[:, at] = (pick(*dq) * scale).astype(LOW)
            score_grads[:, pl.ds(W + pair * PAIR, PAIR)] = (pick(*dk) * scale).astype(LOW)
        x = tokens[...]
        back = grad[...] + extra[...] + dot_nt(value_grad[...], block(weight, 2, r))
        for i in range(2):
            part = score_grads[:, i * W : (i + 1) * W]
            plan.leave_block(place[0], grads, i, 0, dot_tn(x, part).astype(LOW))
            back += dot_nt(part, block(weight, i, r))
        total[...] = back

    ins = [(place, SMEM)] + vmem(grad, extra, tokens, qkv, probs, weight, mixed_grad, value_grad, *small)
    outs = [((L, W), WIDE)] + [(s, LOW) for s in plan.grad_shapes(r + SMALL)]
    got = plan.call(body, ins, outs, [pltpu.VMEM((L, 2 * W), LOW)], 10, deps, 12)
    return got[0], got[1:]


def cross_attention_back(plan, place, grad, query_low, memory_low, kept, query_norm, memory_norm, norms, rows, deps=()):
    L, W, r = plan.length, plan.width, plan.r

    def body(place, grad, query_low, memory_low, qkv, mixed, probs, weight, query_n, query_r, memory_n, memory_r, norms, *rest):
        one_grad, enc_grad, norm_grads, *grads, mixed_grad, qkv_grad = rest
        grad_low = grad[...].astype(LOW)
        plan.leave_block(place[0], grads, 1, 1, dot_tn(mixed[...], grad_low).astype(LOW))
        mixed_grad[...] = dot_nt(grad_low, block(weight, 3, r)).astype(LOW)
        attend_backward(qkv, probs, mixed_grad, qkv_grad)
        plan.leave_block(place[0], grads, 0, 0, dot_tn(query_low[...], qkv_grad[:, :W]).astype(LOW))
        memory = memory_low[...]
        for i in (1, 2):
            value = dot_tn(memory, qkv_grad[:, i * W : (i + 1) * W]).astype(LOW)
            plan.leave_block(place[0], grads, i // 2, i % 2, value)
        back = grad[...] + dot_nt(qkv_grad[:, :W], block(weight, 0, r))
        normal = query_n[...].astype(WIDE)
        out, gain_grad, shift_grad = norm_back(back, normal, query_r[...], norms[rows[0] : rows[0] + 1, :])
        one_grad[...] = out
        norm_grads[0:1, :] = gain_grad
        norm_grads[1:2, :] = shift_grad
        back = dot_nt(qkv_grad[:, W : 2 * W], block(weight, 1, r)) + dot_nt(qkv_grad[:, 2 * W :], block(weight, 2, r))
        normal = memory_n[...].astype(WIDE)
        out, gain_grad, shift_grad = norm_back(back, normal, memory_r[...], norms[rows[1] : rows[1] + 1, :])
        enc_grad[...] = out
        norm_grads[2:3, :] = gain_grad
        norm_grads[3:4, :] = shift_grad

    ins = [(place, SMEM)] + vmem(grad, query_low, memory_low, *kept, *query_norm, *memory_norm, norms)
    outs = [((L, W), WIDE), ((L, W), WIDE), ((4, W), WIDE)] + [(s, LOW) for s in plan.grad_shapes(2 * r)]
    scratch = [pltpu.VMEM((L, W), LOW), pltpu.VMEM((L, 3 * W), LOW)]
    got = plan.call(body, ins, outs, scratch, 0.05, deps, 13)
    return got[:3], got[3:]


def swap(value, bit):
    return lax.ppermute(value, "shard", [(i, i ^ bit) for i in range(8)])


def swap_rep(value, bit):
    return lax.ppermute(value, "rep", [(i, i ^ bit) for i in range(4)])


def local(body, ins, outs, deps=(), room=6, us=0):
    ins = [v if isinstance(v, tuple) else (v, VMEM) for v in ins]

    def run(*refs):
        body(*refs[len(deps) :])

    return pl.pallas_call(
        run,
        in_specs=[ANY] * len(deps) + [spec for _, spec in ins],
        out_shape=[jax.ShapeDtypeStruct(shape, dtype) for shape, dtype in outs],
        out_specs=[VMEM] * len(outs),
        compiler_params=pltpu.CompilerParams(vmem_limit_bytes=room << 20),
        cost_estimate=pl.CostEstimate(flops=int(us * 5e9), bytes_accessed=1 << 20, transcendentals=0),
    )(*deps, *[v for v, _ in ins])


def mark(out):
    out[...] = jnp.zeros_like(out)


def wait_for(plan, deps, us):
    return local(mark, [], [((8, 128), WIDE)], deps, 2, us) if plan.split else []


def pack_self(plan, attn_in, attn_out, small, odd):
    W, r = plan.width, plan.r

    def body(attn_in, attn_out, small, odd, out):
        for k in range(2):
            for i in range(3):
                out[k, i * r : (i + 1) * r, :] = attn_in[k, :, i * W : (i + 1) * W]
            out[k, 3 * r : 4 * r, :] = attn_out[k]
            out[k, 4 * r :, :] = small[...]

    return local(body, [attn_in, attn_out, small, (odd, SMEM)], [((2, 4 * r + SMALL, W), LOW)])[0]


def pack_rest(plan, attn_in, attn_out, ffn_up, ffn_down, deps):
    W, r = plan.width, plan.r

    def body(attn_in, attn_out, ffn_up, ffn_down, out):
        for k, at in enumerate((0, 6 * r)):
            for i in range(4):
                out[0, at + i * r : at + (i + 1) * r, :] = ffn_up[k, :, i * W : (i + 1) * W]
            out[1, at : at + 4 * r] = ffn_down[k]
        for i in range(3):
            at = (4 + i % 2) * r
            out[i // 2, at : at + r, :] = attn_in[2, :, i * W : (i + 1) * W]
        out[1, 5 * r : 6 * r, :] = attn_out[2]

    return local(body, [attn_in, attn_out, ffn_up, ffn_down], [((2, 10 * r, W), LOW)], deps)[0]


class Gather:
    def __init__(self, plan, pair):
        self.plan, self.pair = plan, pair
        if plan.split:
            self.near = [swap(pair, X), swap(pair, Y)]

    def onward(self, deps=()):
        if not self.plan.split:
            return []

        def body(by_x, by_y, first, second):
            first[...] = by_x[0]
            second[...] = by_y[1]

        outs = local(body, self.near, [(self.pair.shape[1:], LOW)] * 2, deps)
        self.far = [swap(outs[0], Y), swap(outs[1], X)]
        return [outs[0]]

    def stack(self, at, deps=()):
        rows = at.stop - at.start
        if not self.plan.split:
            return [lax.all_gather(self.pair[:, at], "shard", axis=0)], []

        def body(pair, by_x, by_y, first, second, out):
            for j, v in enumerate((pair, by_x, by_y)):
                out[2 * j : 2 * j + 2] = v[:, at, :]
            out[6] = first[at, :]
            out[7] = second[at, :]

        ins = [self.pair, *self.near, *self.far]
        mine = local(body, ins, [((8, rows, self.plan.width), LOW)], deps)[0]
        return [mine, swap(mine, CORE)], [mine]


class Reduction:
    def __init__(self, plan, odd):
        self.plan, self.odd = plan, odd
        self.pairs, self.results = [], {}

    def add(self, name, outs):
        if not self.plan.split:
            whole = outs[0]
            flat = whole.reshape((-1,) + whole.shape[2:])
            own = lax.psum_scatter(flat, "shard", scatter_dimension=0, tiled=True)
            self.results[name] = lax.psum(own, "rep").astype(WIDE).reshape(whole.shape[1:])
            return
        mine, other = outs
        self.pairs.append(dict(name=name, rows=mine.shape[1], step=0, keep=mine, slot={}, moving={}, got=swap(other, CORE)))

    def advance(self, deps=(), only=(), never=()):
        pairs = [p for p in self.pairs if (not only or p["name"] in only) and p["name"] not in never]
        if not pairs:
            return []
        self.pairs = [p for p in self.pairs if p not in pairs]
        W = self.plan.width
        sizes = {"x": 0, "y": 0, "n": 0, "f": 0}

        def place(way, count):
            at = sizes[way]
            sizes[way] += count
            return at

        work = []
        for p in pairs:
            R, step = p["rows"], p["step"]
            ways = ({"x": 2 * R, "y": 2 * R}, {"x": R, "y": R}, {"n": R}, {"f": R}, {"n": R}, {})[step]
            work.append(dict(p, out={way: place(way, count) for way, count in ways.items()}, kept=((4, 2, 1, 1, 1, 2)[step] * R, W)))
        ways = [w for w in "xynf" if sizes[w]]
        came = []
        for p in pairs:
            came += [v for v in p["moving"].values() if not any(v is u for u in came)]
        cores = [t for t in work if t["step"] == 0]

        def body(odd, *refs):
            keep_in, refs = refs[: len(work)], refs[len(work) :]
            core_in, refs = refs[: len(cores)], refs[len(cores) :]
            arrived, refs = refs[: len(came)], refs[len(came) :]
            keep_out, refs = refs[: len(work)], refs[len(work) :]
            leave = dict(zip(ways, refs))
            odds = odd[0] != 0

            def total(left, right):
                return (left.astype(WIDE) + right.astype(WIDE)).astype(LOW)

            core = iter(core_in)
            for t, keep, out in zip(work, keep_in, keep_out):
                R, step, slot, to = t["rows"], t["step"], t["slot"], t["out"]
                got = {w: arrived[[v is u for u in came].index(True)] for w, v in t["moving"].items() if w in slot}
                if step == 0:
                    other = next(core)
                    for m, way in enumerate("xy"):
                        at = 4 * m * R
                        out[2 * m * R : 2 * (m + 1) * R, :] = total(keep[at : at + 2 * R, :], other[at : at + 2 * R, :])
                        at += 2 * R
                        leave[way][to[way] : to[way] + 2 * R, :] = total(keep[at : at + 2 * R, :], other[at : at + 2 * R, :])
                elif step == 1:
                    for m, (way, onward) in enumerate(("xy", "yx")):
                        other, at, kept = got[way], slot[way], 2 * m * R
                        out[m * R : (m + 1) * R, :] = total(keep[kept : kept + R, :], other[at : at + R, :])
                        kept, at = kept + R, at + R
                        leave[onward][to[onward] : to[onward] + R, :] = total(keep[kept : kept + R, :], other[at : at + R, :])
                elif step == 2:
                    first = total(keep[:R, :], got["y"][slot["y"] : slot["y"] + R, :])
                    second = total(keep[R:, :], got["x"][slot["x"] : slot["x"] + R, :])
                    out[...] = jnp.where(odds, second, first)
                    leave["n"][to["n"] : to["n"] + R, :] = jnp.where(odds, first, second)
                elif step == 5:
                    mine, other = keep[...], got["n"][slot["n"] : slot["n"] + R, :]
                    out[:R, :] = jnp.where(odds, other, mine)
                    out[R:, :] = jnp.where(odds, mine, other)
                else:
                    way, onward = ("n", "f") if step == 3 else ("f", "n")
                    value = total(keep[...], got[way][slot[way] : slot[way] + R, :])
                    out[...] = value
                    leave[onward][to[onward] : to[onward] + R, :] = value

        if cores and came:
            deps = local(mark, [], [((8, 128), WIDE)], [*deps, *came], 2, 20)
        keeps = [t["keep"].reshape(-1, W) for t in work]
        gots = [t["got"].reshape(-1, W) for t in cores]
        outs = [(t["kept"], LOW) for t in work] + [((sizes[w], W), LOW) for w in ways]
        done = local(body, [(self.odd, SMEM), *keeps, *gots, *came], outs, deps)
        moving = {}
        for way, value in zip(ways, done[len(work) :]):
            moving[way] = swap_rep(value, Z1 if way == "n" else Z2) if way in "nf" else swap(value, X if way == "x" else Y)
        for t, kept in zip(work, done):
            if t["step"] == 5:
                self.results[t["name"]] = (kept, None, 0)
            elif t["step"] == 4 and t["name"] not in FINISHED:
                self.results[t["name"]] = (kept, moving["n"], t["out"]["n"])
            else:
                mine = {w: v for w, v in moving.items() if w in t["out"]}
                self.pairs.append(dict(name=t["name"], rows=t["rows"], step=t["step"] + 1, keep=kept, slot=t["out"], moving=mine))
        return [done[0]]


FINISHED = ("f1u", "f1d")
NAMES = ("a0", "a0v", "a1", "a2", "f0", "f1u", "f1d")


def outputs(plan, sums, place):
    W, r = plan.width, plan.r
    wide = W // plan.shards
    results = sums.results
    if not plan.split:
        me = lax.axis_index("shard")
        scores, small = results["a0"][:, :r], results["a0"][:, r:]
        small = lax.dynamic_slice(small, (0, 0, me * wide), (2, NORMS, wide))
        att = [jnp.concatenate([scores, results["a0v"]]), *(results[k].reshape(4, r, W) for k in ("a1", "a2"))]
        att, ffn = jnp.stack(att), jnp.stack([results["f0"], jnp.stack([results[k].reshape(4 * r, W) for k in ("f1u", "f1d")])])

        def unblocks(v):
            return jnp.moveaxis(v, 1, 2).reshape(v.shape[0], r, -1)

        return unblocks(att[:, :3]), att[:, 3], unblocks(ffn[:, 0].reshape(2, 4, r, W)), ffn[:, 1], small[0], small[1]
    keeps = [results[k][0] for k in NAMES]
    gots = []
    for k in NAMES:
        if k not in FINISHED and not any(results[k][1] is v for v in gots):
            gots.append(results[k][1])

    def body(odd, place, *refs):
        keep, refs = refs[: len(NAMES)], refs[len(NAMES) :]
        got, refs = refs[: len(gots)], refs[len(gots) :]
        attn_in, attn_out, ffn_up, ffn_down, gain, shift = refs
        odds = odd[0] != 0

        def member(name, m, at, rows):
            _, array, offset = results[name]
            i = NAMES.index(name)
            if name in FINISHED:
                at += m * (keep[i].shape[0] // 2)
                return keep[i][at : at + rows, :].astype(WIDE)
            j = [v is array for v in gots].index(True)
            kept, other = keep[i][at : at + rows, :], got[j][offset + at : offset + at + rows, :]
            return (jnp.where(odds, other, kept) if m == 0 else jnp.where(odds, kept, other)).astype(WIDE)

        for i in range(2):
            attn_in[0, :, i * W : (i + 1) * W] = member("a0", i, 0, r)
        attn_in[0, :, 2 * W :] = member("a0v", 0, 0, r)
        attn_out[0] = member("a0v", 1, 0, r)
        for a, name in ((1, "a1"), (2, "a2")):
            for i in range(3):
                attn_in[a, :, i * W : (i + 1) * W] = member(name, i // 2, (i % 2) * r, r)
            attn_out[a] = member(name, 1, r, r)
        for i in range(4):
            ffn_up[0, :, i * W : (i + 1) * W] = member("f0", 0, i * r, r)
            ffn_up[1, :, i * W : (i + 1) * W] = member("f1u", i // 2, (i % 2) * r, r)
        ffn_down[0] = member("f0", 1, 0, 4 * r)
        for m in range(2):
            ffn_down[1, 2 * m * r : 2 * (m + 1) * r] = member("f1d", m, 0, 2 * r)
        turn = lax.rem(W - place[0] * wide, W)
        for m, out in enumerate((gain, shift)):
            out[...] = pltpu.roll(member("a0", m, r, SMALL), turn, axis=1)[:NORMS, :wide]

    outs = [((3, r, 3 * W), WIDE), ((3, r, W), WIDE), ((2, r, 4 * W), WIDE), ((2, 4 * r, W), WIDE)] + [((NORMS, wide), WIDE)] * 2
    return local(body, [(sums.odd, SMEM), (place, SMEM), *keeps, *gots], outs, room=16)


def shards(sizes, source, target, source_seg, target_seg, attn_in, attn_out, ffn_up, ffn_down, norm_gain, norm_bias, cotangent):
    plan = Plan(sizes, source.shape[1], source.shape[2])
    W, r = plan.width, plan.r
    me = lax.axis_index("shard")
    place = (me if plan.split else jnp.zeros_like(me))[None]
    src, tgt = source[0], target[0]

    small = jnp.concatenate([norm_gain, norm_bias])
    small = lax.dynamic_update_slice(jnp.zeros((SMALL, W), LOW), small, (0, me * small.shape[1]))
    odd = (lax.axis_index("rep") & 1).astype(jnp.int32)[None]
    pair = pack_self(plan, attn_in, attn_out, small, odd)
    att = Gather(plan, pair)
    rest = Gather(plan, pack_rest(plan, attn_in, attn_out, ffn_up, ffn_down, [pair]))
    went = att.onward()
    went = rest.onward(wait_for(plan, went, 4))
    self_w, stacked = att.stack(slice(0, 4 * r + SMALL), went)
    first, first_low, n0, r0, *kept_enc, norms = self_attention(
        plan, place, src, source_seg, self_w, 0, 0, False, wait_for(plan, stacked, 6), 0.05
    )
    rest_w, stacked = rest.stack(slice(0, 6 * r), [r0])
    one, one_low, n2, r2, *kept_self, _ = self_attention(
        plan, place, tgt, target_seg, self_w, 1, 2, True, [r0] + stacked
    )
    last_w, stacked = rest.stack(slice(6 * r, 10 * r), [r2])
    enc_low, n1, r1, active, slope, w_f0 = encoder_ffn(
        plan, place, first, first_low, src, rest_w, norms, 1, [r2] + stacked
    )
    two, two_low, n3, r3, *kept_cross = cross_attention(
        plan, place, one, one_low, enc_low, target_seg, source_seg, rest_w, norms, 3
    )
    (decoded, last_grad, norm_a, slope_f1, w_f1), grads = decoder_ffn(
        plan, place, two, two_low, tgt, cotangent[0], last_w, norms, 4
    )
    sums = Reduction(plan, odd)
    sums.add("f1d", grads)
    (two_grad, norm_d), grads = decoder_ffn_back(
        plan, place, last_grad, two_low, slope_f1, n3, r3, w_f1, norms, 3
    )
    deps = sums.advance([norm_d], ["f1d"])
    sums.add("f1u", grads)
    deps = sums.advance(deps, ["f1u"])
    (one_grad, enc_grad, norm_b), grads = cross_attention_back(
        plan, place, two_grad, one_low, enc_low, kept_cross, (n2, r2), (n1, r1), norms, (2, 1), deps
    )
    sums.add("a2", grads)
    deps = sums.advance([norm_b])
    (zero_grad, norm_c), grads = encoder_ffn_back(
        plan, place, enc_grad, first_low, active, slope, n0, r0, w_f0, norms, 0, deps
    )
    sums.add("f0", grads)
    deps = sums.advance([norm_c])
    tgt_grad, grads = self_attention_back(plan, place, one_grad, tgt, kept_self, last_grad, deps)
    sums.add("a1", grads)
    deps = sums.advance(grads[:1], ["f1u", "f1d"])
    halfway, grads = self_attention_back_values(plan, place, zero_grad, src, kept_enc, deps)
    sums.add("a0v", grads)
    deps = sums.advance([halfway[0]], never=["f1u", "f1d"])
    src_grad, grads = self_attention_back_scores(
        plan, place, zero_grad, src, kept_enc, *halfway, enc_grad, (norm_a, norm_d, norm_b, norm_c), deps
    )
    sums.add("a0", grads)
    deps = sums.advance(grads[:1], ["f1u", "f1d"])
    sums.advance(deps or grads[:1], never=["f1u", "f1d"])
    while sums.pairs:
        sums.advance()
    return decoded[None], src_grad[None], tgt_grad[None], *outputs(plan, sums, place)


def solution(mesh):
    sizes = (mesh.shape["shard"], mesh.shape["rep"])
    tokens = P(("shard", "rep"), None, None)
    ids = P(("shard", "rep"), None)
    weight = P(None, "shard", None)
    norm = P(None, "shard")
    return jax.shard_map(
        functools.partial(shards, sizes),
        mesh=mesh,
        in_specs=(tokens, tokens, ids, ids, weight, weight, weight, weight, norm, norm, tokens),
        out_specs=(tokens, tokens, tokens, weight, weight, weight, weight, norm, norm),
        check_vma=False,
    )
```

```python
import functools

import jax
import jax.numpy as jnp
from jax import lax
from jax.experimental import pallas as pl
from jax.experimental.pallas import tpu as pltpu
from jax.sharding import PartitionSpec as P

HEAD = 64
PAIR = 2 * HEAD
EPS = 1e-05
NEG = -1e30
LOW = jnp.bfloat16
WIDE = jnp.float32
CORE, X, Y = 1, 2, 4
Z1, Z2 = 1, 2
SMALL = 16
NORMS = 5
VMEM = pl.BlockSpec(memory_space=pltpu.VMEM)
SMEM = pl.BlockSpec(memory_space=pltpu.SMEM)
ANY = pl.BlockSpec(memory_space=pl.ANY)


def dot(left, right):
    return lax.dot_general(left, right, (((1,), (0,)), ((), ())), preferred_element_type=WIDE)


def dot_nt(left, right):
    return lax.dot_general(left, right, (((1,), (1,)), ((), ())), preferred_element_type=WIDE)


def dot_tn(left, right):
    return lax.dot_general(left, right, (((0,), (0,)), ((), ())), preferred_element_type=WIDE)


def block(unit, i, r):
    part = unit[:, i * r : (i + 1) * r, :]
    return part.reshape(part.shape[0] * r, part.shape[2])


def rows_block(unit, i, r):
    n = unit.shape[0] // 4
    part = unit[i * n : (i + 1) * n, 4 * r :, :]
    return part.reshape(n * part.shape[1], part.shape[2])


def norm(value, gain, shift):
    mean = jnp.mean(value, axis=-1, keepdims=True)
    centred = value - mean
    scale = lax.rsqrt(jnp.mean(centred * centred, axis=-1, keepdims=True) + EPS)
    normal = centred * scale
    return normal * gain + shift, normal, scale


def norm_back(grad, normal, scale, gain):
    gain_grad = jnp.sum(grad * normal, axis=0, keepdims=True)
    shift_grad = jnp.sum(grad, axis=0, keepdims=True)
    inner = grad * gain
    inner_mean = jnp.mean(inner, axis=-1, keepdims=True)
    cross_mean = jnp.mean(inner * normal, axis=-1, keepdims=True)
    return scale * (inner - inner_mean - normal * cross_mean), gain_grad, shift_grad


def lanes_of(head, value):
    lane = lax.broadcasted_iota(jnp.int32, value.shape, 1)
    return jnp.where((lane < HEAD) if head == 0 else (lane >= HEAD), value, jnp.zeros_like(value))


def pick(first, second):
    lane = lax.broadcasted_iota(jnp.int32, first.shape, 1)
    return jnp.where(lane < HEAD, first, second)


def allowed_bias(memory_ids, query_ids, causal):
    tokens = memory_ids.shape[1]
    turned = jnp.transpose(jnp.broadcast_to(memory_ids.astype(WIDE), (PAIR, tokens)))[:, :1]
    allowed = turned == query_ids.astype(WIDE)
    if causal:
        shape = (tokens, query_ids.shape[1])
        allowed = allowed & (lax.broadcasted_iota(jnp.int32, shape, 1) >= lax.broadcasted_iota(jnp.int32, shape, 0))
    return jnp.where(allowed, 0.0, NEG)


def attend_forward(qkv, probs, mixed, bias):
    width = mixed.shape[1]
    for pair in range(width // PAIR):
        at = pl.ds(pair * PAIR, PAIR)
        query = qkv[:, pl.ds(pair * PAIR, PAIR)] * LOW(HEAD ** -0.5)
        keys = qkv[:, pl.ds(width + pair * PAIR, PAIR)]
        values = qkv[:, pl.ds(2 * width + pair * PAIR, PAIR)]
        out = []
        for head in range(2):
            scores = dot_nt(keys, lanes_of(head, query)) + bias[...]
            top = jnp.max(scores, axis=0, keepdims=True)
            weights = jnp.exp(scores - top)
            total = jnp.sum(weights, axis=0, keepdims=True)
            low = (weights * (1.0 / total)).astype(LOW)
            probs[2 * pair + head] = low
            out.append(dot_tn(low, values))
        mixed[:, at] = pick(*out).astype(LOW)


def attend_backward(qkv, probs, mixed_grad, qkv_grad):
    width = mixed_grad.shape[1]
    for pair in range(width // PAIR):
        query = qkv[:, pl.ds(pair * PAIR, PAIR)]
        keys = qkv[:, pl.ds(width + pair * PAIR, PAIR)]
        values = qkv[:, pl.ds(2 * width + pair * PAIR, PAIR)]
        grad = mixed_grad[:, pl.ds(pair * PAIR, PAIR)]
        dq, dk, dv = [], [], []
        for head in range(2):
            low = probs[2 * pair + head]
            prob = low.astype(WIDE)
            prob_grad = dot_nt(values, lanes_of(head, grad))
            delta = jnp.sum(prob * prob_grad, axis=0, keepdims=True)
            score_grad = (prob * (prob_grad - delta)).astype(LOW)
            dv.append(dot(low, grad))
            dk.append(dot(score_grad, query))
            dq.append(dot_tn(score_grad, keys))
        scale = HEAD ** -0.5
        qkv_grad[:, pl.ds(pair * PAIR, PAIR)] = (pick(*dq) * scale).astype(LOW)
        qkv_grad[:, pl.ds(width + pair * PAIR, PAIR)] = (pick(*dk) * scale).astype(LOW)
        qkv_grad[:, pl.ds(2 * width + pair * PAIR, PAIR)] = pick(*dv).astype(LOW)


GELU = 0.7978845608028654


def gelu_and_slope(value):
    square = value * value
    inner = GELU * value * (1.0 + 0.044715 * square)
    t = jnp.tanh(inner)
    half = 0.5 + 0.5 * t
    slope = half + 0.5 * value * (1.0 - t * t) * (GELU * (1.0 + 3 * 0.044715 * square))
    return value * half, slope


def ffn_forward(hidden, weight, active, slope, r):
    W = hidden.shape[1]
    total = None
    for c in range(4):
        at = pl.ds(c * W, W)
        act, sl = gelu_and_slope(dot(hidden, block(weight, c, r)))
        act = act.astype(LOW)
        active[:, at] = act
        slope[:, at] = sl.astype(LOW)
        part = dot(act, rows_block(weight, c, r))
        total = part if total is None else total + part
    return total


def ffn_backward_down(grad, active, put):
    W = grad.shape[1]
    for c in range(4):
        put(c, dot_tn(active[:, pl.ds(c * W, W)], grad).astype(LOW))


def ffn_backward_up(grad, hidden, weight, slope, r, put):
    W = grad.shape[1]
    total = None
    for c in range(4):
        z = (dot_nt(grad, rows_block(weight, c, r)) * slope[:, pl.ds(c * W, W)].astype(WIDE)).astype(LOW)
        put(c, dot_tn(hidden, z).astype(LOW))
        part = dot_nt(z, block(weight, c, r))
        total = part if total is None else total + part
    return total


class Plan:
    def __init__(self, sizes, length, width):
        self.split = sizes == (8, 4)
        self.sizes = sizes
        self.length, self.width = length, width
        self.heads = width // HEAD
        self.shards = sizes[0]
        self.r = width // self.shards
        self.n = self.g = 2 if self.split else 1


    def lay(self, place, stacks, member, rows, unit, at):
        count = rows.stop - rows.start
        if not self.split:
            unit[:, at : at + count, :] = stacks[0][:, member, rows]
            return
        odd, chip = (place & 1) != 0, place >> 1
        for j in range(4):
            k = 2 * (j ^ chip) + member
            mine, other = stacks[0][k, rows, :], stacks[1][k, rows, :]
            unit[2 * j, at : at + count, :] = jnp.where(odd, other, mine)
            unit[2 * j + 1, at : at + count, :] = jnp.where(odd, mine, other)


    def grad_shapes(self, rows):
        if not self.split:
            return [(self.shards, 2, rows, self.width)]
        return [(8, rows, self.width)] * 2

    def leave(self, place, outs, member, at, value, first=0):
        count = value.shape[1]
        if not self.split:
            outs[0][first : first + value.shape[0], member, at : at + count, :] = value
            return
        odd, chip = (place & 1) != 0, place >> 1
        for j in range(value.shape[0] // 2):
            k = (first // 2 + j) ^ chip
            if member == 0:
                k = ((k & 1) << 1) | (k >> 1)
            one, two = value[2 * j], value[2 * j + 1]
            outs[0][4 * member + k, at : at + count, :] = jnp.where(odd, two, one)
            outs[1][4 * member + k, at : at + count, :] = jnp.where(odd, one, two)

    def leave_block(self, place, outs, member, i, value):
        self.leave(place, outs, member, i * self.r, value.reshape(self.shards, self.r, self.width))

    def leave_rows(self, place, outs, member, i, value):
        n = self.shards // 4
        self.leave(place, outs, member, 0, value.reshape(n, 4 * self.r, self.width), i * n)

    def leave_rows_halved(self, place, outs, i, value):
        n, half = self.shards // 4, 2 * self.r
        value = value.reshape(n, 4 * self.r, self.width)
        for m in range(2):
            self.leave(place, outs, m, 0, value[:, m * half : (m + 1) * half, :], i * n)

    def call(self, body, ins, outs, scratch, us, deps, room):
        def run(*refs):
            body(*refs[len(deps) :])

        return pl.pallas_call(
            run,
            in_specs=[ANY] * len(deps) + [spec for _, spec in ins],
            out_shape=[jax.ShapeDtypeStruct(shape, dtype) for shape, dtype in outs],
            out_specs=[VMEM] * len(outs),
            scratch_shapes=scratch,
            compiler_params=pltpu.CompilerParams(vmem_limit_bytes=room << 20),
            cost_estimate=pl.CostEstimate(flops=int(us * 5e9), bytes_accessed=1 << 20, transcendentals=0),
        )(*deps, *[value for value, _ in ins])


def vmem(*arrays):
    return [(v, VMEM) for v in arrays]


def self_attention(plan, place, tokens, ids, stacks, member, row, causal, deps=(), us=10):
    L, W, H, r = plan.length, plan.width, plan.heads, plan.r

    def body(place, tokens, ids, *rest):
        stacks, rest = rest[: plan.n], rest[plan.n :]
        out, out_low, normal, scale, qkv, mixed, probs, weight, norms, bias = rest
        plan.lay(place[0], stacks, member, slice(0, 4 * r), weight, 0)
        bias[...] = allowed_bias(ids[...], ids[...], causal)
        if plan.split:
            norms[...] = sum(jnp.sum(s[...].astype(WIDE), axis=0) for s in (v.at[:, 4 * r : 4 * r + SMALL, :] for v in stacks)) * 0.5
        else:
            norms[...] = jnp.sum(stacks[0][:, member, 4 * r : 4 * r + SMALL].astype(WIDE), axis=0)
        x = tokens[...]
        for i in range(3):
            qkv[:, i * W : (i + 1) * W] = dot(x, block(weight, i, r)).astype(LOW)
        attend_forward(qkv, probs, mixed, bias)
        value = x.astype(WIDE) + dot(mixed[...], block(weight, 3, r))
        y, n, s = norm(value, norms[row : row + 1, :], norms[NORMS + row : NORMS + row + 1, :])
        out[...] = y
        out_low[...] = y.astype(LOW)
        normal[...] = n.astype(LOW)
        scale[...] = s

    ins = [(place, SMEM)] + vmem(tokens, ids, *stacks)
    outs = [((L, W), WIDE), ((L, W), LOW), ((L, W), LOW), ((L, 1), WIDE)]
    outs += [((L, 3 * W), LOW), ((L, W), LOW), ((H, L, L), LOW), ((plan.shards, 4 * r, W), LOW), ((SMALL, W), WIDE)]
    return plan.call(body, ins, outs, [pltpu.VMEM((L, L), WIDE)], us, deps, 11)


def cross_attention(plan, place, query_in, query_low, memory_low, query_ids, memory_ids, stacks, norms, row, deps=()):
    L, W, H, r = plan.length, plan.width, plan.heads, plan.r

    def body(place, query_in, query_low, memory_low, query_ids, memory_ids, norms, *rest):
        stacks, rest = rest[: plan.n], rest[plan.n :]
        out, out_low, normal, scale, qkv, mixed, probs, weight, bias = rest
        at = 4 * r
        for m in range(2):
            plan.lay(place[0], stacks, m, slice(at, at + 2 * r), weight, 2 * m * r)
        bias[...] = allowed_bias(memory_ids[...], query_ids[...], False)
        qkv[:, :W] = dot(query_low[...], block(weight, 0, r)).astype(LOW)
        memory = memory_low[...]
        for i in (1, 2):
            qkv[:, i * W : (i + 1) * W] = dot(memory, block(weight, i, r)).astype(LOW)
        attend_forward(qkv, probs, mixed, bias)
        value = query_in[...] + dot(mixed[...], block(weight, 3, r))
        y, n, s = norm(value, norms[row : row + 1, :], norms[NORMS + row : NORMS + row + 1, :])
        out[...] = y
        out_low[...] = y.astype(LOW)
        normal[...] = n.astype(LOW)
        scale[...] = s

    ins = [(place, SMEM)] + vmem(query_in, query_low, memory_low, query_ids, memory_ids, norms, *stacks)
    outs = [((L, W), WIDE), ((L, W), LOW), ((L, W), LOW), ((L, 1), WIDE)]
    outs += [((L, 3 * W), LOW), ((L, W), LOW), ((H, L, L), LOW), ((plan.shards, 4 * r, W), LOW)]
    return plan.call(body, ins, outs, [pltpu.VMEM((L, L), WIDE)], 10, deps, 11)


def encoder_ffn(plan, place, hidden, hidden_low, tokens, stacks, norms, row, deps=()):
    L, W, F, r = plan.length, plan.width, 4 * plan.width, plan.r

    def body(place, hidden, hidden_low, tokens, norms, *rest):
        stacks, rest = rest[: plan.n], rest[plan.n :]
        out_low, normal, scale, active, slope, weight = rest
        for m in range(2):
            plan.lay(place[0], stacks, m, slice(0, 4 * r), weight, 4 * m * r)
        branch = ffn_forward(hidden_low[...], weight, active, slope, r)
        value = hidden[...] + branch + tokens[...].astype(WIDE)
        y, n, s = norm(value, norms[row : row + 1, :], norms[NORMS + row : NORMS + row + 1, :])
        out_low[...] = y.astype(LOW)
        normal[...] = n.astype(LOW)
        scale[...] = s

    ins = [(place, SMEM)] + vmem(hidden, hidden_low, tokens, norms, *stacks)
    outs = [((L, W), LOW), ((L, W), LOW), ((L, 1), WIDE), ((L, F), LOW), ((L, F), LOW), ((plan.shards, 8 * r, W), LOW)]
    return plan.call(body, ins, outs, [], 9, deps, 11)


def decoder_ffn(plan, place, hidden, hidden_low, tokens, cotangent, stacks, norms, row, deps=()):
    L, W, F, r = plan.length, plan.width, 4 * plan.width, plan.r

    def body(place, hidden, hidden_low, tokens, cotangent, norms, *rest):
        stacks, rest = rest[: plan.n], rest[plan.n :]
        decoded, last_grad, norm_grads, slope, weight, *grads, active = rest
        for m in range(2):
            plan.lay(place[0], stacks, m, slice(0, 4 * r), weight, 4 * m * r)
        branch = ffn_forward(hidden_low[...], weight, active, slope, r)
        value = hidden[...] + branch + tokens[...].astype(WIDE)
        gain = norms[row : row + 1, :]
        y, n, s = norm(value, gain, norms[NORMS + row : NORMS + row + 1, :])
        decoded[...] = y.astype(LOW)
        grad, gain_grad, shift_grad = norm_back(cotangent[...].astype(WIDE), n, s, gain)
        last_grad[...] = grad
        norm_grads[0:1, :] = gain_grad
        norm_grads[1:2, :] = shift_grad
        ffn_backward_down(grad.astype(LOW), active, lambda i, v: plan.leave_rows_halved(place[0], grads, i, v))

    ins = [(place, SMEM)] + vmem(hidden, hidden_low, tokens, cotangent, norms, *stacks)
    outs = [((L, W), LOW), ((L, W), WIDE), ((2, W), WIDE), ((L, F), LOW), ((plan.shards, 8 * r, W), LOW)]
    outs += [(s, LOW) for s in plan.grad_shapes(2 * r)]
    got = plan.call(body, ins, outs, [pltpu.VMEM((L, F), LOW)], 12, deps, 16)
    return got[:5], got[5:]


def decoder_ffn_back(plan, place, grad, hidden_low, slope, hidden_normal, hidden_scale, weight, norms, row, deps=()):
    L, W, r = plan.length, plan.width, plan.r

    def body(place, grad, hidden_low, slope, hidden_normal, hidden_scale, weight, norms, out, norm_grads, *grads):
        def put(i, value):
            plan.leave(place[0], grads, i // 2, (i % 2) * r, value.reshape(plan.shards, r, W))

        back = ffn_backward_up(grad[...].astype(LOW), hidden_low[...], weight, slope, r, put)
        normal = hidden_normal[...].astype(WIDE)
        total, gain_grad, shift_grad = norm_back(grad[...] + back, normal, hidden_scale[...], norms[row : row + 1, :])
        out[...] = total
        norm_grads[0:1, :] = gain_grad
        norm_grads[1:2, :] = shift_grad

    ins = [(place, SMEM)] + vmem(grad, hidden_low, slope, hidden_normal, hidden_scale, weight, norms)
    outs = [((L, W), WIDE), ((2, W), WIDE)] + [(s, LOW) for s in plan.grad_shapes(2 * r)]
    got = plan.call(body, ins, outs, [], 8, deps, 12)
    return got[:2], got[2:]


def encoder_ffn_back(plan, place, grad, hidden_low, active, slope, hidden_normal, hidden_scale, weight, norms, row, deps=()):
    L, W, r = plan.length, plan.width, plan.r

    def body(place, grad, hidden_low, active, slope, hidden_normal, hidden_scale, weight, norms, *rest):
        zero_grad, norm_grads, *grads = rest
        grad_low = grad[...].astype(LOW)
        ffn_backward_down(grad_low, active, lambda i, v: plan.leave_rows(place[0], grads, 1, i, v))
        back = ffn_backward_up(
            grad_low, hidden_low[...], weight, slope, r, lambda i, v: plan.leave_block(place[0], grads, 0, i, v)
        )
        normal = hidden_normal[...].astype(WIDE)
        out, gain_grad, shift_grad = norm_back(grad[...] + back, normal, hidden_scale[...], norms[row : row + 1, :])
        zero_grad[...] = out
        norm_grads[0:1, :] = gain_grad
        norm_grads[1:2, :] = shift_grad

    ins = [(place, SMEM)] + vmem(grad, hidden_low, active, slope, hidden_normal, hidden_scale, weight, norms)
    outs = [((L, W), WIDE), ((2, W), WIDE)] + [(s, LOW) for s in plan.grad_shapes(4 * r)]
    got = plan.call(body, ins, outs, [], 11, deps, 14)
    return got[:2], got[2:]


def self_attention_back(plan, place, grad, tokens, kept, extra, deps=()):
    L, W, r = plan.length, plan.width, plan.r

    def body(place, grad, extra, tokens, qkv, mixed, probs, weight, *rest):
        total, *grads, mixed_grad, qkv_grad = rest
        grad_low = grad[...].astype(LOW)
        plan.leave_block(place[0], grads, 1, 1, dot_tn(mixed[...], grad_low).astype(LOW))
        mixed_grad[...] = dot_nt(grad_low, block(weight, 3, r)).astype(LOW)
        attend_backward(qkv, probs, mixed_grad, qkv_grad)
        x = tokens[...]
        for i in range(3):
            plan.leave_block(place[0], grads, i // 2, i % 2, dot_tn(x, qkv_grad[:, i * W : (i + 1) * W]).astype(LOW))
        back = grad[...] + extra[...]
        for i in range(3):
            back += dot_nt(qkv_grad[:, i * W : (i + 1) * W], block(weight, i, r))
        total[...] = back

    ins = [(place, SMEM)] + vmem(grad, extra, tokens, *kept)
    outs = [((L, W), WIDE)] + [(s, LOW) for s in plan.grad_shapes(2 * r)]
    scratch = [pltpu.VMEM((L, W), LOW), pltpu.VMEM((L, 3 * W), LOW)]
    got = plan.call(body, ins, outs, scratch, 12, deps, 12)
    return got[0], got[1:]


def attend_backward_values(probs, mixed_grad, value_grad):
    for pair in range(mixed_grad.shape[1] // PAIR):
        at = pl.ds(pair * PAIR, PAIR)
        grad = mixed_grad[:, at]
        value_grad[:, at] = pick(*[dot(probs[2 * pair + head], grad) for head in range(2)]).astype(LOW)


def self_attention_back_values(plan, place, grad, tokens, kept, deps=()):
    L, W, r = plan.length, plan.width, plan.r
    _, mixed, probs, weight = kept

    def body(place, grad, tokens, mixed, probs, weight, mixed_grad, value_grad, *grads):
        grad_low = grad[...].astype(LOW)
        plan.leave_block(place[0], grads, 1, 0, dot_tn(mixed[...], grad_low).astype(LOW))
        mixed_grad[...] = dot_nt(grad_low, block(weight, 3, r)).astype(LOW)
        attend_backward_values(probs, mixed_grad, value_grad)
        plan.leave_block(place[0], grads, 0, 0, dot_tn(tokens[...], value_grad[...]).astype(LOW))

    ins = [(place, SMEM)] + vmem(grad, tokens, mixed, probs, weight)
    outs = [((L, W), LOW), ((L, W), LOW)] + [(s, LOW) for s in plan.grad_shapes(r)]
    got = plan.call(body, ins, outs, [], 6, deps, 12)
    return got[:2], got[2:]


def self_attention_back_scores(plan, place, grad, tokens, kept, mixed_grad, value_grad, extra, small, deps=()):
    L, W, r = plan.length, plan.width, plan.r
    qkv, _, probs, weight = kept

    def body(place, grad, extra, tokens, qkv, probs, weight, mixed_grad, value_grad, *rest):
        parts, (total, *grads, score_grads) = rest[:4], rest[4:]
        for m in range(2):
            rows = [parts[j][i + m : i + m + 1, :] for j, i in ((3, 0), (2, 2), (2, 0), (1, 0), (0, 0))]
            rows = jnp.concatenate(rows + [jnp.zeros((SMALL - NORMS, W), WIDE)]).astype(LOW)[None]
            plan.leave(place[0], grads, m, r, jnp.broadcast_to(rows, (plan.shards, SMALL, W)))
        scale = HEAD ** -0.5
        for pair in range(W // PAIR):
            at = pl.ds(pair * PAIR, PAIR)
            query, keys = qkv[:, at], qkv[:, pl.ds(W + pair * PAIR, PAIR)]
            values, out_grad = qkv[:, pl.ds(2 * W + pair * PAIR, PAIR)], mixed_grad[:, at]
            dq, dk = [], []
            for head in range(2):
                prob = probs[2 * pair + head].astype(WIDE)
                prob_grad = dot_nt(values, lanes_of(head, out_grad))
                delta = jnp.sum(prob * prob_grad, axis=0, keepdims=True)
                score_grad = (prob * (prob_grad - delta)).astype(LOW)
                dk.append(dot(score_grad, query))
                dq.append(dot_tn(score_grad, keys))
            score_grads[:, at] = (pick(*dq) * scale).astype(LOW)
            score_grads[:, pl.ds(W + pair * PAIR, PAIR)] = (pick(*dk) * scale).astype(LOW)
        x = tokens[...]
        back = grad[...] + extra[...] + dot_nt(value_grad[...], block(weight, 2, r))
        for i in range(2):
            part = score_grads[:, i * W : (i + 1) * W]
            plan.leave_block(place[0], grads, i, 0, dot_tn(x, part).astype(LOW))
            back += dot_nt(part, block(weight, i, r))
        total[...] = back

    ins = [(place, SMEM)] + vmem(grad, extra, tokens, qkv, probs, weight, mixed_grad, value_grad, *small)
    outs = [((L, W), WIDE)] + [(s, LOW) for s in plan.grad_shapes(r + SMALL)]
    got = plan.call(body, ins, outs, [pltpu.VMEM((L, 2 * W), LOW)], 10, deps, 12)
    return got[0], got[1:]


def cross_attention_back(plan, place, grad, query_low, memory_low, kept, query_norm, memory_norm, norms, rows, deps=()):
    L, W, r = plan.length, plan.width, plan.r

    def body(place, grad, query_low, memory_low, qkv, mixed, probs, weight, query_n, query_r, memory_n, memory_r, norms, *rest):
        one_grad, enc_grad, norm_grads, *grads, mixed_grad, qkv_grad = rest
        grad_low = grad[...].astype(LOW)
        plan.leave_block(place[0], grads, 1, 1, dot_tn(mixed[...], grad_low).astype(LOW))
        mixed_grad[...] = dot_nt(grad_low, block(weight, 3, r)).astype(LOW)
        attend_backward(qkv, probs, mixed_grad, qkv_grad)
        plan.leave_block(place[0], grads, 0, 0, dot_tn(query_low[...], qkv_grad[:, :W]).astype(LOW))
        memory = memory_low[...]
        for i in (1, 2):
            value = dot_tn(memory, qkv_grad[:, i * W : (i + 1) * W]).astype(LOW)
            plan.leave_block(place[0], grads, i // 2, i % 2, value)
        back = grad[...] + dot_nt(qkv_grad[:, :W], block(weight, 0, r))
        normal = query_n[...].astype(WIDE)
        out, gain_grad, shift_grad = norm_back(back, normal, query_r[...], norms[rows[0] : rows[0] + 1, :])
        one_grad[...] = out
        norm_grads[0:1, :] = gain_grad
        norm_grads[1:2, :] = shift_grad
        back = dot_nt(qkv_grad[:, W : 2 * W], block(weight, 1, r)) + dot_nt(qkv_grad[:, 2 * W :], block(weight, 2, r))
        normal = memory_n[...].astype(WIDE)
        out, gain_grad, shift_grad = norm_back(back, normal, memory_r[...], norms[rows[1] : rows[1] + 1, :])
        enc_grad[...] = out
        norm_grads[2:3, :] = gain_grad
        norm_grads[3:4, :] = shift_grad

    ins = [(place, SMEM)] + vmem(grad, query_low, memory_low, *kept, *query_norm, *memory_norm, norms)
    outs = [((L, W), WIDE), ((L, W), WIDE), ((4, W), WIDE)] + [(s, LOW) for s in plan.grad_shapes(2 * r)]
    scratch = [pltpu.VMEM((L, W), LOW), pltpu.VMEM((L, 3 * W), LOW)]
    got = plan.call(body, ins, outs, scratch, 0.05, deps, 13)
    return got[:3], got[3:]


def swap(value, bit):
    return lax.ppermute(value, "shard", [(i, i ^ bit) for i in range(8)])


def swap_rep(value, bit):
    return lax.ppermute(value, "rep", [(i, i ^ bit) for i in range(4)])


def local(body, ins, outs, deps=(), room=6, us=0):
    ins = [v if isinstance(v, tuple) else (v, VMEM) for v in ins]

    def run(*refs):
        body(*refs[len(deps) :])

    return pl.pallas_call(
        run,
        in_specs=[ANY] * len(deps) + [spec for _, spec in ins],
        out_shape=[jax.ShapeDtypeStruct(shape, dtype) for shape, dtype in outs],
        out_specs=[VMEM] * len(outs),
        compiler_params=pltpu.CompilerParams(vmem_limit_bytes=room << 20),
        cost_estimate=pl.CostEstimate(flops=int(us * 5e9), bytes_accessed=1 << 20, transcendentals=0),
    )(*deps, *[v for v, _ in ins])


def mark(out):
    out[...] = jnp.zeros_like(out)


def wait_for(plan, deps, us):
    return local(mark, [], [((8, 128), WIDE)], deps, 2, us) if plan.split else []


def pack_self(plan, attn_in, attn_out, small, odd):
    W, r = plan.width, plan.r

    def body(attn_in, attn_out, small, odd, out):
        for k in range(2):
            for i in range(3):
                out[k, i * r : (i + 1) * r, :] = attn_in[k, :, i * W : (i + 1) * W]
            out[k, 3 * r : 4 * r, :] = attn_out[k]
            out[k, 4 * r :, :] = small[...]

    return local(body, [attn_in, attn_out, small, (odd, SMEM)], [((2, 4 * r + SMALL, W), LOW)])[0]


def pack_rest(plan, attn_in, attn_out, ffn_up, ffn_down, deps):
    W, r = plan.width, plan.r

    def body(attn_in, attn_out, ffn_up, ffn_down, out):
        for k, at in enumerate((0, 6 * r)):
            for i in range(4):
                out[0, at + i * r : at + (i + 1) * r, :] = ffn_up[k, :, i * W : (i + 1) * W]
            out[1, at : at + 4 * r] = ffn_down[k]
        for i in range(3):
            at = (4 + i % 2) * r
            out[i // 2, at : at + r, :] = attn_in[2, :, i * W : (i + 1) * W]
        out[1, 5 * r : 6 * r, :] = attn_out[2]

    return local(body, [attn_in, attn_out, ffn_up, ffn_down], [((2, 10 * r, W), LOW)], deps)[0]


class Gather:
    def __init__(self, plan, pair):
        self.plan, self.pair = plan, pair
        if plan.split:
            self.near = [swap(pair, X), swap(pair, Y)]

    def onward(self, deps=()):
        if not self.plan.split:
            return []

        def body(by_x, by_y, first, second):
            first[...] = by_x[0]
            second[...] = by_y[1]

        outs = local(body, self.near, [(self.pair.shape[1:], LOW)] * 2, deps)
        self.far = [swap(outs[0], Y), swap(outs[1], X)]
        return [outs[0]]

    def stack(self, at, deps=()):
        rows = at.stop - at.start
        if not self.plan.split:
            return [lax.all_gather(self.pair[:, at], "shard", axis=0)], []

        def body(pair, by_x, by_y, first, second, out):
            for j, v in enumerate((pair, by_x, by_y)):
                out[2 * j : 2 * j + 2] = v[:, at, :]
            out[6] = first[at, :]
            out[7] = second[at, :]

        ins = [self.pair, *self.near, *self.far]
        mine = local(body, ins, [((8, rows, self.plan.width), LOW)], deps)[0]
        return [mine, swap(mine, CORE)], [mine]


class Reduction:
    def __init__(self, plan, odd):
        self.plan, self.odd = plan, odd
        self.pairs, self.results = [], {}

    def add(self, name, outs):
        if not self.plan.split:
            whole = outs[0]
            flat = whole.reshape((-1,) + whole.shape[2:])
            own = lax.psum_scatter(flat, "shard", scatter_dimension=0, tiled=True)
            self.results[name] = lax.psum(own, "rep").astype(WIDE).reshape(whole.shape[1:])
            return
        mine, other = outs
        self.pairs.append(dict(name=name, rows=mine.shape[1], step=0, keep=mine, slot={}, moving={}, got=swap(other, CORE)))

    def advance(self, deps=(), only=(), never=()):
        pairs = [p for p in self.pairs if (not only or p["name"] in only) and p["name"] not in never]
        if not pairs:
            return []
        self.pairs = [p for p in self.pairs if p not in pairs]
        W = self.plan.width
        sizes = {"x": 0, "y": 0, "n": 0, "f": 0}

        def place(way, count):
            at = sizes[way]
            sizes[way] += count
            return at

        work = []
        for p in pairs:
            R, step = p["rows"], p["step"]
            ways = ({"x": 2 * R, "y": 2 * R}, {"x": R, "y": R}, {"n": R}, {"f": R}, {"n": R}, {})[step]
            work.append(dict(p, out={way: place(way, count) for way, count in ways.items()}, kept=((4, 2, 1, 1, 1, 2)[step] * R, W)))
        ways = [w for w in "xynf" if sizes[w]]
        came = []
        for p in pairs:
            came += [v for v in p["moving"].values() if not any(v is u for u in came)]
        cores = [t for t in work if t["step"] == 0]

        def body(odd, *refs):
            keep_in, refs = refs[: len(work)], refs[len(work) :]
            core_in, refs = refs[: len(cores)], refs[len(cores) :]
            arrived, refs = refs[: len(came)], refs[len(came) :]
            keep_out, refs = refs[: len(work)], refs[len(work) :]
            leave = dict(zip(ways, refs))
            odds = odd[0] != 0

            def total(left, right):
                return (left.astype(WIDE) + right.astype(WIDE)).astype(LOW)

            core = iter(core_in)
            for t, keep, out in zip(work, keep_in, keep_out):
                R, step, slot, to = t["rows"], t["step"], t["slot"], t["out"]
                got = {w: arrived[[v is u for u in came].index(True)] for w, v in t["moving"].items() if w in slot}
                if step == 0:
                    other = next(core)
                    for m, way in enumerate("xy"):
                        at = 4 * m * R
                        out[2 * m * R : 2 * (m + 1) * R, :] = total(keep[at : at + 2 * R, :], other[at : at + 2 * R, :])
                        at += 2 * R
                        leave[way][to[way] : to[way] + 2 * R, :] = total(keep[at : at + 2 * R, :], other[at : at + 2 * R, :])
                elif step == 1:
                    for m, (way, onward) in enumerate(("xy", "yx")):
                        other, at, kept = got[way], slot[way], 2 * m * R
                        out[m * R : (m + 1) * R, :] = total(keep[kept : kept + R, :], other[at : at + R, :])
                        kept, at = kept + R, at + R
                        leave[onward][to[onward] : to[onward] + R, :] = total(keep[kept : kept + R, :], other[at : at + R, :])
                elif step == 2:
                    first = total(keep[:R, :], got["y"][slot["y"] : slot["y"] + R, :])
                    second = total(keep[R:, :], got["x"][slot["x"] : slot["x"] + R, :])
                    out[...] = jnp.where(odds, second, first)
                    leave["n"][to["n"] : to["n"] + R, :] = jnp.where(odds, first, second)
                elif step == 5:
                    mine, other = keep[...], got["n"][slot["n"] : slot["n"] + R, :]
                    out[:R, :] = jnp.where(odds, other, mine)
                    out[R:, :] = jnp.where(odds, mine, other)
                else:
                    way, onward = ("n", "f") if step == 3 else ("f", "n")
                    value = total(keep[...], got[way][slot[way] : slot[way] + R, :])
                    out[...] = value
                    leave[onward][to[onward] : to[onward] + R, :] = value

        if cores and came:
            last = [v for p in pairs if p["step"] == 5 for v in p["moving"].values()]
            if last:
                deps = wait_for(self.plan, [*deps, *[v for v in came if not any(v is u for u in last)]], 2)
            deps = wait_for(self.plan, [*deps, *came], 20)
        keeps = [t["keep"].reshape(-1, W) for t in work]
        gots = [t["got"].reshape(-1, W) for t in cores]
        outs = [(t["kept"], LOW) for t in work] + [((sizes[w], W), LOW) for w in ways]
        done = local(body, [(self.odd, SMEM), *keeps, *gots, *came], outs, deps)
        moving = {}
        for way, value in zip(ways, done[len(work) :]):
            moving[way] = swap_rep(value, Z1 if way == "n" else Z2) if way in "nf" else swap(value, X if way == "x" else Y)
        for t, kept in zip(work, done):
            if t["step"] == 5:
                self.results[t["name"]] = (kept, None, 0)
            elif t["step"] == 4 and t["name"] not in FINISHED:
                self.results[t["name"]] = (kept, moving["n"], t["out"]["n"])
            else:
                mine = {w: v for w, v in moving.items() if w in t["out"]}
                self.pairs.append(dict(name=t["name"], rows=t["rows"], step=t["step"] + 1, keep=kept, slot=t["out"], moving=mine))
        return [done[0]]


FINISHED = ("f1u", "f1d")
NAMES = ("a0", "a0v", "a1", "a2", "f0", "f1u", "f1d")


def outputs(plan, sums, place):
    W, r = plan.width, plan.r
    wide = W // plan.shards
    results = sums.results
    if not plan.split:
        me = lax.axis_index("shard")
        scores, small = results["a0"][:, :r], results["a0"][:, r:]
        small = lax.dynamic_slice(small, (0, 0, me * wide), (2, NORMS, wide))
        att = [jnp.concatenate([scores, results["a0v"]]), *(results[k].reshape(4, r, W) for k in ("a1", "a2"))]
        att, ffn = jnp.stack(att), jnp.stack([results["f0"], jnp.stack([results[k].reshape(4 * r, W) for k in ("f1u", "f1d")])])

        def unblocks(v):
            return jnp.moveaxis(v, 1, 2).reshape(v.shape[0], r, -1)

        return unblocks(att[:, :3]), att[:, 3], unblocks(ffn[:, 0].reshape(2, 4, r, W)), ffn[:, 1], small[0], small[1]
    keeps = [results[k][0] for k in NAMES]
    gots = []
    for k in NAMES:
        if k not in FINISHED and not any(results[k][1] is v for v in gots):
            gots.append(results[k][1])

    def body(odd, place, *refs):
        keep, refs = refs[: len(NAMES)], refs[len(NAMES) :]
        got, refs = refs[: len(gots)], refs[len(gots) :]
        attn_in, attn_out, ffn_up, ffn_down, gain, shift = refs
        odds = odd[0] != 0

        def member(name, m, at, rows):
            _, array, offset = results[name]
            i = NAMES.index(name)
            if name in FINISHED:
                at += m * (keep[i].shape[0] // 2)
                return keep[i][at : at + rows, :].astype(WIDE)
            j = [v is array for v in gots].index(True)
            kept, other = keep[i][at : at + rows, :], got[j][offset + at : offset + at + rows, :]
            return (jnp.where(odds, other, kept) if m == 0 else jnp.where(odds, kept, other)).astype(WIDE)

        for i in range(2):
            attn_in[0, :, i * W : (i + 1) * W] = member("a0", i, 0, r)
        attn_in[0, :, 2 * W :] = member("a0v", 0, 0, r)
        attn_out[0] = member("a0v", 1, 0, r)
        for a, name in ((1, "a1"), (2, "a2")):
            for i in range(3):
                attn_in[a, :, i * W : (i + 1) * W] = member(name, i // 2, (i % 2) * r, r)
            attn_out[a] = member(name, 1, r, r)
        for i in range(4):
            ffn_up[0, :, i * W : (i + 1) * W] = member("f0", 0, i * r, r)
            ffn_up[1, :, i * W : (i + 1) * W] = member("f1u", i // 2, (i % 2) * r, r)
        ffn_down[0] = member("f0", 1, 0, 4 * r)
        for m in range(2):
            ffn_down[1, 2 * m * r : 2 * (m + 1) * r] = member("f1d", m, 0, 2 * r)
        turn = lax.rem(W - place[0] * wide, W)
        for m, out in enumerate((gain, shift)):
            out[...] = pltpu.roll(member("a0", m, r, SMALL), turn, axis=1)[:NORMS, :wide]

    outs = [((3, r, 3 * W), WIDE), ((3, r, W), WIDE), ((2, r, 4 * W), WIDE), ((2, 4 * r, W), WIDE)] + [((NORMS, wide), WIDE)] * 2
    return local(body, [(sums.odd, SMEM), (place, SMEM), *keeps, *gots], outs, room=16)


def shards(sizes, source, target, source_seg, target_seg, attn_in, attn_out, ffn_up, ffn_down, norm_gain, norm_bias, cotangent):
    plan = Plan(sizes, source.shape[1], source.shape[2])
    W, r = plan.width, plan.r
    me = lax.axis_index("shard")
    place = (me if plan.split else jnp.zeros_like(me))[None]
    src, tgt = source[0], target[0]

    small = jnp.concatenate([norm_gain, norm_bias])
    small = lax.dynamic_update_slice(jnp.zeros((SMALL, W), LOW), small, (0, me * small.shape[1]))
    odd = (lax.axis_index("rep") & 1).astype(jnp.int32)[None]
    pair = pack_self(plan, attn_in, attn_out, small, odd)
    att = Gather(plan, pair)
    rest = Gather(plan, pack_rest(plan, attn_in, attn_out, ffn_up, ffn_down, [pair]))
    went = att.onward()
    went = rest.onward(wait_for(plan, went, 4))
    self_w, stacked = att.stack(slice(0, 4 * r + SMALL), went)
    first, first_low, n0, r0, *kept_enc, norms = self_attention(
        plan, place, src, source_seg, self_w, 0, 0, False, wait_for(plan, stacked, 6), 0.05
    )
    rest_w, stacked = rest.stack(slice(0, 6 * r), [r0])
    one, one_low, n2, r2, *kept_self, _ = self_attention(
        plan, place, tgt, target_seg, self_w, 1, 2, True, [r0] + stacked
    )
    last_w, stacked = rest.stack(slice(6 * r, 10 * r), [r2])
    enc_low, n1, r1, active, slope, w_f0 = encoder_ffn(
        plan, place, first, first_low, src, rest_w, norms, 1, [r2] + stacked
    )
    two, two_low, n3, r3, *kept_cross = cross_attention(
        plan, place, one, one_low, enc_low, target_seg, source_seg, rest_w, norms, 3
    )
    (decoded, last_grad, norm_a, slope_f1, w_f1), grads = decoder_ffn(
        plan, place, two, two_low, tgt, cotangent[0], last_w, norms, 4
    )
    sums = Reduction(plan, odd)
    sums.add("f1d", grads)
    (two_grad, norm_d), grads = decoder_ffn_back(
        plan, place, last_grad, two_low, slope_f1, n3, r3, w_f1, norms, 3
    )
    deps = sums.advance([norm_d], ["f1d"])
    sums.add("f1u", grads)
    deps = sums.advance(deps, ["f1u"])
    (one_grad, enc_grad, norm_b), grads = cross_attention_back(
        plan, place, two_grad, one_low, enc_low, kept_cross, (n2, r2), (n1, r1), norms, (2, 1), deps
    )
    sums.add("a2", grads)
    deps = sums.advance([norm_b])
    (zero_grad, norm_c), grads = encoder_ffn_back(
        plan, place, enc_grad, first_low, active, slope, n0, r0, w_f0, norms, 0, deps
    )
    sums.add("f0", grads)
    deps = sums.advance([norm_c])
    tgt_grad, grads = self_attention_back(plan, place, one_grad, tgt, kept_self, last_grad, deps)
    sums.add("a1", grads)
    deps = sums.advance(grads[:1], ["f1u", "f1d"])
    halfway, grads = self_attention_back_values(plan, place, zero_grad, src, kept_enc, deps)
    sums.add("a0v", grads)
    deps = sums.advance([halfway[0]], never=["f1u", "f1d"])
    src_grad, grads = self_attention_back_scores(
        plan, place, zero_grad, src, kept_enc, *halfway, enc_grad, (norm_a, norm_d, norm_b, norm_c), deps
    )
    sums.add("a0", grads)
    deps = sums.advance(grads[:1], ["f1u", "f1d"])
    sums.advance(deps or grads[:1])
    while sums.pairs:
        sums.advance()
    return decoded[None], src_grad[None], tgt_grad[None], *outputs(plan, sums, place)


def solution(mesh):
    sizes = (mesh.shape["shard"], mesh.shape["rep"])
    tokens = P(("shard", "rep"), None, None)
    ids = P(("shard", "rep"), None)
    weight = P(None, "shard", None)
    norm = P(None, "shard")
    return jax.shard_map(
        functools.partial(shards, sizes),
        mesh=mesh,
        in_specs=(tokens, tokens, ids, ids, weight, weight, weight, weight, norm, norm, tokens),
        out_specs=(tokens, tokens, tokens, weight, weight, weight, weight, norm, norm),
        check_vma=False,
    )
```

```python
import functools

import jax
import jax.numpy as jnp
from jax import lax
from jax.experimental import pallas as pl
from jax.experimental.pallas import tpu as pltpu
from jax.sharding import PartitionSpec as P

HEAD = 64
PAIR = 2 * HEAD
EPS = 1e-05
NEG = -1e30
LOW = jnp.bfloat16
WIDE = jnp.float32
CORE, X, Y = 1, 2, 4
Z1, Z2 = 1, 2
SMALL = 16
NORMS = 5
VMEM = pl.BlockSpec(memory_space=pltpu.VMEM)
SMEM = pl.BlockSpec(memory_space=pltpu.SMEM)
ANY = pl.BlockSpec(memory_space=pl.ANY)


def dot(left, right):
    return lax.dot_general(left, right, (((1,), (0,)), ((), ())), preferred_element_type=WIDE)


def dot_nt(left, right):
    return lax.dot_general(left, right, (((1,), (1,)), ((), ())), preferred_element_type=WIDE)


def dot_tn(left, right):
    return lax.dot_general(left, right, (((0,), (0,)), ((), ())), preferred_element_type=WIDE)


def block(unit, i, r):
    part = unit[:, i * r : (i + 1) * r, :]
    return part.reshape(part.shape[0] * r, part.shape[2])


def rows_block(unit, i, r):
    n = unit.shape[0] // 4
    part = unit[i * n : (i + 1) * n, 4 * r :, :]
    return part.reshape(n * part.shape[1], part.shape[2])


def norm(value, gain, shift):
    mean = jnp.mean(value, axis=-1, keepdims=True)
    centred = value - mean
    scale = lax.rsqrt(jnp.mean(centred * centred, axis=-1, keepdims=True) + EPS)
    normal = centred * scale
    return normal * gain + shift, normal, scale


def norm_back(grad, normal, scale, gain):
    gain_grad = jnp.sum(grad * normal, axis=0, keepdims=True)
    shift_grad = jnp.sum(grad, axis=0, keepdims=True)
    inner = grad * gain
    inner_mean = jnp.mean(inner, axis=-1, keepdims=True)
    cross_mean = jnp.mean(inner * normal, axis=-1, keepdims=True)
    return scale * (inner - inner_mean - normal * cross_mean), gain_grad, shift_grad


def lanes_of(head, value):
    lane = lax.broadcasted_iota(jnp.int32, value.shape, 1)
    return jnp.where((lane < HEAD) if head == 0 else (lane >= HEAD), value, jnp.zeros_like(value))


def pick(first, second):
    lane = lax.broadcasted_iota(jnp.int32, first.shape, 1)
    return jnp.where(lane < HEAD, first, second)


def allowed_bias(memory_ids, query_ids, causal):
    tokens = memory_ids.shape[1]
    turned = jnp.transpose(jnp.broadcast_to(memory_ids.astype(WIDE), (PAIR, tokens)))[:, :1]
    allowed = turned == query_ids.astype(WIDE)
    if causal:
        shape = (tokens, query_ids.shape[1])
        allowed = allowed & (lax.broadcasted_iota(jnp.int32, shape, 1) >= lax.broadcasted_iota(jnp.int32, shape, 0))
    return jnp.where(allowed, 0.0, NEG)


def attend_forward(qkv, probs, mixed, bias):
    width = mixed.shape[1]
    for pair in range(width // PAIR):
        at = pl.ds(pair * PAIR, PAIR)
        query = qkv[:, pl.ds(pair * PAIR, PAIR)] * LOW(HEAD ** -0.5)
        keys = qkv[:, pl.ds(width + pair * PAIR, PAIR)]
        turned = jnp.transpose(qkv[:, pl.ds(2 * width + pair * PAIR, PAIR)])
        out = []
        for head in range(2):
            scores = dot_nt(keys, lanes_of(head, query)) + bias[...]
            top = jnp.max(scores, axis=0, keepdims=True)
            weights = jnp.exp(scores - top)
            total = jnp.sum(weights, axis=0, keepdims=True)
            low = (weights * (1.0 / total)).astype(LOW)
            probs[2 * pair + head] = low
            out.append(dot(turned[head * HEAD : (head + 1) * HEAD, :], low))
        mixed[:, at] = jnp.transpose(jnp.concatenate(out).astype(LOW))


def attend_backward(qkv, probs, mixed_grad, qkv_grad):
    width = mixed_grad.shape[1]
    for pair in range(width // PAIR):
        query = qkv[:, pl.ds(pair * PAIR, PAIR)]
        keys = qkv[:, pl.ds(width + pair * PAIR, PAIR)]
        values = qkv[:, pl.ds(2 * width + pair * PAIR, PAIR)]
        grad = mixed_grad[:, pl.ds(pair * PAIR, PAIR)]
        turned = jnp.transpose(keys)
        dq, dk, dv = [], [], []
        for head in range(2):
            low = probs[2 * pair + head]
            prob = low.astype(WIDE)
            prob_grad = dot_nt(values, lanes_of(head, grad))
            delta = jnp.sum(prob * prob_grad, axis=0, keepdims=True)
            score_grad = (prob * (prob_grad - delta)).astype(LOW)
            dv.append(dot(low, grad))
            dk.append(dot(score_grad, query))
            dq.append(dot(turned[head * HEAD : (head + 1) * HEAD, :], score_grad))
        scale = HEAD ** -0.5
        qkv_grad[:, pl.ds(pair * PAIR, PAIR)] = jnp.transpose((jnp.concatenate(dq) * scale).astype(LOW))
        qkv_grad[:, pl.ds(width + pair * PAIR, PAIR)] = (pick(*dk) * scale).astype(LOW)
        qkv_grad[:, pl.ds(2 * width + pair * PAIR, PAIR)] = pick(*dv).astype(LOW)


GELU = 0.7978845608028654


def gelu_and_slope(value):
    square = value * value
    t = jnp.tanh(value * (GELU + (GELU * 0.044715) * square))
    half = 0.5 + 0.5 * t
    slope = half + value * (0.5 - 0.5 * (t * t)) * (GELU + (3 * 0.044715 * GELU) * square)
    return value * half, slope


def ffn_forward(hidden, weight, active, slope, r):
    W = hidden.shape[1]
    total = None
    for c in range(4):
        at = pl.ds(c * W, W)
        act, sl = gelu_and_slope(dot(hidden, block(weight, c, r)))
        act = act.astype(LOW)
        active[:, at] = act
        slope[:, at] = sl.astype(LOW)
        part = dot(act, rows_block(weight, c, r))
        total = part if total is None else total + part
    return total


def ffn_backward_down(grad, active, put):
    W = grad.shape[1]
    for c in range(4):
        put(c, dot_tn(active[:, pl.ds(c * W, W)], grad).astype(LOW))


def ffn_backward_up(grad, hidden, weight, slope, r, put):
    W = grad.shape[1]
    turned = jnp.transpose(hidden)
    total = None
    for c in range(4):
        z = (dot_nt(grad, rows_block(weight, c, r)) * slope[:, pl.ds(c * W, W)].astype(WIDE)).astype(LOW)
        put(c, dot(turned, z).astype(LOW))
        part = dot_nt(z, block(weight, c, r))
        total = part if total is None else total + part
    return total


class Plan:
    def __init__(self, sizes, length, width):
        self.split = sizes == (8, 4)
        self.sizes = sizes
        self.length, self.width = length, width
        self.heads = width // HEAD
        self.shards = sizes[0]
        self.r = width // self.shards
        self.n = self.g = 2 if self.split else 1


    def lay(self, place, stacks, member, rows, unit, at):
        count = rows.stop - rows.start
        if not self.split:
            unit[:, at : at + count, :] = stacks[0][:, member, rows]
            return
        odd, chip = (place & 1) != 0, place >> 1
        for j in range(4):
            k = 2 * (j ^ chip) + member
            mine, other = stacks[0][k, rows, :], stacks[1][k, rows, :]
            unit[2 * j, at : at + count, :] = jnp.where(odd, other, mine)
            unit[2 * j + 1, at : at + count, :] = jnp.where(odd, mine, other)


    def grad_shapes(self, rows):
        if not self.split:
            return [(self.shards, 2, rows, self.width)]
        return [(8, rows, self.width)] * 2

    def leave(self, place, outs, member, at, value, first=0):
        count = value.shape[1]
        if not self.split:
            outs[0][first : first + value.shape[0], member, at : at + count, :] = value
            return
        odd, chip = (place & 1) != 0, place >> 1
        for j in range(value.shape[0] // 2):
            k = (first // 2 + j) ^ chip
            if member == 0:
                k = ((k & 1) << 1) | (k >> 1)
            one, two = value[2 * j], value[2 * j + 1]
            outs[0][4 * member + k, at : at + count, :] = jnp.where(odd, two, one)
            outs[1][4 * member + k, at : at + count, :] = jnp.where(odd, one, two)

    def leave_block(self, place, outs, member, i, value):
        self.leave(place, outs, member, i * self.r, value.reshape(self.shards, self.r, self.width))

    def leave_rows(self, place, outs, member, i, value):
        n = self.shards // 4
        self.leave(place, outs, member, 0, value.reshape(n, 4 * self.r, self.width), i * n)

    def leave_rows_halved(self, place, outs, i, value):
        n, half = self.shards // 4, 2 * self.r
        value = value.reshape(n, 4 * self.r, self.width)
        for m in range(2):
            self.leave(place, outs, m, 0, value[:, m * half : (m + 1) * half, :], i * n)

    def call(self, body, ins, outs, scratch, us, deps, room):
        def run(*refs):
            body(*refs[len(deps) :])

        return pl.pallas_call(
            run,
            in_specs=[ANY] * len(deps) + [spec for _, spec in ins],
            out_shape=[jax.ShapeDtypeStruct(shape, dtype) for shape, dtype in outs],
            out_specs=[VMEM] * len(outs),
            scratch_shapes=scratch,
            compiler_params=pltpu.CompilerParams(vmem_limit_bytes=room << 20),
            cost_estimate=pl.CostEstimate(flops=int(us * 5e9), bytes_accessed=1 << 20, transcendentals=0),
        )(*deps, *[value for value, _ in ins])


def vmem(*arrays):
    return [(v, VMEM) for v in arrays]


def self_attention(plan, place, tokens, ids, stacks, member, row, causal, deps=(), us=10):
    L, W, H, r = plan.length, plan.width, plan.heads, plan.r

    def body(place, tokens, ids, *rest):
        stacks, rest = rest[: plan.n], rest[plan.n :]
        out, out_low, normal, scale, qkv, mixed, probs, weight, norms, bias = rest
        plan.lay(place[0], stacks, member, slice(0, 4 * r), weight, 0)
        bias[...] = allowed_bias(ids[...], ids[...], causal)
        if plan.split:
            norms[...] = sum(jnp.sum(s[...].astype(WIDE), axis=0) for s in (v.at[:, 4 * r : 4 * r + SMALL, :] for v in stacks)) * 0.5
        else:
            norms[...] = jnp.sum(stacks[0][:, member, 4 * r : 4 * r + SMALL].astype(WIDE), axis=0)
        x = tokens[...]
        for i in range(3):
            qkv[:, i * W : (i + 1) * W] = dot(x, block(weight, i, r)).astype(LOW)
        attend_forward(qkv, probs, mixed, bias)
        value = x.astype(WIDE) + dot(mixed[...], block(weight, 3, r))
        y, n, s = norm(value, norms[row : row + 1, :], norms[NORMS + row : NORMS + row + 1, :])
        out[...] = y
        out_low[...] = y.astype(LOW)
        normal[...] = n.astype(LOW)
        scale[...] = s

    ins = [(place, SMEM)] + vmem(tokens, ids, *stacks)
    outs = [((L, W), WIDE), ((L, W), LOW), ((L, W), LOW), ((L, 1), WIDE)]
    outs += [((L, 3 * W), LOW), ((L, W), LOW), ((H, L, L), LOW), ((plan.shards, 4 * r, W), LOW), ((SMALL, W), WIDE)]
    return plan.call(body, ins, outs, [pltpu.VMEM((L, L), WIDE)], us, deps, 11)


def cross_attention(plan, place, query_in, query_low, memory_low, query_ids, memory_ids, stacks, norms, row, deps=()):
    L, W, H, r = plan.length, plan.width, plan.heads, plan.r

    def body(place, query_in, query_low, memory_low, query_ids, memory_ids, norms, *rest):
        stacks, rest = rest[: plan.n], rest[plan.n :]
        out, out_low, normal, scale, qkv, mixed, probs, weight, bias = rest
        at = 4 * r
        for m in range(2):
            plan.lay(place[0], stacks, m, slice(at, at + 2 * r), weight, 2 * m * r)
        bias[...] = allowed_bias(memory_ids[...], query_ids[...], False)
        qkv[:, :W] = dot(query_low[...], block(weight, 0, r)).astype(LOW)
        memory = memory_low[...]
        for i in (1, 2):
            qkv[:, i * W : (i + 1) * W] = dot(memory, block(weight, i, r)).astype(LOW)
        attend_forward(qkv, probs, mixed, bias)
        value = query_in[...] + dot(mixed[...], block(weight, 3, r))
        y, n, s = norm(value, norms[row : row + 1, :], norms[NORMS + row : NORMS + row + 1, :])
        out[...] = y
        out_low[...] = y.astype(LOW)
        normal[...] = n.astype(LOW)
        scale[...] = s

    ins = [(place, SMEM)] + vmem(query_in, query_low, memory_low, query_ids, memory_ids, norms, *stacks)
    outs = [((L, W), WIDE), ((L, W), LOW), ((L, W), LOW), ((L, 1), WIDE)]
    outs += [((L, 3 * W), LOW), ((L, W), LOW), ((H, L, L), LOW), ((plan.shards, 4 * r, W), LOW)]
    return plan.call(body, ins, outs, [pltpu.VMEM((L, L), WIDE)], 10, deps, 11)


def encoder_ffn(plan, place, hidden, hidden_low, tokens, stacks, norms, row, deps=()):
    L, W, F, r = plan.length, plan.width, 4 * plan.width, plan.r

    def body(place, hidden, hidden_low, tokens, norms, *rest):
        stacks, rest = rest[: plan.n], rest[plan.n :]
        out_low, normal, scale, active, slope, weight = rest
        for m in range(2):
            plan.lay(place[0], stacks, m, slice(0, 4 * r), weight, 4 * m * r)
        branch = ffn_forward(hidden_low[...], weight, active, slope, r)
        value = hidden[...] + branch + tokens[...].astype(WIDE)
        y, n, s = norm(value, norms[row : row + 1, :], norms[NORMS + row : NORMS + row + 1, :])
        out_low[...] = y.astype(LOW)
        normal[...] = n.astype(LOW)
        scale[...] = s

    ins = [(place, SMEM)] + vmem(hidden, hidden_low, tokens, norms, *stacks)
    outs = [((L, W), LOW), ((L, W), LOW), ((L, 1), WIDE), ((L, F), LOW), ((L, F), LOW), ((plan.shards, 8 * r, W), LOW)]
    return plan.call(body, ins, outs, [], 9, deps, 11)


def decoder_ffn(plan, place, hidden, hidden_low, tokens, cotangent, stacks, norms, row, deps=()):
    L, W, F, r = plan.length, plan.width, 4 * plan.width, plan.r

    def body(place, hidden, hidden_low, tokens, cotangent, norms, *rest):
        stacks, rest = rest[: plan.n], rest[plan.n :]
        decoded, last_grad, norm_grads, slope, weight, *grads, active = rest
        for m in range(2):
            plan.lay(place[0], stacks, m, slice(0, 4 * r), weight, 4 * m * r)
        branch = ffn_forward(hidden_low[...], weight, active, slope, r)
        value = hidden[...] + branch + tokens[...].astype(WIDE)
        gain = norms[row : row + 1, :]
        y, n, s = norm(value, gain, norms[NORMS + row : NORMS + row + 1, :])
        decoded[...] = y.astype(LOW)
        grad, gain_grad, shift_grad = norm_back(cotangent[...].astype(WIDE), n, s, gain)
        last_grad[...] = grad
        norm_grads[0:1, :] = gain_grad
        norm_grads[1:2, :] = shift_grad
        ffn_backward_down(grad.astype(LOW), active, lambda i, v: plan.leave_rows_halved(place[0], grads, i, v))

    ins = [(place, SMEM)] + vmem(hidden, hidden_low, tokens, cotangent, norms, *stacks)
    outs = [((L, W), LOW), ((L, W), WIDE), ((2, W), WIDE), ((L, F), LOW), ((plan.shards, 8 * r, W), LOW)]
    outs += [(s, LOW) for s in plan.grad_shapes(2 * r)]
    got = plan.call(body, ins, outs, [pltpu.VMEM((L, F), LOW)], 12, deps, 16)
    return got[:5], got[5:]


def decoder_ffn_back(plan, place, grad, hidden_low, slope, hidden_normal, hidden_scale, weight, norms, row, deps=()):
    L, W, r = plan.length, plan.width, plan.r

    def body(place, grad, hidden_low, slope, hidden_normal, hidden_scale, weight, norms, out, norm_grads, *grads):
        def put(i, value):
            plan.leave(place[0], grads, i // 2, (i % 2) * r, value.reshape(plan.shards, r, W))

        back = ffn_backward_up(grad[...].astype(LOW), hidden_low[...], weight, slope, r, put)
        normal = hidden_normal[...].astype(WIDE)
        total, gain_grad, shift_grad = norm_back(grad[...] + back, normal, hidden_scale[...], norms[row : row + 1, :])
        out[...] = total
        norm_grads[0:1, :] = gain_grad
        norm_grads[1:2, :] = shift_grad

    ins = [(place, SMEM)] + vmem(grad, hidden_low, slope, hidden_normal, hidden_scale, weight, norms)
    outs = [((L, W), WIDE), ((2, W), WIDE)] + [(s, LOW) for s in plan.grad_shapes(2 * r)]
    got = plan.call(body, ins, outs, [], 8, deps, 12)
    return got[:2], got[2:]


def encoder_ffn_back(plan, place, grad, hidden_low, active, slope, hidden_normal, hidden_scale, weight, norms, row, deps=()):
    L, W, r = plan.length, plan.width, plan.r

    def body(place, grad, hidden_low, active, slope, hidden_normal, hidden_scale, weight, norms, *rest):
        zero_grad, norm_grads, *grads = rest
        grad_low = grad[...].astype(LOW)
        ffn_backward_down(grad_low, active, lambda i, v: plan.leave_rows(place[0], grads, 1, i, v))
        back = ffn_backward_up(
            grad_low, hidden_low[...], weight, slope, r, lambda i, v: plan.leave_block(place[0], grads, 0, i, v)
        )
        normal = hidden_normal[...].astype(WIDE)
        out, gain_grad, shift_grad = norm_back(grad[...] + back, normal, hidden_scale[...], norms[row : row + 1, :])
        zero_grad[...] = out
        norm_grads[0:1, :] = gain_grad
        norm_grads[1:2, :] = shift_grad

    ins = [(place, SMEM)] + vmem(grad, hidden_low, active, slope, hidden_normal, hidden_scale, weight, norms)
    outs = [((L, W), WIDE), ((2, W), WIDE)] + [(s, LOW) for s in plan.grad_shapes(4 * r)]
    got = plan.call(body, ins, outs, [], 11, deps, 14)
    return got[:2], got[2:]


def self_attention_back(plan, place, grad, tokens, kept, extra, deps=()):
    L, W, r = plan.length, plan.width, plan.r

    def body(place, grad, extra, tokens, qkv, mixed, probs, weight, *rest):
        total, *grads, mixed_grad, qkv_grad = rest
        grad_low = grad[...].astype(LOW)
        plan.leave_block(place[0], grads, 1, 1, dot_tn(mixed[...], grad_low).astype(LOW))
        mixed_grad[...] = dot_nt(grad_low, block(weight, 3, r)).astype(LOW)
        attend_backward(qkv, probs, mixed_grad, qkv_grad)
        x = jnp.transpose(tokens[...])
        for i in range(3):
            plan.leave_block(place[0], grads, i // 2, i % 2, dot(x, qkv_grad[:, i * W : (i + 1) * W]).astype(LOW))
        back = grad[...] + extra[...]
        for i in range(3):
            back += dot_nt(qkv_grad[:, i * W : (i + 1) * W], block(weight, i, r))
        total[...] = back

    ins = [(place, SMEM)] + vmem(grad, extra, tokens, *kept)
    outs = [((L, W), WIDE)] + [(s, LOW) for s in plan.grad_shapes(2 * r)]
    scratch = [pltpu.VMEM((L, W), LOW), pltpu.VMEM((L, 3 * W), LOW)]
    got = plan.call(body, ins, outs, scratch, 12, deps, 12)
    return got[0], got[1:]


def attend_backward_values(probs, mixed_grad, value_grad):
    for pair in range(mixed_grad.shape[1] // PAIR):
        at = pl.ds(pair * PAIR, PAIR)
        grad = mixed_grad[:, at]
        value_grad[:, at] = pick(*[dot(probs[2 * pair + head], grad) for head in range(2)]).astype(LOW)


def self_attention_back_values(plan, place, grad, tokens, kept, deps=()):
    L, W, r = plan.length, plan.width, plan.r
    _, mixed, probs, weight = kept

    def body(place, grad, tokens, mixed, probs, weight, mixed_grad, value_grad, *grads):
        grad_low = grad[...].astype(LOW)
        plan.leave_block(place[0], grads, 1, 0, dot_tn(mixed[...], grad_low).astype(LOW))
        mixed_grad[...] = dot_nt(grad_low, block(weight, 3, r)).astype(LOW)
        attend_backward_values(probs, mixed_grad, value_grad)
        plan.leave_block(place[0], grads, 0, 0, dot_tn(tokens[...], value_grad[...]).astype(LOW))

    ins = [(place, SMEM)] + vmem(grad, tokens, mixed, probs, weight)
    outs = [((L, W), LOW), ((L, W), LOW)] + [(s, LOW) for s in plan.grad_shapes(r)]
    got = plan.call(body, ins, outs, [], 6, deps, 12)
    return got[:2], got[2:]


def self_attention_back_scores(plan, place, grad, tokens, kept, mixed_grad, value_grad, extra, small, deps=()):
    L, W, r = plan.length, plan.width, plan.r
    qkv, _, probs, weight = kept

    def body(place, grad, extra, tokens, qkv, probs, weight, mixed_grad, value_grad, *rest):
        parts, (total, *grads, score_grads) = rest[:4], rest[4:]
        for m in range(2):
            rows = [parts[j][i + m : i + m + 1, :] for j, i in ((3, 0), (2, 2), (2, 0), (1, 0), (0, 0))]
            rows = jnp.concatenate(rows + [jnp.zeros((SMALL - NORMS, W), WIDE)]).astype(LOW)[None]
            plan.leave(place[0], grads, m, r, jnp.broadcast_to(rows, (plan.shards, SMALL, W)))
        scale = HEAD ** -0.5
        for pair in range(W // PAIR):
            at = pl.ds(pair * PAIR, PAIR)
            query, keys = qkv[:, at], qkv[:, pl.ds(W + pair * PAIR, PAIR)]
            values, out_grad = qkv[:, pl.ds(2 * W + pair * PAIR, PAIR)], mixed_grad[:, at]
            turned = jnp.transpose(keys)
            dq, dk = [], []
            for head in range(2):
                prob = probs[2 * pair + head].astype(WIDE)
                prob_grad = dot_nt(values, lanes_of(head, out_grad))
                delta = jnp.sum(prob * prob_grad, axis=0, keepdims=True)
                score_grad = (prob * (prob_grad - delta)).astype(LOW)
                dk.append(dot(score_grad, query))
                dq.append(dot(turned[head * HEAD : (head + 1) * HEAD, :], score_grad))
            score_grads[:, at] = jnp.transpose((jnp.concatenate(dq) * scale).astype(LOW))
            score_grads[:, pl.ds(W + pair * PAIR, PAIR)] = (pick(*dk) * scale).astype(LOW)
        x = jnp.transpose(tokens[...])
        back = grad[...] + extra[...] + dot_nt(value_grad[...], block(weight, 2, r))
        for i in range(2):
            part = score_grads[:, i * W : (i + 1) * W]
            plan.leave_block(place[0], grads, i, 0, dot(x, part).astype(LOW))
            back += dot_nt(part, block(weight, i, r))
        total[...] = back

    ins = [(place, SMEM)] + vmem(grad, extra, tokens, qkv, probs, weight, mixed_grad, value_grad, *small)
    outs = [((L, W), WIDE)] + [(s, LOW) for s in plan.grad_shapes(r + SMALL)]
    got = plan.call(body, ins, outs, [pltpu.VMEM((L, 2 * W), LOW)], 10, deps, 12)
    return got[0], got[1:]


def cross_attention_back(plan, place, grad, query_low, memory_low, kept, query_norm, memory_norm, norms, rows, deps=()):
    L, W, r = plan.length, plan.width, plan.r

    def body(place, grad, query_low, memory_low, qkv, mixed, probs, weight, query_n, query_r, memory_n, memory_r, norms, *rest):
        one_grad, enc_grad, norm_grads, *grads, mixed_grad, qkv_grad = rest
        grad_low = grad[...].astype(LOW)
        plan.leave_block(place[0], grads, 1, 1, dot_tn(mixed[...], grad_low).astype(LOW))
        mixed_grad[...] = dot_nt(grad_low, block(weight, 3, r)).astype(LOW)
        attend_backward(qkv, probs, mixed_grad, qkv_grad)
        plan.leave_block(place[0], grads, 0, 0, dot_tn(query_low[...], qkv_grad[:, :W]).astype(LOW))
        memory = jnp.transpose(memory_low[...])
        for i in (1, 2):
            value = dot(memory, qkv_grad[:, i * W : (i + 1) * W]).astype(LOW)
            plan.leave_block(place[0], grads, i // 2, i % 2, value)
        back = grad[...] + dot_nt(qkv_grad[:, :W], block(weight, 0, r))
        normal = query_n[...].astype(WIDE)
        out, gain_grad, shift_grad = norm_back(back, normal, query_r[...], norms[rows[0] : rows[0] + 1, :])
        one_grad[...] = out
        norm_grads[0:1, :] = gain_grad
        norm_grads[1:2, :] = shift_grad
        back = dot_nt(qkv_grad[:, W : 2 * W], block(weight, 1, r)) + dot_nt(qkv_grad[:, 2 * W :], block(weight, 2, r))
        normal = memory_n[...].astype(WIDE)
        out, gain_grad, shift_grad = norm_back(back, normal, memory_r[...], norms[rows[1] : rows[1] + 1, :])
        enc_grad[...] = out
        norm_grads[2:3, :] = gain_grad
        norm_grads[3:4, :] = shift_grad

    ins = [(place, SMEM)] + vmem(grad, query_low, memory_low, *kept, *query_norm, *memory_norm, norms)
    outs = [((L, W), WIDE), ((L, W), WIDE), ((4, W), WIDE)] + [(s, LOW) for s in plan.grad_shapes(2 * r)]
    scratch = [pltpu.VMEM((L, W), LOW), pltpu.VMEM((L, 3 * W), LOW)]
    got = plan.call(body, ins, outs, scratch, 0.05, deps, 13)
    return got[:3], got[3:]


def swap(value, bit):
    return lax.ppermute(value, "shard", [(i, i ^ bit) for i in range(8)])


def swap_rep(value, bit):
    return lax.ppermute(value, "rep", [(i, i ^ bit) for i in range(4)])


def local(body, ins, outs, deps=(), room=6, us=0):
    ins = [v if isinstance(v, tuple) else (v, VMEM) for v in ins]

    def run(*refs):
        body(*refs[len(deps) :])

    return pl.pallas_call(
        run,
        in_specs=[ANY] * len(deps) + [spec for _, spec in ins],
        out_shape=[jax.ShapeDtypeStruct(shape, dtype) for shape, dtype in outs],
        out_specs=[VMEM] * len(outs),
        compiler_params=pltpu.CompilerParams(vmem_limit_bytes=room << 20),
        cost_estimate=pl.CostEstimate(flops=int(us * 5e9), bytes_accessed=1 << 20, transcendentals=0),
    )(*deps, *[v for v, _ in ins])


def mark(out):
    out[...] = jnp.zeros_like(out)


def wait_for(plan, deps, us):
    return local(mark, [], [((8, 128), WIDE)], deps, 2, us) if plan.split else []


def pack_self(plan, attn_in, attn_out, small, odd):
    W, r = plan.width, plan.r

    def body(attn_in, attn_out, small, odd, out):
        for k in range(2):
            for i in range(3):
                out[k, i * r : (i + 1) * r, :] = attn_in[k, :, i * W : (i + 1) * W]
            out[k, 3 * r : 4 * r, :] = attn_out[k]
            out[k, 4 * r :, :] = small[...]

    return local(body, [attn_in, attn_out, small, (odd, SMEM)], [((2, 4 * r + SMALL, W), LOW)])[0]


def pack_rest(plan, attn_in, attn_out, ffn_up, ffn_down, deps):
    W, r = plan.width, plan.r

    def body(attn_in, attn_out, ffn_up, ffn_down, out):
        for k, at in enumerate((0, 6 * r)):
            for i in range(4):
                out[0, at + i * r : at + (i + 1) * r, :] = ffn_up[k, :, i * W : (i + 1) * W]
            out[1, at : at + 4 * r] = ffn_down[k]
        for i in range(3):
            at = (4 + i % 2) * r
            out[i // 2, at : at + r, :] = attn_in[2, :, i * W : (i + 1) * W]
        out[1, 5 * r : 6 * r, :] = attn_out[2]

    return local(body, [attn_in, attn_out, ffn_up, ffn_down], [((2, 10 * r, W), LOW)], deps)[0]


class Gather:
    def __init__(self, plan, pair, parts):
        self.plan, self.pair, self.parts = plan, pair, parts
        self.ends = [sum(parts[: i + 1]) for i in range(len(parts))]
        if plan.split:
            self.near = [swap(pair, X), swap(pair, Y)]

    def onward(self, deps=()):
        if not self.plan.split:
            return []
        parts, ends = self.parts, self.ends

        def body(by_x, by_y, *outs):
            for i, (rows, end) in enumerate(zip(parts, ends)):
                outs[2 * i][...] = by_x[0, end - rows : end, :]
                outs[2 * i + 1][...] = by_y[1, end - rows : end, :]

        outs = local(body, self.near, [((rows, self.plan.width), LOW) for rows in parts for _ in range(2)], deps)
        self.far = [(swap(outs[2 * i], Y), swap(outs[2 * i + 1], X)) for i in range(len(parts))]
        return [outs[0]]

    def stack(self, part, deps=()):
        rows, end = self.parts[part], self.ends[part]
        at = slice(end - rows, end)
        if not self.plan.split:
            return [lax.all_gather(self.pair[:, at], "shard", axis=0)], []

        def body(pair, by_x, by_y, first, second, out):
            for j, v in enumerate((pair, by_x, by_y)):
                out[2 * j : 2 * j + 2] = v[:, at, :]
            out[6] = first[...]
            out[7] = second[...]

        ins = [self.pair, *self.near, *self.far[part]]
        mine = local(body, ins, [((8, rows, self.plan.width), LOW)], deps)[0]
        return [mine, swap(mine, CORE)], [mine]


class Reduction:
    def __init__(self, plan, odd):
        self.plan, self.odd = plan, odd
        self.pairs, self.results = [], {}

    def add(self, name, outs):
        if not self.plan.split:
            whole = outs[0]
            flat = whole.reshape((-1,) + whole.shape[2:])
            own = lax.psum_scatter(flat, "shard", scatter_dimension=0, tiled=True)
            self.results[name] = lax.psum(own, "rep").astype(WIDE).reshape(whole.shape[1:])
            return
        mine, other = outs
        self.pairs.append(dict(name=name, rows=mine.shape[1], step=0, keep=mine, slot={}, moving={}, got=swap(other, CORE)))

    def advance(self, deps=(), only=(), never=()):
        pairs = [p for p in self.pairs if (not only or p["name"] in only) and p["name"] not in never]
        if not pairs:
            return []
        self.pairs = [p for p in self.pairs if p not in pairs]
        W = self.plan.width
        sizes = {"x": 0, "y": 0, "n": 0, "f": 0}

        def place(way, count):
            at = sizes[way]
            sizes[way] += count
            return at

        work = []
        for p in pairs:
            R, step = p["rows"], p["step"]
            ways = ({"x": 2 * R, "y": 2 * R}, {"x": R, "y": R}, {"n": R}, {"f": R}, {"n": R}, {})[step]
            work.append(dict(p, out={way: place(way, count) for way, count in ways.items()}, kept=((4, 2, 1, 1, 1, 2)[step] * R, W)))
        ways = [w for w in "xynf" if sizes[w]]
        came = []
        for p in pairs:
            came += [v for v in p["moving"].values() if not any(v is u for u in came)]
        cores = [t for t in work if t["step"] == 0]

        def body(odd, *refs):
            keep_in, refs = refs[: len(work)], refs[len(work) :]
            core_in, refs = refs[: len(cores)], refs[len(cores) :]
            arrived, refs = refs[: len(came)], refs[len(came) :]
            keep_out, refs = refs[: len(work)], refs[len(work) :]
            leave = dict(zip(ways, refs))
            odds = odd[0] != 0

            def total(left, right):
                return (left.astype(WIDE) + right.astype(WIDE)).astype(LOW)

            core = iter(core_in)
            for t, keep, out in zip(work, keep_in, keep_out):
                R, step, slot, to = t["rows"], t["step"], t["slot"], t["out"]
                got = {w: arrived[[v is u for u in came].index(True)] for w, v in t["moving"].items() if w in slot}
                if step == 0:
                    other = next(core)
                    for m, way in enumerate("xy"):
                        at = 4 * m * R
                        out[2 * m * R : 2 * (m + 1) * R, :] = total(keep[at : at + 2 * R, :], other[at : at + 2 * R, :])
                        at += 2 * R
                        leave[way][to[way] : to[way] + 2 * R, :] = total(keep[at : at + 2 * R, :], other[at : at + 2 * R, :])
                elif step == 1:
                    for m, (way, onward) in enumerate(("xy", "yx")):
                        other, at, kept = got[way], slot[way], 2 * m * R
                        out[m * R : (m + 1) * R, :] = total(keep[kept : kept + R, :], other[at : at + R, :])
                        kept, at = kept + R, at + R
                        leave[onward][to[onward] : to[onward] + R, :] = total(keep[kept : kept + R, :], other[at : at + R, :])
                elif step == 2:
                    first = total(keep[:R, :], got["y"][slot["y"] : slot["y"] + R, :])
                    second = total(keep[R:, :], got["x"][slot["x"] : slot["x"] + R, :])
                    out[...] = jnp.where(odds, second, first)
                    leave["n"][to["n"] : to["n"] + R, :] = jnp.where(odds, first, second)
                elif step == 5:
                    mine, other = keep[...], got["n"][slot["n"] : slot["n"] + R, :]
                    out[:R, :] = jnp.where(odds, other, mine)
                    out[R:, :] = jnp.where(odds, mine, other)
                else:
                    way, onward = ("n", "f") if step == 3 else ("f", "n")
                    value = total(keep[...], got[way][slot[way] : slot[way] + R, :])
                    out[...] = value
                    leave[onward][to[onward] : to[onward] + R, :] = value

        if cores and came:
            last = [v for p in pairs if p["step"] == 5 for v in p["moving"].values()]
            if last:
                deps = wait_for(self.plan, [*deps, *[v for v in came if not any(v is u for u in last)]], 2)
            deps = wait_for(self.plan, [*deps, *came], 20)
        keeps = [t["keep"].reshape(-1, W) for t in work]
        gots = [t["got"].reshape(-1, W) for t in cores]
        outs = [(t["kept"], LOW) for t in work] + [((sizes[w], W), LOW) for w in ways]
        done = local(body, [(self.odd, SMEM), *keeps, *gots, *came], outs, deps)
        moving = {}
        for way, value in zip(ways, done[len(work) :]):
            moving[way] = swap_rep(value, Z1 if way == "n" else Z2) if way in "nf" else swap(value, X if way == "x" else Y)
        for t, kept in zip(work, done):
            if t["step"] == 5:
                self.results[t["name"]] = (kept, None, 0)
            elif t["step"] == 4 and t["name"] not in FINISHED:
                self.results[t["name"]] = (kept, moving["n"], t["out"]["n"])
            else:
                mine = {w: v for w, v in moving.items() if w in t["out"]}
                self.pairs.append(dict(name=t["name"], rows=t["rows"], step=t["step"] + 1, keep=kept, slot=t["out"], moving=mine))
        return [done[0]]


FINISHED = ("f1u", "f1d")
NAMES = ("a0", "a0v", "a1", "a2", "f0", "f1u", "f1d")


def outputs(plan, sums, place):
    W, r = plan.width, plan.r
    wide = W // plan.shards
    results = sums.results
    if not plan.split:
        me = lax.axis_index("shard")
        scores, small = results["a0"][:, :r], results["a0"][:, r:]
        small = lax.dynamic_slice(small, (0, 0, me * wide), (2, NORMS, wide))
        att = [jnp.concatenate([scores, results["a0v"]]), *(results[k].reshape(4, r, W) for k in ("a1", "a2"))]
        att, ffn = jnp.stack(att), jnp.stack([results["f0"], jnp.stack([results[k].reshape(4 * r, W) for k in ("f1u", "f1d")])])

        def unblocks(v):
            return jnp.moveaxis(v, 1, 2).reshape(v.shape[0], r, -1)

        return unblocks(att[:, :3]), att[:, 3], unblocks(ffn[:, 0].reshape(2, 4, r, W)), ffn[:, 1], small[0], small[1]
    keeps = [results[k][0] for k in NAMES]
    gots = []
    for k in NAMES:
        if k not in FINISHED and not any(results[k][1] is v for v in gots):
            gots.append(results[k][1])

    def body(odd, place, *refs):
        keep, refs = refs[: len(NAMES)], refs[len(NAMES) :]
        got, refs = refs[: len(gots)], refs[len(gots) :]
        attn_in, attn_out, ffn_up, ffn_down, gain, shift = refs
        odds = odd[0] != 0

        def member(name, m, at, rows):
            _, array, offset = results[name]
            i = NAMES.index(name)
            if name in FINISHED:
                at += m * (keep[i].shape[0] // 2)
                return keep[i][at : at + rows, :].astype(WIDE)
            j = [v is array for v in gots].index(True)
            kept, other = keep[i][at : at + rows, :], got[j][offset + at : offset + at + rows, :]
            return (jnp.where(odds, other, kept) if m == 0 else jnp.where(odds, kept, other)).astype(WIDE)

        for i in range(2):
            attn_in[0, :, i * W : (i + 1) * W] = member("a0", i, 0, r)
        attn_in[0, :, 2 * W :] = member("a0v", 0, 0, r)
        attn_out[0] = member("a0v", 1, 0, r)
        for a, name in ((1, "a1"), (2, "a2")):
            for i in range(3):
                attn_in[a, :, i * W : (i + 1) * W] = member(name, i // 2, (i % 2) * r, r)
            attn_out[a] = member(name, 1, r, r)
        for i in range(4):
            ffn_up[0, :, i * W : (i + 1) * W] = member("f0", 0, i * r, r)
            ffn_up[1, :, i * W : (i + 1) * W] = member("f1u", i // 2, (i % 2) * r, r)
        ffn_down[0] = member("f0", 1, 0, 4 * r)
        for m in range(2):
            ffn_down[1, 2 * m * r : 2 * (m + 1) * r] = member("f1d", m, 0, 2 * r)
        turn = lax.rem(W - place[0] * wide, W)
        for m, out in enumerate((gain, shift)):
            out[...] = pltpu.roll(member("a0", m, r, SMALL), turn, axis=1)[:NORMS, :wide]

    outs = [((3, r, 3 * W), WIDE), ((3, r, W), WIDE), ((2, r, 4 * W), WIDE), ((2, 4 * r, W), WIDE)] + [((NORMS, wide), WIDE)] * 2
    return local(body, [(sums.odd, SMEM), (place, SMEM), *keeps, *gots], outs, room=16)


def shards(sizes, source, target, source_seg, target_seg, attn_in, attn_out, ffn_up, ffn_down, norm_gain, norm_bias, cotangent):
    plan = Plan(sizes, source.shape[1], source.shape[2])
    W, r = plan.width, plan.r
    me = lax.axis_index("shard")
    place = (me if plan.split else jnp.zeros_like(me))[None]
    src, tgt = source[0], target[0]

    small = jnp.concatenate([norm_gain, norm_bias])
    small = lax.dynamic_update_slice(jnp.zeros((SMALL, W), LOW), small, (0, me * small.shape[1]))
    odd = (lax.axis_index("rep") & 1).astype(jnp.int32)[None]
    pair = pack_self(plan, attn_in, attn_out, small, odd)
    att = Gather(plan, pair, (4 * r + SMALL,))
    rest = Gather(plan, pack_rest(plan, attn_in, attn_out, ffn_up, ffn_down, [pair]), (6 * r, 4 * r))
    went = att.onward()
    went = rest.onward(wait_for(plan, went, 4))
    self_w, stacked = att.stack(0, went)
    first, first_low, n0, r0, *kept_enc, norms = self_attention(
        plan, place, src, source_seg, self_w, 0, 0, False, wait_for(plan, stacked, 6), 0.05
    )
    rest_w, stacked = rest.stack(0, [r0])
    one, one_low, n2, r2, *kept_self, _ = self_attention(
        plan, place, tgt, target_seg, self_w, 1, 2, True, [r0] + stacked, 10
    )
    last_w, stacked = rest.stack(1, [r2])
    enc_low, n1, r1, active, slope, w_f0 = encoder_ffn(
        plan, place, first, first_low, src, rest_w, norms, 1, [r2] + stacked
    )
    two, two_low, n3, r3, *kept_cross = cross_attention(
        plan, place, one, one_low, enc_low, target_seg, source_seg, rest_w, norms, 3
    )
    (decoded, last_grad, norm_a, slope_f1, w_f1), grads = decoder_ffn(
        plan, place, two, two_low, tgt, cotangent[0], last_w, norms, 4
    )
    sums = Reduction(plan, odd)
    sums.add("f1d", grads)
    (two_grad, norm_d), grads = decoder_ffn_back(
        plan, place, last_grad, two_low, slope_f1, n3, r3, w_f1, norms, 3
    )
    deps = sums.advance([norm_d], ["f1d"])
    sums.add("f1u", grads)
    deps = sums.advance(deps, ["f1u"])
    (one_grad, enc_grad, norm_b), grads = cross_attention_back(
        plan, place, two_grad, one_low, enc_low, kept_cross, (n2, r2), (n1, r1), norms, (2, 1), deps
    )
    sums.add("a2", grads)
    deps = sums.advance([norm_b])
    (zero_grad, norm_c), grads = encoder_ffn_back(
        plan, place, enc_grad, first_low, active, slope, n0, r0, w_f0, norms, 0, deps
    )
    sums.add("f0", grads)
    deps = sums.advance([norm_c])
    tgt_grad, grads = self_attention_back(plan, place, one_grad, tgt, kept_self, last_grad, deps)
    sums.add("a1", grads)
    deps = sums.advance(grads[:1], ["f1u", "f1d"])
    halfway, grads = self_attention_back_values(plan, place, zero_grad, src, kept_enc, deps)
    sums.add("a0v", grads)
    deps = sums.advance([halfway[0]], never=["f1u", "f1d"])
    src_grad, grads = self_attention_back_scores(
        plan, place, zero_grad, src, kept_enc, *halfway, enc_grad, (norm_a, norm_d, norm_b, norm_c), deps
    )
    sums.add("a0", grads)
    deps = sums.advance(grads[:1], ["f1u", "f1d"])
    sums.advance(deps or grads[:1])
    while sums.pairs:
        sums.advance()
    return decoded[None], src_grad[None], tgt_grad[None], *outputs(plan, sums, place)


def solution(mesh):
    sizes = (mesh.shape["shard"], mesh.shape["rep"])
    tokens = P(("shard", "rep"), None, None)
    ids = P(("shard", "rep"), None)
    weight = P(None, "shard", None)
    norm = P(None, "shard")
    return jax.shard_map(
        functools.partial(shards, sizes),
        mesh=mesh,
        in_specs=(tokens, tokens, ids, ids, weight, weight, weight, weight, norm, norm, tokens),
        out_specs=(tokens, tokens, tokens, weight, weight, weight, weight, norm, norm),
        check_vma=False,
    )
```

```python
import functools

import jax
import jax.numpy as jnp
from jax import lax
from jax.experimental import pallas as pl
from jax.experimental.pallas import tpu as pltpu
from jax.sharding import PartitionSpec as P

HEAD = 64
PAIR = 2 * HEAD
EPS = 1e-05
NEG = -1e30
LOW = jnp.bfloat16
WIDE = jnp.float32
CORE, X, Y = 1, 2, 4
Z1, Z2 = 1, 2
SMALL = 16
NORMS = 5
VMEM = pl.BlockSpec(memory_space=pltpu.VMEM)
SMEM = pl.BlockSpec(memory_space=pltpu.SMEM)
ANY = pl.BlockSpec(memory_space=pl.ANY)


def dot(left, right):
    return lax.dot_general(left, right, (((1,), (0,)), ((), ())), preferred_element_type=WIDE)


def dot_nt(left, right):
    return lax.dot_general(left, right, (((1,), (1,)), ((), ())), preferred_element_type=WIDE)


def dot_tn(left, right):
    return lax.dot_general(left, right, (((0,), (0,)), ((), ())), preferred_element_type=WIDE)


def block(unit, i, r):
    part = unit[:, i * r : (i + 1) * r, :]
    return part.reshape(part.shape[0] * r, part.shape[2])


def rows_block(unit, i, r):
    n = unit.shape[0] // 4
    part = unit[i * n : (i + 1) * n, 4 * r :, :]
    return part.reshape(n * part.shape[1], part.shape[2])


def norm(value, gain, shift):
    mean = jnp.mean(value, axis=-1, keepdims=True)
    centred = value - mean
    scale = lax.rsqrt(jnp.mean(centred * centred, axis=-1, keepdims=True) + EPS)
    normal = centred * scale
    return normal * gain + shift, normal, scale


def norm_back(grad, normal, scale, gain):
    gain_grad = jnp.sum(grad * normal, axis=0, keepdims=True)
    shift_grad = jnp.sum(grad, axis=0, keepdims=True)
    inner = grad * gain
    inner_mean = jnp.mean(inner, axis=-1, keepdims=True)
    cross_mean = jnp.mean(inner * normal, axis=-1, keepdims=True)
    return scale * (inner - inner_mean - normal * cross_mean), gain_grad, shift_grad


def lanes_of(head, value):
    lane = lax.broadcasted_iota(jnp.int32, value.shape, 1)
    return jnp.where((lane < HEAD) if head == 0 else (lane >= HEAD), value, jnp.zeros_like(value))


def pick(first, second):
    lane = lax.broadcasted_iota(jnp.int32, first.shape, 1)
    return jnp.where(lane < HEAD, first, second)


def allowed_bias(memory_ids, query_ids, causal):
    tokens = memory_ids.shape[1]
    turned = jnp.transpose(jnp.broadcast_to(memory_ids.astype(WIDE), (PAIR, tokens)))[:, :1]
    allowed = turned == query_ids.astype(WIDE)
    if causal:
        shape = (tokens, query_ids.shape[1])
        allowed = allowed & (lax.broadcasted_iota(jnp.int32, shape, 1) >= lax.broadcasted_iota(jnp.int32, shape, 0))
    return jnp.where(allowed, 0.0, NEG)


def attend_forward(qkv, probs, mixed, bias):
    width = mixed.shape[1]
    for pair in range(width // PAIR):
        at = pl.ds(pair * PAIR, PAIR)
        query = qkv[:, pl.ds(pair * PAIR, PAIR)] * LOW(HEAD ** -0.5)
        keys = qkv[:, pl.ds(width + pair * PAIR, PAIR)]
        turned = jnp.transpose(qkv[:, pl.ds(2 * width + pair * PAIR, PAIR)])
        out = []
        for head in range(2):
            scores = dot_nt(keys, lanes_of(head, query)) + bias[...]
            top = jnp.max(scores, axis=0, keepdims=True)
            weights = jnp.exp(scores - top)
            total = jnp.sum(weights, axis=0, keepdims=True)
            low = (weights * (1.0 / total)).astype(LOW)
            probs[2 * pair + head] = low
            out.append(dot(turned[head * HEAD : (head + 1) * HEAD, :], low))
        mixed[:, at] = jnp.transpose(jnp.concatenate(out).astype(LOW))


def attend_backward(qkv, probs, mixed_grad, qkv_grad):
    width = mixed_grad.shape[1]
    for pair in range(width // PAIR):
        query = qkv[:, pl.ds(pair * PAIR, PAIR)]
        keys = qkv[:, pl.ds(width + pair * PAIR, PAIR)]
        values = qkv[:, pl.ds(2 * width + pair * PAIR, PAIR)]
        grad = mixed_grad[:, pl.ds(pair * PAIR, PAIR)]
        turned = jnp.transpose(keys)
        dq, dk, dv = [], [], []
        for head in range(2):
            low = probs[2 * pair + head]
            prob = low.astype(WIDE)
            prob_grad = dot_nt(values, lanes_of(head, grad))
            delta = jnp.sum(prob * prob_grad, axis=0, keepdims=True)
            score_grad = (prob * (prob_grad - delta)).astype(LOW)
            dv.append(dot(low, grad))
            dk.append(dot(score_grad, query))
            dq.append(dot(turned[head * HEAD : (head + 1) * HEAD, :], score_grad))
        scale = HEAD ** -0.5
        qkv_grad[:, pl.ds(pair * PAIR, PAIR)] = jnp.transpose((jnp.concatenate(dq) * scale).astype(LOW))
        qkv_grad[:, pl.ds(width + pair * PAIR, PAIR)] = (pick(*dk) * scale).astype(LOW)
        qkv_grad[:, pl.ds(2 * width + pair * PAIR, PAIR)] = pick(*dv).astype(LOW)


GELU = 0.7978845608028654


def gelu_and_slope(value):
    square = value * value
    t = jnp.tanh(value * (GELU + (GELU * 0.044715) * square))
    half = 0.5 + 0.5 * t
    slope = half + value * (0.5 - 0.5 * (t * t)) * (GELU + (3 * 0.044715 * GELU) * square)
    return value * half, slope


def ffn_forward(hidden, weight, active, slope, r):
    W = hidden.shape[1]
    total = None
    for c in range(4):
        at = pl.ds(c * W, W)
        act, sl = gelu_and_slope(dot(hidden, block(weight, c, r)))
        act = act.astype(LOW)
        active[:, at] = act
        slope[:, at] = sl.astype(LOW)
        part = dot(act, rows_block(weight, c, r))
        total = part if total is None else total + part
    return total


def ffn_backward_down(grad, active, put):
    W = grad.shape[1]
    for c in range(4):
        put(c, dot_tn(active[:, pl.ds(c * W, W)], grad).astype(LOW))


def ffn_backward_up(grad, hidden, weight, slope, r, put):
    W = grad.shape[1]
    turned = jnp.transpose(hidden)
    total = None
    for c in range(4):
        z = (dot_nt(grad, rows_block(weight, c, r)) * slope[:, pl.ds(c * W, W)].astype(WIDE)).astype(LOW)
        put(c, dot(turned, z).astype(LOW))
        part = dot_nt(z, block(weight, c, r))
        total = part if total is None else total + part
    return total


class Plan:
    def __init__(self, sizes, length, width):
        self.split = sizes == (8, 4)
        self.sizes = sizes
        self.length, self.width = length, width
        self.heads = width // HEAD
        self.shards = sizes[0]
        self.r = width // self.shards
        self.n = self.g = 2 if self.split else 1


    def lay(self, place, stacks, member, rows, unit, at):
        count = rows.stop - rows.start
        if not self.split:
            unit[:, at : at + count, :] = stacks[0][:, member, rows]
            return
        odd, chip = (place & 1) != 0, place >> 1
        for j in range(4):
            k = 2 * (j ^ chip) + member
            mine, other = stacks[0][k, rows, :], stacks[1][k, rows, :]
            unit[2 * j, at : at + count, :] = jnp.where(odd, other, mine)
            unit[2 * j + 1, at : at + count, :] = jnp.where(odd, mine, other)


    def grad_shapes(self, rows):
        if not self.split:
            return [(self.shards, 2, rows, self.width)]
        return [(8, rows, self.width)] * 2

    def leave(self, place, outs, member, at, value, first=0):
        count = value.shape[1]
        if not self.split:
            outs[0][first : first + value.shape[0], member, at : at + count, :] = value
            return
        odd, chip = (place & 1) != 0, place >> 1
        for j in range(value.shape[0] // 2):
            k = (first // 2 + j) ^ chip
            if member == 0:
                k = ((k & 1) << 1) | (k >> 1)
            one, two = value[2 * j], value[2 * j + 1]
            outs[0][4 * member + k, at : at + count, :] = jnp.where(odd, two, one)
            outs[1][4 * member + k, at : at + count, :] = jnp.where(odd, one, two)

    def leave_block(self, place, outs, member, i, value):
        self.leave(place, outs, member, i * self.r, value.reshape(self.shards, self.r, self.width))

    def leave_rows(self, place, outs, member, i, value):
        n = self.shards // 4
        self.leave(place, outs, member, 0, value.reshape(n, 4 * self.r, self.width), i * n)

    def leave_rows_halved(self, place, outs, i, value):
        n, half = self.shards // 4, 2 * self.r
        value = value.reshape(n, 4 * self.r, self.width)
        for m in range(2):
            self.leave(place, outs, m, 0, value[:, m * half : (m + 1) * half, :], i * n)

    def call(self, body, ins, outs, scratch, us, deps, room):
        def run(*refs):
            body(*refs[len(deps) :])

        return pl.pallas_call(
            run,
            in_specs=[ANY] * len(deps) + [spec for _, spec in ins],
            out_shape=[jax.ShapeDtypeStruct(shape, dtype) for shape, dtype in outs],
            out_specs=[VMEM] * len(outs),
            scratch_shapes=scratch,
            compiler_params=pltpu.CompilerParams(vmem_limit_bytes=room << 20),
            cost_estimate=pl.CostEstimate(flops=int(us * 5e9), bytes_accessed=1 << 20, transcendentals=0),
        )(*deps, *[value for value, _ in ins])


def vmem(*arrays):
    return [(v, VMEM) for v in arrays]


def self_attention(plan, place, tokens, ids, stacks, member, row, causal, deps=(), us=10):
    L, W, H, r = plan.length, plan.width, plan.heads, plan.r

    def body(place, tokens, ids, *rest):
        stacks, rest = rest[: plan.n], rest[plan.n :]
        out, out_low, normal, scale, qkv, mixed, probs, weight, norms, bias = rest
        plan.lay(place[0], stacks, member, slice(0, 4 * r), weight, 0)
        bias[...] = allowed_bias(ids[...], ids[...], causal)
        if plan.split:
            norms[...] = sum(jnp.sum(s[...].astype(WIDE), axis=0) for s in (v.at[:, 4 * r : 4 * r + SMALL, :] for v in stacks)) * 0.5
        else:
            norms[...] = jnp.sum(stacks[0][:, member, 4 * r : 4 * r + SMALL].astype(WIDE), axis=0)
        x = tokens[...]
        for i in range(3):
            qkv[:, i * W : (i + 1) * W] = dot(x, block(weight, i, r)).astype(LOW)
        attend_forward(qkv, probs, mixed, bias)
        value = x.astype(WIDE) + dot(mixed[...], block(weight, 3, r))
        y, n, s = norm(value, norms[row : row + 1, :], norms[NORMS + row : NORMS + row + 1, :])
        out[...] = y
        out_low[...] = y.astype(LOW)
        normal[...] = n.astype(LOW)
        scale[...] = s

    ins = [(place, SMEM)] + vmem(tokens, ids, *stacks)
    outs = [((L, W), WIDE), ((L, W), LOW), ((L, W), LOW), ((L, 1), WIDE)]
    outs += [((L, 3 * W), LOW), ((L, W), LOW), ((H, L, L), LOW), ((plan.shards, 4 * r, W), LOW), ((SMALL, W), WIDE)]
    return plan.call(body, ins, outs, [pltpu.VMEM((L, L), WIDE)], us, deps, 11)


def cross_attention(plan, place, query_in, query_low, memory_low, query_ids, memory_ids, stacks, norms, row, deps=()):
    L, W, H, r = plan.length, plan.width, plan.heads, plan.r

    def body(place, query_in, query_low, memory_low, query_ids, memory_ids, norms, *rest):
        stacks, rest = rest[: plan.n], rest[plan.n :]
        out, out_low, normal, scale, qkv, mixed, probs, weight, bias = rest
        at = 4 * r
        for m in range(2):
            plan.lay(place[0], stacks, m, slice(at, at + 2 * r), weight, 2 * m * r)
        bias[...] = allowed_bias(memory_ids[...], query_ids[...], False)
        qkv[:, :W] = dot(query_low[...], block(weight, 0, r)).astype(LOW)
        memory = memory_low[...]
        for i in (1, 2):
            qkv[:, i * W : (i + 1) * W] = dot(memory, block(weight, i, r)).astype(LOW)
        attend_forward(qkv, probs, mixed, bias)
        value = query_in[...] + dot(mixed[...], block(weight, 3, r))
        y, n, s = norm(value, norms[row : row + 1, :], norms[NORMS + row : NORMS + row + 1, :])
        out[...] = y
        out_low[...] = y.astype(LOW)
        normal[...] = n.astype(LOW)
        scale[...] = s

    ins = [(place, SMEM)] + vmem(query_in, query_low, memory_low, query_ids, memory_ids, norms, *stacks)
    outs = [((L, W), WIDE), ((L, W), LOW), ((L, W), LOW), ((L, 1), WIDE)]
    outs += [((L, 3 * W), LOW), ((L, W), LOW), ((H, L, L), LOW), ((plan.shards, 4 * r, W), LOW)]
    return plan.call(body, ins, outs, [pltpu.VMEM((L, L), WIDE)], 10, deps, 11)


def encoder_ffn(plan, place, hidden, hidden_low, tokens, stacks, norms, row, deps=()):
    L, W, F, r = plan.length, plan.width, 4 * plan.width, plan.r

    def body(place, hidden, hidden_low, tokens, norms, *rest):
        stacks, rest = rest[: plan.n], rest[plan.n :]
        out_low, normal, scale, active, slope, weight = rest
        for m in range(2):
            plan.lay(place[0], stacks, m, slice(0, 4 * r), weight, 4 * m * r)
        branch = ffn_forward(hidden_low[...], weight, active, slope, r)
        value = hidden[...] + branch + tokens[...].astype(WIDE)
        y, n, s = norm(value, norms[row : row + 1, :], norms[NORMS + row : NORMS + row + 1, :])
        out_low[...] = y.astype(LOW)
        normal[...] = n.astype(LOW)
        scale[...] = s

    ins = [(place, SMEM)] + vmem(hidden, hidden_low, tokens, norms, *stacks)
    outs = [((L, W), LOW), ((L, W), LOW), ((L, 1), WIDE), ((L, F), LOW), ((L, F), LOW), ((plan.shards, 8 * r, W), LOW)]
    return plan.call(body, ins, outs, [], 9, deps, 11)


def decoder_ffn(plan, place, hidden, hidden_low, tokens, cotangent, stacks, norms, row, deps=()):
    L, W, F, r = plan.length, plan.width, 4 * plan.width, plan.r

    def body(place, hidden, hidden_low, tokens, cotangent, norms, *rest):
        stacks, rest = rest[: plan.n], rest[plan.n :]
        decoded, last_grad, norm_grads, slope, weight, *grads, active = rest
        for m in range(2):
            plan.lay(place[0], stacks, m, slice(0, 4 * r), weight, 4 * m * r)
        branch = ffn_forward(hidden_low[...], weight, active, slope, r)
        value = hidden[...] + branch + tokens[...].astype(WIDE)
        gain = norms[row : row + 1, :]
        y, n, s = norm(value, gain, norms[NORMS + row : NORMS + row + 1, :])
        decoded[...] = y.astype(LOW)
        grad, gain_grad, shift_grad = norm_back(cotangent[...].astype(WIDE), n, s, gain)
        last_grad[...] = grad
        norm_grads[0:1, :] = gain_grad
        norm_grads[1:2, :] = shift_grad
        ffn_backward_down(grad.astype(LOW), active, lambda i, v: plan.leave_rows_halved(place[0], grads, i, v))

    ins = [(place, SMEM)] + vmem(hidden, hidden_low, tokens, cotangent, norms, *stacks)
    outs = [((L, W), LOW), ((L, W), WIDE), ((2, W), WIDE), ((L, F), LOW), ((plan.shards, 8 * r, W), LOW)]
    outs += [(s, LOW) for s in plan.grad_shapes(2 * r)]
    got = plan.call(body, ins, outs, [pltpu.VMEM((L, F), LOW)], 12, deps, 16)
    return got[:5], got[5:]


def decoder_ffn_back(plan, place, grad, hidden_low, slope, hidden_normal, hidden_scale, weight, norms, row, deps=()):
    L, W, r = plan.length, plan.width, plan.r

    def body(place, grad, hidden_low, slope, hidden_normal, hidden_scale, weight, norms, out, norm_grads, *grads):
        def put(i, value):
            plan.leave(place[0], grads, i // 2, (i % 2) * r, value.reshape(plan.shards, r, W))

        back = ffn_backward_up(grad[...].astype(LOW), hidden_low[...], weight, slope, r, put)
        normal = hidden_normal[...].astype(WIDE)
        total, gain_grad, shift_grad = norm_back(grad[...] + back, normal, hidden_scale[...], norms[row : row + 1, :])
        out[...] = total
        norm_grads[0:1, :] = gain_grad
        norm_grads[1:2, :] = shift_grad

    ins = [(place, SMEM)] + vmem(grad, hidden_low, slope, hidden_normal, hidden_scale, weight, norms)
    outs = [((L, W), WIDE), ((2, W), WIDE)] + [(s, LOW) for s in plan.grad_shapes(2 * r)]
    got = plan.call(body, ins, outs, [], 8, deps, 12)
    return got[:2], got[2:]


def encoder_ffn_back(plan, place, grad, hidden_low, active, slope, hidden_normal, hidden_scale, weight, norms, row, deps=()):
    L, W, r = plan.length, plan.width, plan.r

    def body(place, grad, hidden_low, active, slope, hidden_normal, hidden_scale, weight, norms, *rest):
        zero_grad, norm_grads, *grads = rest
        grad_low = grad[...].astype(LOW)
        ffn_backward_down(grad_low, active, lambda i, v: plan.leave_rows(place[0], grads, 1, i, v))
        back = ffn_backward_up(
            grad_low, hidden_low[...], weight, slope, r, lambda i, v: plan.leave_block(place[0], grads, 0, i, v)
        )
        normal = hidden_normal[...].astype(WIDE)
        out, gain_grad, shift_grad = norm_back(grad[...] + back, normal, hidden_scale[...], norms[row : row + 1, :])
        zero_grad[...] = out
        norm_grads[0:1, :] = gain_grad
        norm_grads[1:2, :] = shift_grad

    ins = [(place, SMEM)] + vmem(grad, hidden_low, active, slope, hidden_normal, hidden_scale, weight, norms)
    outs = [((L, W), WIDE), ((2, W), WIDE)] + [(s, LOW) for s in plan.grad_shapes(4 * r)]
    got = plan.call(body, ins, outs, [], 11, deps, 14)
    return got[:2], got[2:]


def self_attention_back(plan, place, grad, tokens, kept, extra, deps=()):
    L, W, r = plan.length, plan.width, plan.r

    def body(place, grad, extra, tokens, qkv, mixed, probs, weight, *rest):
        total, *grads, mixed_grad, qkv_grad = rest
        grad_low = grad[...].astype(LOW)
        plan.leave_block(place[0], grads, 1, 1, dot_tn(mixed[...], grad_low).astype(LOW))
        mixed_grad[...] = dot_nt(grad_low, block(weight, 3, r)).astype(LOW)
        attend_backward(qkv, probs, mixed_grad, qkv_grad)
        x = jnp.transpose(tokens[...])
        for i in range(3):
            plan.leave_block(place[0], grads, i // 2, i % 2, dot(x, qkv_grad[:, i * W : (i + 1) * W]).astype(LOW))
        back = grad[...] + extra[...]
        for i in range(3):
            back += dot_nt(qkv_grad[:, i * W : (i + 1) * W], block(weight, i, r))
        total[...] = back

    ins = [(place, SMEM)] + vmem(grad, extra, tokens, *kept)
    outs = [((L, W), WIDE)] + [(s, LOW) for s in plan.grad_shapes(2 * r)]
    scratch = [pltpu.VMEM((L, W), LOW), pltpu.VMEM((L, 3 * W), LOW)]
    got = plan.call(body, ins, outs, scratch, 12, deps, 12)
    return got[0], got[1:]


def attend_backward_values(probs, mixed_grad, value_grad):
    for pair in range(mixed_grad.shape[1] // PAIR):
        at = pl.ds(pair * PAIR, PAIR)
        grad = mixed_grad[:, at]
        value_grad[:, at] = pick(*[dot(probs[2 * pair + head], grad) for head in range(2)]).astype(LOW)


def self_attention_back_values(plan, place, grad, tokens, kept, deps=()):
    L, W, r = plan.length, plan.width, plan.r
    _, mixed, probs, weight = kept

    def body(place, grad, tokens, mixed, probs, weight, mixed_grad, value_grad, *grads):
        grad_low = grad[...].astype(LOW)
        plan.leave_block(place[0], grads, 1, 0, dot_tn(mixed[...], grad_low).astype(LOW))
        mixed_grad[...] = dot_nt(grad_low, block(weight, 3, r)).astype(LOW)
        attend_backward_values(probs, mixed_grad, value_grad)
        plan.leave_block(place[0], grads, 0, 0, dot_tn(tokens[...], value_grad[...]).astype(LOW))

    ins = [(place, SMEM)] + vmem(grad, tokens, mixed, probs, weight)
    outs = [((L, W), LOW), ((L, W), LOW)] + [(s, LOW) for s in plan.grad_shapes(r)]
    got = plan.call(body, ins, outs, [], 6, deps, 12)
    return got[:2], got[2:]


def self_attention_back_scores(plan, place, grad, tokens, kept, mixed_grad, value_grad, extra, small, deps=()):
    L, W, r = plan.length, plan.width, plan.r
    qkv, _, probs, weight = kept

    def body(place, grad, extra, tokens, qkv, probs, weight, mixed_grad, value_grad, *rest):
        parts, (total, *grads, score_grads) = rest[:4], rest[4:]
        for m in range(2):
            rows = [parts[j][i + m : i + m + 1, :] for j, i in ((3, 0), (2, 2), (2, 0), (1, 0), (0, 0))]
            rows = jnp.concatenate(rows + [jnp.zeros((SMALL - NORMS, W), WIDE)]).astype(LOW)[None]
            plan.leave(place[0], grads, m, r, jnp.broadcast_to(rows, (plan.shards, SMALL, W)))
        scale = HEAD ** -0.5
        for pair in range(W // PAIR):
            at = pl.ds(pair * PAIR, PAIR)
            query, keys = qkv[:, at], qkv[:, pl.ds(W + pair * PAIR, PAIR)]
            values, out_grad = qkv[:, pl.ds(2 * W + pair * PAIR, PAIR)], mixed_grad[:, at]
            turned = jnp.transpose(keys)
            dq, dk = [], []
            for head in range(2):
                prob = probs[2 * pair + head].astype(WIDE)
                prob_grad = dot_nt(values, lanes_of(head, out_grad))
                delta = jnp.sum(prob * prob_grad, axis=0, keepdims=True)
                score_grad = (prob * (prob_grad - delta)).astype(LOW)
                dk.append(dot(score_grad, query))
                dq.append(dot(turned[head * HEAD : (head + 1) * HEAD, :], score_grad))
            score_grads[:, at] = jnp.transpose((jnp.concatenate(dq) * scale).astype(LOW))
            score_grads[:, pl.ds(W + pair * PAIR, PAIR)] = (pick(*dk) * scale).astype(LOW)
        x = jnp.transpose(tokens[...])
        back = grad[...] + extra[...] + dot_nt(value_grad[...], block(weight, 2, r))
        for i in range(2):
            part = score_grads[:, i * W : (i + 1) * W]
            plan.leave_block(place[0], grads, i, 0, dot(x, part).astype(LOW))
            back += dot_nt(part, block(weight, i, r))
        total[...] = back

    ins = [(place, SMEM)] + vmem(grad, extra, tokens, qkv, probs, weight, mixed_grad, value_grad, *small)
    outs = [((L, W), WIDE)] + [(s, LOW) for s in plan.grad_shapes(r + SMALL)]
    got = plan.call(body, ins, outs, [pltpu.VMEM((L, 2 * W), LOW)], 10, deps, 12)
    return got[0], got[1:]


def cross_attention_back(plan, place, grad, query_low, memory_low, kept, query_norm, memory_norm, norms, rows, deps=()):
    L, W, r = plan.length, plan.width, plan.r

    def body(place, grad, query_low, memory_low, qkv, mixed, probs, weight, query_n, query_r, memory_n, memory_r, norms, *rest):
        one_grad, enc_grad, norm_grads, *grads, mixed_grad, qkv_grad = rest
        grad_low = grad[...].astype(LOW)
        plan.leave_block(place[0], grads, 1, 1, dot_tn(mixed[...], grad_low).astype(LOW))
        mixed_grad[...] = dot_nt(grad_low, block(weight, 3, r)).astype(LOW)
        attend_backward(qkv, probs, mixed_grad, qkv_grad)
        plan.leave_block(place[0], grads, 0, 0, dot_tn(query_low[...], qkv_grad[:, :W]).astype(LOW))
        memory = jnp.transpose(memory_low[...])
        for i in (1, 2):
            value = dot(memory, qkv_grad[:, i * W : (i + 1) * W]).astype(LOW)
            plan.leave_block(place[0], grads, i // 2, i % 2, value)
        back = grad[...] + dot_nt(qkv_grad[:, :W], block(weight, 0, r))
        normal = query_n[...].astype(WIDE)
        out, gain_grad, shift_grad = norm_back(back, normal, query_r[...], norms[rows[0] : rows[0] + 1, :])
        one_grad[...] = out
        norm_grads[0:1, :] = gain_grad
        norm_grads[1:2, :] = shift_grad
        back = dot_nt(qkv_grad[:, W : 2 * W], block(weight, 1, r)) + dot_nt(qkv_grad[:, 2 * W :], block(weight, 2, r))
        normal = memory_n[...].astype(WIDE)
        out, gain_grad, shift_grad = norm_back(back, normal, memory_r[...], norms[rows[1] : rows[1] + 1, :])
        enc_grad[...] = out
        norm_grads[2:3, :] = gain_grad
        norm_grads[3:4, :] = shift_grad

    ins = [(place, SMEM)] + vmem(grad, query_low, memory_low, *kept, *query_norm, *memory_norm, norms)
    outs = [((L, W), WIDE), ((L, W), WIDE), ((4, W), WIDE)] + [(s, LOW) for s in plan.grad_shapes(2 * r)]
    scratch = [pltpu.VMEM((L, W), LOW), pltpu.VMEM((L, 3 * W), LOW)]
    got = plan.call(body, ins, outs, scratch, 0.05, deps, 13)
    return got[:3], got[3:]


def swap(value, bit):
    return lax.ppermute(value, "shard", [(i, i ^ bit) for i in range(8)])


def swap_rep(value, bit):
    return lax.ppermute(value, "rep", [(i, i ^ bit) for i in range(4)])


def local(body, ins, outs, deps=(), room=6, us=0):
    ins = [v if isinstance(v, tuple) else (v, VMEM) for v in ins]

    def run(*refs):
        body(*refs[len(deps) :])

    return pl.pallas_call(
        run,
        in_specs=[ANY] * len(deps) + [spec for _, spec in ins],
        out_shape=[jax.ShapeDtypeStruct(shape, dtype) for shape, dtype in outs],
        out_specs=[VMEM] * len(outs),
        compiler_params=pltpu.CompilerParams(vmem_limit_bytes=room << 20),
        cost_estimate=pl.CostEstimate(flops=int(us * 5e9), bytes_accessed=1 << 20, transcendentals=0),
    )(*deps, *[v for v, _ in ins])


def mark(out):
    out[...] = jnp.zeros_like(out)


def wait_for(plan, deps, us):
    return local(mark, [], [((8, 128), WIDE)], deps, 2, us) if plan.split else []


def pack_self(plan, attn_in, attn_out, small, odd):
    W, r = plan.width, plan.r

    def body(attn_in, attn_out, small, odd, out):
        for k in range(2):
            for i in range(3):
                out[k, i * r : (i + 1) * r, :] = attn_in[k, :, i * W : (i + 1) * W]
            out[k, 3 * r : 4 * r, :] = attn_out[k]
            out[k, 4 * r :, :] = small[...]

    return local(body, [attn_in, attn_out, small, (odd, SMEM)], [((2, 4 * r + SMALL, W), LOW)])[0]


def pack_rest(plan, attn_in, attn_out, ffn_up, ffn_down, deps):
    W, r = plan.width, plan.r

    def body(attn_in, attn_out, ffn_up, ffn_down, first, second):
        for k, out in enumerate((first, second)):
            for i in range(4):
                out[0, i * r : (i + 1) * r, :] = ffn_up[k, :, i * W : (i + 1) * W]
            out[1, : 4 * r] = ffn_down[k]
        for i in range(3):
            at = (4 + i % 2) * r
            first[i // 2, at : at + r, :] = attn_in[2, :, i * W : (i + 1) * W]
        first[1, 5 * r :, :] = attn_out[2]

    outs = [((2, 6 * r, W), LOW), ((2, 4 * r, W), LOW)]
    return local(body, [attn_in, attn_out, ffn_up, ffn_down], outs, deps)


class Gather:
    def __init__(self, plan, pair, parts):
        self.plan, self.pair, self.parts = plan, pair, parts
        self.ends = [sum(parts[: i + 1]) for i in range(len(parts))]
        if plan.split:
            self.near = [swap(pair, X), swap(pair, Y)]

    def onward(self, deps=()):
        if not self.plan.split:
            return []
        parts, ends = self.parts, self.ends

        def body(by_x, by_y, *outs):
            for i, (rows, end) in enumerate(zip(parts, ends)):
                outs[2 * i][...] = by_x[0, end - rows : end, :]
                outs[2 * i + 1][...] = by_y[1, end - rows : end, :]

        outs = local(body, self.near, [((rows, self.plan.width), LOW) for rows in parts for _ in range(2)], deps)
        self.far = [(swap(outs[2 * i], Y), swap(outs[2 * i + 1], X)) for i in range(len(parts))]
        return [outs[0]]

    def stack(self, part, deps=()):
        rows, end = self.parts[part], self.ends[part]
        at = slice(end - rows, end)
        if not self.plan.split:
            return [lax.all_gather(self.pair[:, at], "shard", axis=0)], []

        def body(pair, by_x, by_y, first, second, out):
            for j, v in enumerate((pair, by_x, by_y)):
                out[2 * j : 2 * j + 2] = v[:, at, :]
            out[6] = first[...]
            out[7] = second[...]

        ins = [self.pair, *self.near, *self.far[part]]
        mine = local(body, ins, [((8, rows, self.plan.width), LOW)], deps)[0]
        return [mine, swap(mine, CORE)], [mine]


class Reduction:
    def __init__(self, plan, odd):
        self.plan, self.odd = plan, odd
        self.pairs, self.results = [], {}

    def add(self, name, outs):
        if not self.plan.split:
            whole = outs[0]
            flat = whole.reshape((-1,) + whole.shape[2:])
            own = lax.psum_scatter(flat, "shard", scatter_dimension=0, tiled=True)
            self.results[name] = lax.psum(own, "rep").astype(WIDE).reshape(whole.shape[1:])
            return
        mine, other = outs
        self.pairs.append(dict(name=name, rows=mine.shape[1], step=0, keep=mine, slot={}, moving={}, got=swap(other, CORE)))

    def advance(self, deps=(), only=(), never=()):
        pairs = [p for p in self.pairs if (not only or p["name"] in only) and p["name"] not in never]
        if not pairs:
            return []
        self.pairs = [p for p in self.pairs if p not in pairs]
        W = self.plan.width
        sizes = {"x": 0, "y": 0, "n": 0, "f": 0}

        def place(way, count):
            at = sizes[way]
            sizes[way] += count
            return at

        work = []
        for p in pairs:
            R, step = p["rows"], p["step"]
            ways = ({"x": 2 * R, "y": 2 * R}, {"x": R, "y": R}, {"n": R}, {"f": R}, {"n": R}, {})[step]
            work.append(dict(p, out={way: place(way, count) for way, count in ways.items()}, kept=((4, 2, 1, 1, 1, 2)[step] * R, W)))
        ways = [w for w in "xynf" if sizes[w]]
        came = []
        for p in pairs:
            came += [v for v in p["moving"].values() if not any(v is u for u in came)]
        cores = [t for t in work if t["step"] == 0]

        def body(odd, *refs):
            keep_in, refs = refs[: len(work)], refs[len(work) :]
            core_in, refs = refs[: len(cores)], refs[len(cores) :]
            arrived, refs = refs[: len(came)], refs[len(came) :]
            keep_out, refs = refs[: len(work)], refs[len(work) :]
            leave = dict(zip(ways, refs))
            odds = odd[0] != 0

            def total(left, right):
                return (left.astype(WIDE) + right.astype(WIDE)).astype(LOW)

            core = iter(core_in)
            for t, keep, out in zip(work, keep_in, keep_out):
                R, step, slot, to = t["rows"], t["step"], t["slot"], t["out"]
                got = {w: arrived[[v is u for u in came].index(True)] for w, v in t["moving"].items() if w in slot}
                if step == 0:
                    other = next(core)
                    for m, way in enumerate("xy"):
                        at = 4 * m * R
                        out[2 * m * R : 2 * (m + 1) * R, :] = total(keep[at : at + 2 * R, :], other[at : at + 2 * R, :])
                        at += 2 * R
                        leave[way][to[way] : to[way] + 2 * R, :] = total(keep[at : at + 2 * R, :], other[at : at + 2 * R, :])
                elif step == 1:
                    for m, (way, onward) in enumerate(("xy", "yx")):
                        other, at, kept = got[way], slot[way], 2 * m * R
                        out[m * R : (m + 1) * R, :] = total(keep[kept : kept + R, :], other[at : at + R, :])
                        kept, at = kept + R, at + R
                        leave[onward][to[onward] : to[onward] + R, :] = total(keep[kept : kept + R, :], other[at : at + R, :])
                elif step == 2:
                    first = total(keep[:R, :], got["y"][slot["y"] : slot["y"] + R, :])
                    second = total(keep[R:, :], got["x"][slot["x"] : slot["x"] + R, :])
                    out[...] = jnp.where(odds, second, first)
                    leave["n"][to["n"] : to["n"] + R, :] = jnp.where(odds, first, second)
                elif step == 5:
                    mine, other = keep[...], got["n"][slot["n"] : slot["n"] + R, :]
                    out[:R, :] = jnp.where(odds, other, mine)
                    out[R:, :] = jnp.where(odds, mine, other)
                else:
                    way, onward = ("n", "f") if step == 3 else ("f", "n")
                    value = total(keep[...], got[way][slot[way] : slot[way] + R, :])
                    out[...] = value
                    leave[onward][to[onward] : to[onward] + R, :] = value

        if cores and came:
            last = [v for p in pairs if p["step"] == 5 for v in p["moving"].values()]
            if last:
                deps = wait_for(self.plan, [*deps, *[v for v in came if not any(v is u for u in last)]], 2)
            deps = wait_for(self.plan, [*deps, *came], 20)
        keeps = [t["keep"].reshape(-1, W) for t in work]
        gots = [t["got"].reshape(-1, W) for t in cores]
        outs = [(t["kept"], LOW) for t in work] + [((sizes[w], W), LOW) for w in ways]
        done = local(body, [(self.odd, SMEM), *keeps, *gots, *came], outs, deps)
        moving = {}
        for way, value in zip(ways, done[len(work) :]):
            moving[way] = swap_rep(value, Z1 if way == "n" else Z2) if way in "nf" else swap(value, X if way == "x" else Y)
        for t, kept in zip(work, done):
            if t["step"] == 5:
                self.results[t["name"]] = (kept, None, 0)
            elif t["step"] == 4 and t["name"] not in FINISHED:
                self.results[t["name"]] = (kept, moving["n"], t["out"]["n"])
            else:
                mine = {w: v for w, v in moving.items() if w in t["out"]}
                self.pairs.append(dict(name=t["name"], rows=t["rows"], step=t["step"] + 1, keep=kept, slot=t["out"], moving=mine))
        return [done[0]]


FINISHED = ("f1u", "f1d")
NAMES = ("a0", "a0v", "a1", "a2", "f0", "f1u", "f1d")


def outputs(plan, sums, place):
    W, r = plan.width, plan.r
    wide = W // plan.shards
    results = sums.results
    if not plan.split:
        me = lax.axis_index("shard")
        scores, small = results["a0"][:, :r], results["a0"][:, r:]
        small = lax.dynamic_slice(small, (0, 0, me * wide), (2, NORMS, wide))
        att = [jnp.concatenate([scores, results["a0v"]]), *(results[k].reshape(4, r, W) for k in ("a1", "a2"))]
        att, ffn = jnp.stack(att), jnp.stack([results["f0"], jnp.stack([results[k].reshape(4 * r, W) for k in ("f1u", "f1d")])])

        def unblocks(v):
            return jnp.moveaxis(v, 1, 2).reshape(v.shape[0], r, -1)

        return unblocks(att[:, :3]), att[:, 3], unblocks(ffn[:, 0].reshape(2, 4, r, W)), ffn[:, 1], small[0], small[1]
    keeps = [results[k][0] for k in NAMES]
    gots = []
    for k in NAMES:
        if k not in FINISHED and not any(results[k][1] is v for v in gots):
            gots.append(results[k][1])

    def body(odd, place, *refs):
        keep, refs = refs[: len(NAMES)], refs[len(NAMES) :]
        got, refs = refs[: len(gots)], refs[len(gots) :]
        attn_in, attn_out, ffn_up, ffn_down, gain, shift = refs
        odds = odd[0] != 0

        def member(name, m, at, rows):
            _, array, offset = results[name]
            i = NAMES.index(name)
            if name in FINISHED:
                at += m * (keep[i].shape[0] // 2)
                return keep[i][at : at + rows, :].astype(WIDE)
            j = [v is array for v in gots].index(True)
            kept, other = keep[i][at : at + rows, :], got[j][offset + at : offset + at + rows, :]
            return (jnp.where(odds, other, kept) if m == 0 else jnp.where(odds, kept, other)).astype(WIDE)

        for i in range(2):
            attn_in[0, :, i * W : (i + 1) * W] = member("a0", i, 0, r)
        attn_in[0, :, 2 * W :] = member("a0v", 0, 0, r)
        attn_out[0] = member("a0v", 1, 0, r)
        for a, name in ((1, "a1"), (2, "a2")):
            for i in range(3):
                attn_in[a, :, i * W : (i + 1) * W] = member(name, i // 2, (i % 2) * r, r)
            attn_out[a] = member(name, 1, r, r)
        for i in range(4):
            ffn_up[0, :, i * W : (i + 1) * W] = member("f0", 0, i * r, r)
            ffn_up[1, :, i * W : (i + 1) * W] = member("f1u", i // 2, (i % 2) * r, r)
        ffn_down[0] = member("f0", 1, 0, 4 * r)
        for m in range(2):
            ffn_down[1, 2 * m * r : 2 * (m + 1) * r] = member("f1d", m, 0, 2 * r)
        turn = lax.rem(W - place[0] * wide, W)
        for m, out in enumerate((gain, shift)):
            out[...] = pltpu.roll(member("a0", m, r, SMALL), turn, axis=1)[:NORMS, :wide]

    outs = [((3, r, 3 * W), WIDE), ((3, r, W), WIDE), ((2, r, 4 * W), WIDE), ((2, 4 * r, W), WIDE)] + [((NORMS, wide), WIDE)] * 2
    return local(body, [(sums.odd, SMEM), (place, SMEM), *keeps, *gots], outs, room=16)


def shards(sizes, source, target, source_seg, target_seg, attn_in, attn_out, ffn_up, ffn_down, norm_gain, norm_bias, cotangent):
    plan = Plan(sizes, source.shape[1], source.shape[2])
    W, r = plan.width, plan.r
    me = lax.axis_index("shard")
    place = (me if plan.split else jnp.zeros_like(me))[None]
    src, tgt = source[0], target[0]

    small = jnp.concatenate([norm_gain, norm_bias])
    small = lax.dynamic_update_slice(jnp.zeros((SMALL, W), LOW), small, (0, me * small.shape[1]))
    odd = (lax.axis_index("rep") & 1).astype(jnp.int32)[None]
    pair = pack_self(plan, attn_in, attn_out, small, odd)
    att = Gather(plan, pair, (4 * r + SMALL,))
    rest_pair, last_pair = pack_rest(plan, attn_in, attn_out, ffn_up, ffn_down, [pair])
    rest = Gather(plan, rest_pair, (6 * r,))
    went = att.onward()
    went = rest.onward(wait_for(plan, went, 4))
    last = Gather(plan, after(last_pair, went), (4 * r,))
    self_w, stacked = att.stack(0, went)
    first, first_low, n0, r0, *kept_enc, norms = self_attention(
        plan, place, src, source_seg, self_w, 0, 0, False, wait_for(plan, stacked, 6), 0.05
    )
    one, one_low, n2, r2, *kept_self, _ = self_attention(
        plan, place, tgt, target_seg, self_w, 1, 2, True, [r0], 10
    )
    went = last.onward([r2])
    rest_w, stacked = rest.stack(0, went)
    enc_low, n1, r1, active, slope, w_f0 = encoder_ffn(
        plan, place, first, first_low, src, rest_w, norms, 1, [r2]
    )
    last_w, stacked = last.stack(0, [r1])
    two, two_low, n3, r3, *kept_cross = cross_attention(
        plan, place, one, one_low, enc_low, target_seg, source_seg, rest_w, norms, 3, stacked
    )
    (decoded, last_grad, norm_a, slope_f1, w_f1), grads = decoder_ffn(
        plan, place, two, two_low, tgt, cotangent[0], last_w, norms, 4
    )
    sums = Reduction(plan, odd)
    sums.add("f1d", grads)
    (two_grad, norm_d), grads = decoder_ffn_back(
        plan, place, last_grad, two_low, slope_f1, n3, r3, w_f1, norms, 3
    )
    deps = sums.advance([norm_d], ["f1d"])
    sums.add("f1u", grads)
    deps = sums.advance(deps, ["f1u"])
    (one_grad, enc_grad, norm_b), grads = cross_attention_back(
        plan, place, two_grad, one_low, enc_low, kept_cross, (n2, r2), (n1, r1), norms, (2, 1), deps
    )
    sums.add("a2", grads)
    deps = sums.advance([norm_b])
    (zero_grad, norm_c), grads = encoder_ffn_back(
        plan, place, enc_grad, first_low, active, slope, n0, r0, w_f0, norms, 0, deps
    )
    sums.add("f0", grads)
    deps = sums.advance([norm_c])
    tgt_grad, grads = self_attention_back(plan, place, one_grad, tgt, kept_self, last_grad, deps)
    sums.add("a1", grads)
    deps = sums.advance(grads[:1], ["f1u", "f1d"])
    halfway, grads = self_attention_back_values(plan, place, zero_grad, src, kept_enc, deps)
    sums.add("a0v", grads)
    deps = sums.advance([halfway[0]], never=["f1u", "f1d"])
    src_grad, grads = self_attention_back_scores(
        plan, place, zero_grad, src, kept_enc, *halfway, enc_grad, (norm_a, norm_d, norm_b, norm_c), deps
    )
    sums.add("a0", grads)
    deps = sums.advance(grads[:1], ["f1u", "f1d"])
    sums.advance(deps or grads[:1])
    while sums.pairs:
        sums.advance()
    return decoded[None], src_grad[None], tgt_grad[None], *outputs(plan, sums, place)


def after(value, deps):
    if not deps:
        return value

    def body(*refs):
        pass

    return pl.pallas_call(
        body,
        in_specs=[ANY] * (1 + len(deps)),
        out_shape=jax.ShapeDtypeStruct(value.shape, value.dtype),
        out_specs=ANY,
        input_output_aliases={0: 0},
        compiler_params=pltpu.CompilerParams(vmem_limit_bytes=1 << 20),
        cost_estimate=pl.CostEstimate(flops=0, bytes_accessed=0, transcendentals=0),
    )(value, *deps)


def solution(mesh):
    sizes = (mesh.shape["shard"], mesh.shape["rep"])
    tokens = P(("shard", "rep"), None, None)
    ids = P(("shard", "rep"), None)
    weight = P(None, "shard", None)
    norm = P(None, "shard")
    return jax.shard_map(
        functools.partial(shards, sizes),
        mesh=mesh,
        in_specs=(tokens, tokens, ids, ids, weight, weight, weight, weight, norm, norm, tokens),
        out_specs=(tokens, tokens, tokens, weight, weight, weight, weight, norm, norm),
        check_vma=False,
    )
```

```python
import functools

import jax
import jax.numpy as jnp
from jax import lax
from jax.experimental import pallas as pl
from jax.experimental.pallas import tpu as pltpu
from jax.sharding import PartitionSpec as P

HEAD = 64
PAIR = 2 * HEAD
EPS = 1e-05
NEG = -1e30
LOW = jnp.bfloat16
WIDE = jnp.float32
CORE, X, Y = 1, 2, 4
Z1, Z2 = 1, 2
SMALL = 16
NORMS = 5
VMEM = pl.BlockSpec(memory_space=pltpu.VMEM)
SMEM = pl.BlockSpec(memory_space=pltpu.SMEM)
ANY = pl.BlockSpec(memory_space=pl.ANY)


def dot(left, right):
    return lax.dot_general(left, right, (((1,), (0,)), ((), ())), preferred_element_type=WIDE)


def dot_nt(left, right):
    return lax.dot_general(left, right, (((1,), (1,)), ((), ())), preferred_element_type=WIDE)


def dot_tn(left, right):
    return lax.dot_general(left, right, (((0,), (0,)), ((), ())), preferred_element_type=WIDE)


def block(unit, i, r):
    part = unit[:, i * r : (i + 1) * r, :]
    return part.reshape(part.shape[0] * r, part.shape[2])


def rows_block(unit, i, r):
    n = unit.shape[0] // 4
    part = unit[i * n : (i + 1) * n, 4 * r :, :]
    return part.reshape(n * part.shape[1], part.shape[2])


def norm(value, gain, shift):
    mean = jnp.mean(value, axis=-1, keepdims=True)
    centred = value - mean
    scale = lax.rsqrt(jnp.mean(centred * centred, axis=-1, keepdims=True) + EPS)
    normal = centred * scale
    return normal * gain + shift, normal, scale


def norm_back(grad, normal, scale, gain):
    gain_grad = jnp.sum(grad * normal, axis=0, keepdims=True)
    shift_grad = jnp.sum(grad, axis=0, keepdims=True)
    inner = grad * gain
    inner_mean = jnp.mean(inner, axis=-1, keepdims=True)
    cross_mean = jnp.mean(inner * normal, axis=-1, keepdims=True)
    return scale * (inner - inner_mean - normal * cross_mean), gain_grad, shift_grad


def lanes_of(head, value):
    lane = lax.broadcasted_iota(jnp.int32, value.shape, 1)
    return jnp.where((lane < HEAD) if head == 0 else (lane >= HEAD), value, jnp.zeros_like(value))


def pick(first, second):
    lane = lax.broadcasted_iota(jnp.int32, first.shape, 1)
    return jnp.where(lane < HEAD, first, second)


def allowed_bias(memory_ids, query_ids, causal):
    tokens = memory_ids.shape[1]
    turned = jnp.transpose(jnp.broadcast_to(memory_ids.astype(WIDE), (PAIR, tokens)))[:, :1]
    allowed = turned == query_ids.astype(WIDE)
    if causal:
        shape = (tokens, query_ids.shape[1])
        allowed = allowed & (lax.broadcasted_iota(jnp.int32, shape, 1) >= lax.broadcasted_iota(jnp.int32, shape, 0))
    return jnp.where(allowed, 0.0, NEG)


def attend_forward(qkv, probs, mixed, bias):
    width = mixed.shape[1]
    for pair in range(width // PAIR):
        at = pl.ds(pair * PAIR, PAIR)
        query = qkv[:, pl.ds(pair * PAIR, PAIR)] * LOW(HEAD ** -0.5)
        keys = qkv[:, pl.ds(width + pair * PAIR, PAIR)]
        turned = jnp.transpose(qkv[:, pl.ds(2 * width + pair * PAIR, PAIR)])
        out = []
        for head in range(2):
            scores = dot_nt(keys, lanes_of(head, query)) + bias[...]
            top = jnp.max(scores, axis=0, keepdims=True)
            weights = jnp.exp(scores - top)
            total = jnp.sum(weights, axis=0, keepdims=True)
            low = (weights * (1.0 / total)).astype(LOW)
            probs[2 * pair + head] = low
            out.append(dot(turned[head * HEAD : (head + 1) * HEAD, :], low))
        mixed[:, at] = jnp.transpose(jnp.concatenate(out).astype(LOW))


def attend_backward(qkv, probs, mixed_grad, qkv_grad):
    width = mixed_grad.shape[1]
    for pair in range(width // PAIR):
        query = qkv[:, pl.ds(pair * PAIR, PAIR)]
        keys = qkv[:, pl.ds(width + pair * PAIR, PAIR)]
        values = qkv[:, pl.ds(2 * width + pair * PAIR, PAIR)]
        grad = mixed_grad[:, pl.ds(pair * PAIR, PAIR)]
        turned = jnp.transpose(keys)
        dq, dk, dv = [], [], []
        for head in range(2):
            low = probs[2 * pair + head]
            prob = low.astype(WIDE)
            prob_grad = dot_nt(values, lanes_of(head, grad))
            delta = jnp.sum(prob * prob_grad, axis=0, keepdims=True)
            score_grad = (prob * (prob_grad - delta)).astype(LOW)
            dv.append(dot(low, grad))
            dk.append(dot(score_grad, query))
            dq.append(dot(turned[head * HEAD : (head + 1) * HEAD, :], score_grad))
        scale = HEAD ** -0.5
        qkv_grad[:, pl.ds(pair * PAIR, PAIR)] = jnp.transpose((jnp.concatenate(dq) * scale).astype(LOW))
        qkv_grad[:, pl.ds(width + pair * PAIR, PAIR)] = (pick(*dk) * scale).astype(LOW)
        qkv_grad[:, pl.ds(2 * width + pair * PAIR, PAIR)] = pick(*dv).astype(LOW)


GELU = 0.7978845608028654


def gelu_and_slope(value):
    square = value * value
    t = jnp.tanh(value * (GELU + (GELU * 0.044715) * square))
    half = 0.5 + 0.5 * t
    slope = half + value * (0.5 - 0.5 * (t * t)) * (GELU + (3 * 0.044715 * GELU) * square)
    return value * half, slope


def ffn_forward(hidden, weight, active, slope, r):
    W = hidden.shape[1]
    total = None
    for c in range(4):
        at = pl.ds(c * W, W)
        act, sl = gelu_and_slope(dot(hidden, block(weight, c, r)))
        act = act.astype(LOW)
        active[:, at] = act
        slope[:, at] = sl.astype(LOW)
        part = dot(act, rows_block(weight, c, r))
        total = part if total is None else total + part
    return total


def ffn_backward_down(grad, active, put):
    W = grad.shape[1]
    for c in range(4):
        put(c, dot_tn(active[:, pl.ds(c * W, W)], grad).astype(LOW))


def ffn_backward_up(grad, hidden, weight, slope, r, put):
    W = grad.shape[1]
    turned = jnp.transpose(hidden)
    total = None
    for c in range(4):
        z = (dot_nt(grad, rows_block(weight, c, r)) * slope[:, pl.ds(c * W, W)].astype(WIDE)).astype(LOW)
        put(c, dot(turned, z).astype(LOW))
        part = dot_nt(z, block(weight, c, r))
        total = part if total is None else total + part
    return total


class Plan:
    def __init__(self, sizes, length, width):
        self.split = sizes == (8, 4)
        self.sizes = sizes
        self.length, self.width = length, width
        self.heads = width // HEAD
        self.shards = sizes[0]
        self.r = width // self.shards
        self.n = self.g = 2 if self.split else 1


    def lay(self, place, stacks, member, rows, unit, at):
        count = rows.stop - rows.start
        if not self.split:
            unit[:, at : at + count, :] = stacks[0][:, member, rows]
            return
        odd, chip = (place & 1) != 0, place >> 1
        for j in range(4):
            k = 2 * (j ^ chip) + member
            mine, other = stacks[0][k, rows, :], stacks[1][k, rows, :]
            unit[2 * j, at : at + count, :] = jnp.where(odd, other, mine)
            unit[2 * j + 1, at : at + count, :] = jnp.where(odd, mine, other)


    def grad_shapes(self, rows):
        if not self.split:
            return [(self.shards, 2, rows, self.width)]
        return [(8, rows, self.width)] * 2

    def leave(self, place, outs, member, at, value, first=0):
        count = value.shape[1]
        if not self.split:
            outs[0][first : first + value.shape[0], member, at : at + count, :] = value
            return
        odd, chip = (place & 1) != 0, place >> 1
        for j in range(value.shape[0] // 2):
            k = (first // 2 + j) ^ chip
            if member == 0:
                k = ((k & 1) << 1) | (k >> 1)
            one, two = value[2 * j], value[2 * j + 1]
            outs[0][4 * member + k, at : at + count, :] = jnp.where(odd, two, one)
            outs[1][4 * member + k, at : at + count, :] = jnp.where(odd, one, two)

    def leave_block(self, place, outs, member, i, value):
        self.leave(place, outs, member, i * self.r, value.reshape(self.shards, self.r, self.width))

    def leave_rows(self, place, outs, member, i, value):
        n = self.shards // 4
        self.leave(place, outs, member, 0, value.reshape(n, 4 * self.r, self.width), i * n)

    def leave_rows_halved(self, place, outs, i, value):
        n, half = self.shards // 4, 2 * self.r
        value = value.reshape(n, 4 * self.r, self.width)
        for m in range(2):
            self.leave(place, outs, m, 0, value[:, m * half : (m + 1) * half, :], i * n)

    def call(self, body, ins, outs, scratch, us, deps, room):
        def run(*refs):
            body(*refs[len(deps) :])

        return pl.pallas_call(
            run,
            in_specs=[ANY] * len(deps) + [spec for _, spec in ins],
            out_shape=[jax.ShapeDtypeStruct(shape, dtype) for shape, dtype in outs],
            out_specs=[VMEM] * len(outs),
            scratch_shapes=scratch,
            compiler_params=pltpu.CompilerParams(vmem_limit_bytes=room << 20),
            cost_estimate=pl.CostEstimate(flops=int(us * 5e9), bytes_accessed=1 << 20, transcendentals=0),
        )(*deps, *[value for value, _ in ins])


def vmem(*arrays):
    return [(v, VMEM) for v in arrays]


def self_attention(plan, place, tokens, ids, stacks, member, row, causal, deps=(), us=10):
    L, W, H, r = plan.length, plan.width, plan.heads, plan.r

    def body(place, tokens, ids, *rest):
        stacks, rest = rest[: plan.n], rest[plan.n :]
        out, out_low, normal, scale, qkv, mixed, probs, weight, norms, bias = rest
        plan.lay(place[0], stacks, member, slice(0, 4 * r), weight, 0)
        bias[...] = allowed_bias(ids[...], ids[...], causal)
        if plan.split:
            norms[...] = sum(jnp.sum(s[...].astype(WIDE), axis=0) for s in (v.at[:, 4 * r : 4 * r + SMALL, :] for v in stacks)) * 0.5
        else:
            norms[...] = jnp.sum(stacks[0][:, member, 4 * r : 4 * r + SMALL].astype(WIDE), axis=0)
        x = tokens[...]
        for i in range(3):
            qkv[:, i * W : (i + 1) * W] = dot(x, block(weight, i, r)).astype(LOW)
        attend_forward(qkv, probs, mixed, bias)
        value = x.astype(WIDE) + dot(mixed[...], block(weight, 3, r))
        y, n, s = norm(value, norms[row : row + 1, :], norms[NORMS + row : NORMS + row + 1, :])
        out[...] = y
        out_low[...] = y.astype(LOW)
        normal[...] = n.astype(LOW)
        scale[...] = s

    ins = [(place, SMEM)] + vmem(tokens, ids, *stacks)
    outs = [((L, W), WIDE), ((L, W), LOW), ((L, W), LOW), ((L, 1), WIDE)]
    outs += [((L, 3 * W), LOW), ((L, W), LOW), ((H, L, L), LOW), ((plan.shards, 4 * r, W), LOW), ((SMALL, W), WIDE)]
    return plan.call(body, ins, outs, [pltpu.VMEM((L, L), WIDE)], us, deps, 11)


def cross_attention(plan, place, query_in, query_low, memory_low, query_ids, memory_ids, stacks, norms, row, deps=()):
    L, W, H, r = plan.length, plan.width, plan.heads, plan.r

    def body(place, query_in, query_low, memory_low, query_ids, memory_ids, norms, *rest):
        stacks, rest = rest[: plan.n], rest[plan.n :]
        out, out_low, normal, scale, qkv, mixed, probs, weight, bias = rest
        for m in range(2):
            plan.lay(place[0], stacks, m, slice(0, 2 * r), weight, 2 * m * r)
        bias[...] = allowed_bias(memory_ids[...], query_ids[...], False)
        qkv[:, :W] = dot(query_low[...], block(weight, 0, r)).astype(LOW)
        memory = memory_low[...]
        for i in (1, 2):
            qkv[:, i * W : (i + 1) * W] = dot(memory, block(weight, i, r)).astype(LOW)
        attend_forward(qkv, probs, mixed, bias)
        value = query_in[...] + dot(mixed[...], block(weight, 3, r))
        y, n, s = norm(value, norms[row : row + 1, :], norms[NORMS + row : NORMS + row + 1, :])
        out[...] = y
        out_low[...] = y.astype(LOW)
        normal[...] = n.astype(LOW)
        scale[...] = s

    ins = [(place, SMEM)] + vmem(query_in, query_low, memory_low, query_ids, memory_ids, norms, *stacks)
    outs = [((L, W), WIDE), ((L, W), LOW), ((L, W), LOW), ((L, 1), WIDE)]
    outs += [((L, 3 * W), LOW), ((L, W), LOW), ((H, L, L), LOW), ((plan.shards, 4 * r, W), LOW)]
    return plan.call(body, ins, outs, [pltpu.VMEM((L, L), WIDE)], 10, deps, 11)


def encoder_ffn(plan, place, hidden, hidden_low, tokens, stacks, norms, row, deps=()):
    L, W, F, r = plan.length, plan.width, 4 * plan.width, plan.r

    def body(place, hidden, hidden_low, tokens, norms, *rest):
        stacks, rest = rest[: plan.n], rest[plan.n :]
        out_low, normal, scale, active, slope, weight = rest
        for m in range(2):
            plan.lay(place[0], stacks, m, slice(0, 4 * r), weight, 4 * m * r)
        branch = ffn_forward(hidden_low[...], weight, active, slope, r)
        value = hidden[...] + branch + tokens[...].astype(WIDE)
        y, n, s = norm(value, norms[row : row + 1, :], norms[NORMS + row : NORMS + row + 1, :])
        out_low[...] = y.astype(LOW)
        normal[...] = n.astype(LOW)
        scale[...] = s

    ins = [(place, SMEM)] + vmem(hidden, hidden_low, tokens, norms, *stacks)
    outs = [((L, W), LOW), ((L, W), LOW), ((L, 1), WIDE), ((L, F), LOW), ((L, F), LOW), ((plan.shards, 8 * r, W), LOW)]
    return plan.call(body, ins, outs, [], 9, deps, 11)


def decoder_ffn(plan, place, hidden, hidden_low, tokens, cotangent, stacks, norms, row, deps=()):
    L, W, F, r = plan.length, plan.width, 4 * plan.width, plan.r

    def body(place, hidden, hidden_low, tokens, cotangent, norms, *rest):
        stacks, rest = rest[: plan.n], rest[plan.n :]
        decoded, last_grad, norm_grads, slope, weight, *grads, active = rest
        for m in range(2):
            plan.lay(place[0], stacks, m, slice(0, 4 * r), weight, 4 * m * r)
        branch = ffn_forward(hidden_low[...], weight, active, slope, r)
        value = hidden[...] + branch + tokens[...].astype(WIDE)
        gain = norms[row : row + 1, :]
        y, n, s = norm(value, gain, norms[NORMS + row : NORMS + row + 1, :])
        decoded[...] = y.astype(LOW)
        grad, gain_grad, shift_grad = norm_back(cotangent[...].astype(WIDE), n, s, gain)
        last_grad[...] = grad
        norm_grads[0:1, :] = gain_grad
        norm_grads[1:2, :] = shift_grad
        ffn_backward_down(grad.astype(LOW), active, lambda i, v: plan.leave_rows_halved(place[0], grads, i, v))

    ins = [(place, SMEM)] + vmem(hidden, hidden_low, tokens, cotangent, norms, *stacks)
    outs = [((L, W), LOW), ((L, W), WIDE), ((2, W), WIDE), ((L, F), LOW), ((plan.shards, 8 * r, W), LOW)]
    outs += [(s, LOW) for s in plan.grad_shapes(2 * r)]
    got = plan.call(body, ins, outs, [pltpu.VMEM((L, F), LOW)], 12, deps, 16)
    return got[:5], got[5:]


def decoder_ffn_back(plan, place, grad, hidden_low, slope, hidden_normal, hidden_scale, weight, norms, row, deps=()):
    L, W, r = plan.length, plan.width, plan.r

    def body(place, grad, hidden_low, slope, hidden_normal, hidden_scale, weight, norms, out, norm_grads, *grads):
        def put(i, value):
            plan.leave(place[0], grads, i // 2, (i % 2) * r, value.reshape(plan.shards, r, W))

        back = ffn_backward_up(grad[...].astype(LOW), hidden_low[...], weight, slope, r, put)
        normal = hidden_normal[...].astype(WIDE)
        total, gain_grad, shift_grad = norm_back(grad[...] + back, normal, hidden_scale[...], norms[row : row + 1, :])
        out[...] = total
        norm_grads[0:1, :] = gain_grad
        norm_grads[1:2, :] = shift_grad

    ins = [(place, SMEM)] + vmem(grad, hidden_low, slope, hidden_normal, hidden_scale, weight, norms)
    outs = [((L, W), WIDE), ((2, W), WIDE)] + [(s, LOW) for s in plan.grad_shapes(2 * r)]
    got = plan.call(body, ins, outs, [], 8, deps, 12)
    return got[:2], got[2:]


def encoder_ffn_back(plan, place, grad, hidden_low, active, slope, hidden_normal, hidden_scale, weight, norms, row, deps=()):
    L, W, r = plan.length, plan.width, plan.r

    def body(place, grad, hidden_low, active, slope, hidden_normal, hidden_scale, weight, norms, *rest):
        zero_grad, norm_grads, *grads = rest
        grad_low = grad[...].astype(LOW)
        ffn_backward_down(grad_low, active, lambda i, v: plan.leave_rows(place[0], grads, 1, i, v))
        back = ffn_backward_up(
            grad_low, hidden_low[...], weight, slope, r, lambda i, v: plan.leave_block(place[0], grads, 0, i, v)
        )
        normal = hidden_normal[...].astype(WIDE)
        out, gain_grad, shift_grad = norm_back(grad[...] + back, normal, hidden_scale[...], norms[row : row + 1, :])
        zero_grad[...] = out
        norm_grads[0:1, :] = gain_grad
        norm_grads[1:2, :] = shift_grad

    ins = [(place, SMEM)] + vmem(grad, hidden_low, active, slope, hidden_normal, hidden_scale, weight, norms)
    outs = [((L, W), WIDE), ((2, W), WIDE)] + [(s, LOW) for s in plan.grad_shapes(4 * r)]
    got = plan.call(body, ins, outs, [], 11, deps, 14)
    return got[:2], got[2:]


def self_attention_back(plan, place, grad, tokens, kept, extra, deps=()):
    L, W, r = plan.length, plan.width, plan.r

    def body(place, grad, extra, tokens, qkv, mixed, probs, weight, *rest):
        total, *grads, mixed_grad, qkv_grad = rest
        grad_low = grad[...].astype(LOW)
        plan.leave_block(place[0], grads, 1, 1, dot_tn(mixed[...], grad_low).astype(LOW))
        mixed_grad[...] = dot_nt(grad_low, block(weight, 3, r)).astype(LOW)
        attend_backward(qkv, probs, mixed_grad, qkv_grad)
        x = jnp.transpose(tokens[...])
        for i in range(3):
            plan.leave_block(place[0], grads, i // 2, i % 2, dot(x, qkv_grad[:, i * W : (i + 1) * W]).astype(LOW))
        back = grad[...] + extra[...]
        for i in range(3):
            back += dot_nt(qkv_grad[:, i * W : (i + 1) * W], block(weight, i, r))
        total[...] = back

    ins = [(place, SMEM)] + vmem(grad, extra, tokens, *kept)
    outs = [((L, W), WIDE)] + [(s, LOW) for s in plan.grad_shapes(2 * r)]
    scratch = [pltpu.VMEM((L, W), LOW), pltpu.VMEM((L, 3 * W), LOW)]
    got = plan.call(body, ins, outs, scratch, 12, deps, 12)
    return got[0], got[1:]


def attend_backward_values(probs, mixed_grad, value_grad):
    for pair in range(mixed_grad.shape[1] // PAIR):
        at = pl.ds(pair * PAIR, PAIR)
        grad = mixed_grad[:, at]
        value_grad[:, at] = pick(*[dot(probs[2 * pair + head], grad) for head in range(2)]).astype(LOW)


def self_attention_back_values(plan, place, grad, tokens, kept, deps=()):
    L, W, r = plan.length, plan.width, plan.r
    _, mixed, probs, weight = kept

    def body(place, grad, tokens, mixed, probs, weight, mixed_grad, value_grad, *grads):
        grad_low = grad[...].astype(LOW)
        plan.leave_block(place[0], grads, 1, 0, dot_tn(mixed[...], grad_low).astype(LOW))
        mixed_grad[...] = dot_nt(grad_low, block(weight, 3, r)).astype(LOW)
        attend_backward_values(probs, mixed_grad, value_grad)
        plan.leave_block(place[0], grads, 0, 0, dot_tn(tokens[...], value_grad[...]).astype(LOW))

    ins = [(place, SMEM)] + vmem(grad, tokens, mixed, probs, weight)
    outs = [((L, W), LOW), ((L, W), LOW)] + [(s, LOW) for s in plan.grad_shapes(r)]
    got = plan.call(body, ins, outs, [], 6, deps, 12)
    return got[:2], got[2:]


def self_attention_back_scores(plan, place, grad, tokens, kept, mixed_grad, value_grad, extra, small, deps=()):
    L, W, r = plan.length, plan.width, plan.r
    qkv, _, probs, weight = kept

    def body(place, grad, extra, tokens, qkv, probs, weight, mixed_grad, value_grad, *rest):
        parts, (total, *grads, score_grads) = rest[:4], rest[4:]
        for m in range(2):
            rows = [parts[j][i + m : i + m + 1, :] for j, i in ((3, 0), (2, 2), (2, 0), (1, 0), (0, 0))]
            rows = jnp.concatenate(rows + [jnp.zeros((SMALL - NORMS, W), WIDE)]).astype(LOW)[None]
            plan.leave(place[0], grads, m, r, jnp.broadcast_to(rows, (plan.shards, SMALL, W)))
        scale = HEAD ** -0.5
        for pair in range(W // PAIR):
            at = pl.ds(pair * PAIR, PAIR)
            query, keys = qkv[:, at], qkv[:, pl.ds(W + pair * PAIR, PAIR)]
            values, out_grad = qkv[:, pl.ds(2 * W + pair * PAIR, PAIR)], mixed_grad[:, at]
            turned = jnp.transpose(keys)
            dq, dk = [], []
            for head in range(2):
                prob = probs[2 * pair + head].astype(WIDE)
                prob_grad = dot_nt(values, lanes_of(head, out_grad))
                delta = jnp.sum(prob * prob_grad, axis=0, keepdims=True)
                score_grad = (prob * (prob_grad - delta)).astype(LOW)
                dk.append(dot(score_grad, query))
                dq.append(dot(turned[head * HEAD : (head + 1) * HEAD, :], score_grad))
            score_grads[:, at] = jnp.transpose((jnp.concatenate(dq) * scale).astype(LOW))
            score_grads[:, pl.ds(W + pair * PAIR, PAIR)] = (pick(*dk) * scale).astype(LOW)
        x = jnp.transpose(tokens[...])
        back = grad[...] + extra[...] + dot_nt(value_grad[...], block(weight, 2, r))
        for i in range(2):
            part = score_grads[:, i * W : (i + 1) * W]
            plan.leave_block(place[0], grads, i, 0, dot(x, part).astype(LOW))
            back += dot_nt(part, block(weight, i, r))
        total[...] = back

    ins = [(place, SMEM)] + vmem(grad, extra, tokens, qkv, probs, weight, mixed_grad, value_grad, *small)
    outs = [((L, W), WIDE)] + [(s, LOW) for s in plan.grad_shapes(r + SMALL)]
    got = plan.call(body, ins, outs, [pltpu.VMEM((L, 2 * W), LOW)], 10, deps, 12)
    return got[0], got[1:]


def cross_attention_back(plan, place, grad, query_low, memory_low, kept, query_norm, memory_norm, norms, rows, deps=()):
    L, W, r = plan.length, plan.width, plan.r

    def body(place, grad, query_low, memory_low, qkv, mixed, probs, weight, query_n, query_r, memory_n, memory_r, norms, *rest):
        one_grad, enc_grad, norm_grads, *grads, mixed_grad, qkv_grad = rest
        grad_low = grad[...].astype(LOW)
        plan.leave_block(place[0], grads, 1, 1, dot_tn(mixed[...], grad_low).astype(LOW))
        mixed_grad[...] = dot_nt(grad_low, block(weight, 3, r)).astype(LOW)
        attend_backward(qkv, probs, mixed_grad, qkv_grad)
        plan.leave_block(place[0], grads, 0, 0, dot_tn(query_low[...], qkv_grad[:, :W]).astype(LOW))
        memory = jnp.transpose(memory_low[...])
        for i in (1, 2):
            value = dot(memory, qkv_grad[:, i * W : (i + 1) * W]).astype(LOW)
            plan.leave_block(place[0], grads, i // 2, i % 2, value)
        back = grad[...] + dot_nt(qkv_grad[:, :W], block(weight, 0, r))
        normal = query_n[...].astype(WIDE)
        out, gain_grad, shift_grad = norm_back(back, normal, query_r[...], norms[rows[0] : rows[0] + 1, :])
        one_grad[...] = out
        norm_grads[0:1, :] = gain_grad
        norm_grads[1:2, :] = shift_grad
        back = dot_nt(qkv_grad[:, W : 2 * W], block(weight, 1, r)) + dot_nt(qkv_grad[:, 2 * W :], block(weight, 2, r))
        normal = memory_n[...].astype(WIDE)
        out, gain_grad, shift_grad = norm_back(back, normal, memory_r[...], norms[rows[1] : rows[1] + 1, :])
        enc_grad[...] = out
        norm_grads[2:3, :] = gain_grad
        norm_grads[3:4, :] = shift_grad

    ins = [(place, SMEM)] + vmem(grad, query_low, memory_low, *kept, *query_norm, *memory_norm, norms)
    outs = [((L, W), WIDE), ((L, W), WIDE), ((4, W), WIDE)] + [(s, LOW) for s in plan.grad_shapes(2 * r)]
    scratch = [pltpu.VMEM((L, W), LOW), pltpu.VMEM((L, 3 * W), LOW)]
    got = plan.call(body, ins, outs, scratch, 0.05, deps, 13)
    return got[:3], got[3:]


def swap(value, bit):
    return lax.ppermute(value, "shard", [(i, i ^ bit) for i in range(8)])


def swap_rep(value, bit):
    return lax.ppermute(value, "rep", [(i, i ^ bit) for i in range(4)])


def local(body, ins, outs, deps=(), room=6, us=0):
    ins = [v if isinstance(v, tuple) else (v, VMEM) for v in ins]

    def run(*refs):
        body(*refs[len(deps) :])

    return pl.pallas_call(
        run,
        in_specs=[ANY] * len(deps) + [spec for _, spec in ins],
        out_shape=[jax.ShapeDtypeStruct(shape, dtype) for shape, dtype in outs],
        out_specs=[VMEM] * len(outs),
        compiler_params=pltpu.CompilerParams(vmem_limit_bytes=room << 20),
        cost_estimate=pl.CostEstimate(flops=int(us * 5e9), bytes_accessed=1 << 20, transcendentals=0),
    )(*deps, *[v for v, _ in ins])


def mark(out):
    out[...] = jnp.zeros_like(out)


def wait_for(plan, deps, us):
    return local(mark, [], [((8, 128), WIDE)], deps, 2, us) if plan.split else []


def pack_self(plan, attn_in, attn_out, small, odd):
    W, r = plan.width, plan.r

    def body(attn_in, attn_out, small, odd, out):
        for k in range(2):
            for i in range(3):
                out[k, i * r : (i + 1) * r, :] = attn_in[k, :, i * W : (i + 1) * W]
            out[k, 3 * r : 4 * r, :] = attn_out[k]
            out[k, 4 * r :, :] = small[...]

    return local(body, [attn_in, attn_out, small, (odd, SMEM)], [((2, 4 * r + SMALL, W), LOW)])[0]


def pack_rest(plan, attn_in, attn_out, ffn_up, ffn_down, deps):
    W, r = plan.width, plan.r

    def body(attn_in, attn_out, ffn_up, ffn_down, first, second):
        for k, out in enumerate((first, second)):
            for i in range(4):
                out[0, i * r : (i + 1) * r, :] = ffn_up[k, :, i * W : (i + 1) * W]
            out[1, : 4 * r] = ffn_down[k]
        for i in range(3):
            at = (4 + i % 2) * r
            first[i // 2, at : at + r, :] = attn_in[2, :, i * W : (i + 1) * W]
        first[1, 5 * r :, :] = attn_out[2]

    outs = [((2, 6 * r, W), LOW), ((2, 4 * r, W), LOW)]
    return local(body, [attn_in, attn_out, ffn_up, ffn_down], outs, deps)


class Gather:
    def __init__(self, plan, pair, parts):
        self.plan, self.pair, self.parts = plan, pair, parts
        self.ends = [sum(parts[: i + 1]) for i in range(len(parts))]
        if plan.split:
            self.near = [swap(pair, X), swap(pair, Y)]

    def onward(self, deps=()):
        if not self.plan.split:
            return []
        parts, ends = self.parts, self.ends

        def body(by_x, by_y, *outs):
            for i, (rows, end) in enumerate(zip(parts, ends)):
                outs[2 * i][...] = by_x[0, end - rows : end, :]
                outs[2 * i + 1][...] = by_y[1, end - rows : end, :]

        outs = local(body, self.near, [((rows, self.plan.width), LOW) for rows in parts for _ in range(2)], deps)
        self.far = [(swap(outs[2 * i], Y), swap(outs[2 * i + 1], X)) for i in range(len(parts))]
        return [outs[0]]

    def stack(self, part, deps=(), within=None):
        rows, end = self.parts[part], self.ends[part]
        within = within or slice(0, rows)
        at = slice(end - rows + within.start, end - rows + within.stop)
        rows = within.stop - within.start
        if not self.plan.split:
            return [lax.all_gather(self.pair[:, at], "shard", axis=0)], []

        def body(pair, by_x, by_y, first, second, out):
            for j, v in enumerate((pair, by_x, by_y)):
                out[2 * j : 2 * j + 2] = v[:, at, :]
            out[6] = first[within, :]
            out[7] = second[within, :]

        ins = [self.pair, *self.near, *self.far[part]]
        mine = local(body, ins, [((8, rows, self.plan.width), LOW)], deps)[0]
        return [mine, swap(mine, CORE)], [mine]


class Reduction:
    def __init__(self, plan, odd):
        self.plan, self.odd = plan, odd
        self.pairs, self.results = [], {}

    def add(self, name, outs):
        if not self.plan.split:
            whole = outs[0]
            flat = whole.reshape((-1,) + whole.shape[2:])
            own = lax.psum_scatter(flat, "shard", scatter_dimension=0, tiled=True)
            self.results[name] = lax.psum(own, "rep").astype(WIDE).reshape(whole.shape[1:])
            return
        mine, other = outs
        self.pairs.append(dict(name=name, rows=mine.shape[1], step=0, keep=mine, slot={}, moving={}, got=swap(other, CORE)))

    def advance(self, deps=(), only=(), never=()):
        pairs = [p for p in self.pairs if (not only or p["name"] in only) and p["name"] not in never]
        if not pairs:
            return []
        self.pairs = [p for p in self.pairs if p not in pairs]
        W = self.plan.width
        sizes = {"x": 0, "y": 0, "n": 0, "f": 0}

        def place(way, count):
            at = sizes[way]
            sizes[way] += count
            return at

        work = []
        for p in pairs:
            R, step = p["rows"], p["step"]
            ways = ({"x": 2 * R, "y": 2 * R}, {"x": R, "y": R}, {"n": R}, {"f": R}, {"n": R}, {})[step]
            work.append(dict(p, out={way: place(way, count) for way, count in ways.items()}, kept=((4, 2, 1, 1, 1, 2)[step] * R, W)))
        ways = [w for w in "xynf" if sizes[w]]
        came = []
        for p in pairs:
            came += [v for v in p["moving"].values() if not any(v is u for u in came)]
        cores = [t for t in work if t["step"] == 0]

        def body(odd, *refs):
            keep_in, refs = refs[: len(work)], refs[len(work) :]
            core_in, refs = refs[: len(cores)], refs[len(cores) :]
            arrived, refs = refs[: len(came)], refs[len(came) :]
            keep_out, refs = refs[: len(work)], refs[len(work) :]
            leave = dict(zip(ways, refs))
            odds = odd[0] != 0

            def total(left, right):
                return (left.astype(WIDE) + right.astype(WIDE)).astype(LOW)

            core = iter(core_in)
            for t, keep, out in zip(work, keep_in, keep_out):
                R, step, slot, to = t["rows"], t["step"], t["slot"], t["out"]
                got = {w: arrived[[v is u for u in came].index(True)] for w, v in t["moving"].items() if w in slot}
                if step == 0:
                    other = next(core)
                    for m, way in enumerate("xy"):
                        at = 4 * m * R
                        out[2 * m * R : 2 * (m + 1) * R, :] = total(keep[at : at + 2 * R, :], other[at : at + 2 * R, :])
                        at += 2 * R
                        leave[way][to[way] : to[way] + 2 * R, :] = total(keep[at : at + 2 * R, :], other[at : at + 2 * R, :])
                elif step == 1:
                    for m, (way, onward) in enumerate(("xy", "yx")):
                        other, at, kept = got[way], slot[way], 2 * m * R
                        out[m * R : (m + 1) * R, :] = total(keep[kept : kept + R, :], other[at : at + R, :])
                        kept, at = kept + R, at + R
                        leave[onward][to[onward] : to[onward] + R, :] = total(keep[kept : kept + R, :], other[at : at + R, :])
                elif step == 2:
                    first = total(keep[:R, :], got["y"][slot["y"] : slot["y"] + R, :])
                    second = total(keep[R:, :], got["x"][slot["x"] : slot["x"] + R, :])
                    out[...] = jnp.where(odds, second, first)
                    leave["n"][to["n"] : to["n"] + R, :] = jnp.where(odds, first, second)
                elif step == 5:
                    mine, other = keep[...], got["n"][slot["n"] : slot["n"] + R, :]
                    out[:R, :] = jnp.where(odds, other, mine)
                    out[R:, :] = jnp.where(odds, mine, other)
                else:
                    way, onward = ("n", "f") if step == 3 else ("f", "n")
                    value = total(keep[...], got[way][slot[way] : slot[way] + R, :])
                    out[...] = value
                    leave[onward][to[onward] : to[onward] + R, :] = value

        if cores and came:
            last = [v for p in pairs if p["step"] == 5 for v in p["moving"].values()]
            if last:
                deps = wait_for(self.plan, [*deps, *[v for v in came if not any(v is u for u in last)]], 2)
            deps = wait_for(self.plan, [*deps, *came], 20)
        keeps = [t["keep"].reshape(-1, W) for t in work]
        gots = [t["got"].reshape(-1, W) for t in cores]
        outs = [(t["kept"], LOW) for t in work] + [((sizes[w], W), LOW) for w in ways]
        done = local(body, [(self.odd, SMEM), *keeps, *gots, *came], outs, deps)
        moving = {}
        for way, value in zip(ways, done[len(work) :]):
            moving[way] = swap_rep(value, Z1 if way == "n" else Z2) if way in "nf" else swap(value, X if way == "x" else Y)
        for t, kept in zip(work, done):
            if t["step"] == 5:
                self.results[t["name"]] = (kept, None, 0)
            elif t["step"] == 4 and t["name"] not in FINISHED:
                self.results[t["name"]] = (kept, moving["n"], t["out"]["n"])
            else:
                mine = {w: v for w, v in moving.items() if w in t["out"]}
                self.pairs.append(dict(name=t["name"], rows=t["rows"], step=t["step"] + 1, keep=kept, slot=t["out"], moving=mine))
        return [done[0]]


FINISHED = ("f1u", "f1d")
NAMES = ("a0", "a0v", "a1", "a2", "f0", "f1u", "f1d")


def outputs(plan, sums, place):
    W, r = plan.width, plan.r
    wide = W // plan.shards
    results = sums.results
    if not plan.split:
        me = lax.axis_index("shard")
        scores, small = results["a0"][:, :r], results["a0"][:, r:]
        small = lax.dynamic_slice(small, (0, 0, me * wide), (2, NORMS, wide))
        att = [jnp.concatenate([scores, results["a0v"]]), *(results[k].reshape(4, r, W) for k in ("a1", "a2"))]
        att, ffn = jnp.stack(att), jnp.stack([results["f0"], jnp.stack([results[k].reshape(4 * r, W) for k in ("f1u", "f1d")])])

        def unblocks(v):
            return jnp.moveaxis(v, 1, 2).reshape(v.shape[0], r, -1)

        return unblocks(att[:, :3]), att[:, 3], unblocks(ffn[:, 0].reshape(2, 4, r, W)), ffn[:, 1], small[0], small[1]
    keeps = [results[k][0] for k in NAMES]
    gots = []
    for k in NAMES:
        if k not in FINISHED and not any(results[k][1] is v for v in gots):
            gots.append(results[k][1])

    def body(odd, place, *refs):
        keep, refs = refs[: len(NAMES)], refs[len(NAMES) :]
        got, refs = refs[: len(gots)], refs[len(gots) :]
        attn_in, attn_out, ffn_up, ffn_down, gain, shift = refs
        odds = odd[0] != 0

        def member(name, m, at, rows):
            _, array, offset = results[name]
            i = NAMES.index(name)
            if name in FINISHED:
                at += m * (keep[i].shape[0] // 2)
                return keep[i][at : at + rows, :].astype(WIDE)
            j = [v is array for v in gots].index(True)
            kept, other = keep[i][at : at + rows, :], got[j][offset + at : offset + at + rows, :]
            return (jnp.where(odds, other, kept) if m == 0 else jnp.where(odds, kept, other)).astype(WIDE)

        for i in range(2):
            attn_in[0, :, i * W : (i + 1) * W] = member("a0", i, 0, r)
        attn_in[0, :, 2 * W :] = member("a0v", 0, 0, r)
        attn_out[0] = member("a0v", 1, 0, r)
        for a, name in ((1, "a1"), (2, "a2")):
            for i in range(3):
                attn_in[a, :, i * W : (i + 1) * W] = member(name, i // 2, (i % 2) * r, r)
            attn_out[a] = member(name, 1, r, r)
        for i in range(4):
            ffn_up[0, :, i * W : (i + 1) * W] = member("f0", 0, i * r, r)
            ffn_up[1, :, i * W : (i + 1) * W] = member("f1u", i // 2, (i % 2) * r, r)
        ffn_down[0] = member("f0", 1, 0, 4 * r)
        for m in range(2):
            ffn_down[1, 2 * m * r : 2 * (m + 1) * r] = member("f1d", m, 0, 2 * r)
        turn = lax.rem(W - place[0] * wide, W)
        for m, out in enumerate((gain, shift)):
            out[...] = pltpu.roll(member("a0", m, r, SMALL), turn, axis=1)[:NORMS, :wide]

    outs = [((3, r, 3 * W), WIDE), ((3, r, W), WIDE), ((2, r, 4 * W), WIDE), ((2, 4 * r, W), WIDE)] + [((NORMS, wide), WIDE)] * 2
    return local(body, [(sums.odd, SMEM), (place, SMEM), *keeps, *gots], outs, room=16)


def shards(sizes, source, target, source_seg, target_seg, attn_in, attn_out, ffn_up, ffn_down, norm_gain, norm_bias, cotangent):
    plan = Plan(sizes, source.shape[1], source.shape[2])
    W, r = plan.width, plan.r
    me = lax.axis_index("shard")
    place = (me if plan.split else jnp.zeros_like(me))[None]
    src, tgt = source[0], target[0]

    small = jnp.concatenate([norm_gain, norm_bias])
    small = lax.dynamic_update_slice(jnp.zeros((SMALL, W), LOW), small, (0, me * small.shape[1]))
    odd = (lax.axis_index("rep") & 1).astype(jnp.int32)[None]
    pair = pack_self(plan, attn_in, attn_out, small, odd)
    att = Gather(plan, pair, (4 * r + SMALL,))
    rest_pair, last_pair = pack_rest(plan, attn_in, attn_out, ffn_up, ffn_down, [pair])
    rest = Gather(plan, rest_pair, (6 * r,))
    went = att.onward()
    went = rest.onward(wait_for(plan, went, 4))
    last = Gather(plan, after(last_pair, went), (4 * r,))
    self_w, stacked = att.stack(0, went)
    first, first_low, n0, r0, *kept_enc, norms = self_attention(
        plan, place, src, source_seg, self_w, 0, 0, False, wait_for(plan, stacked, 6), 0.05
    )
    one, one_low, n2, r2, *kept_self, _ = self_attention(
        plan, place, tgt, target_seg, self_w, 1, 2, True, [r0], 10
    )
    went = last.onward([r2])
    ffn_w, stacked = rest.stack(0, went, slice(0, 4 * r))
    cross_w, stacked = rest.stack(0, stacked, slice(4 * r, 6 * r))
    enc_low, n1, r1, active, slope, w_f0 = encoder_ffn(
        plan, place, first, first_low, src, ffn_w, norms, 1, [r2] + stacked
    )
    last_w, stacked = last.stack(0, [r1])
    two, two_low, n3, r3, *kept_cross = cross_attention(
        plan, place, one, one_low, enc_low, target_seg, source_seg, cross_w, norms, 3, stacked
    )
    (decoded, last_grad, norm_a, slope_f1, w_f1), grads = decoder_ffn(
        plan, place, two, two_low, tgt, cotangent[0], last_w, norms, 4
    )
    sums = Reduction(plan, odd)
    sums.add("f1d", grads)
    (two_grad, norm_d), grads = decoder_ffn_back(
        plan, place, last_grad, two_low, slope_f1, n3, r3, w_f1, norms, 3
    )
    deps = sums.advance([norm_d], ["f1d"])
    sums.add("f1u", grads)
    deps = sums.advance(deps, ["f1u"])
    (one_grad, enc_grad, norm_b), grads = cross_attention_back(
        plan, place, two_grad, one_low, enc_low, kept_cross, (n2, r2), (n1, r1), norms, (2, 1), deps
    )
    sums.add("a2", grads)
    deps = sums.advance([norm_b])
    (zero_grad, norm_c), grads = encoder_ffn_back(
        plan, place, enc_grad, first_low, active, slope, n0, r0, w_f0, norms, 0, deps
    )
    sums.add("f0", grads)
    deps = sums.advance([norm_c])
    tgt_grad, grads = self_attention_back(plan, place, one_grad, tgt, kept_self, last_grad, deps)
    sums.add("a1", grads)
    deps = sums.advance(grads[:1], ["f1u", "f1d"])
    halfway, grads = self_attention_back_values(plan, place, zero_grad, src, kept_enc, deps)
    sums.add("a0v", grads)
    deps = sums.advance([halfway[0]], never=["f1u", "f1d"])
    src_grad, grads = self_attention_back_scores(
        plan, place, zero_grad, src, kept_enc, *halfway, enc_grad, (norm_a, norm_d, norm_b, norm_c), deps
    )
    sums.add("a0", grads)
    deps = sums.advance(grads[:1], ["f1u", "f1d"])
    sums.advance(deps or grads[:1])
    while sums.pairs:
        sums.advance()
    return decoded[None], src_grad[None], tgt_grad[None], *outputs(plan, sums, place)


def after(value, deps):
    if not deps:
        return value

    def body(*refs):
        pass

    return pl.pallas_call(
        body,
        in_specs=[ANY] * (1 + len(deps)),
        out_shape=jax.ShapeDtypeStruct(value.shape, value.dtype),
        out_specs=ANY,
        input_output_aliases={0: 0},
        compiler_params=pltpu.CompilerParams(vmem_limit_bytes=1 << 20),
        cost_estimate=pl.CostEstimate(flops=0, bytes_accessed=0, transcendentals=0),
    )(value, *deps)


def solution(mesh):
    sizes = (mesh.shape["shard"], mesh.shape["rep"])
    tokens = P(("shard", "rep"), None, None)
    ids = P(("shard", "rep"), None)
    weight = P(None, "shard", None)
    norm = P(None, "shard")
    return jax.shard_map(
        functools.partial(shards, sizes),
        mesh=mesh,
        in_specs=(tokens, tokens, ids, ids, weight, weight, weight, weight, norm, norm, tokens),
        out_specs=(tokens, tokens, tokens, weight, weight, weight, weight, norm, norm),
        check_vma=False,
    )
```

```python
import functools

import jax
import jax.numpy as jnp
from jax import lax
from jax.experimental import pallas as pl
from jax.experimental.pallas import tpu as pltpu
from jax.sharding import PartitionSpec as P

HEAD = 64
PAIR = 2 * HEAD
EPS = 1e-05
NEG = -1e30
LOW = jnp.bfloat16
WIDE = jnp.float32
CORE, X, Y = 1, 2, 4
Z1, Z2 = 1, 2
SMALL = 16
NORMS = 5
VMEM = pl.BlockSpec(memory_space=pltpu.VMEM)
SMEM = pl.BlockSpec(memory_space=pltpu.SMEM)
ANY = pl.BlockSpec(memory_space=pl.ANY)


def dot(left, right):
    return lax.dot_general(left, right, (((1,), (0,)), ((), ())), preferred_element_type=WIDE)


def dot_nt(left, right):
    return lax.dot_general(left, right, (((1,), (1,)), ((), ())), preferred_element_type=WIDE)


def dot_tn(left, right):
    return lax.dot_general(left, right, (((0,), (0,)), ((), ())), preferred_element_type=WIDE)


def block(unit, i, r):
    part = unit[:, i * r : (i + 1) * r, :]
    return part.reshape(part.shape[0] * r, part.shape[2])


def rows_block(unit, i, r):
    n = unit.shape[0] // 4
    part = unit[i * n : (i + 1) * n, 4 * r :, :]
    return part.reshape(n * part.shape[1], part.shape[2])


def norm(value, gain, shift):
    mean = jnp.mean(value, axis=-1, keepdims=True)
    centred = value - mean
    scale = lax.rsqrt(jnp.mean(centred * centred, axis=-1, keepdims=True) + EPS)
    normal = centred * scale
    return normal * gain + shift, normal, scale


def norm_back(grad, normal, scale, gain):
    gain_grad = jnp.sum(grad * normal, axis=0, keepdims=True)
    shift_grad = jnp.sum(grad, axis=0, keepdims=True)
    inner = grad * gain
    inner_mean = jnp.mean(inner, axis=-1, keepdims=True)
    cross_mean = jnp.mean(inner * normal, axis=-1, keepdims=True)
    return scale * (inner - inner_mean - normal * cross_mean), gain_grad, shift_grad


def lanes_of(head, value):
    lane = lax.broadcasted_iota(jnp.int32, value.shape, 1)
    return jnp.where((lane < HEAD) if head == 0 else (lane >= HEAD), value, jnp.zeros_like(value))


def pick(first, second):
    lane = lax.broadcasted_iota(jnp.int32, first.shape, 1)
    return jnp.where(lane < HEAD, first, second)


def allowed_bias(memory_ids, query_ids, causal):
    tokens = memory_ids.shape[1]
    turned = jnp.transpose(jnp.broadcast_to(memory_ids.astype(WIDE), (PAIR, tokens)))[:, :1]
    allowed = turned == query_ids.astype(WIDE)
    if causal:
        shape = (tokens, query_ids.shape[1])
        allowed = allowed & (lax.broadcasted_iota(jnp.int32, shape, 1) >= lax.broadcasted_iota(jnp.int32, shape, 0))
    return jnp.where(allowed, 0.0, NEG)


def attend_forward(qkv, probs, mixed, bias):
    width = mixed.shape[1]
    for pair in range(width // PAIR):
        at = pl.ds(pair * PAIR, PAIR)
        query = qkv[:, pl.ds(pair * PAIR, PAIR)] * LOW(HEAD ** -0.5)
        keys = qkv[:, pl.ds(width + pair * PAIR, PAIR)]
        turned = jnp.transpose(qkv[:, pl.ds(2 * width + pair * PAIR, PAIR)])
        out = []
        for head in range(2):
            scores = dot_nt(keys, lanes_of(head, query)) + bias[...]
            top = jnp.max(scores, axis=0, keepdims=True)
            weights = jnp.exp(scores - top)
            total = jnp.sum(weights, axis=0, keepdims=True)
            low = (weights * (1.0 / total)).astype(LOW)
            probs[2 * pair + head] = low
            out.append(dot(turned[head * HEAD : (head + 1) * HEAD, :], low))
        mixed[:, at] = jnp.transpose(jnp.concatenate(out).astype(LOW))


def attend_backward(qkv, probs, mixed_grad, qkv_grad):
    width = mixed_grad.shape[1]
    for pair in range(width // PAIR):
        query = qkv[:, pl.ds(pair * PAIR, PAIR)]
        keys = qkv[:, pl.ds(width + pair * PAIR, PAIR)]
        values = qkv[:, pl.ds(2 * width + pair * PAIR, PAIR)]
        grad = mixed_grad[:, pl.ds(pair * PAIR, PAIR)]
        turned = jnp.transpose(keys)
        dq, dk, dv = [], [], []
        for head in range(2):
            low = probs[2 * pair + head]
            prob = low.astype(WIDE)
            prob_grad = dot_nt(values, lanes_of(head, grad))
            delta = jnp.sum(prob * prob_grad, axis=0, keepdims=True)
            score_grad = (prob * (prob_grad - delta)).astype(LOW)
            dv.append(dot(low, grad))
            dk.append(dot(score_grad, query))
            dq.append(dot(turned[head * HEAD : (head + 1) * HEAD, :], score_grad))
        scale = HEAD ** -0.5
        qkv_grad[:, pl.ds(pair * PAIR, PAIR)] = jnp.transpose((jnp.concatenate(dq) * scale).astype(LOW))
        qkv_grad[:, pl.ds(width + pair * PAIR, PAIR)] = (pick(*dk) * scale).astype(LOW)
        qkv_grad[:, pl.ds(2 * width + pair * PAIR, PAIR)] = pick(*dv).astype(LOW)


GELU = 0.7978845608028654


def gelu_and_slope(value):
    square = value * value
    t = jnp.tanh(value * (GELU + (GELU * 0.044715) * square))
    half = 0.5 + 0.5 * t
    slope = half + value * (0.5 - 0.5 * (t * t)) * (GELU + (3 * 0.044715 * GELU) * square)
    return value * half, slope


def ffn_forward(hidden, weight, active, slope, r):
    W = hidden.shape[1]
    total = None
    for c in range(4):
        at = pl.ds(c * W, W)
        act, sl = gelu_and_slope(dot(hidden, block(weight, c, r)))
        act = act.astype(LOW)
        active[:, at] = act
        slope[:, at] = sl.astype(LOW)
        part = dot(act, rows_block(weight, c, r))
        total = part if total is None else total + part
    return total


def ffn_backward_down(grad, active, put):
    W = grad.shape[1]
    for c in range(4):
        put(c, dot_tn(active[:, pl.ds(c * W, W)], grad).astype(LOW))


def ffn_backward_up(grad, hidden, weight, slope, r, put):
    W = grad.shape[1]
    turned = jnp.transpose(hidden)
    total = None
    for c in range(4):
        z = (dot_nt(grad, rows_block(weight, c, r)) * slope[:, pl.ds(c * W, W)].astype(WIDE)).astype(LOW)
        put(c, dot(turned, z).astype(LOW))
        part = dot_nt(z, block(weight, c, r))
        total = part if total is None else total + part
    return total


class Plan:
    def __init__(self, sizes, length, width):
        self.split = sizes == (8, 4)
        self.sizes = sizes
        self.length, self.width = length, width
        self.heads = width // HEAD
        self.shards = sizes[0]
        self.r = width // self.shards
        self.n = self.g = 2 if self.split else 1


    def lay(self, place, stacks, member, rows, unit, at):
        count = rows.stop - rows.start
        if not self.split:
            unit[:, at : at + count, :] = stacks[0][:, member, rows]
            return
        odd, chip = (place & 1) != 0, place >> 1
        for j in range(4):
            k = 2 * (j ^ chip) + member
            mine, other = stacks[0][k, rows, :], stacks[1][k, rows, :]
            unit[2 * j, at : at + count, :] = jnp.where(odd, other, mine)
            unit[2 * j + 1, at : at + count, :] = jnp.where(odd, mine, other)


    def grad_shapes(self, rows):
        if not self.split:
            return [(self.shards, 2, rows, self.width)]
        return [(8, rows, self.width)] * 2

    def leave(self, place, outs, member, at, value, first=0):
        count = value.shape[1]
        if not self.split:
            outs[0][first : first + value.shape[0], member, at : at + count, :] = value
            return
        odd, chip = (place & 1) != 0, place >> 1
        for j in range(value.shape[0] // 2):
            k = (first // 2 + j) ^ chip
            if member == 0:
                k = ((k & 1) << 1) | (k >> 1)
            one, two = value[2 * j], value[2 * j + 1]
            outs[0][4 * member + k, at : at + count, :] = jnp.where(odd, two, one)
            outs[1][4 * member + k, at : at + count, :] = jnp.where(odd, one, two)

    def leave_block(self, place, outs, member, i, value):
        self.leave(place, outs, member, i * self.r, value.reshape(self.shards, self.r, self.width))

    def leave_rows(self, place, outs, member, i, value):
        n = self.shards // 4
        self.leave(place, outs, member, 0, value.reshape(n, 4 * self.r, self.width), i * n)

    def leave_rows_halved(self, place, outs, i, value):
        n, half = self.shards // 4, 2 * self.r
        value = value.reshape(n, 4 * self.r, self.width)
        for m in range(2):
            self.leave(place, outs, m, 0, value[:, m * half : (m + 1) * half, :], i * n)

    def call(self, body, ins, outs, scratch, us, deps, room):
        def run(*refs):
            body(*refs[len(deps) :])

        return pl.pallas_call(
            run,
            in_specs=[ANY] * len(deps) + [spec for _, spec in ins],
            out_shape=[jax.ShapeDtypeStruct(shape, dtype) for shape, dtype in outs],
            out_specs=[VMEM] * len(outs),
            scratch_shapes=scratch,
            compiler_params=pltpu.CompilerParams(vmem_limit_bytes=room << 20),
            cost_estimate=pl.CostEstimate(flops=int(us * 5e9), bytes_accessed=1 << 20, transcendentals=0),
        )(*deps, *[value for value, _ in ins])


def vmem(*arrays):
    return [(v, VMEM) for v in arrays]


def self_attention(plan, place, tokens, ids, stacks, member, row, causal, deps=(), us=10):
    L, W, H, r = plan.length, plan.width, plan.heads, plan.r

    def body(place, tokens, ids, *rest):
        stacks, rest = rest[: plan.n], rest[plan.n :]
        out, out_low, normal, scale, qkv, mixed, probs, weight, norms, bias = rest
        plan.lay(place[0], stacks, member, slice(0, 4 * r), weight, 0)
        bias[...] = allowed_bias(ids[...], ids[...], causal)
        if plan.split:
            norms[...] = sum(jnp.sum(s[...].astype(WIDE), axis=0) for s in (v.at[:, 4 * r : 4 * r + SMALL, :] for v in stacks)) * 0.5
        else:
            norms[...] = jnp.sum(stacks[0][:, member, 4 * r : 4 * r + SMALL].astype(WIDE), axis=0)
        x = tokens[...]
        for i in range(3):
            qkv[:, i * W : (i + 1) * W] = dot(x, block(weight, i, r)).astype(LOW)
        attend_forward(qkv, probs, mixed, bias)
        value = x.astype(WIDE) + dot(mixed[...], block(weight, 3, r))
        y, n, s = norm(value, norms[row : row + 1, :], norms[NORMS + row : NORMS + row + 1, :])
        out[...] = y
        out_low[...] = y.astype(LOW)
        normal[...] = n.astype(LOW)
        scale[...] = s

    ins = [(place, SMEM)] + vmem(tokens, ids, *stacks)
    outs = [((L, W), WIDE), ((L, W), LOW), ((L, W), LOW), ((L, 1), WIDE)]
    outs += [((L, 3 * W), LOW), ((L, W), LOW), ((H, L, L), LOW), ((plan.shards, 4 * r, W), LOW), ((SMALL, W), WIDE)]
    return plan.call(body, ins, outs, [pltpu.VMEM((L, L), WIDE)], us, deps, 11)


def cross_attention(plan, place, query_in, query_low, memory_low, query_ids, memory_ids, stacks, norms, row, deps=()):
    L, W, H, r = plan.length, plan.width, plan.heads, plan.r

    def body(place, query_in, query_low, memory_low, query_ids, memory_ids, norms, *rest):
        stacks, rest = rest[: plan.n], rest[plan.n :]
        out, out_low, normal, scale, qkv, mixed, probs, weight, bias = rest
        for m in range(2):
            plan.lay(place[0], stacks, m, slice(0, 2 * r), weight, 2 * m * r)
        bias[...] = allowed_bias(memory_ids[...], query_ids[...], False)
        qkv[:, :W] = dot(query_low[...], block(weight, 0, r)).astype(LOW)
        memory = memory_low[...]
        for i in (1, 2):
            qkv[:, i * W : (i + 1) * W] = dot(memory, block(weight, i, r)).astype(LOW)
        attend_forward(qkv, probs, mixed, bias)
        value = query_in[...] + dot(mixed[...], block(weight, 3, r))
        y, n, s = norm(value, norms[row : row + 1, :], norms[NORMS + row : NORMS + row + 1, :])
        out[...] = y
        out_low[...] = y.astype(LOW)
        normal[...] = n.astype(LOW)
        scale[...] = s

    ins = [(place, SMEM)] + vmem(query_in, query_low, memory_low, query_ids, memory_ids, norms, *stacks)
    outs = [((L, W), WIDE), ((L, W), LOW), ((L, W), LOW), ((L, 1), WIDE)]
    outs += [((L, 3 * W), LOW), ((L, W), LOW), ((H, L, L), LOW), ((plan.shards, 4 * r, W), LOW)]
    return plan.call(body, ins, outs, [pltpu.VMEM((L, L), WIDE)], 10, deps, 11)


def encoder_ffn(plan, place, hidden, hidden_low, tokens, stacks, norms, row, deps=()):
    L, W, F, r = plan.length, plan.width, 4 * plan.width, plan.r

    def body(place, hidden, hidden_low, tokens, norms, *rest):
        stacks, rest = rest[: plan.n], rest[plan.n :]
        out_low, normal, scale, active, slope, weight = rest
        for m in range(2):
            plan.lay(place[0], stacks, m, slice(0, 4 * r), weight, 4 * m * r)
        branch = ffn_forward(hidden_low[...], weight, active, slope, r)
        value = hidden[...] + branch + tokens[...].astype(WIDE)
        y, n, s = norm(value, norms[row : row + 1, :], norms[NORMS + row : NORMS + row + 1, :])
        out_low[...] = y.astype(LOW)
        normal[...] = n.astype(LOW)
        scale[...] = s

    ins = [(place, SMEM)] + vmem(hidden, hidden_low, tokens, norms, *stacks)
    outs = [((L, W), LOW), ((L, W), LOW), ((L, 1), WIDE), ((L, F), LOW), ((L, F), LOW), ((plan.shards, 8 * r, W), LOW)]
    return plan.call(body, ins, outs, [], 9, deps, 11)


def decoder_ffn(plan, place, hidden, hidden_low, tokens, cotangent, stacks, norms, row, deps=()):
    L, W, F, r = plan.length, plan.width, 4 * plan.width, plan.r

    def body(place, hidden, hidden_low, tokens, cotangent, norms, *rest):
        stacks, rest = rest[: plan.n], rest[plan.n :]
        decoded, last_grad, norm_grads, slope, weight, *grads, active = rest
        for m in range(2):
            plan.lay(place[0], stacks, m, slice(0, 4 * r), weight, 4 * m * r)
        branch = ffn_forward(hidden_low[...], weight, active, slope, r)
        value = hidden[...] + branch + tokens[...].astype(WIDE)
        gain = norms[row : row + 1, :]
        y, n, s = norm(value, gain, norms[NORMS + row : NORMS + row + 1, :])
        decoded[...] = y.astype(LOW)
        grad, gain_grad, shift_grad = norm_back(cotangent[...].astype(WIDE), n, s, gain)
        last_grad[...] = grad
        norm_grads[0:1, :] = gain_grad
        norm_grads[1:2, :] = shift_grad
        ffn_backward_down(grad.astype(LOW), active, lambda i, v: plan.leave_rows_halved(place[0], grads, i, v))

    ins = [(place, SMEM)] + vmem(hidden, hidden_low, tokens, cotangent, norms, *stacks)
    outs = [((L, W), LOW), ((L, W), WIDE), ((2, W), WIDE), ((L, F), LOW), ((plan.shards, 8 * r, W), LOW)]
    outs += [(s, LOW) for s in plan.grad_shapes(2 * r)]
    got = plan.call(body, ins, outs, [pltpu.VMEM((L, F), LOW)], 12, deps, 16)
    return got[:5], got[5:]


def decoder_ffn_back(plan, place, grad, hidden_low, slope, hidden_normal, hidden_scale, weight, norms, row, deps=()):
    L, W, r = plan.length, plan.width, plan.r

    def body(place, grad, hidden_low, slope, hidden_normal, hidden_scale, weight, norms, out, norm_grads, *grads):
        def put(i, value):
            plan.leave(place[0], grads, i // 2, (i % 2) * r, value.reshape(plan.shards, r, W))

        back = ffn_backward_up(grad[...].astype(LOW), hidden_low[...], weight, slope, r, put)
        normal = hidden_normal[...].astype(WIDE)
        total, gain_grad, shift_grad = norm_back(grad[...] + back, normal, hidden_scale[...], norms[row : row + 1, :])
        out[...] = total
        norm_grads[0:1, :] = gain_grad
        norm_grads[1:2, :] = shift_grad

    ins = [(place, SMEM)] + vmem(grad, hidden_low, slope, hidden_normal, hidden_scale, weight, norms)
    outs = [((L, W), WIDE), ((2, W), WIDE)] + [(s, LOW) for s in plan.grad_shapes(2 * r)]
    got = plan.call(body, ins, outs, [], 8, deps, 12)
    return got[:2], got[2:]


def encoder_ffn_back(plan, place, grad, hidden_low, active, slope, hidden_normal, hidden_scale, weight, norms, row, deps=()):
    L, W, r = plan.length, plan.width, plan.r

    def body(place, grad, hidden_low, active, slope, hidden_normal, hidden_scale, weight, norms, *rest):
        zero_grad, norm_grads, *grads = rest
        grad_low = grad[...].astype(LOW)
        ffn_backward_down(grad_low, active, lambda i, v: plan.leave_rows(place[0], grads, 1, i, v))
        back = ffn_backward_up(
            grad_low, hidden_low[...], weight, slope, r, lambda i, v: plan.leave_block(place[0], grads, 0, i, v)
        )
        normal = hidden_normal[...].astype(WIDE)
        out, gain_grad, shift_grad = norm_back(grad[...] + back, normal, hidden_scale[...], norms[row : row + 1, :])
        zero_grad[...] = out
        norm_grads[0:1, :] = gain_grad
        norm_grads[1:2, :] = shift_grad

    ins = [(place, SMEM)] + vmem(grad, hidden_low, active, slope, hidden_normal, hidden_scale, weight, norms)
    outs = [((L, W), WIDE), ((2, W), WIDE)] + [(s, LOW) for s in plan.grad_shapes(4 * r)]
    got = plan.call(body, ins, outs, [], 11, deps, 14)
    return got[:2], got[2:]


def self_attention_back(plan, place, grad, tokens, kept, extra, deps=()):
    L, W, r = plan.length, plan.width, plan.r

    def body(place, grad, extra, tokens, qkv, mixed, probs, weight, *rest):
        total, *grads, mixed_grad, qkv_grad = rest
        grad_low = grad[...].astype(LOW)
        plan.leave_block(place[0], grads, 1, 1, dot_tn(mixed[...], grad_low).astype(LOW))
        mixed_grad[...] = dot_nt(grad_low, block(weight, 3, r)).astype(LOW)
        attend_backward(qkv, probs, mixed_grad, qkv_grad)
        x = jnp.transpose(tokens[...])
        for i in range(3):
            plan.leave_block(place[0], grads, i // 2, i % 2, dot(x, qkv_grad[:, i * W : (i + 1) * W]).astype(LOW))
        back = grad[...] + extra[...]
        for i in range(3):
            back += dot_nt(qkv_grad[:, i * W : (i + 1) * W], block(weight, i, r))
        total[...] = back

    ins = [(place, SMEM)] + vmem(grad, extra, tokens, *kept)
    outs = [((L, W), WIDE)] + [(s, LOW) for s in plan.grad_shapes(2 * r)]
    scratch = [pltpu.VMEM((L, W), LOW), pltpu.VMEM((L, 3 * W), LOW)]
    got = plan.call(body, ins, outs, scratch, 12, deps, 12)
    return got[0], got[1:]


def attend_backward_values(probs, mixed_grad, value_grad):
    for pair in range(mixed_grad.shape[1] // PAIR):
        at = pl.ds(pair * PAIR, PAIR)
        grad = mixed_grad[:, at]
        value_grad[:, at] = pick(*[dot(probs[2 * pair + head], grad) for head in range(2)]).astype(LOW)


def self_attention_back_values(plan, place, grad, tokens, kept, deps=()):
    L, W, r = plan.length, plan.width, plan.r
    _, mixed, probs, weight = kept

    def body(place, grad, tokens, mixed, probs, weight, mixed_grad, value_grad, *grads):
        grad_low = grad[...].astype(LOW)
        plan.leave_block(place[0], grads, 1, 0, dot_tn(mixed[...], grad_low).astype(LOW))
        mixed_grad[...] = dot_nt(grad_low, block(weight, 3, r)).astype(LOW)
        attend_backward_values(probs, mixed_grad, value_grad)
        plan.leave_block(place[0], grads, 0, 0, dot_tn(tokens[...], value_grad[...]).astype(LOW))

    ins = [(place, SMEM)] + vmem(grad, tokens, mixed, probs, weight)
    outs = [((L, W), LOW), ((L, W), LOW)] + [(s, LOW) for s in plan.grad_shapes(r)]
    got = plan.call(body, ins, outs, [], 6, deps, 12)
    return got[:2], got[2:]


def self_attention_back_scores(plan, place, grad, tokens, kept, mixed_grad, value_grad, extra, small, deps=()):
    L, W, r = plan.length, plan.width, plan.r
    qkv, _, probs, weight = kept

    def body(place, grad, extra, tokens, qkv, probs, weight, mixed_grad, value_grad, *rest):
        parts, (total, *grads, score_grads) = rest[:4], rest[4:]
        for m in range(2):
            rows = [parts[j][i + m : i + m + 1, :] for j, i in ((3, 0), (2, 2), (2, 0), (1, 0), (0, 0))]
            rows = jnp.concatenate(rows + [jnp.zeros((SMALL - NORMS, W), WIDE)]).astype(LOW)[None]
            plan.leave(place[0], grads, m, r, jnp.broadcast_to(rows, (plan.shards, SMALL, W)))
        scale = HEAD ** -0.5
        for pair in range(W // PAIR):
            at = pl.ds(pair * PAIR, PAIR)
            query, keys = qkv[:, at], qkv[:, pl.ds(W + pair * PAIR, PAIR)]
            values, out_grad = qkv[:, pl.ds(2 * W + pair * PAIR, PAIR)], mixed_grad[:, at]
            turned = jnp.transpose(keys)
            dq, dk = [], []
            for head in range(2):
                prob = probs[2 * pair + head].astype(WIDE)
                prob_grad = dot_nt(values, lanes_of(head, out_grad))
                delta = jnp.sum(prob * prob_grad, axis=0, keepdims=True)
                score_grad = (prob * (prob_grad - delta)).astype(LOW)
                dk.append(dot(score_grad, query))
                dq.append(dot(turned[head * HEAD : (head + 1) * HEAD, :], score_grad))
            score_grads[:, at] = jnp.transpose((jnp.concatenate(dq) * scale).astype(LOW))
            score_grads[:, pl.ds(W + pair * PAIR, PAIR)] = (pick(*dk) * scale).astype(LOW)
        x = jnp.transpose(tokens[...])
        back = grad[...] + extra[...] + dot_nt(value_grad[...], block(weight, 2, r))
        for i in range(2):
            part = score_grads[:, i * W : (i + 1) * W]
            plan.leave_block(place[0], grads, i, 0, dot(x, part).astype(LOW))
            back += dot_nt(part, block(weight, i, r))
        total[...] = back

    ins = [(place, SMEM)] + vmem(grad, extra, tokens, qkv, probs, weight, mixed_grad, value_grad, *small)
    outs = [((L, W), WIDE)] + [(s, LOW) for s in plan.grad_shapes(r + SMALL)]
    got = plan.call(body, ins, outs, [pltpu.VMEM((L, 2 * W), LOW)], 10, deps, 12)
    return got[0], got[1:]


def cross_attention_back(plan, place, grad, query_low, memory_low, kept, query_norm, memory_norm, norms, rows, deps=()):
    L, W, r = plan.length, plan.width, plan.r

    def body(place, grad, query_low, memory_low, qkv, mixed, probs, weight, query_n, query_r, memory_n, memory_r, norms, *rest):
        one_grad, enc_grad, norm_grads, *grads, mixed_grad, qkv_grad = rest
        grad_low = grad[...].astype(LOW)
        plan.leave_block(place[0], grads, 1, 1, dot_tn(mixed[...], grad_low).astype(LOW))
        mixed_grad[...] = dot_nt(grad_low, block(weight, 3, r)).astype(LOW)
        attend_backward(qkv, probs, mixed_grad, qkv_grad)
        plan.leave_block(place[0], grads, 0, 0, dot_tn(query_low[...], qkv_grad[:, :W]).astype(LOW))
        memory = jnp.transpose(memory_low[...])
        for i in (1, 2):
            value = dot(memory, qkv_grad[:, i * W : (i + 1) * W]).astype(LOW)
            plan.leave_block(place[0], grads, i // 2, i % 2, value)
        back = grad[...] + dot_nt(qkv_grad[:, :W], block(weight, 0, r))
        normal = query_n[...].astype(WIDE)
        out, gain_grad, shift_grad = norm_back(back, normal, query_r[...], norms[rows[0] : rows[0] + 1, :])
        one_grad[...] = out
        norm_grads[0:1, :] = gain_grad
        norm_grads[1:2, :] = shift_grad
        back = dot_nt(qkv_grad[:, W : 2 * W], block(weight, 1, r)) + dot_nt(qkv_grad[:, 2 * W :], block(weight, 2, r))
        normal = memory_n[...].astype(WIDE)
        out, gain_grad, shift_grad = norm_back(back, normal, memory_r[...], norms[rows[1] : rows[1] + 1, :])
        enc_grad[...] = out
        norm_grads[2:3, :] = gain_grad
        norm_grads[3:4, :] = shift_grad

    ins = [(place, SMEM)] + vmem(grad, query_low, memory_low, *kept, *query_norm, *memory_norm, norms)
    outs = [((L, W), WIDE), ((L, W), WIDE), ((4, W), WIDE)] + [(s, LOW) for s in plan.grad_shapes(2 * r)]
    scratch = [pltpu.VMEM((L, W), LOW), pltpu.VMEM((L, 3 * W), LOW)]
    got = plan.call(body, ins, outs, scratch, 0.05, deps, 13)
    return got[:3], got[3:]


def swap(value, bit):
    return lax.ppermute(value, "shard", [(i, i ^ bit) for i in range(8)])


def swap_rep(value, bit):
    return lax.ppermute(value, "rep", [(i, i ^ bit) for i in range(4)])


def local(body, ins, outs, deps=(), room=6, us=0):
    ins = [v if isinstance(v, tuple) else (v, VMEM) for v in ins]

    def run(*refs):
        body(*refs[len(deps) :])

    return pl.pallas_call(
        run,
        in_specs=[ANY] * len(deps) + [spec for _, spec in ins],
        out_shape=[jax.ShapeDtypeStruct(shape, dtype) for shape, dtype in outs],
        out_specs=[VMEM] * len(outs),
        compiler_params=pltpu.CompilerParams(vmem_limit_bytes=room << 20),
        cost_estimate=pl.CostEstimate(flops=int(us * 5e9), bytes_accessed=1 << 20, transcendentals=0),
    )(*deps, *[v for v, _ in ins])


def mark(out):
    out[...] = jnp.zeros_like(out)


def wait_for(plan, deps, us):
    return local(mark, [], [((8, 128), WIDE)], deps, 2, us) if plan.split else []


def pack_self(plan, attn_in, attn_out, small, odd):
    W, r = plan.width, plan.r

    def body(attn_in, attn_out, small, odd, out):
        for k in range(2):
            for i in range(3):
                out[k, i * r : (i + 1) * r, :] = attn_in[k, :, i * W : (i + 1) * W]
            out[k, 3 * r : 4 * r, :] = attn_out[k]
            out[k, 4 * r :, :] = small[...]

    return local(body, [attn_in, attn_out, small, (odd, SMEM)], [((2, 4 * r + SMALL, W), LOW)])[0]


def pack_rest(plan, attn_in, attn_out, ffn_up, ffn_down, deps):
    W, r = plan.width, plan.r

    def body(attn_in, attn_out, ffn_up, ffn_down, first, second):
        for k, out in enumerate((first, second)):
            for i in range(4):
                out[0, i * r : (i + 1) * r, :] = ffn_up[k, :, i * W : (i + 1) * W]
            out[1, : 4 * r] = ffn_down[k]
        for i in range(3):
            at = (4 + i % 2) * r
            first[i // 2, at : at + r, :] = attn_in[2, :, i * W : (i + 1) * W]
        first[1, 5 * r :, :] = attn_out[2]

    outs = [((2, 6 * r, W), LOW), ((2, 4 * r, W), LOW)]
    return local(body, [attn_in, attn_out, ffn_up, ffn_down], outs, deps)


class Gather:
    def __init__(self, plan, pair, parts):
        self.plan, self.pair, self.parts = plan, pair, parts
        self.ends = [sum(parts[: i + 1]) for i in range(len(parts))]
        if plan.split:
            self.near = [swap(pair, X), swap(pair, Y)]

    def onward(self, deps=()):
        if not self.plan.split:
            return []
        parts, ends = self.parts, self.ends

        def body(by_x, by_y, *outs):
            for i, (rows, end) in enumerate(zip(parts, ends)):
                outs[2 * i][...] = by_x[0, end - rows : end, :]
                outs[2 * i + 1][...] = by_y[1, end - rows : end, :]

        outs = local(body, self.near, [((rows, self.plan.width), LOW) for rows in parts for _ in range(2)], deps)
        self.far = [(swap(outs[2 * i], Y), swap(outs[2 * i + 1], X)) for i in range(len(parts))]
        return [outs[0]]

    def stack(self, part, deps=(), within=None):
        rows, end = self.parts[part], self.ends[part]
        within = within or slice(0, rows)
        at = slice(end - rows + within.start, end - rows + within.stop)
        rows = within.stop - within.start
        if not self.plan.split:
            return [lax.all_gather(self.pair[:, at], "shard", axis=0)], []

        def body(pair, by_x, by_y, first, second, out):
            for j, v in enumerate((pair, by_x, by_y)):
                out[2 * j : 2 * j + 2] = v[:, at, :]
            out[6] = first[within, :]
            out[7] = second[within, :]

        ins = [self.pair, *self.near, *self.far[part]]
        mine = local(body, ins, [((8, rows, self.plan.width), LOW)], deps)[0]
        return [mine, swap(mine, CORE)], [mine]


class Reduction:
    def __init__(self, plan, odd):
        self.plan, self.odd = plan, odd
        self.pairs, self.results = [], {}

    def add(self, name, outs):
        if not self.plan.split:
            whole = outs[0]
            flat = whole.reshape((-1,) + whole.shape[2:])
            own = lax.psum_scatter(flat, "shard", scatter_dimension=0, tiled=True)
            self.results[name] = lax.psum(own, "rep").astype(WIDE).reshape(whole.shape[1:])
            return
        mine, other = outs
        self.pairs.append(dict(name=name, rows=mine.shape[1], step=0, keep=mine, slot={}, moving={}, got=swap(other, CORE)))

    def advance(self, deps=(), only=(), never=()):
        pairs = [p for p in self.pairs if (not only or p["name"] in only) and p["name"] not in never]
        if not pairs:
            return []
        self.pairs = [p for p in self.pairs if p not in pairs]
        W = self.plan.width
        sizes = {"x": 0, "y": 0, "n": 0, "f": 0}

        def place(way, count):
            at = sizes[way]
            sizes[way] += count
            return at

        work = []
        for p in pairs:
            R, step = p["rows"], p["step"]
            ways = ({"x": 2 * R, "y": 2 * R}, {"x": R, "y": R}, {"n": R}, {"f": R}, {"n": R}, {})[step]
            work.append(dict(p, out={way: place(way, count) for way, count in ways.items()}, kept=((4, 2, 1, 1, 1, 2)[step] * R, W)))
        ways = [w for w in "xynf" if sizes[w]]
        came = []
        for p in pairs:
            came += [v for v in p["moving"].values() if not any(v is u for u in came)]
        cores = [t for t in work if t["step"] == 0]

        def body(odd, *refs):
            keep_in, refs = refs[: len(work)], refs[len(work) :]
            core_in, refs = refs[: len(cores)], refs[len(cores) :]
            arrived, refs = refs[: len(came)], refs[len(came) :]
            keep_out, refs = refs[: len(work)], refs[len(work) :]
            leave = dict(zip(ways, refs))
            odds = odd[0] != 0

            def total(left, right):
                return left + right

            core = iter(core_in)
            for t, keep, out in zip(work, keep_in, keep_out):
                R, step, slot, to = t["rows"], t["step"], t["slot"], t["out"]
                got = {w: arrived[[v is u for u in came].index(True)] for w, v in t["moving"].items() if w in slot}
                if step == 0:
                    other = next(core)
                    for m, way in enumerate("xy"):
                        at = 4 * m * R
                        out[2 * m * R : 2 * (m + 1) * R, :] = total(keep[at : at + 2 * R, :], other[at : at + 2 * R, :])
                        at += 2 * R
                        leave[way][to[way] : to[way] + 2 * R, :] = total(keep[at : at + 2 * R, :], other[at : at + 2 * R, :])
                elif step == 1:
                    for m, (way, onward) in enumerate(("xy", "yx")):
                        other, at, kept = got[way], slot[way], 2 * m * R
                        out[m * R : (m + 1) * R, :] = total(keep[kept : kept + R, :], other[at : at + R, :])
                        kept, at = kept + R, at + R
                        leave[onward][to[onward] : to[onward] + R, :] = total(keep[kept : kept + R, :], other[at : at + R, :])
                elif step == 2:
                    first = total(keep[:R, :], got["y"][slot["y"] : slot["y"] + R, :])
                    second = total(keep[R:, :], got["x"][slot["x"] : slot["x"] + R, :])
                    out[...] = jnp.where(odds, second, first)
                    leave["n"][to["n"] : to["n"] + R, :] = jnp.where(odds, first, second)
                elif step == 5:
                    mine, other = keep[...], got["n"][slot["n"] : slot["n"] + R, :]
                    out[:R, :] = jnp.where(odds, other, mine)
                    out[R:, :] = jnp.where(odds, mine, other)
                else:
                    way, onward = ("n", "f") if step == 3 else ("f", "n")
                    value = total(keep[...], got[way][slot[way] : slot[way] + R, :])
                    out[...] = value
                    leave[onward][to[onward] : to[onward] + R, :] = value

        if cores and came:
            last = [v for p in pairs if p["step"] == 5 for v in p["moving"].values()]
            if last:
                deps = wait_for(self.plan, [*deps, *[v for v in came if not any(v is u for u in last)]], 2)
            deps = wait_for(self.plan, [*deps, *came], 20)
        keeps = [t["keep"].reshape(-1, W) for t in work]
        gots = [t["got"].reshape(-1, W) for t in cores]
        outs = [(t["kept"], LOW) for t in work] + [((sizes[w], W), LOW) for w in ways]
        done = local(body, [(self.odd, SMEM), *keeps, *gots, *came], outs, deps)
        moving = {}
        for way, value in zip(ways, done[len(work) :]):
            moving[way] = swap_rep(value, Z1 if way == "n" else Z2) if way in "nf" else swap(value, X if way == "x" else Y)
        for t, kept in zip(work, done):
            if t["step"] == 5:
                self.results[t["name"]] = (kept, None, 0)
            elif t["step"] == 4 and t["name"] not in FINISHED:
                self.results[t["name"]] = (kept, moving["n"], t["out"]["n"])
            else:
                mine = {w: v for w, v in moving.items() if w in t["out"]}
                self.pairs.append(dict(name=t["name"], rows=t["rows"], step=t["step"] + 1, keep=kept, slot=t["out"], moving=mine))
        return [done[0]]


FINISHED = ("f1u", "f1d")
NAMES = ("a0", "a0v", "a1", "a2", "f0", "f1u", "f1d")


def outputs(plan, sums, place):
    W, r = plan.width, plan.r
    wide = W // plan.shards
    results = sums.results
    if not plan.split:
        me = lax.axis_index("shard")
        scores, small = results["a0"][:, :r], results["a0"][:, r:]
        small = lax.dynamic_slice(small, (0, 0, me * wide), (2, NORMS, wide))
        att = [jnp.concatenate([scores, results["a0v"]]), *(results[k].reshape(4, r, W) for k in ("a1", "a2"))]
        att, ffn = jnp.stack(att), jnp.stack([results["f0"], jnp.stack([results[k].reshape(4 * r, W) for k in ("f1u", "f1d")])])

        def unblocks(v):
            return jnp.moveaxis(v, 1, 2).reshape(v.shape[0], r, -1)

        return unblocks(att[:, :3]), att[:, 3], unblocks(ffn[:, 0].reshape(2, 4, r, W)), ffn[:, 1], small[0], small[1]
    keeps = [results[k][0] for k in NAMES]
    gots = []
    for k in NAMES:
        if k not in FINISHED and not any(results[k][1] is v for v in gots):
            gots.append(results[k][1])

    def body(odd, place, *refs):
        keep, refs = refs[: len(NAMES)], refs[len(NAMES) :]
        got, refs = refs[: len(gots)], refs[len(gots) :]
        attn_in, attn_out, ffn_up, ffn_down, gain, shift = refs
        odds = odd[0] != 0

        def member(name, m, at, rows):
            _, array, offset = results[name]
            i = NAMES.index(name)
            if name in FINISHED:
                at += m * (keep[i].shape[0] // 2)
                return keep[i][at : at + rows, :].astype(WIDE)
            j = [v is array for v in gots].index(True)
            kept, other = keep[i][at : at + rows, :], got[j][offset + at : offset + at + rows, :]
            return (jnp.where(odds, other, kept) if m == 0 else jnp.where(odds, kept, other)).astype(WIDE)

        for i in range(2):
            attn_in[0, :, i * W : (i + 1) * W] = member("a0", i, 0, r)
        attn_in[0, :, 2 * W :] = member("a0v", 0, 0, r)
        attn_out[0] = member("a0v", 1, 0, r)
        for a, name in ((1, "a1"), (2, "a2")):
            for i in range(3):
                attn_in[a, :, i * W : (i + 1) * W] = member(name, i // 2, (i % 2) * r, r)
            attn_out[a] = member(name, 1, r, r)
        for i in range(4):
            ffn_up[0, :, i * W : (i + 1) * W] = member("f0", 0, i * r, r)
            ffn_up[1, :, i * W : (i + 1) * W] = member("f1u", i // 2, (i % 2) * r, r)
        ffn_down[0] = member("f0", 1, 0, 4 * r)
        for m in range(2):
            ffn_down[1, 2 * m * r : 2 * (m + 1) * r] = member("f1d", m, 0, 2 * r)
        turn = lax.rem(W - place[0] * wide, W)
        for m, out in enumerate((gain, shift)):
            out[...] = pltpu.roll(member("a0", m, r, SMALL), turn, axis=1)[:NORMS, :wide]

    outs = [((3, r, 3 * W), WIDE), ((3, r, W), WIDE), ((2, r, 4 * W), WIDE), ((2, 4 * r, W), WIDE)] + [((NORMS, wide), WIDE)] * 2
    return local(body, [(sums.odd, SMEM), (place, SMEM), *keeps, *gots], outs, room=16)


def shards(sizes, source, target, source_seg, target_seg, attn_in, attn_out, ffn_up, ffn_down, norm_gain, norm_bias, cotangent):
    plan = Plan(sizes, source.shape[1], source.shape[2])
    W, r = plan.width, plan.r
    me = lax.axis_index("shard")
    place = (me if plan.split else jnp.zeros_like(me))[None]
    src, tgt = source[0], target[0]

    small = jnp.concatenate([norm_gain, norm_bias])
    small = lax.dynamic_update_slice(jnp.zeros((SMALL, W), LOW), small, (0, me * small.shape[1]))
    odd = (lax.axis_index("rep") & 1).astype(jnp.int32)[None]
    pair = pack_self(plan, attn_in, attn_out, small, odd)
    att = Gather(plan, pair, (4 * r + SMALL,))
    rest_pair, last_pair = pack_rest(plan, attn_in, attn_out, ffn_up, ffn_down, [pair])
    rest = Gather(plan, rest_pair, (6 * r,))
    went = att.onward()
    went = rest.onward(wait_for(plan, went, 4))
    last = Gather(plan, after(last_pair, went), (4 * r,))
    self_w, stacked = att.stack(0, went)
    first, first_low, n0, r0, *kept_enc, norms = self_attention(
        plan, place, src, source_seg, self_w, 0, 0, False, wait_for(plan, stacked, 6), 0.05
    )
    one, one_low, n2, r2, *kept_self, _ = self_attention(
        plan, place, tgt, target_seg, self_w, 1, 2, True, [r0], 10
    )
    went = last.onward([r2])
    ffn_w, stacked = rest.stack(0, went, slice(0, 4 * r))
    cross_w, stacked = rest.stack(0, stacked, slice(4 * r, 6 * r))
    enc_low, n1, r1, active, slope, w_f0 = encoder_ffn(
        plan, place, first, first_low, src, ffn_w, norms, 1, [r2] + stacked
    )
    last_w, stacked = last.stack(0, [r1])
    two, two_low, n3, r3, *kept_cross = cross_attention(
        plan, place, one, one_low, enc_low, target_seg, source_seg, cross_w, norms, 3, stacked
    )
    (decoded, last_grad, norm_a, slope_f1, w_f1), grads = decoder_ffn(
        plan, place, two, two_low, tgt, cotangent[0], last_w, norms, 4
    )
    sums = Reduction(plan, odd)
    sums.add("f1d", grads)
    (two_grad, norm_d), grads = decoder_ffn_back(
        plan, place, last_grad, two_low, slope_f1, n3, r3, w_f1, norms, 3
    )
    deps = sums.advance([norm_d], ["f1d"])
    sums.add("f1u", grads)
    deps = sums.advance(deps, ["f1u"])
    (one_grad, enc_grad, norm_b), grads = cross_attention_back(
        plan, place, two_grad, one_low, enc_low, kept_cross, (n2, r2), (n1, r1), norms, (2, 1), deps
    )
    sums.add("a2", grads)
    deps = sums.advance([norm_b])
    (zero_grad, norm_c), grads = encoder_ffn_back(
        plan, place, enc_grad, first_low, active, slope, n0, r0, w_f0, norms, 0, deps
    )
    sums.add("f0", grads)
    deps = sums.advance([norm_c])
    tgt_grad, grads = self_attention_back(plan, place, one_grad, tgt, kept_self, last_grad, deps)
    sums.add("a1", grads)
    deps = sums.advance(grads[:1], ["f1u", "f1d"])
    halfway, grads = self_attention_back_values(plan, place, zero_grad, src, kept_enc, deps)
    sums.add("a0v", grads)
    deps = sums.advance([halfway[0]], never=["f1u", "f1d"])
    src_grad, grads = self_attention_back_scores(
        plan, place, zero_grad, src, kept_enc, *halfway, enc_grad, (norm_a, norm_d, norm_b, norm_c), deps
    )
    sums.add("a0", grads)
    deps = sums.advance(grads[:1], ["f1u", "f1d"])
    sums.advance(deps or grads[:1])
    while sums.pairs:
        sums.advance()
    return decoded[None], src_grad[None], tgt_grad[None], *outputs(plan, sums, place)


def after(value, deps):
    if not deps:
        return value

    def body(*refs):
        pass

    return pl.pallas_call(
        body,
        in_specs=[ANY] * (1 + len(deps)),
        out_shape=jax.ShapeDtypeStruct(value.shape, value.dtype),
        out_specs=ANY,
        input_output_aliases={0: 0},
        compiler_params=pltpu.CompilerParams(vmem_limit_bytes=1 << 20),
        cost_estimate=pl.CostEstimate(flops=0, bytes_accessed=0, transcendentals=0),
    )(value, *deps)


def solution(mesh):
    sizes = (mesh.shape["shard"], mesh.shape["rep"])
    tokens = P(("shard", "rep"), None, None)
    ids = P(("shard", "rep"), None)
    weight = P(None, "shard", None)
    norm = P(None, "shard")
    return jax.shard_map(
        functools.partial(shards, sizes),
        mesh=mesh,
        in_specs=(tokens, tokens, ids, ids, weight, weight, weight, weight, norm, norm, tokens),
        out_specs=(tokens, tokens, tokens, weight, weight, weight, weight, norm, norm),
        check_vma=False,
    )
```

```python
import functools

import jax
import jax.numpy as jnp
from jax import lax
from jax.experimental import pallas as pl
from jax.experimental.pallas import tpu as pltpu
from jax.sharding import PartitionSpec as P

HEAD = 64
PAIR = 2 * HEAD
EPS = 1e-05
NEG = -1e30
LOW = jnp.bfloat16
WIDE = jnp.float32
CORE, X, Y = 1, 2, 4
Z1, Z2 = 1, 2
SMALL = 16
NORMS = 5
VMEM = pl.BlockSpec(memory_space=pltpu.VMEM)
SMEM = pl.BlockSpec(memory_space=pltpu.SMEM)
ANY = pl.BlockSpec(memory_space=pl.ANY)


def dot(left, right):
    return lax.dot_general(left, right, (((1,), (0,)), ((), ())), preferred_element_type=WIDE)


def dot_nt(left, right):
    return lax.dot_general(left, right, (((1,), (1,)), ((), ())), preferred_element_type=WIDE)


def dot_tn(left, right):
    return lax.dot_general(left, right, (((0,), (0,)), ((), ())), preferred_element_type=WIDE)


def block(unit, i, r):
    part = unit[:, i * r : (i + 1) * r, :]
    return part.reshape(part.shape[0] * r, part.shape[2])


def rows_block(unit, i, r):
    n = unit.shape[0] // 4
    part = unit[i * n : (i + 1) * n, 4 * r :, :]
    return part.reshape(n * part.shape[1], part.shape[2])


def norm(value, gain, shift):
    mean = jnp.mean(value, axis=-1, keepdims=True)
    centred = value - mean
    scale = lax.rsqrt(jnp.mean(centred * centred, axis=-1, keepdims=True) + EPS)
    normal = centred * scale
    return normal * gain + shift, normal, scale


def norm_back(grad, normal, scale, gain):
    gain_grad = jnp.sum(grad * normal, axis=0, keepdims=True)
    shift_grad = jnp.sum(grad, axis=0, keepdims=True)
    inner = grad * gain
    inner_mean = jnp.mean(inner, axis=-1, keepdims=True)
    cross_mean = jnp.mean(inner * normal, axis=-1, keepdims=True)
    return scale * (inner - inner_mean - normal * cross_mean), gain_grad, shift_grad


def lanes_of(head, value):
    lane = lax.broadcasted_iota(jnp.int32, value.shape, 1)
    return jnp.where((lane < HEAD) if head == 0 else (lane >= HEAD), value, jnp.zeros_like(value))


def pick(first, second):
    lane = lax.broadcasted_iota(jnp.int32, first.shape, 1)
    return jnp.where(lane < HEAD, first, second)


def allowed_bias(memory_ids, query_ids, causal):
    tokens = memory_ids.shape[1]
    turned = jnp.transpose(jnp.broadcast_to(memory_ids.astype(WIDE), (PAIR, tokens)))[:, :1]
    allowed = turned == query_ids.astype(WIDE)
    if causal:
        shape = (tokens, query_ids.shape[1])
        allowed = allowed & (lax.broadcasted_iota(jnp.int32, shape, 1) >= lax.broadcasted_iota(jnp.int32, shape, 0))
    return jnp.where(allowed, 0.0, NEG)


def attend_forward(qkv, probs, mixed, bias):
    width = mixed.shape[1]
    for pair in range(width // PAIR):
        at = pl.ds(pair * PAIR, PAIR)
        query = qkv[:, pl.ds(pair * PAIR, PAIR)] * LOW(HEAD ** -0.5)
        keys = qkv[:, pl.ds(width + pair * PAIR, PAIR)]
        turned = jnp.transpose(qkv[:, pl.ds(2 * width + pair * PAIR, PAIR)])
        out = []
        for head in range(2):
            scores = dot_nt(keys, lanes_of(head, query)) + bias[...]
            top = jnp.max(scores, axis=0, keepdims=True)
            weights = jnp.exp(scores - top)
            total = jnp.sum(weights, axis=0, keepdims=True)
            low = (weights * (1.0 / total)).astype(LOW)
            probs[2 * pair + head] = low
            out.append(dot(turned[head * HEAD : (head + 1) * HEAD, :], low))
        mixed[:, at] = jnp.transpose(jnp.concatenate(out).astype(LOW))


def attend_backward(qkv, probs, mixed_grad, qkv_grad):
    width = mixed_grad.shape[1]
    for pair in range(width // PAIR):
        query = qkv[:, pl.ds(pair * PAIR, PAIR)]
        keys = qkv[:, pl.ds(width + pair * PAIR, PAIR)]
        values = qkv[:, pl.ds(2 * width + pair * PAIR, PAIR)]
        grad = mixed_grad[:, pl.ds(pair * PAIR, PAIR)]
        turned = jnp.transpose(keys)
        dq, dk, dv = [], [], []
        for head in range(2):
            low = probs[2 * pair + head]
            prob = low.astype(WIDE)
            prob_grad = dot_nt(values, lanes_of(head, grad))
            delta = jnp.sum(prob * prob_grad, axis=0, keepdims=True)
            score_grad = (prob * (prob_grad - delta)).astype(LOW)
            dv.append(dot(low, grad))
            dk.append(dot(score_grad, query))
            dq.append(dot(turned[head * HEAD : (head + 1) * HEAD, :], score_grad))
        scale = HEAD ** -0.5
        qkv_grad[:, pl.ds(pair * PAIR, PAIR)] = jnp.transpose((jnp.concatenate(dq) * scale).astype(LOW))
        qkv_grad[:, pl.ds(width + pair * PAIR, PAIR)] = (pick(*dk) * scale).astype(LOW)
        qkv_grad[:, pl.ds(2 * width + pair * PAIR, PAIR)] = pick(*dv).astype(LOW)


GELU = 0.7978845608028654


def gelu_and_slope(value):
    square = value * value
    t = jnp.tanh(value * (GELU + (GELU * 0.044715) * square))
    half = 0.5 + 0.5 * t
    slope = half + value * (0.5 - 0.5 * (t * t)) * (GELU + (3 * 0.044715 * GELU) * square)
    return value * half, slope


def ffn_forward(hidden, weight, active, slope, r):
    W = hidden.shape[1]
    total = None
    for c in range(4):
        at = pl.ds(c * W, W)
        act, sl = gelu_and_slope(dot(hidden, block(weight, c, r)))
        act = act.astype(LOW)
        active[:, at] = act
        slope[:, at] = sl.astype(LOW)
        part = dot(act, rows_block(weight, c, r))
        total = part if total is None else total + part
    return total


def ffn_backward_down(grad, active, put):
    W = grad.shape[1]
    for c in range(4):
        put(c, dot_tn(active[:, pl.ds(c * W, W)], grad).astype(LOW))


def ffn_backward_up(grad, hidden, weight, slope, r, put):
    W = grad.shape[1]
    turned = jnp.transpose(hidden)
    total = None
    for c in range(4):
        z = (dot_nt(grad, rows_block(weight, c, r)) * slope[:, pl.ds(c * W, W)].astype(WIDE)).astype(LOW)
        put(c, dot(turned, z).astype(LOW))
        part = dot_nt(z, block(weight, c, r))
        total = part if total is None else total + part
    return total


class Plan:
    def __init__(self, sizes, length, width):
        self.split = sizes == (8, 4)
        self.sizes = sizes
        self.length, self.width = length, width
        self.heads = width // HEAD
        self.shards = sizes[0]
        self.r = width // self.shards
        self.n = self.g = 2 if self.split else 1


    def lay(self, place, stacks, member, rows, unit, at):
        count = rows.stop - rows.start
        if not self.split:
            unit[:, at : at + count, :] = stacks[0][:, member, rows]
            return
        odd, chip = (place & 1) != 0, place >> 1
        for j in range(4):
            k = 2 * (j ^ chip) + member
            mine, other = stacks[0][k, rows, :], stacks[1][k, rows, :]
            unit[2 * j, at : at + count, :] = jnp.where(odd, other, mine)
            unit[2 * j + 1, at : at + count, :] = jnp.where(odd, mine, other)


    def grad_shapes(self, rows):
        if not self.split:
            return [(self.shards, 2, rows, self.width)]
        return [(8, rows, self.width)] * 2

    def leave(self, place, outs, member, at, value, first=0):
        count = value.shape[1]
        if not self.split:
            outs[0][first : first + value.shape[0], member, at : at + count, :] = value
            return
        odd, chip = (place & 1) != 0, place >> 1
        for j in range(value.shape[0] // 2):
            k = (first // 2 + j) ^ chip
            if member == 0:
                k = ((k & 1) << 1) | (k >> 1)
            one, two = value[2 * j], value[2 * j + 1]
            outs[0][4 * member + k, at : at + count, :] = jnp.where(odd, two, one)
            outs[1][4 * member + k, at : at + count, :] = jnp.where(odd, one, two)

    def leave_block(self, place, outs, member, i, value):
        self.leave(place, outs, member, i * self.r, value.reshape(self.shards, self.r, self.width))

    def leave_rows(self, place, outs, member, i, value):
        n = self.shards // 4
        self.leave(place, outs, member, 0, value.reshape(n, 4 * self.r, self.width), i * n)

    def leave_rows_halved(self, place, outs, i, value):
        n, half = self.shards // 4, 2 * self.r
        value = value.reshape(n, 4 * self.r, self.width)
        for m in range(2):
            self.leave(place, outs, m, 0, value[:, m * half : (m + 1) * half, :], i * n)

    def call(self, body, ins, outs, scratch, us, deps, room):
        def run(*refs):
            body(*refs[len(deps) :])

        return pl.pallas_call(
            run,
            in_specs=[ANY] * len(deps) + [spec for _, spec in ins],
            out_shape=[jax.ShapeDtypeStruct(shape, dtype) for shape, dtype in outs],
            out_specs=[VMEM] * len(outs),
            scratch_shapes=scratch,
            compiler_params=pltpu.CompilerParams(vmem_limit_bytes=room << 20),
            cost_estimate=pl.CostEstimate(flops=int(us * 5e9), bytes_accessed=1 << 20, transcendentals=0),
        )(*deps, *[value for value, _ in ins])


def vmem(*arrays):
    return [(v, VMEM) for v in arrays]


def self_attention(plan, place, tokens, ids, stacks, member, row, causal, deps=(), us=10, norms=None):
    L, W, H, r = plan.length, plan.width, plan.heads, plan.r

    given = norms is not None

    def body(place, tokens, ids, *rest):
        stacks, rest = rest[: plan.n], rest[plan.n :]
        if given:
            norms, out, out_low, normal, scale, qkv, mixed, probs, weight, bias = rest
        else:
            out, out_low, normal, scale, qkv, mixed, probs, weight, norms, bias = rest
        plan.lay(place[0], stacks, member, slice(0, 4 * r), weight, 0)
        bias[...] = allowed_bias(ids[...], ids[...], causal)
        if given:
            pass
        elif plan.split:
            norms[...] = sum(jnp.sum(s[...].astype(WIDE), axis=0) for s in (v.at[:, 4 * r : 4 * r + SMALL, :] for v in stacks)) * 0.5
        else:
            norms[...] = jnp.sum(stacks[0][:, member, 4 * r : 4 * r + SMALL].astype(WIDE), axis=0)
        x = tokens[...]
        for i in range(3):
            qkv[:, i * W : (i + 1) * W] = dot(x, block(weight, i, r)).astype(LOW)
        attend_forward(qkv, probs, mixed, bias)
        value = x.astype(WIDE) + dot(mixed[...], block(weight, 3, r))
        y, n, s = norm(value, norms[row : row + 1, :], norms[NORMS + row : NORMS + row + 1, :])
        out[...] = y
        out_low[...] = y.astype(LOW)
        normal[...] = n.astype(LOW)
        scale[...] = s

    ins = [(place, SMEM)] + vmem(tokens, ids, *stacks, *([norms] if given else []))
    outs = [((L, W), WIDE), ((L, W), LOW), ((L, W), LOW), ((L, 1), WIDE)]
    outs += [((L, 3 * W), LOW), ((L, W), LOW), ((H, L, L), LOW), ((plan.shards, 4 * r, W), LOW)]
    outs += [] if given else [((SMALL, W), WIDE)]
    return plan.call(body, ins, outs, [pltpu.VMEM((L, L), WIDE)], us, deps, 11)


def cross_attention(plan, place, query_in, query_low, memory_low, query_ids, memory_ids, stacks, norms, row, deps=()):
    L, W, H, r = plan.length, plan.width, plan.heads, plan.r

    def body(place, query_in, query_low, memory_low, query_ids, memory_ids, norms, *rest):
        stacks, rest = rest[: plan.n], rest[plan.n :]
        out, out_low, normal, scale, qkv, mixed, probs, weight, bias = rest
        for m in range(2):
            plan.lay(place[0], stacks, m, slice(0, 2 * r), weight, 2 * m * r)
        bias[...] = allowed_bias(memory_ids[...], query_ids[...], False)
        qkv[:, :W] = dot(query_low[...], block(weight, 0, r)).astype(LOW)
        memory = memory_low[...]
        for i in (1, 2):
            qkv[:, i * W : (i + 1) * W] = dot(memory, block(weight, i, r)).astype(LOW)
        attend_forward(qkv, probs, mixed, bias)
        value = query_in[...] + dot(mixed[...], block(weight, 3, r))
        y, n, s = norm(value, norms[row : row + 1, :], norms[NORMS + row : NORMS + row + 1, :])
        out[...] = y
        out_low[...] = y.astype(LOW)
        normal[...] = n.astype(LOW)
        scale[...] = s

    ins = [(place, SMEM)] + vmem(query_in, query_low, memory_low, query_ids, memory_ids, norms, *stacks)
    outs = [((L, W), WIDE), ((L, W), LOW), ((L, W), LOW), ((L, 1), WIDE)]
    outs += [((L, 3 * W), LOW), ((L, W), LOW), ((H, L, L), LOW), ((plan.shards, 4 * r, W), LOW)]
    return plan.call(body, ins, outs, [pltpu.VMEM((L, L), WIDE)], 10, deps, 11)


def encoder_ffn(plan, place, hidden, hidden_low, tokens, stacks, norms, row, deps=()):
    L, W, F, r = plan.length, plan.width, 4 * plan.width, plan.r

    def body(place, hidden, hidden_low, tokens, norms, *rest):
        stacks, rest = rest[: plan.n], rest[plan.n :]
        out_low, normal, scale, active, slope, weight = rest
        for m in range(2):
            plan.lay(place[0], stacks, m, slice(0, 4 * r), weight, 4 * m * r)
        branch = ffn_forward(hidden_low[...], weight, active, slope, r)
        value = hidden[...] + branch + tokens[...].astype(WIDE)
        y, n, s = norm(value, norms[row : row + 1, :], norms[NORMS + row : NORMS + row + 1, :])
        out_low[...] = y.astype(LOW)
        normal[...] = n.astype(LOW)
        scale[...] = s

    ins = [(place, SMEM)] + vmem(hidden, hidden_low, tokens, norms, *stacks)
    outs = [((L, W), LOW), ((L, W), LOW), ((L, 1), WIDE), ((L, F), LOW), ((L, F), LOW), ((plan.shards, 8 * r, W), LOW)]
    return plan.call(body, ins, outs, [], 9, deps, 11)


def decoder_ffn(plan, place, hidden, hidden_low, tokens, cotangent, stacks, norms, row, deps=()):
    L, W, F, r = plan.length, plan.width, 4 * plan.width, plan.r

    def body(place, hidden, hidden_low, tokens, cotangent, norms, *rest):
        stacks, rest = rest[: plan.n], rest[plan.n :]
        decoded, last_grad, norm_grads, slope, weight, *grads, active = rest
        for m in range(2):
            plan.lay(place[0], stacks, m, slice(0, 4 * r), weight, 4 * m * r)
        branch = ffn_forward(hidden_low[...], weight, active, slope, r)
        value = hidden[...] + branch + tokens[...].astype(WIDE)
        gain = norms[row : row + 1, :]
        y, n, s = norm(value, gain, norms[NORMS + row : NORMS + row + 1, :])
        decoded[...] = y.astype(LOW)
        grad, gain_grad, shift_grad = norm_back(cotangent[...].astype(WIDE), n, s, gain)
        last_grad[...] = grad
        norm_grads[0:1, :] = gain_grad
        norm_grads[1:2, :] = shift_grad
        ffn_backward_down(grad.astype(LOW), active, lambda i, v: plan.leave_rows_halved(place[0], grads, i, v))

    ins = [(place, SMEM)] + vmem(hidden, hidden_low, tokens, cotangent, norms, *stacks)
    outs = [((L, W), LOW), ((L, W), WIDE), ((2, W), WIDE), ((L, F), LOW), ((plan.shards, 8 * r, W), LOW)]
    outs += [(s, LOW) for s in plan.grad_shapes(2 * r)]
    got = plan.call(body, ins, outs, [pltpu.VMEM((L, F), LOW)], 12, deps, 16)
    return got[:5], got[5:]


def decoder_ffn_back(plan, place, grad, hidden_low, slope, hidden_normal, hidden_scale, weight, norms, row, deps=()):
    L, W, r = plan.length, plan.width, plan.r

    def body(place, grad, hidden_low, slope, hidden_normal, hidden_scale, weight, norms, out, norm_grads, *grads):
        def put(i, value):
            plan.leave(place[0], grads, i // 2, (i % 2) * r, value.reshape(plan.shards, r, W))

        back = ffn_backward_up(grad[...].astype(LOW), hidden_low[...], weight, slope, r, put)
        normal = hidden_normal[...].astype(WIDE)
        total, gain_grad, shift_grad = norm_back(grad[...] + back, normal, hidden_scale[...], norms[row : row + 1, :])
        out[...] = total
        norm_grads[0:1, :] = gain_grad
        norm_grads[1:2, :] = shift_grad

    ins = [(place, SMEM)] + vmem(grad, hidden_low, slope, hidden_normal, hidden_scale, weight, norms)
    outs = [((L, W), WIDE), ((2, W), WIDE)] + [(s, LOW) for s in plan.grad_shapes(2 * r)]
    got = plan.call(body, ins, outs, [], 8, deps, 12)
    return got[:2], got[2:]


def encoder_ffn_back(plan, place, grad, hidden_low, active, slope, hidden_normal, hidden_scale, weight, norms, row, deps=()):
    L, W, r = plan.length, plan.width, plan.r

    def body(place, grad, hidden_low, active, slope, hidden_normal, hidden_scale, weight, norms, *rest):
        zero_grad, norm_grads, *grads = rest
        grad_low = grad[...].astype(LOW)
        ffn_backward_down(grad_low, active, lambda i, v: plan.leave_rows(place[0], grads, 1, i, v))
        back = ffn_backward_up(
            grad_low, hidden_low[...], weight, slope, r, lambda i, v: plan.leave_block(place[0], grads, 0, i, v)
        )
        normal = hidden_normal[...].astype(WIDE)
        out, gain_grad, shift_grad = norm_back(grad[...] + back, normal, hidden_scale[...], norms[row : row + 1, :])
        zero_grad[...] = out
        norm_grads[0:1, :] = gain_grad
        norm_grads[1:2, :] = shift_grad

    ins = [(place, SMEM)] + vmem(grad, hidden_low, active, slope, hidden_normal, hidden_scale, weight, norms)
    outs = [((L, W), WIDE), ((2, W), WIDE)] + [(s, LOW) for s in plan.grad_shapes(4 * r)]
    got = plan.call(body, ins, outs, [], 11, deps, 14)
    return got[:2], got[2:]


def self_attention_back(plan, place, grad, tokens, kept, extra, deps=()):
    L, W, r = plan.length, plan.width, plan.r

    def body(place, grad, extra, tokens, qkv, mixed, probs, weight, *rest):
        total, *grads, mixed_grad, qkv_grad = rest
        grad_low = grad[...].astype(LOW)
        plan.leave_block(place[0], grads, 1, 1, dot_tn(mixed[...], grad_low).astype(LOW))
        mixed_grad[...] = dot_nt(grad_low, block(weight, 3, r)).astype(LOW)
        attend_backward(qkv, probs, mixed_grad, qkv_grad)
        x = jnp.transpose(tokens[...])
        for i in range(3):
            plan.leave_block(place[0], grads, i // 2, i % 2, dot(x, qkv_grad[:, i * W : (i + 1) * W]).astype(LOW))
        back = grad[...] + extra[...]
        for i in range(3):
            back += dot_nt(qkv_grad[:, i * W : (i + 1) * W], block(weight, i, r))
        total[...] = back

    ins = [(place, SMEM)] + vmem(grad, extra, tokens, *kept)
    outs = [((L, W), WIDE)] + [(s, LOW) for s in plan.grad_shapes(2 * r)]
    scratch = [pltpu.VMEM((L, W), LOW), pltpu.VMEM((L, 3 * W), LOW)]
    got = plan.call(body, ins, outs, scratch, 12, deps, 12)
    return got[0], got[1:]


def attend_backward_values(probs, mixed_grad, value_grad):
    for pair in range(mixed_grad.shape[1] // PAIR):
        at = pl.ds(pair * PAIR, PAIR)
        grad = mixed_grad[:, at]
        value_grad[:, at] = pick(*[dot(probs[2 * pair + head], grad) for head in range(2)]).astype(LOW)


def self_attention_back_values(plan, place, grad, tokens, kept, deps=()):
    L, W, r = plan.length, plan.width, plan.r
    _, mixed, probs, weight = kept

    def body(place, grad, tokens, mixed, probs, weight, mixed_grad, value_grad, *grads):
        grad_low = grad[...].astype(LOW)
        plan.leave_block(place[0], grads, 1, 0, dot_tn(mixed[...], grad_low).astype(LOW))
        mixed_grad[...] = dot_nt(grad_low, block(weight, 3, r)).astype(LOW)
        attend_backward_values(probs, mixed_grad, value_grad)
        plan.leave_block(place[0], grads, 0, 0, dot_tn(tokens[...], value_grad[...]).astype(LOW))

    ins = [(place, SMEM)] + vmem(grad, tokens, mixed, probs, weight)
    outs = [((L, W), LOW), ((L, W), LOW)] + [(s, LOW) for s in plan.grad_shapes(r)]
    got = plan.call(body, ins, outs, [], 6, deps, 12)
    return got[:2], got[2:]


def self_attention_back_scores(plan, place, grad, tokens, kept, mixed_grad, value_grad, extra, small, deps=()):
    L, W, r = plan.length, plan.width, plan.r
    qkv, _, probs, weight = kept

    def body(place, grad, extra, tokens, qkv, probs, weight, mixed_grad, value_grad, *rest):
        parts, (total, *grads, score_grads) = rest[:4], rest[4:]
        for m in range(2):
            rows = [parts[j][i + m : i + m + 1, :] for j, i in ((3, 0), (2, 2), (2, 0), (1, 0), (0, 0))]
            rows = jnp.concatenate(rows + [jnp.zeros((SMALL - NORMS, W), WIDE)]).astype(LOW)[None]
            plan.leave(place[0], grads, m, r, jnp.broadcast_to(rows, (plan.shards, SMALL, W)))
        scale = HEAD ** -0.5
        for pair in range(W // PAIR):
            at = pl.ds(pair * PAIR, PAIR)
            query, keys = qkv[:, at], qkv[:, pl.ds(W + pair * PAIR, PAIR)]
            values, out_grad = qkv[:, pl.ds(2 * W + pair * PAIR, PAIR)], mixed_grad[:, at]
            turned = jnp.transpose(keys)
            dq, dk = [], []
            for head in range(2):
                prob = probs[2 * pair + head].astype(WIDE)
                prob_grad = dot_nt(values, lanes_of(head, out_grad))
                delta = jnp.sum(prob * prob_grad, axis=0, keepdims=True)
                score_grad = (prob * (prob_grad - delta)).astype(LOW)
                dk.append(dot(score_grad, query))
                dq.append(dot(turned[head * HEAD : (head + 1) * HEAD, :], score_grad))
            score_grads[:, at] = jnp.transpose((jnp.concatenate(dq) * scale).astype(LOW))
            score_grads[:, pl.ds(W + pair * PAIR, PAIR)] = (pick(*dk) * scale).astype(LOW)
        x = jnp.transpose(tokens[...])
        back = grad[...] + extra[...] + dot_nt(value_grad[...], block(weight, 2, r))
        for i in range(2):
            part = score_grads[:, i * W : (i + 1) * W]
            plan.leave_block(place[0], grads, i, 0, dot(x, part).astype(LOW))
            back += dot_nt(part, block(weight, i, r))
        total[...] = back

    ins = [(place, SMEM)] + vmem(grad, extra, tokens, qkv, probs, weight, mixed_grad, value_grad, *small)
    outs = [((L, W), WIDE)] + [(s, LOW) for s in plan.grad_shapes(r + SMALL)]
    got = plan.call(body, ins, outs, [pltpu.VMEM((L, 2 * W), LOW)], 10, deps, 12)
    return got[0], got[1:]


def cross_attention_back(plan, place, grad, query_low, memory_low, kept, query_norm, memory_norm, norms, rows, deps=()):
    L, W, r = plan.length, plan.width, plan.r

    def body(place, grad, query_low, memory_low, qkv, mixed, probs, weight, query_n, query_r, memory_n, memory_r, norms, *rest):
        one_grad, enc_grad, norm_grads, *grads, mixed_grad, qkv_grad = rest
        grad_low = grad[...].astype(LOW)
        plan.leave_block(place[0], grads, 1, 1, dot_tn(mixed[...], grad_low).astype(LOW))
        mixed_grad[...] = dot_nt(grad_low, block(weight, 3, r)).astype(LOW)
        attend_backward(qkv, probs, mixed_grad, qkv_grad)
        plan.leave_block(place[0], grads, 0, 0, dot_tn(query_low[...], qkv_grad[:, :W]).astype(LOW))
        memory = jnp.transpose(memory_low[...])
        for i in (1, 2):
            value = dot(memory, qkv_grad[:, i * W : (i + 1) * W]).astype(LOW)
            plan.leave_block(place[0], grads, i // 2, i % 2, value)
        back = grad[...] + dot_nt(qkv_grad[:, :W], block(weight, 0, r))
        normal = query_n[...].astype(WIDE)
        out, gain_grad, shift_grad = norm_back(back, normal, query_r[...], norms[rows[0] : rows[0] + 1, :])
        one_grad[...] = out
        norm_grads[0:1, :] = gain_grad
        norm_grads[1:2, :] = shift_grad
        back = dot_nt(qkv_grad[:, W : 2 * W], block(weight, 1, r)) + dot_nt(qkv_grad[:, 2 * W :], block(weight, 2, r))
        normal = memory_n[...].astype(WIDE)
        out, gain_grad, shift_grad = norm_back(back, normal, memory_r[...], norms[rows[1] : rows[1] + 1, :])
        enc_grad[...] = out
        norm_grads[2:3, :] = gain_grad
        norm_grads[3:4, :] = shift_grad

    ins = [(place, SMEM)] + vmem(grad, query_low, memory_low, *kept, *query_norm, *memory_norm, norms)
    outs = [((L, W), WIDE), ((L, W), WIDE), ((4, W), WIDE)] + [(s, LOW) for s in plan.grad_shapes(2 * r)]
    scratch = [pltpu.VMEM((L, W), LOW), pltpu.VMEM((L, 3 * W), LOW)]
    got = plan.call(body, ins, outs, scratch, 0.05, deps, 13)
    return got[:3], got[3:]


def swap(value, bit):
    return lax.ppermute(value, "shard", [(i, i ^ bit) for i in range(8)])


def swap_rep(value, bit):
    return lax.ppermute(value, "rep", [(i, i ^ bit) for i in range(4)])


def local(body, ins, outs, deps=(), room=6, us=0):
    ins = [v if isinstance(v, tuple) else (v, VMEM) for v in ins]

    def run(*refs):
        body(*refs[len(deps) :])

    return pl.pallas_call(
        run,
        in_specs=[ANY] * len(deps) + [spec for _, spec in ins],
        out_shape=[jax.ShapeDtypeStruct(shape, dtype) for shape, dtype in outs],
        out_specs=[VMEM] * len(outs),
        compiler_params=pltpu.CompilerParams(vmem_limit_bytes=room << 20),
        cost_estimate=pl.CostEstimate(flops=int(us * 5e9), bytes_accessed=1 << 20, transcendentals=0),
    )(*deps, *[v for v, _ in ins])


def mark(out):
    out[...] = jnp.zeros_like(out)


def wait_for(plan, deps, us):
    return local(mark, [], [((8, 128), WIDE)], deps, 2, us) if plan.split else []


def pack_self(plan, attn_in, attn_out, small, odd):
    W, r = plan.width, plan.r

    def body(attn_in, attn_out, small, odd, out):
        for k in range(2):
            for i in range(3):
                out[k, i * r : (i + 1) * r, :] = attn_in[k, :, i * W : (i + 1) * W]
            out[k, 3 * r : 4 * r, :] = attn_out[k]
            out[k, 4 * r :, :] = small[...]

    return local(body, [attn_in, attn_out, small, (odd, SMEM)], [((2, 4 * r + SMALL, W), LOW)])[0]


def pack_rest(plan, attn_in, attn_out, ffn_up, ffn_down, deps):
    W, r = plan.width, plan.r

    def body(attn_in, attn_out, ffn_up, ffn_down, first, second):
        for k, out in enumerate((first, second)):
            for i in range(4):
                out[0, i * r : (i + 1) * r, :] = ffn_up[k, :, i * W : (i + 1) * W]
            out[1, : 4 * r] = ffn_down[k]
        for i in range(3):
            at = (4 + i % 2) * r
            first[i // 2, at : at + r, :] = attn_in[2, :, i * W : (i + 1) * W]
        first[1, 5 * r :, :] = attn_out[2]

    outs = [((2, 6 * r, W), LOW), ((2, 4 * r, W), LOW)]
    return local(body, [attn_in, attn_out, ffn_up, ffn_down], outs, deps)


class Gather:
    def __init__(self, plan, pair, parts):
        self.plan, self.pair, self.parts = plan, pair, parts
        self.ends = [sum(parts[: i + 1]) for i in range(len(parts))]
        if plan.split:
            self.near = [swap(pair, X), swap(pair, Y)]

    def onward(self, deps=()):
        if not self.plan.split:
            return []
        parts, ends = self.parts, self.ends

        def body(by_x, by_y, *outs):
            for i, (rows, end) in enumerate(zip(parts, ends)):
                outs[2 * i][...] = by_x[0, end - rows : end, :]
                outs[2 * i + 1][...] = by_y[1, end - rows : end, :]

        outs = local(body, self.near, [((rows, self.plan.width), LOW) for rows in parts for _ in range(2)], deps)
        self.far = [(swap(outs[2 * i], Y), swap(outs[2 * i + 1], X)) for i in range(len(parts))]
        return [outs[0]]

    def stack(self, part, deps=(), within=None):
        rows, end = self.parts[part], self.ends[part]
        within = within or slice(0, rows)
        at = slice(end - rows + within.start, end - rows + within.stop)
        rows = within.stop - within.start
        if not self.plan.split:
            return [lax.all_gather(self.pair[:, at], "shard", axis=0)], []

        def body(pair, by_x, by_y, first, second, out):
            for j, v in enumerate((pair, by_x, by_y)):
                out[2 * j : 2 * j + 2] = v[:, at, :]
            out[6] = first[within, :]
            out[7] = second[within, :]

        ins = [self.pair, *self.near, *self.far[part]]
        mine = local(body, ins, [((8, rows, self.plan.width), LOW)], deps)[0]
        return [mine, swap(mine, CORE)], [mine]


class Reduction:
    def __init__(self, plan, odd):
        self.plan, self.odd = plan, odd
        self.pairs, self.results = [], {}

    def add(self, name, outs):
        if not self.plan.split:
            whole = outs[0]
            flat = whole.reshape((-1,) + whole.shape[2:])
            own = lax.psum_scatter(flat, "shard", scatter_dimension=0, tiled=True)
            self.results[name] = lax.psum(own, "rep").astype(WIDE).reshape(whole.shape[1:])
            return
        mine, other = outs
        self.pairs.append(dict(name=name, rows=mine.shape[1], step=0, keep=mine, slot={}, moving={}, got=swap(other, CORE)))

    def advance(self, deps=(), only=(), never=()):
        pairs = [p for p in self.pairs if (not only or p["name"] in only) and p["name"] not in never]
        if not pairs:
            return []
        self.pairs = [p for p in self.pairs if p not in pairs]
        W = self.plan.width
        sizes = {"x": 0, "y": 0, "n": 0, "f": 0}

        def place(way, count):
            at = sizes[way]
            sizes[way] += count
            return at

        work = []
        for p in pairs:
            R, step = p["rows"], p["step"]
            ways = ({"x": 2 * R, "y": 2 * R}, {"x": R, "y": R}, {"n": R}, {"f": R}, {"n": R}, {})[step]
            work.append(dict(p, out={way: place(way, count) for way, count in ways.items()}, kept=((4, 2, 1, 1, 1, 2)[step] * R, W)))
        ways = [w for w in "xynf" if sizes[w]]
        came = []
        for p in pairs:
            came += [v for v in p["moving"].values() if not any(v is u for u in came)]
        cores = [t for t in work if t["step"] == 0]

        def body(odd, *refs):
            keep_in, refs = refs[: len(work)], refs[len(work) :]
            core_in, refs = refs[: len(cores)], refs[len(cores) :]
            arrived, refs = refs[: len(came)], refs[len(came) :]
            keep_out, refs = refs[: len(work)], refs[len(work) :]
            leave = dict(zip(ways, refs))
            odds = odd[0] != 0

            def total(left, right):
                return left + right

            core = iter(core_in)
            for t, keep, out in zip(work, keep_in, keep_out):
                R, step, slot, to = t["rows"], t["step"], t["slot"], t["out"]
                got = {w: arrived[[v is u for u in came].index(True)] for w, v in t["moving"].items() if w in slot}
                if step == 0:
                    other = next(core)
                    for m, way in enumerate("xy"):
                        at = 4 * m * R
                        out[2 * m * R : 2 * (m + 1) * R, :] = total(keep[at : at + 2 * R, :], other[at : at + 2 * R, :])
                        at += 2 * R
                        leave[way][to[way] : to[way] + 2 * R, :] = total(keep[at : at + 2 * R, :], other[at : at + 2 * R, :])
                elif step == 1:
                    for m, (way, onward) in enumerate(("xy", "yx")):
                        other, at, kept = got[way], slot[way], 2 * m * R
                        out[m * R : (m + 1) * R, :] = total(keep[kept : kept + R, :], other[at : at + R, :])
                        kept, at = kept + R, at + R
                        leave[onward][to[onward] : to[onward] + R, :] = total(keep[kept : kept + R, :], other[at : at + R, :])
                elif step == 2:
                    first = total(keep[:R, :], got["y"][slot["y"] : slot["y"] + R, :])
                    second = total(keep[R:, :], got["x"][slot["x"] : slot["x"] + R, :])
                    out[...] = jnp.where(odds, second, first)
                    leave["n"][to["n"] : to["n"] + R, :] = jnp.where(odds, first, second)
                elif step == 5:
                    mine, other = keep[...], got["n"][slot["n"] : slot["n"] + R, :]
                    out[:R, :] = jnp.where(odds, other, mine)
                    out[R:, :] = jnp.where(odds, mine, other)
                else:
                    way, onward = ("n", "f") if step == 3 else ("f", "n")
                    value = total(keep[...], got[way][slot[way] : slot[way] + R, :])
                    out[...] = value
                    leave[onward][to[onward] : to[onward] + R, :] = value

        if cores and came:
            last = [v for p in pairs if p["step"] == 5 for v in p["moving"].values()]
            if last:
                deps = wait_for(self.plan, [*deps, *[v for v in came if not any(v is u for u in last)]], 2)
            deps = wait_for(self.plan, [*deps, *came], 20)
        keeps = [t["keep"].reshape(-1, W) for t in work]
        gots = [t["got"].reshape(-1, W) for t in cores]
        outs = [(t["kept"], LOW) for t in work] + [((sizes[w], W), LOW) for w in ways]
        done = local(body, [(self.odd, SMEM), *keeps, *gots, *came], outs, deps)
        moving = {}
        for way, value in zip(ways, done[len(work) :]):
            moving[way] = swap_rep(value, Z1 if way == "n" else Z2) if way in "nf" else swap(value, X if way == "x" else Y)
        for t, kept in zip(work, done):
            if t["step"] == 5:
                self.results[t["name"]] = (kept, None, 0)
            elif t["step"] == 4 and t["name"] not in FINISHED:
                self.results[t["name"]] = (kept, moving["n"], t["out"]["n"])
            else:
                mine = {w: v for w, v in moving.items() if w in t["out"]}
                self.pairs.append(dict(name=t["name"], rows=t["rows"], step=t["step"] + 1, keep=kept, slot=t["out"], moving=mine))
        return [done[0]]


FINISHED = ("f1u", "f1d")
NAMES = ("a0", "a0v", "a1", "a2", "f0", "f1u", "f1d")


def outputs(plan, sums, place):
    W, r = plan.width, plan.r
    wide = W // plan.shards
    results = sums.results
    if not plan.split:
        me = lax.axis_index("shard")
        scores, small = results["a0"][:, :r], results["a0"][:, r:]
        small = lax.dynamic_slice(small, (0, 0, me * wide), (2, NORMS, wide))
        att = [jnp.concatenate([scores, results["a0v"]]), *(results[k].reshape(4, r, W) for k in ("a1", "a2"))]
        att, ffn = jnp.stack(att), jnp.stack([results["f0"], jnp.stack([results[k].reshape(4 * r, W) for k in ("f1u", "f1d")])])

        def unblocks(v):
            return jnp.moveaxis(v, 1, 2).reshape(v.shape[0], r, -1)

        return unblocks(att[:, :3]), att[:, 3], unblocks(ffn[:, 0].reshape(2, 4, r, W)), ffn[:, 1], small[0], small[1]
    keeps = [results[k][0] for k in NAMES]
    gots = []
    for k in NAMES:
        if k not in FINISHED and not any(results[k][1] is v for v in gots):
            gots.append(results[k][1])

    def body(odd, place, *refs):
        keep, refs = refs[: len(NAMES)], refs[len(NAMES) :]
        got, refs = refs[: len(gots)], refs[len(gots) :]
        attn_in, attn_out, ffn_up, ffn_down, gain, shift = refs
        odds = odd[0] != 0

        def member(name, m, at, rows):
            _, array, offset = results[name]
            i = NAMES.index(name)
            if name in FINISHED:
                at += m * (keep[i].shape[0] // 2)
                return keep[i][at : at + rows, :].astype(WIDE)
            j = [v is array for v in gots].index(True)
            kept, other = keep[i][at : at + rows, :], got[j][offset + at : offset + at + rows, :]
            return (jnp.where(odds, other, kept) if m == 0 else jnp.where(odds, kept, other)).astype(WIDE)

        for i in range(2):
            attn_in[0, :, i * W : (i + 1) * W] = member("a0", i, 0, r)
        attn_in[0, :, 2 * W :] = member("a0v", 0, 0, r)
        attn_out[0] = member("a0v", 1, 0, r)
        for a, name in ((1, "a1"), (2, "a2")):
            for i in range(3):
                attn_in[a, :, i * W : (i + 1) * W] = member(name, i // 2, (i % 2) * r, r)
            attn_out[a] = member(name, 1, r, r)
        for i in range(4):
            ffn_up[0, :, i * W : (i + 1) * W] = member("f0", 0, i * r, r)
            ffn_up[1, :, i * W : (i + 1) * W] = member("f1u", i // 2, (i % 2) * r, r)
        ffn_down[0] = member("f0", 1, 0, 4 * r)
        for m in range(2):
            ffn_down[1, 2 * m * r : 2 * (m + 1) * r] = member("f1d", m, 0, 2 * r)
        turn = lax.rem(W - place[0] * wide, W)
        for m, out in enumerate((gain, shift)):
            out[...] = pltpu.roll(member("a0", m, r, SMALL), turn, axis=1)[:NORMS, :wide]

    outs = [((3, r, 3 * W), WIDE), ((3, r, W), WIDE), ((2, r, 4 * W), WIDE), ((2, 4 * r, W), WIDE)] + [((NORMS, wide), WIDE)] * 2
    return local(body, [(sums.odd, SMEM), (place, SMEM), *keeps, *gots], outs, room=16)


def shards(sizes, source, target, source_seg, target_seg, attn_in, attn_out, ffn_up, ffn_down, norm_gain, norm_bias, cotangent):
    plan = Plan(sizes, source.shape[1], source.shape[2])
    W, r = plan.width, plan.r
    me = lax.axis_index("shard")
    place = (me if plan.split else jnp.zeros_like(me))[None]
    src, tgt = source[0], target[0]

    small = jnp.concatenate([norm_gain, norm_bias])
    small = lax.dynamic_update_slice(jnp.zeros((SMALL, W), LOW), small, (0, me * small.shape[1]))
    odd = (lax.axis_index("rep") & 1).astype(jnp.int32)[None]
    pair = pack_self(plan, attn_in, attn_out, small, odd)
    att = Gather(plan, pair, (4 * r + SMALL,))
    rest_pair, last_pair = pack_rest(plan, attn_in, attn_out, ffn_up, ffn_down, [pair])
    rest = Gather(plan, rest_pair, (6 * r,))
    went = att.onward()
    went = rest.onward(wait_for(plan, went, 4))
    last = Gather(plan, after(last_pair, went), (4 * r,))
    self_w, stacked = att.stack(0, went)
    first, first_low, n0, r0, *kept_enc, norms = self_attention(
        plan, place, src, source_seg, self_w, 0, 0, False, wait_for(plan, stacked, 6), 0.05
    )
    one, one_low, n2, r2, *kept_self = self_attention(
        plan, place, tgt, target_seg, self_w, 1, 2, True, [r0], 10, norms
    )
    went = last.onward([r2])
    ffn_w, stacked = rest.stack(0, went, slice(0, 4 * r))
    cross_w, stacked = rest.stack(0, stacked, slice(4 * r, 6 * r))
    enc_low, n1, r1, active, slope, w_f0 = encoder_ffn(
        plan, place, first, first_low, src, ffn_w, norms, 1, [r2] + stacked
    )
    last_w, stacked = last.stack(0, [r1])
    two, two_low, n3, r3, *kept_cross = cross_attention(
        plan, place, one, one_low, enc_low, target_seg, source_seg, cross_w, norms, 3, stacked
    )
    (decoded, last_grad, norm_a, slope_f1, w_f1), grads = decoder_ffn(
        plan, place, two, two_low, tgt, cotangent[0], last_w, norms, 4
    )
    sums = Reduction(plan, odd)
    sums.add("f1d", grads)
    (two_grad, norm_d), grads = decoder_ffn_back(
        plan, place, last_grad, two_low, slope_f1, n3, r3, w_f1, norms, 3
    )
    deps = sums.advance([norm_d], ["f1d"])
    sums.add("f1u", grads)
    deps = sums.advance(deps, ["f1u"])
    (one_grad, enc_grad, norm_b), grads = cross_attention_back(
        plan, place, two_grad, one_low, enc_low, kept_cross, (n2, r2), (n1, r1), norms, (2, 1), deps
    )
    sums.add("a2", grads)
    deps = sums.advance([norm_b])
    (zero_grad, norm_c), grads = encoder_ffn_back(
        plan, place, enc_grad, first_low, active, slope, n0, r0, w_f0, norms, 0, deps
    )
    sums.add("f0", grads)
    deps = sums.advance([norm_c])
    tgt_grad, grads = self_attention_back(plan, place, one_grad, tgt, kept_self, last_grad, deps)
    sums.add("a1", grads)
    deps = sums.advance(grads[:1], ["f1u", "f1d"])
    halfway, grads = self_attention_back_values(plan, place, zero_grad, src, kept_enc, deps)
    sums.add("a0v", grads)
    deps = sums.advance([halfway[0]], never=["f1u", "f1d"])
    src_grad, grads = self_attention_back_scores(
        plan, place, zero_grad, src, kept_enc, *halfway, enc_grad, (norm_a, norm_d, norm_b, norm_c), deps
    )
    sums.add("a0", grads)
    deps = sums.advance(grads[:1], ["f1u", "f1d"])
    sums.advance(deps or grads[:1])
    while sums.pairs:
        sums.advance()
    return decoded[None], src_grad[None], tgt_grad[None], *outputs(plan, sums, place)


def after(value, deps):
    if not deps:
        return value

    def body(*refs):
        pass

    return pl.pallas_call(
        body,
        in_specs=[ANY] * (1 + len(deps)),
        out_shape=jax.ShapeDtypeStruct(value.shape, value.dtype),
        out_specs=ANY,
        input_output_aliases={0: 0},
        compiler_params=pltpu.CompilerParams(vmem_limit_bytes=1 << 20),
        cost_estimate=pl.CostEstimate(flops=0, bytes_accessed=0, transcendentals=0),
    )(value, *deps)


def solution(mesh):
    sizes = (mesh.shape["shard"], mesh.shape["rep"])
    tokens = P(("shard", "rep"), None, None)
    ids = P(("shard", "rep"), None)
    weight = P(None, "shard", None)
    norm = P(None, "shard")
    return jax.shard_map(
        functools.partial(shards, sizes),
        mesh=mesh,
        in_specs=(tokens, tokens, ids, ids, weight, weight, weight, weight, norm, norm, tokens),
        out_specs=(tokens, tokens, tokens, weight, weight, weight, weight, norm, norm),
        check_vma=False,
    )
```
